32 devices in a mesh: batch: 8 (over z, x), height: 4 (over y, core).
Axes of the slice: x: 2, y: 2, z: 4, core: 2. Of those that a mesh axis runs over, the one named last changes fastest.
Arguments:
- inputs: bfloat16 [16, 24, 32, 512], P('batch', 'height'), may hold values from -13 to 13
- bucket: int32 [16], P('batch'), may hold values from 0 to 2, as said below
- norm1_gain: float32 [512], replicated, may hold values from 0.1 to 1.9
- norm1_shift: float32 [512], replicated, may hold values from -3 to 3
- conv1_weight: bfloat16 [4608, 512], replicated, may hold values from -0.09375 to 0.09375
- conv1_bias: float32 [512], replicated, may hold values from -3 to 3
- norm2_gain: float32 [512], replicated, may hold values from 0.1 to 1.9
- norm2_shift: float32 [512], replicated, may hold values from -3 to 3
- conv2_weight: bfloat16 [4608, 512], replicated, may hold values from -0.09375 to 0.09375
- conv2_bias: float32 [512], replicated, may hold values from -3 to 3
- norm3_gain: float32 [512], replicated, may hold values from 0.1 to 1.9
- norm3_shift: float32 [512], replicated, may hold values from -3 to 3
- query_weight: bfloat16 [512, 512], replicated, may hold values from -0.375 to 0.375
- query_bias: float32 [512], replicated, may hold values from -3 to 3
- key_weight: bfloat16 [512, 512], replicated, may hold values from -0.375 to 0.375
- value_weight: bfloat16 [512, 512], replicated, may hold values from -0.25 to 0.25
- value_bias: float32 [512], replicated, may hold values from -3 to 3
- proj_weight: bfloat16 [512, 512], replicated, may hold values from -1 to 1
- proj_bias: float32 [512], replicated, may hold values from -1.75 to 1.75
- cotangent: bfloat16 [16, 24, 32, 512], P('batch', 'height'), may hold values from -6 to 6
Outputs:
- outputs: bfloat16 [16, 24, 32, 512], P('batch', 'height')
- input_grad: bfloat16 [16, 24, 32, 512], P('batch', 'height')
- grad_norm1_gain: float32 [512], P('batch')
- grad_norm1_shift: float32 [512], P('batch')
- grad_conv1_weight: float32 [4608, 512], P('batch')
- grad_conv1_bias: float32 [512], P('batch')
- grad_norm2_gain: float32 [512], P('batch')
- grad_norm2_shift: float32 [512], P('batch')
- grad_conv2_weight: float32 [4608, 512], P('batch')
- grad_conv2_bias: float32 [512], P('batch')
- grad_norm3_gain: float32 [512], P('batch')
- grad_norm3_shift: float32 [512], P('batch')
- grad_query_weight: float32 [512, 512], P('batch')
- grad_query_bias: float32 [512], P('batch')
- grad_key_weight: float32 [512, 512], P('batch')
- grad_value_weight: float32 [512, 512], P('batch')
- grad_value_bias: float32 [512], P('batch')
- grad_proj_weight: float32 [512, 512], P('batch')
- grad_proj_bias: float32 [512], P('batch')
The draws below stay inside these ranges and needn't reach their ends.
Inputs may be any that keep to these rules, and one draw needn't show every extreme that they name: Among the 2 images on each index of batch, at least one is of bucket 1.
All inputs are finite; a program needn't handle non-finite values.
Results may differ from the reference program's by a relative error of at most 0.025.
Values may be sent and summed in bfloat16 or wider, within the bound.
No kernel may reach another device: no remote copies, remote signals or barrier semaphores. Data moves between devices by JAX's collectives and lax.ppermute only.
A program may use at most 128 MiB of HBM per device.

```python
import jax
import jax.numpy as jnp
from jax import lax

C = 512
GROUPS = 32
UNIT = 8
IMG_DEV = 2
HP = 24
WP = 32
IMAGES = 16


def draw_inputs(key, part):
    key = jax.random.fold_in(key, 11)
    key_noise, key_shift = jax.random.split(key)
    row_frac = jnp.arange(HP, dtype=jnp.float32)[None, :, None, None] / (HP - 1)
    channel_shift = jnp.clip(jax.random.normal(key_shift, (IMAGES, 1, 1, C), jnp.float32), -3.0, 3.0)
    noise_draw = jnp.clip(jax.random.normal(key_noise, (IMAGES, HP, WP, C), jnp.float32), -5.0, 5.0)
    row_scale = 0.5 + 1.5 * row_frac
    return (noise_draw * row_scale + 0.8 * row_frac * channel_shift).astype(jnp.bfloat16)


def draw_bucket(key, part):
    key = jax.random.fold_in(key, 5)
    key_base, key_pick = jax.random.split(key)
    batch_groups = IMAGES // IMG_DEV
    drawn = jax.random.randint(key_base, (batch_groups, IMG_DEV), 0, 3)
    picked = jax.random.randint(key_pick, (batch_groups, 1), 0, IMG_DEV)
    slots = lax.broadcasted_iota(jnp.int32, (batch_groups, IMG_DEV), 1)
    return jnp.where(slots == picked, 1, drawn).reshape(IMAGES).astype(jnp.int32)


def block_levels(own_key, extent, cuts, least, top_value):
    loudness = 1.0
    for position, shards_of in cuts:
        draws = jax.random.uniform(jax.random.fold_in(jax.random.fold_in(own_key, 6), position), (shards_of,), jnp.float32, least / len(cuts), top_value / len(cuts))
        loudness = loudness * jnp.repeat(jnp.exp(draws), extent[position] // shards_of).reshape((-1,) + (1,) * (len(extent) - 1 - position))
    return loudness


def normal_values(stream_key, extent, width, most, cuts=(), kind=jnp.bfloat16):
    result = jax.random.normal(stream_key, extent, jnp.float32) * width
    if len(cuts) > 0:
        result = block_levels(stream_key, extent, cuts, -0.22, 0.18) * result
    return jnp.clip(result, min=-most, max=most).astype(kind)


def setup_inputs(seed: int = 0) -> dict:
    splits = jax.random.split(jax.random.key(seed), 21)
    inputs = draw_inputs(jax.random.fold_in(splits[20], 71), 0)
    bucket = draw_bucket(jax.random.fold_in(splits[20], 71), 0)
    norm1_gain = jnp.clip(1.0 + 0.18 * jax.random.normal(splits[2], (C,), jnp.float32), 0.1, 1.9)
    norm1_shift = normal_values(splits[3], (C,), 0.5, 3.0, (), jnp.float32)
    conv1_weight = normal_values(splits[4], (9 * C, C), (9 * C) ** -0.5, 0.09375)
    conv1_bias = normal_values(splits[5], (C,), 0.5, 3.0, (), jnp.float32)
    norm2_gain = jnp.clip(1.0 + 0.18 * jax.random.normal(splits[6], (C,), jnp.float32), 0.1, 1.9)
    norm2_shift = normal_values(splits[7], (C,), 0.5, 3.0, (), jnp.float32)
    conv2_weight = normal_values(splits[8], (9 * C, C), (9 * C) ** -0.5, 0.09375)
    conv2_bias = normal_values(splits[9], (C,), 0.5, 3.0, (), jnp.float32)
    norm3_gain = jnp.clip(1.0 + 0.18 * jax.random.normal(splits[10], (C,), jnp.float32), 0.1, 1.9)
    norm3_shift = normal_values(splits[11], (C,), 0.5, 3.0, (), jnp.float32)
    query_weight = normal_values(splits[12], (C, C), (C // 2) ** -0.5, 0.375)
    query_bias = normal_values(splits[13], (C,), 0.5, 3.0, (), jnp.float32)
    key_weight = normal_values(splits[14], (C, C), (C // 2) ** -0.5, 0.375)
    value_weight = normal_values(splits[15], (C, C), C ** -0.5, 0.25)
    value_bias = normal_values(splits[16], (C,), 0.5, 3.0, (), jnp.float32)
    proj_weight = normal_values(splits[17], (C, C), (C // 16) ** -0.5, 1.0)
    proj_bias = normal_values(splits[18], (C,), 0.3, 1.75, (), jnp.float32)
    cotangent = normal_values(splits[19], (IMAGES, HP, WP, C), 1.0, 6.0, ((0, 8), (1, 4)))
    return {"inputs": inputs, "bucket": bucket, "norm1_gain": norm1_gain, "norm1_shift": norm1_shift, "conv1_weight": conv1_weight, "conv1_bias": conv1_bias, "norm2_gain": norm2_gain, "norm2_shift": norm2_shift, "conv2_weight": conv2_weight, "conv2_bias": conv2_bias, "norm3_gain": norm3_gain, "norm3_shift": norm3_shift, "query_weight": query_weight, "query_bias": query_bias, "key_weight": key_weight, "value_weight": value_weight, "value_bias": value_bias, "proj_weight": proj_weight, "proj_bias": proj_bias, "cotangent": cotangent}


@jax.custom_vjp
def low(v):
    return lax.optimization_barrier(v.astype(jnp.bfloat16)).astype(jnp.float32)

@jax.custom_vjp
def low_back(v):
    return v

def low_keep(v):
    return (low(v), None)

def low_pass(kept, grad):
    return (grad,)

def back_keep(v):
    return (v, None)

def back_low(kept, grad):
    return (low(grad),)
low.defvjp(low_keep, low_pass)
low_back.defvjp(back_keep, back_low)
epsilon = 1e-05
highest = lax.Precision.HIGHEST

def image_inside(bucket):
    heights = jnp.where(bucket == 1, 3 * UNIT, 2 * UNIT)
    widths = jnp.where(bucket == 0, 3 * UNIT, jnp.where(bucket == 1, 2 * UNIT, 4 * UNIT))
    row_ids = lax.broadcasted_iota(jnp.int32, (1, HP, 1), 1)
    col_ids = lax.broadcasted_iota(jnp.int32, (1, 1, WP), 2)
    inside = (row_ids < heights[:, None, None]) & (col_ids < widths[:, None, None])
    group_size = (heights * widths * (C // GROUPS)).astype(jnp.float32)
    return (inside.astype(jnp.float32), group_size)

def group_norm(values, inside4, group_size, norm_gain, norm_shift):
    images = values.shape[0]
    grouped = values.reshape(images, HP * WP, GROUPS, C // GROUPS)
    weights = inside4.reshape(images, HP * WP, 1, 1)
    mean_value = lax.optimization_barrier(jnp.sum(grouped * weights, axis=(1, 3))) / group_size[:, None]
    centered = grouped - mean_value[:, None, :, None]
    variance = lax.optimization_barrier(jnp.sum(centered * centered * weights, axis=(1, 3))) / group_size[:, None]
    normal = centered * lax.rsqrt(variance + epsilon)[:, None, :, None]
    return normal.reshape(values.shape) * norm_gain + norm_shift

def convolve(activation, weight):
    padded = jnp.pad(activation, ((0, 0), (1, 1), (1, 1), (0, 0)))
    stacked = jnp.concatenate([padded[:, row_step:row_step + HP, col_step:col_step + WP, :] for row_step in range(3) for col_step in range(3)], axis=-1)
    return jnp.einsum('ihwk,kc->ihwc', stacked, weight, precision=highest)

def layer(start_act, params, inside, group_size):
    norm1_gain, norm1_shift, conv1_weight, conv1_bias, norm2_gain, norm2_shift, conv2_weight, conv2_bias, norm3_gain, norm3_shift, query_weight, query_bias, key_weight, value_weight, value_bias, proj_weight, proj_bias = params
    images = start_act.shape[0]
    inside4 = inside[..., None]
    kept_input = inside4 * start_act
    first_act = low(inside4 * jax.nn.silu(group_norm(kept_input, inside4, group_size, norm1_gain, norm1_shift)))
    first_conv = low_back(convolve(first_act, conv1_weight) + conv1_bias)
    second_act = low(inside4 * jax.nn.silu(group_norm(first_conv, inside4, group_size, norm2_gain, norm2_shift)))
    second_conv = low_back(convolve(second_act, conv2_weight) + conv2_bias)
    middle = inside4 * (kept_input + second_conv)
    normed = low(group_norm(middle, inside4, group_size, norm3_gain, norm3_shift)).reshape(images, HP * WP, C)
    queries = low(low_back(jnp.einsum('ipc,cd->ipd', normed, query_weight, precision=highest) + query_bias))
    key_rows = low(low_back(jnp.einsum('ipc,cd->ipd', normed, key_weight, precision=highest)))
    values = low(low_back(jnp.einsum('ipc,cd->ipd', normed, value_weight, precision=highest) + value_bias))
    scores = low_back(jnp.einsum('iqc,ikc->iqk', queries, key_rows, precision=highest) * C ** (-0.5))
    scores = jnp.where(inside.reshape(images, 1, HP * WP) > 0.5, scores, -1000000000.0)
    highest_score = lax.optimization_barrier(jnp.max(scores, axis=-1, keepdims=True))
    raised = jnp.exp(scores - highest_score)
    soft_weights = low(raised / lax.optimization_barrier(jnp.sum(raised, axis=-1, keepdims=True)))
    mixed_rows = low(low_back(jnp.einsum('iqk,ikc->iqc', soft_weights, values, precision=highest)))
    projected = jnp.einsum('iqc,cd->iqd', mixed_rows, proj_weight, precision=highest) + proj_bias
    return inside4 * (middle + projected.reshape(start_act.shape))

def reference(inputs, bucket, norm1_gain, norm1_shift, conv1_weight, conv1_bias, norm2_gain, norm2_shift, conv2_weight, conv2_bias, norm3_gain, norm3_shift, query_weight, query_bias, key_weight, value_weight, value_bias, proj_weight, proj_bias, cotangent):
    params = tuple((param.astype(jnp.float32) for param in (norm1_gain, norm1_shift, conv1_weight, conv1_bias, norm2_gain, norm2_shift, conv2_weight, conv2_bias, norm3_gain, norm3_shift, query_weight, query_bias, key_weight, value_weight, value_bias, proj_weight, proj_bias)))
    blocks = IMAGES // 4

    def block_step(running, slices_in):
        start_act, block_bucket, block_cot = slices_in
        inside, group_size = image_inside(block_bucket)

        def forward(activation, *weights):
            return layer(activation, weights, inside, group_size)
        output, pullback = jax.vjp(forward, start_act, *params)
        gradients = pullback(block_cot)
        running = tuple((running_sum + block_part for running_sum, block_part in zip(running, gradients[1:])))
        return (running, (output.astype(jnp.bfloat16), gradients[0].astype(jnp.bfloat16)))
    zeros_init = tuple((jnp.zeros_like(param) for param in params))
    slices_in = (inputs.astype(jnp.float32).reshape(blocks, 4, HP, WP, C), bucket.reshape(blocks, 4), cotangent.astype(jnp.float32).reshape(blocks, 4, HP, WP, C))
    sums, (outputs, input_grad) = lax.scan(block_step, zeros_init, slices_in)
    return (outputs.reshape(IMAGES, HP, WP, C), input_grad.reshape(IMAGES, HP, WP, C), sums[0], sums[1], sums[2], sums[3], sums[4], sums[5], sums[6], sums[7], sums[8], sums[9], sums[10], sums[11], sums[12], sums[13], sums[14], sums[15], sums[16])
```

```python
import functools

import jax
import jax.numpy as jnp
from jax import lax
from jax.experimental import pallas as pl
from jax.experimental.pallas import tpu as pltpu
from jax.sharding import PartitionSpec as P

GROUPS = 32
UNIT = 8
PIX = 512
PAD = 32
BLK = 128
F32 = jnp.float32
BF16 = jnp.bfloat16
epsilon = 1e-05

VM = pl.BlockSpec(memory_space=pltpu.VMEM)
SM = pl.BlockSpec(memory_space=pltpu.SMEM)


def place(bucket_ref):
    h = lax.axis_index("height")
    upper = lax.div(h, 2)
    tall_first = bucket_ref[0] == 1
    tall_image = jnp.where(tall_first, 0, 1)
    home = jnp.where(upper == 1, tall_image, 1 - tall_image)
    away = 1 - home

    def facts(image):
        kind = bucket_ref[image]
        tall = kind == 1
        stride = jnp.where(tall, 2 * UNIT, 4 * UNIT)
        width = jnp.where(kind == 0, 3 * UNIT, stride)
        return (image, tall, stride, width)

    return h, facts(home), facts(away)


def pixel_col(stride, lanes=1):
    rows = lax.broadcasted_iota(jnp.int32, (PIX, lanes), 0)
    return rows, rows & (stride - 1)


def pixel_mask(facts):
    unused, tall, stride, width = facts
    rows, cols = pixel_col(stride)
    limit = jnp.where(tall, 6 * UNIT * UNIT, 8 * UNIT * UNIT)
    mask = jnp.where((cols < width) & (rows < limit), 1.0, 0.0).astype(F32)
    size = jnp.where(tall | (width == 3 * UNIT), 6 * UNIT * UNIT, 8 * UNIT * UNIT)
    return mask, size.astype(F32)


def group_total(row):
    channels = row.shape[-1]
    lane = lax.broadcasted_iota(jnp.int32, row.shape, 1)
    step = 1
    while step < channels // GROUPS:
        up = pltpu.roll(row, channels - step, 1)
        down = pltpu.roll(row, step, 1)
        row = row + jnp.where((lane & step) == 0, up, down)
        step *= 2
    return row


def total(values):
    return jnp.sum(values, axis=0, keepdims=True)


def wide_total(row):
    return group_total(jnp.broadcast_to(row, (8, row.shape[-1])))[0:1]


def norm_stats(values, mask, group_size):
    mean = wide_total(total(values * mask)) / group_size
    centered = values - mean
    variance = wide_total(total(centered * centered * mask)) / group_size
    return mean, lax.rsqrt(variance + epsilon)


def norm_back(grad, normal, inverse, mask, group_size, gain):
    scaled = grad * gain
    plain = wide_total(total(scaled)) / group_size
    cross = wide_total(total(scaled * normal)) / group_size
    grad_in = inverse * (scaled - mask * (plain + normal * cross))
    return grad_in, total(grad * normal), total(grad)


def sigmoid(u):
    return 1.0 / (1.0 + jnp.exp(-u))


def silu_slope(u):
    s = sigmoid(u)
    return s * (1.0 + u * (1.0 - s))


def mm(a, b):
    return jnp.dot(a, b, preferred_element_type=F32)


def mm_nt(a, b):
    return lax.dot_general(a, b, (((1,), (1,)), ((), ())), preferred_element_type=F32)


def mm_tn(a, b):
    return lax.dot_general(a, b, (((0,), (0,)), ((), ())), preferred_element_type=F32)


def fill_shifts(shift_ref, values, stride):
    unused, cols = pixel_col(stride)
    lanes = values.shape[1]
    zeros = jnp.zeros((PAD, lanes), BF16)
    for q in range(3):
        shift_ref[q, 0:PAD, :] = zeros
        shift_ref[q, PAD + PIX : 2 * PAD + PIX, :] = zeros
    left = jnp.where(cols == 0, 0.0, pltpu.roll(values, 1, 0))
    right = jnp.where(cols == stride - 1, 0.0, pltpu.roll(values, PIX - 1, 0))
    shift_ref[0, PAD : PAD + PIX, :] = left.astype(BF16)
    shift_ref[1, PAD : PAD + PIX, :] = values.astype(BF16)
    shift_ref[2, PAD : PAD + PIX, :] = right.astype(BF16)


def tap(shift_ref, p, q, stride, first=0, count=PIX):
    start = pl.multiple_of(PAD + first + (p - 1) * stride, 16)
    return shift_ref[q, pl.ds(start, count), :]


def conv_forward(shift_ref, weight_ref, stride, out_ref, tile=256):
    for first in range(0, PIX, tile):
        stacked = jnp.concatenate(
            [tap(shift_ref, p, q, stride, first, tile) for p in range(3) for q in range(3)], axis=1
        )
        out_ref[first : first + tile, :] = mm(stacked, weight_ref[...])


def conv_backward(shift_ref, weight_ref, stride, out_ref, tile=256):
    channels = weight_ref.shape[1]
    for first in range(0, PIX, tile):
        acc = None
        for p in range(3):
            for q in range(3):
                row = (8 - (3 * p + q)) * channels
                part = mm_nt(
                    tap(shift_ref, p, q, stride, first, tile), weight_ref[row : row + channels, :]
                )
                acc = part if acc is None else acc + part
        out_ref[first : first + tile, :] = acc


def assemble(out_ref, facts, h, pieces):
    unused, tall, stride, width = facts
    own, partner, received, partner_received = pieces
    other = h ^ 1

    @pl.when(tall)
    def _():
        for ref, index in (
            (own, h),
            (partner, other),
            (received, h ^ 2),
            (partner_received, other ^ 2),
        ):
            out_ref[pl.ds(pl.multiple_of(96 * index, 16), 96), :] = ref[0:96, :]
        out_ref[384:512, :] = jnp.zeros((128, out_ref.shape[1]), out_ref.dtype)

    @pl.when(jnp.logical_not(tall))
    def _():
        low = h & 1
        out_ref[pl.ds(pl.multiple_of(192 * low, 16), 192), :] = own[...]
        out_ref[pl.ds(pl.multiple_of(192 * (1 - low), 16), 192), :] = partner[...]

        @pl.when(low == 0)
        def _():
            out_ref[384:512, :] = received[...]

        @pl.when(low == 1)
        def _():
            out_ref[384:512, :] = partner_received[...]


def split_out(full_ref, facts, h, own_ref, send_ref):
    unused, tall, stride, width = facts
    send_h = h ^ 2

    @pl.when(tall)
    def _():
        own_ref[0:96, :] = full_ref[pl.ds(pl.multiple_of(96 * h, 16), 96), :]
        own_ref[96:192, :] = jnp.zeros((96, own_ref.shape[1]), own_ref.dtype)
        send_ref[0:96, :] = full_ref[pl.ds(pl.multiple_of(96 * send_h, 16), 96), :]
        send_ref[96:128, :] = jnp.zeros((32, own_ref.shape[1]), own_ref.dtype)

    @pl.when(jnp.logical_not(tall))
    def _():
        own_ref[...] = full_ref[pl.ds(pl.multiple_of(192 * (h & 1), 16), 192), :]
        send_ref[...] = full_ref[384:512, :]


def pack_kernel(bucket_ref, x_ref, cot_ref, away_x, home_x, away_c, home_c):
    h, home, away = place(bucket_ref)
    for src, away_ref, home_ref in ((x_ref, away_x, home_x), (cot_ref, away_c, home_c)):
        for facts, dst, wide_rows in ((away, away_ref, 4), (home, home_ref, 6)):
            image, tall, stride, width = facts

            @pl.when(tall)
            def _():
                for row in range(6):
                    dst[16 * row : 16 * row + 16, :] = src[image, row, 0:16, :]
                dst[96 : dst.shape[0], :] = jnp.zeros((dst.shape[0] - 96, dst.shape[1]), dst.dtype)

            @pl.when(jnp.logical_not(tall))
            def _():
                for row in range(wide_rows):
                    dst[32 * row : 32 * row + 32, :] = src[image, row]


def first_kernel(
    bucket_ref, own, partner, received, partner_received,
    gain1, shift1, weight1, bias1, gain2, shift2,
    image_ref, conv_ref, act1_t, act2_t, act2_ref, stats_ref, send_t,
    shift_ref,
):
    h, home, away = place(bucket_ref)
    stride = home[2]
    mask, pixels = pixel_mask(home)
    channels = gain1.shape[1]
    group_size = pixels * (channels // GROUPS)
    assemble(image_ref, home, h, (own, partner, received, partner_received))
    values = image_ref[...].astype(F32) * mask
    mean1, inverse1 = norm_stats(values, mask, group_size)
    u = (values - mean1) * inverse1 * gain1[...] + shift1[...]
    act = u * sigmoid(u) * mask
    fill_shifts(shift_ref, act, stride)
    act1_t[...] = act.astype(BF16).T
    conv_forward(shift_ref, weight1, stride, conv_ref)
    values = conv_ref[...] + bias1[...]
    conv_ref[...] = values
    mean2, inverse2 = norm_stats(values, mask, group_size)
    u = (values - mean2) * inverse2 * gain2[...] + shift2[...]
    act = (u * sigmoid(u) * mask).astype(BF16)
    act2_ref[...] = act
    act2_t[...] = act.T
    half = pl.multiple_of((h & 1) * (channels // 2), 16)
    send_t[0] = act1_t[pl.ds(half, channels // 2), :]
    send_t[1] = act2_t[pl.ds(half, channels // 2), :]
    stats_ref[0:1, :] = mean1
    stats_ref[1:2, :] = inverse1
    stats_ref[2:3, :] = mean2
    stats_ref[3:4, :] = inverse2
    stats_ref[4:8, :] = jnp.zeros((4, channels), F32)


def second_kernel(
    bucket_ref, image_ref, act2_ref, own, partner, received, partner_received,
    weight2, bias2, gain3, shift3, wq, bq, wk, wv, bv, wp, bp,
    out_own, out_send, grad2_ref, grad_middle_ref, attn_keep, attn_send, vec_ref,
    block_keep, block_send,
    shift_ref, full_ref, middle_ref, scratch,
):
    h, home, away = place(bucket_ref)
    stride = home[2]
    mask, pixels = pixel_mask(home)
    channels = gain3.shape[1]
    group_size = pixels * (channels // GROUPS)
    scaling = channels ** (-0.5)
    fill_shifts(shift_ref, act2_ref[...].astype(F32), stride)
    conv_forward(shift_ref, weight2, stride, middle_ref)
    middle = mask * (image_ref[...].astype(F32) + (middle_ref[...] + bias2[...]))
    middle_ref[...] = middle
    mean3, inverse3 = norm_stats(middle, mask, group_size)
    normal = (middle - mean3) * inverse3
    normed = (normal * gain3[...] + shift3[...]).astype(BF16)
    queries = (mm(normed, wq[...]) + bq[...]).astype(BF16)
    keys = mm(normed, wk[...]).astype(BF16)
    values = (mm(normed, wv[...]) + bv[...]).astype(BF16)
    lanes = lax.broadcasted_iota(jnp.int32, (1, PIX), 1)
    key_cols = lanes & (stride - 1)
    key_valid = (key_cols < home[3]) & (lanes < jnp.where(home[1], 384, 512))
    scores = jnp.where(key_valid, mm_nt(queries, keys) * scaling, -1000000000.0)
    raised = jnp.exp(scores - jnp.max(scores, axis=1, keepdims=True))
    soft = raised * (1.0 / jnp.sum(raised, axis=1, keepdims=True))
    soft16 = soft.astype(BF16)
    mixed = mm(soft16, values).astype(BF16)
    projected = mm(mixed, wp[...]) + bp[...]
    full_ref[...] = (mask * (middle_ref[...] + projected)).astype(BF16)
    split_out(full_ref, home, h, out_own, out_send)

    assemble(full_ref, home, h, (own, partner, received, partner_received))
    grad_top = full_ref[...].astype(F32) * mask
    grad_rows = grad_top.astype(BF16)
    grad_mixed = mm_nt(grad_rows, wp[...]).astype(BF16)
    grad_soft = mm_nt(grad_mixed, values)
    grad_values = mm_tn(soft16, grad_mixed).astype(BF16)
    grad_scores = soft * (grad_soft - jnp.sum(soft * grad_soft, axis=1, keepdims=True))
    grad_scores = grad_scores.astype(BF16)
    grad_queries = (mm(grad_scores, keys) * scaling).astype(BF16)
    grad_keys = (mm_tn(grad_scores, queries) * scaling).astype(BF16)
    grad_normed = (
        mm_nt(grad_queries, wq[...]) + mm_nt(grad_keys, wk[...]) + mm_nt(grad_values, wv[...])
    )
    grad_in, gain_grad, shift_grad = norm_back(
        grad_normed, normal, inverse3, mask, group_size, gain3[...]
    )
    grad_middle = mask * (grad_top + grad_in)
    grad_middle_ref[...] = grad_middle
    grad2 = grad_middle.astype(BF16)
    grad2_ref[...] = grad2
    vec_ref[0:1, :] = gain_grad
    vec_ref[1:2, :] = shift_grad
    vec_ref[2:3, :] = total(grad_queries.astype(F32))
    vec_ref[3:4, :] = total(grad_values.astype(F32))
    vec_ref[4:5, :] = total(grad_top)
    vec_ref[5:6, :] = total(grad2.astype(F32))
    vec_ref[6:8, :] = jnp.zeros((2, channels), F32)

    keep_at = pl.multiple_of(BLK * h, BLK)
    send_at = pl.multiple_of(BLK * (h ^ 2), BLK)
    block_keep[...] = grad2_ref[:, pl.ds(keep_at, BLK)]
    block_send[...] = grad2_ref[:, pl.ds(send_at, BLK)]
    for index, grad in enumerate((grad_queries, grad_keys, grad_values, grad_rows)):
        scratch[...] = grad
        column = (index % 3) * 2 * BLK
        full_ref[:, 0:BLK] = scratch[:, pl.ds(keep_at, BLK)]
        full_ref[:, BLK : 2 * BLK] = scratch[:, pl.ds(send_at, BLK)]
        result = mm_tn(mixed if index == 3 else normed, full_ref[:, 0 : 2 * BLK]).astype(BF16)
        attn_keep[index] = result[:, 0:BLK]
        attn_send[index] = result[:, BLK : 2 * BLK]


def third_kernel(
    bucket_ref, grad2_ref, conv_ref, stats_ref, weight2, gain2, shift2,
    grad1_ref, block_keep, block_send, vec_ref,
    shift_ref, acc_ref,
):
    h, home, away = place(bucket_ref)
    stride = home[2]
    mask, pixels = pixel_mask(home)
    channels = gain2.shape[1]
    group_size = pixels * (channels // GROUPS)
    fill_shifts(shift_ref, grad2_ref[...].astype(F32), stride)
    conv_backward(shift_ref, weight2, stride, acc_ref)
    inverse = stats_ref[3:4, :]
    normal = (conv_ref[...] - stats_ref[2:3, :]) * inverse
    u = normal * gain2[...] + shift2[...]
    grad = mask * acc_ref[...] * silu_slope(u)
    grad_in, gain_grad, shift_grad = norm_back(grad, normal, inverse, mask, group_size, gain2[...])
    grad1 = grad_in.astype(BF16)
    grad1_ref[...] = grad1
    vec_ref[0:1, :] = gain_grad
    vec_ref[1:2, :] = shift_grad
    vec_ref[2:3, :] = total(grad1.astype(F32))
    vec_ref[3:8, :] = jnp.zeros((5, channels), F32)
    block_keep[...] = grad1_ref[:, pl.ds(pl.multiple_of(BLK * h, BLK), BLK)]
    block_send[...] = grad1_ref[:, pl.ds(pl.multiple_of(BLK * (h ^ 2), BLK), BLK)]


def fourth_kernel(
    bucket_ref, grad1_ref, image_ref, stats_ref, grad_middle_ref, weight1, gain1, shift1,
    grad_own, grad_send, vec_ref,
    shift_ref, acc_ref, full_ref,
):
    h, home, away = place(bucket_ref)
    stride = home[2]
    mask, pixels = pixel_mask(home)
    channels = gain1.shape[1]
    group_size = pixels * (channels // GROUPS)
    fill_shifts(shift_ref, grad1_ref[...].astype(F32), stride)
    conv_backward(shift_ref, weight1, stride, acc_ref)
    inverse = stats_ref[1:2, :]
    normal = (image_ref[...].astype(F32) * mask - stats_ref[0:1, :]) * inverse
    u = normal * gain1[...] + shift1[...]
    grad = mask * acc_ref[...] * silu_slope(u)
    grad_in, gain_grad, shift_grad = norm_back(grad, normal, inverse, mask, group_size, gain1[...])
    full_ref[...] = (mask * (grad_middle_ref[...] + grad_in)).astype(BF16)
    vec_ref[0:1, :] = gain_grad
    vec_ref[1:2, :] = shift_grad
    vec_ref[2:8, :] = jnp.zeros((6, channels), F32)
    split_out(full_ref, home, h, grad_own, grad_send)


def weight_kernel(
    bucket_ref, act_t, half_t, partner_half_t, block_own, block_away,
    keep_ref, send_ref,
    left_ref, right_ref, shift_ref, sum_ref,
):
    h, home, away = place(bucket_ref)
    channels = act_t.shape[0]
    half = channels // 2
    left_ref[:, 0:PIX] = act_t[...]
    left_ref[pl.ds(pl.multiple_of((h & 1) * half, 16), half), PIX : 2 * PIX] = half_t[...]
    left_ref[pl.ds(pl.multiple_of((1 - (h & 1)) * half, 16), half), PIX : 2 * PIX] = partner_half_t[...]
    for index, (facts, block) in enumerate(((home, block_own), (away, block_away))):
        stride = facts[2]
        fill_shifts(shift_ref, block[...].astype(F32), stride)
        for p in range(3):
            for q in range(3):
                column = (3 * p + q) * BLK
                right_ref[index * PIX : (index + 1) * PIX, column : column + BLK] = tap(
                    shift_ref, 2 - p, 2 - q, stride
                )
    for t in range(0, 9):
        sum_ref[t * channels : (t + 1) * channels, :] = mm(
            left_ref[...], right_ref[:, t * BLK : (t + 1) * BLK]
        )
    mine = lax.axis_index("batch") & 1
    pairs, rows = keep_ref.shape[0], keep_ref.shape[1]
    for pair in range(pairs):
        keep_ref[pair] = sum_ref[pl.ds(pl.multiple_of((2 * pair + mine) * rows, 8), rows), :].astype(BF16)
        send_ref[pair] = sum_ref[pl.ds(pl.multiple_of((2 * pair + 1 - mine) * rows, 8), rows), :].astype(BF16)


def unpack_kernel(bucket_ref, out_own, out_away, grad_own, grad_away, out_ref, grad_ref):
    h, home, away = place(bucket_ref)
    for own, received, dst in ((out_own, out_away, out_ref), (grad_own, grad_away, grad_ref)):
        channels = dst.shape[3]
        for facts, src, wide_rows in ((away, received, 4), (home, own, 6)):
            image, tall, stride, width = facts

            @pl.when(tall)
            def _():
                for row in range(6):
                    dst[image, row, 0:16, :] = src[16 * row : 16 * row + 16, :]
                    dst[image, row, 16:32, :] = jnp.zeros((16, channels), dst.dtype)

            @pl.when(jnp.logical_not(tall))
            def _():
                for row in range(wide_rows):
                    dst[image, row] = src[32 * row : 32 * row + 32, :]
                for row in range(wide_rows, 6):
                    dst[image, row] = jnp.zeros((32, channels), dst.dtype)

            if wide_rows == 4:

                @pl.when(jnp.logical_not(tall) & (h == 3))
                def _():
                    for row in range(6):
                        dst[image, row] = jnp.zeros((32, channels), dst.dtype)


def call(kernel, name, outs, scratch, flops, nbytes, *operands):
    return pl.pallas_call(
        kernel,
        name=name,
        out_shape=[jax.ShapeDtypeStruct(shape, dtype) for shape, dtype in outs],
        in_specs=[SM] + [VM] * (len(operands) - 1),
        out_specs=[VM] * len(outs),
        scratch_shapes=[pltpu.VMEM(shape, dtype) for shape, dtype in scratch],
        compiler_params=pltpu.CompilerParams(vmem_limit_bytes=48 * 1024 * 1024),
        cost_estimate=pl.CostEstimate(flops=flops, bytes_accessed=nbytes, transcendentals=0),
    )(*operands)


def on_device(
    inputs,
    bucket,
    norm1_gain,
    norm1_shift,
    conv1_weight,
    conv1_bias,
    norm2_gain,
    norm2_shift,
    conv2_weight,
    conv2_bias,
    norm3_gain,
    norm3_shift,
    query_weight,
    query_bias,
    key_weight,
    value_weight,
    value_bias,
    proj_weight,
    proj_bias,
    cotangent,
):
    channels = inputs.shape[-1]
    batches = lax.axis_size("batch")
    bits = batches.bit_length() - 1
    shard_rows = 9 * channels // batches
    small_rows = channels // batches
    C = channels

    def row(v):
        return v.reshape(1, channels)

    def to_core(v):
        return lax.ppermute(v, "height", [(i, i ^ 1) for i in range(4)])

    def to_chip(v):
        return lax.ppermute(v, "height", [(i, i ^ 2) for i in range(4)])

    def to_batch(v, bit):
        return lax.ppermute(v, "batch", [(i, i ^ (1 << bit)) for i in range(batches)])

    img16 = ((PIX, C), BF16)
    img32 = ((PIX, C), F32)
    vec = ((8, C), F32)
    block = ((PIX, BLK), BF16)
    shifts = ((3, PIX + 2 * PAD, C), BF16)
    unit = 2 * PIX * C * C

    away_x, home_x, away_c, home_c = call(
        pack_kernel, "pack",
        [((128, C), BF16), ((192, C), BF16), ((128, C), BF16), ((192, C), BF16)],
        [], 0, 1 << 21, bucket, inputs, cotangent,
    )
    recv_x = to_chip(away_x)
    core_x = to_core(home_x)
    recv_c = to_chip(away_c)
    core_c = to_core(home_c)
    core_recv_x = to_core(recv_x)
    core_recv_c = to_core(recv_c)

    image, conv, act1_t, act2_t, act2, stats, send_t = call(
        first_kernel, "first",
        [img16, img32, ((C, PIX), BF16), ((C, PIX), BF16), img16, vec, ((2, C // 2, PIX), BF16)],
        [shifts], 9 * unit, 9 << 20,
        bucket, home_x, core_x, recv_x, core_recv_x, row(norm1_gain), row(norm1_shift),
        conv1_weight, row(conv1_bias), row(norm2_gain), row(norm2_shift),
    )
    half_t = to_chip(send_t)
    core_half_t = to_core(half_t)

    out_own, out_send, grad2, grad_middle, attn_keep, attn_send, vec_a, block2, block2_send = call(
        second_kernel, "second",
        [((192, C), BF16), ((128, C), BF16), img16, img32, ((4, C, BLK), BF16), ((4, C, BLK), BF16),
         vec, block, block],
        [shifts, img16, img32, img16], 32 * unit, 12 << 20,
        bucket, image, act2, home_c, core_c, recv_c, core_recv_c,
        conv2_weight, row(conv2_bias), row(norm3_gain), row(norm3_shift),
        query_weight, row(query_bias), key_weight, value_weight, row(value_bias),
        proj_weight, row(proj_bias),
    )
    block2_away = to_chip(block2_send)
    attn_recv = to_chip(attn_send)
    out_away = to_chip(out_send)

    grad1, block1, block1_send, vec_b = call(
        third_kernel, "third",
        [img16, block, block, vec],
        [shifts, img32], 9 * unit, 9 << 20,
        bucket, grad2, conv, stats, conv2_weight, row(norm2_gain), row(norm2_shift),
    )
    block1_away = to_chip(block1_send)

    def weight_grad(name, act_t, index, own, away):
        return call(
            weight_kernel, name,
            [((batches // 2, shard_rows, BLK), BF16)] * 2,
            [((C, 2 * PIX), BF16), ((2 * PIX, 9 * BLK), BF16), ((3, PIX + 2 * PAD, BLK), BF16),
             ((9 * C, BLK), F32)],
            5 * unit, 4 << 20,
            bucket, act_t, half_t[index], core_half_t[index], own, away,
        )

    keep2, send2 = weight_grad("weight2", act2_t, 1, block2, block2_away)
    attn = attn_keep.astype(F32) + attn_recv.astype(F32)
    attn = attn.astype(BF16).reshape(4, batches // 2, 2, small_rows, BLK)
    me = lax.axis_index("batch")

    def pick(v, axis, bit):
        mine = (me >> bit) & 1
        return (
            lax.dynamic_index_in_dim(v, mine, axis, keepdims=False),
            lax.dynamic_index_in_dim(v, 1 - mine, axis, keepdims=False),
        )

    attn_mine, attn_other = pick(attn, 2, 0)

    def lay(v):
        return jnp.transpose(v, (1, 0, 2, 3)).reshape(batches // 2, 4 * small_rows, BLK)

    def scatter(keep, send):
        bit = 0
        while True:
            got = to_batch(send, bit)
            added = (keep.astype(F32) + got.astype(F32)).astype(BF16)
            bit += 1
            if bit == bits:
                return added[0]
            added = added.reshape(added.shape[0] // 2, 2, *added.shape[1:])
            keep, send = pick(added, 1, bit)

    shard2 = scatter(
        jnp.concatenate([keep2, lay(attn_mine)], axis=1),
        jnp.concatenate([send2, lay(attn_other)], axis=1),
    )

    grad_own, grad_send, vec_c = call(
        fourth_kernel, "fourth",
        [((192, C), BF16), ((128, C), BF16), vec],
        [shifts, img32, img16], 9 * unit, 9 << 20,
        bucket, grad1, image, stats, grad_middle, conv1_weight, row(norm1_gain), row(norm1_shift),
    )
    grad_away = to_chip(grad_send)

    keep1, send1 = weight_grad("weight1", act1_t, 0, block1, block1_away)
    vectors = jnp.concatenate([vec_a[:6], vec_b[:3], vec_c[:2]], axis=0)
    count = vectors.shape[0]
    vec_rows = -(-count * small_rows // BLK)
    vec_rows = -(-vec_rows // 8) * 8
    vectors = jnp.transpose(vectors.reshape(count, batches, small_rows), (1, 0, 2))
    vectors = vectors.reshape(batches, count * small_rows)
    vectors = jnp.pad(vectors, ((0, 0), (0, vec_rows * BLK - count * small_rows)))
    vectors = vectors.astype(BF16).reshape(batches // 2, 2, vec_rows, BLK)
    vec_mine, vec_other = pick(vectors, 1, 0)
    shard1 = scatter(
        jnp.concatenate([keep1, vec_mine], axis=1),
        jnp.concatenate([send1, vec_other], axis=1),
    )

    def gather(shard):
        h = lax.axis_index("height")
        far = to_chip(shard)
        near_pair = jnp.where(h < 2, jnp.stack([shard, far]), jnp.stack([far, shard]))
        core_pair = to_core(near_pair)
        odd = (h & 1) == 1
        even_part = jnp.where(odd, core_pair, near_pair)
        odd_part = jnp.where(odd, near_pair, core_pair)
        return jnp.concatenate([even_part[0], odd_part[0], even_part[1], odd_part[1]], axis=-1).astype(F32)

    whole2 = gather(shard2)
    whole1 = gather(shard1)
    tail = whole1[shard_rows:].reshape(vec_rows, 4, BLK)
    sums = (tail[:, 0] + tail[:, 2]).reshape(vec_rows * BLK)
    v = [sums[i * small_rows : (i + 1) * small_rows] for i in range(count)]
    small = [whole2[shard_rows + i * small_rows : shard_rows + (i + 1) * small_rows] for i in range(4)]

    outputs, input_grad = call(
        unpack_kernel, "unpack",
        [(inputs.shape, BF16)] * 2, [], 0, 1 << 21,
        bucket, out_own, out_away, grad_own, grad_away,
    )
    return (
        outputs, input_grad,
        v[9], v[10], whole1[:shard_rows], v[8],
        v[6], v[7], whole2[:shard_rows], v[5],
        v[0], v[1],
        small[0], v[2], small[1], small[2], v[3], small[3], v[4],
    )


def solution(mesh):
    image = P("batch", "height", None, None)
    vector = P("batch")
    matrix = P("batch", None)
    return jax.shard_map(
        on_device,
        mesh=mesh,
        in_specs=(image, vector) + (P(),) * 17 + (image,),
        out_specs=(
            image, image,
            vector, vector, matrix, vector,
            vector, vector, matrix, vector,
            vector, vector,
            matrix, vector, matrix, matrix, vector, matrix, vector,
        ),
        check_vma=False,
    )
```

```python
import functools

import jax
import jax.numpy as jnp
from jax import lax
from jax.experimental import pallas as pl
from jax.experimental.pallas import tpu as pltpu
from jax.sharding import PartitionSpec as P

GROUPS = 32
UNIT = 8
PIX = 512
PAD = 32
BLK = 128
F32 = jnp.float32
BF16 = jnp.bfloat16
epsilon = 1e-05

VM = pl.BlockSpec(memory_space=pltpu.VMEM)
SM = pl.BlockSpec(memory_space=pltpu.SMEM)
HB = pl.BlockSpec(memory_space=pl.ANY)
RATE = 1 << 30
LENGTH = {
    "pack": 1, "first": 6, "second": 11, "third": 5, "fourth": 5, "weight2": 3, "weight1": 3, "unpack": 2,
}


def place(bucket_ref):
    h = lax.axis_index("height")
    upper = lax.div(h, 2)
    tall_first = bucket_ref[0] == 1
    tall_image = jnp.where(tall_first, 0, 1)
    home = jnp.where(upper == 1, tall_image, 1 - tall_image)
    away = 1 - home

    def facts(image):
        kind = bucket_ref[image]
        tall = kind == 1
        stride = jnp.where(tall, 2 * UNIT, 4 * UNIT)
        width = jnp.where(kind == 0, 3 * UNIT, stride)
        return (image, tall, stride, width)

    return h, facts(home), facts(away)


def pixel_col(stride, lanes=1):
    rows = lax.broadcasted_iota(jnp.int32, (PIX, lanes), 0)
    return rows, rows & (stride - 1)


def pixel_mask(facts):
    unused, tall, stride, width = facts
    rows, cols = pixel_col(stride)
    limit = jnp.where(tall, 6 * UNIT * UNIT, 8 * UNIT * UNIT)
    mask = jnp.where((cols < width) & (rows < limit), 1.0, 0.0).astype(F32)
    size = jnp.where(tall | (width == 3 * UNIT), 6 * UNIT * UNIT, 8 * UNIT * UNIT)
    return mask, size.astype(F32)


def group_total(row):
    channels = row.shape[-1]
    lane = lax.broadcasted_iota(jnp.int32, row.shape, 1)
    step = 1
    while step < channels // GROUPS:
        up = pltpu.roll(row, channels - step, 1)
        down = pltpu.roll(row, step, 1)
        row = row + jnp.where((lane & step) == 0, up, down)
        step *= 2
    return row


def total(values):
    return jnp.sum(values, axis=0, keepdims=True)


def wide_total(row):
    return group_total(jnp.broadcast_to(row, (8, row.shape[-1])))[0:1]


def norm_stats(values, mask, group_size):
    mean = wide_total(total(values)) / group_size
    centered = (values - mean) * mask
    variance = wide_total(total(centered * centered)) / group_size
    return mean, lax.rsqrt(variance + epsilon)


def silu_norm(values, mean, inverse, gain, shift, mask):
    scale = 0.5 * inverse * gain
    half = values * scale + (0.5 * shift - mean * scale)
    return (half + half * jnp.tanh(half)) * mask


def norm_back(grad, normal, inverse, mask, group_size, gain):
    plain_row = total(grad)
    cross_row = total(grad * normal)
    plain = wide_total(plain_row * gain) / group_size
    cross = wide_total(cross_row * gain) / group_size
    grad_in = grad * (inverse * gain) - mask * (plain * inverse + normal * (cross * inverse))
    return grad_in, cross_row, plain_row


def silu_slope(u):
    half = 0.5 * u
    t = jnp.tanh(half)
    return (0.5 + 0.5 * t) * (1.0 + half * (1.0 - t))


def mm(a, b):
    return jnp.dot(a, b, preferred_element_type=F32)


def mm_nt(a, b):
    return lax.dot_general(a, b, (((1,), (1,)), ((), ())), preferred_element_type=F32)


def mm_tn(a, b):
    return lax.dot_general(a, b, (((0,), (0,)), ((), ())), preferred_element_type=F32)


def fill_shifts(shift_ref, values, stride):
    unused, cols = pixel_col(stride)
    lanes = values.shape[1]
    zeros = jnp.zeros((PAD, lanes), BF16)
    for q in range(3):
        shift_ref[q, 0:PAD, :] = zeros
        shift_ref[q, PAD + PIX : 2 * PAD + PIX, :] = zeros
    left = jnp.where(cols == 0, 0.0, pltpu.roll(values, 1, 0))
    right = jnp.where(cols == stride - 1, 0.0, pltpu.roll(values, PIX - 1, 0))
    shift_ref[0, PAD : PAD + PIX, :] = left.astype(BF16)
    shift_ref[1, PAD : PAD + PIX, :] = values.astype(BF16)
    shift_ref[2, PAD : PAD + PIX, :] = right.astype(BF16)


def tap(shift_ref, p, q, stride, first=0, count=PIX):
    start = pl.multiple_of(PAD + first + (p - 1) * stride, 16)
    return shift_ref[q, pl.ds(start, count), :]


def conv_forward(shift_ref, weight_ref, stride, out_ref, tile=256):
    for first in range(0, PIX, tile):
        stacked = jnp.concatenate(
            [tap(shift_ref, p, q, stride, first, tile) for p in range(3) for q in range(3)], axis=1
        )
        out_ref[first : first + tile, :] = mm(stacked, weight_ref[...])


def conv_backward(shift_ref, weight_ref, stride, out_ref, tile=256):
    channels = weight_ref.shape[1]
    for first in range(0, PIX, tile):
        acc = None
        for p in range(3):
            for q in range(3):
                row = (8 - (3 * p + q)) * channels
                part = mm_nt(
                    tap(shift_ref, p, q, stride, first, tile), weight_ref[row : row + channels, :]
                )
                acc = part if acc is None else acc + part
        out_ref[first : first + tile, :] = acc


def assemble(out_ref, facts, h, pieces):
    unused, tall, stride, width = facts
    own, partner, received, partner_received = pieces
    other = h ^ 1

    @pl.when(tall)
    def _():
        for ref, index in (
            (own, h),
            (partner, other),
            (received, h ^ 2),
            (partner_received, other ^ 2),
        ):
            out_ref[pl.ds(pl.multiple_of(96 * index, 16), 96), :] = ref[0:96, :]
        out_ref[384:512, :] = jnp.zeros((128, out_ref.shape[1]), out_ref.dtype)

    @pl.when(jnp.logical_not(tall))
    def _():
        low = h & 1
        out_ref[pl.ds(pl.multiple_of(192 * low, 16), 192), :] = own[...]
        out_ref[pl.ds(pl.multiple_of(192 * (1 - low), 16), 192), :] = partner[...]

        @pl.when(low == 0)
        def _():
            out_ref[384:512, :] = received[...]

        @pl.when(low == 1)
        def _():
            out_ref[384:512, :] = partner_received[...]


def split_out(full_ref, facts, h, own_ref, send_ref):
    unused, tall, stride, width = facts
    send_h = h ^ 2

    @pl.when(tall)
    def _():
        own_ref[0:96, :] = full_ref[pl.ds(pl.multiple_of(96 * h, 16), 96), :]
        own_ref[96:192, :] = jnp.zeros((96, own_ref.shape[1]), own_ref.dtype)
        send_ref[0:96, :] = full_ref[pl.ds(pl.multiple_of(96 * send_h, 16), 96), :]
        send_ref[96:128, :] = jnp.zeros((32, own_ref.shape[1]), own_ref.dtype)

    @pl.when(jnp.logical_not(tall))
    def _():
        own_ref[...] = full_ref[pl.ds(pl.multiple_of(192 * (h & 1), 16), 192), :]
        send_ref[...] = full_ref[384:512, :]


GAIN1, SHIFT1, BIAS1, GAIN2, SHIFT2, BIAS2, GAIN3, SHIFT3, QB, VB, PB = range(11)
VECS = 16


def vec(vec_ref, index):
    return vec_ref[index : index + 1, :]


def pack_kernel(bucket_ref, x_ref, cot_ref, kinds, away_x, home_x, away_c, home_c, sems):
    h, home, away = place(bucket_ref)
    kinds[0] = bucket_ref[0]
    kinds[1] = bucket_ref[1]

    def each(act):
        slot = 0
        for src, away_ref, home_ref in ((x_ref, away_x, home_x), (cot_ref, away_c, home_c)):
            for facts, dst, wide_rows in ((away, away_ref, 4), (home, home_ref, 6)):
                image, tall, stride, width = facts

                @pl.when(tall)
                def _():
                    for row in range(6):
                        act(
                            src.at[image, row, pl.ds(0, 16), :],
                            dst.at[pl.ds(16 * row, 16), :],
                            sems.at[slot + row],
                        )

                @pl.when(jnp.logical_not(tall))
                def _():
                    for row in range(wide_rows):
                        act(src.at[image, row], dst.at[pl.ds(32 * row, 32), :], sems.at[slot + row])

                slot += 6

    each(lambda a, b, sem: pltpu.make_async_copy(a, b, sem).start())
    each(lambda a, b, sem: pltpu.make_async_copy(a, b, sem).wait())


def first_kernel(
    bucket_ref, own, partner, received, partner_received, vecs, weight1,
    image_ref, conv_ref, act2_ref, stats_ref, act1_t, act2_t, send1_t, send2_t,
    shift_ref,
):
    h, home, away = place(bucket_ref)
    stride = home[2]
    mask, pixels = pixel_mask(home)
    channels = vecs.shape[1]
    group_size = pixels * (channels // GROUPS)
    assemble(image_ref, home, h, (own, partner, received, partner_received))
    values = image_ref[...].astype(F32) * mask
    mean1, inverse1 = norm_stats(values, mask, group_size)
    act = silu_norm(values, mean1, inverse1, vec(vecs, GAIN1), vec(vecs, SHIFT1), mask)
    fill_shifts(shift_ref, act, stride)
    act1_t[...] = act.astype(BF16).T
    conv_forward(shift_ref, weight1, stride, conv_ref)
    values = (conv_ref[...] + vec(vecs, BIAS1)) * mask
    conv_ref[...] = values
    mean2, inverse2 = norm_stats(values, mask, group_size)
    act = silu_norm(values, mean2, inverse2, vec(vecs, GAIN2), vec(vecs, SHIFT2), mask)
    act = act.astype(BF16)
    act2_ref[...] = act
    act2_t[...] = act.T
    half = pl.multiple_of((h & 1) * (channels // 2), 16)
    send1_t[...] = act1_t[pl.ds(half, channels // 2), :]
    send2_t[...] = act2_t[pl.ds(half, channels // 2), :]
    stats_ref[0:1, :] = mean1
    stats_ref[1:2, :] = inverse1
    stats_ref[2:3, :] = mean2
    stats_ref[3:4, :] = inverse2
    stats_ref[4:8, :] = jnp.zeros((4, channels), F32)


def second_kernel(
    bucket_ref, image_ref, act2_ref, own, partner, received, partner_received, vecs,
    weight2, wq, wk, wv, wp,
    out_own, out_send, grad2_ref, grad_middle_ref, attn_keep, attn_send, vec_ref,
    block_keep, block_send,
    shift_ref, full_ref, middle_ref, grads_ref, sum_ref,
):
    h, home, away = place(bucket_ref)
    stride = home[2]
    mask, pixels = pixel_mask(home)
    channels = vecs.shape[1]
    group_size = pixels * (channels // GROUPS)
    scaling = channels ** (-0.5)
    fill_shifts(shift_ref, act2_ref[...].astype(F32), stride)
    conv_forward(shift_ref, weight2, stride, middle_ref)
    middle = mask * (image_ref[...].astype(F32) + (middle_ref[...] + vec(vecs, BIAS2)))
    middle_ref[...] = middle
    mean3, inverse3 = norm_stats(middle, mask, group_size)
    normal = (middle - mean3) * inverse3
    normed = (normal * vec(vecs, GAIN3) + vec(vecs, SHIFT3)).astype(BF16)
    wide = jnp.concatenate([wq[...], wk[...], wv[...]], axis=1)
    joint = mm(normed, wide)
    queries = (joint[:, 0:channels] + vec(vecs, QB)).astype(BF16)
    keys = joint[:, channels : 2 * channels].astype(BF16)
    values = (joint[:, 2 * channels :] + vec(vecs, VB)).astype(BF16)
    lanes = lax.broadcasted_iota(jnp.int32, (1, PIX), 1)
    key_cols = lanes & (stride - 1)
    key_valid = (key_cols < home[3]) & (lanes < jnp.where(home[1], 384, 512))
    scores = jnp.where(key_valid, mm_nt(queries, keys) * scaling, -1000000000.0)
    raised = jnp.exp(scores - jnp.max(scores, axis=1, keepdims=True))
    soft = raised * (1.0 / jnp.sum(raised, axis=1, keepdims=True))
    soft16 = soft.astype(BF16)
    mixed = mm(soft16, values).astype(BF16)
    projected = mm(mixed, wp[...]) + vec(vecs, PB)
    full_ref[...] = (mask * (middle_ref[...] + projected)).astype(BF16)
    split_out(full_ref, home, h, out_own, out_send)

    assemble(full_ref, home, h, (own, partner, received, partner_received))
    grad_top = full_ref[...].astype(F32) * mask
    grad_rows = grad_top.astype(BF16)
    grad_mixed = mm_nt(grad_rows, wp[...]).astype(BF16)
    grad_soft = mm_nt(grad_mixed, values)
    grad_values = mm_tn(soft16, grad_mixed).astype(BF16)
    grad_scores = soft * (grad_soft - jnp.sum(soft * grad_soft, axis=1, keepdims=True))
    grad_scores = grad_scores.astype(BF16)
    grad_queries = (mm(grad_scores, keys) * scaling).astype(BF16)
    grad_keys = (mm_tn(grad_scores, queries) * scaling).astype(BF16)
    grads_ref[:, 0:channels] = grad_queries
    grads_ref[:, channels : 2 * channels] = grad_keys
    grads_ref[:, 2 * channels : 3 * channels] = grad_values
    grads_ref[:, 3 * channels : 4 * channels] = grad_rows
    grad_normed = mm_nt(grads_ref[:, 0 : 3 * channels], wide)
    grad_in, gain_grad, shift_grad = norm_back(
        grad_normed, normal, inverse3, mask, group_size, vec(vecs, GAIN3)
    )
    grad_middle = mask * (grad_top + grad_in)
    grad_middle_ref[...] = grad_middle
    grad2 = grad_middle.astype(BF16)
    grad2_ref[...] = grad2
    vec_ref[0:1, :] = gain_grad
    vec_ref[1:2, :] = shift_grad
    vec_ref[2:3, :] = total(grad_queries.astype(F32))
    vec_ref[3:4, :] = total(grad_values.astype(F32))
    vec_ref[4:5, :] = total(grad_top)
    vec_ref[5:6, :] = total(grad2.astype(F32))
    vec_ref[6:8, :] = jnp.zeros((2, channels), F32)

    keep_at = pl.multiple_of(BLK * h, BLK)
    send_at = pl.multiple_of(BLK * (h ^ 2), BLK)
    block_keep[...] = grad2_ref[:, pl.ds(keep_at, BLK)]
    block_send[...] = grad2_ref[:, pl.ds(send_at, BLK)]

    def blocks(index):
        start = index * channels
        return [
            grads_ref[:, pl.ds(pl.multiple_of(start + BLK * h, BLK), BLK)],
            grads_ref[:, pl.ds(pl.multiple_of(start + BLK * (h ^ 2), BLK), BLK)],
        ]

    sum_ref[:, 0 : 6 * BLK] = mm_tn(normed, jnp.concatenate(blocks(0) + blocks(1) + blocks(2), axis=1))
    sum_ref[:, 6 * BLK : 8 * BLK] = mm_tn(mixed, jnp.concatenate(blocks(3), axis=1))
    mine = lax.axis_index("batch") & 1
    pairs = attn_keep.shape[0]
    rows = channels // (2 * pairs)
    for pair in range(pairs):
        for dst, which in ((attn_keep, mine), (attn_send, 1 - mine)):
            part = sum_ref[pl.ds(pl.multiple_of((2 * pair + which) * rows, 8), rows), :].astype(BF16)
            for index in range(4):
                dst[pair, index * rows : (index + 1) * rows, :] = part[:, index * 2 * BLK : (index + 1) * 2 * BLK]


def third_kernel(
    bucket_ref, grad2_ref, conv_ref, stats_ref, vecs, weight2,
    grad1_ref, block_keep, block_send, vec_ref,
    shift_ref, acc_ref,
):
    h, home, away = place(bucket_ref)
    stride = home[2]
    mask, pixels = pixel_mask(home)
    channels = vecs.shape[1]
    group_size = pixels * (channels // GROUPS)
    fill_shifts(shift_ref, grad2_ref[...].astype(F32), stride)
    conv_backward(shift_ref, weight2, stride, acc_ref)
    inverse = stats_ref[3:4, :]
    normal = (conv_ref[...] - stats_ref[2:3, :]) * inverse
    u = normal * vec(vecs, GAIN2) + vec(vecs, SHIFT2)
    grad = mask * acc_ref[...] * silu_slope(u)
    grad_in, gain_grad, shift_grad = norm_back(
        grad, normal, inverse, mask, group_size, vec(vecs, GAIN2)
    )
    grad1 = grad_in.astype(BF16)
    grad1_ref[...] = grad1
    vec_ref[0:1, :] = gain_grad
    vec_ref[1:2, :] = shift_grad
    vec_ref[2:3, :] = total(grad1.astype(F32))
    vec_ref[3:8, :] = jnp.zeros((5, channels), F32)
    block_keep[...] = grad1_ref[:, pl.ds(pl.multiple_of(BLK * h, BLK), BLK)]
    block_send[...] = grad1_ref[:, pl.ds(pl.multiple_of(BLK * (h ^ 2), BLK), BLK)]


def fourth_kernel(
    bucket_ref, grad1_ref, image_ref, stats_ref, grad_middle_ref, vecs, weight1, vec_a, vec_b,
    grad_own, grad_send, vec_out,
    shift_ref, acc_ref, full_ref, vec_ref,
):
    h, home, away = place(bucket_ref)
    stride = home[2]
    mask, pixels = pixel_mask(home)
    channels = vecs.shape[1]
    group_size = pixels * (channels // GROUPS)
    fill_shifts(shift_ref, grad1_ref[...].astype(F32), stride)
    conv_backward(shift_ref, weight1, stride, acc_ref)
    inverse = stats_ref[1:2, :]
    normal = (image_ref[...].astype(F32) * mask - stats_ref[0:1, :]) * inverse
    u = normal * vec(vecs, GAIN1) + vec(vecs, SHIFT1)
    grad = mask * acc_ref[...] * silu_slope(u)
    grad_in, gain_grad, shift_grad = norm_back(
        grad, normal, inverse, mask, group_size, vec(vecs, GAIN1)
    )
    full_ref[...] = (mask * (grad_middle_ref[...] + grad_in)).astype(BF16)
    split_out(full_ref, home, h, grad_own, grad_send)
    vec_ref[0:6, :] = vec_a[0:6, :]
    vec_ref[6:9, :] = vec_b[0:3, :]
    vec_ref[9:10, :] = gain_grad
    vec_ref[10:11, :] = shift_grad
    vec_ref[11:VECS, :] = jnp.zeros((VECS - 11, channels), F32)
    batches = vec_out.shape[0]
    rows = channels // batches
    for shard in range(batches):
        start = shard * rows
        tile = start // BLK * BLK
        part = vec_ref[:, tile : tile + BLK]
        if start > tile:
            part = pltpu.roll(part, BLK - (start - tile), 1)
        vec_out[shard] = part


def weight_kernel(
    bucket_ref, act_t, half_t, partner_half_t, block_own, block_away, *rest, tail
):
    vec_in = rest[0] if tail else None
    keep_ref, send_ref, left_ref, right_ref, shift_ref, sum_ref = rest[tail:]
    h, home, away = place(bucket_ref)
    channels = act_t.shape[0]
    half = channels // 2
    left_ref[:, 0:PIX] = act_t[...]
    left_ref[pl.ds(pl.multiple_of((h & 1) * half, 16), half), PIX : 2 * PIX] = half_t[...]
    left_ref[pl.ds(pl.multiple_of((1 - (h & 1)) * half, 16), half), PIX : 2 * PIX] = (
        partner_half_t[...]
    )
    for index, (facts, block) in enumerate(((home, block_own), (away, block_away))):
        stride = facts[2]
        fill_shifts(shift_ref, block[...].astype(F32), stride)
        for p in range(3):
            for q in range(3):
                column = (3 * p + q) * BLK
                right_ref[index * PIX : (index + 1) * PIX, column : column + BLK] = tap(
                    shift_ref, 2 - p, 2 - q, stride
                )
    joint = mm(left_ref[...], right_ref[...])
    for t in range(9):
        sum_ref[t * channels : (t + 1) * channels, :] = joint[:, t * BLK : (t + 1) * BLK]
    mine = lax.axis_index("batch") & 1
    pairs = keep_ref.shape[0]
    rows = 9 * channels // (2 * pairs)
    for pair in range(pairs):
        for dst, which in ((keep_ref, mine), (send_ref, 1 - mine)):
            shard = 2 * pair + which
            dst[pair, 0:rows, :] = sum_ref[pl.ds(pl.multiple_of(shard * rows, 8), rows), :].astype(BF16)
            if tail:
                dst[pair, rows : rows + VECS, :] = vec_in[shard].astype(BF16)


def route_kernel(bit, keep_ref, got_ref, own_ref, *out_refs):
    group = (lax.axis_index("batch") >> bit) & (len(out_refs))
    count = own_ref.shape[0]
    for step, dst in enumerate((own_ref,) + out_refs):
        which = group ^ step
        for index in range(count):
            at = index * (len(out_refs) + 1) + which
            dst[index] = (keep_ref[at].astype(F32) + got_ref[at].astype(F32)).astype(BF16)


def join_kernel(own_ref, far_ref, near_ref, diagonal_ref, out_ref, *tail_ref):
    h = lax.axis_index("height")
    rows = out_ref.shape[0]
    for ref, index in ((own_ref, h), (far_ref, h ^ 2), (near_ref, h ^ 1), (diagonal_ref, h ^ 3)):
        out_ref[:, pl.ds(pl.multiple_of(BLK * index, BLK), BLK)] = ref[0:rows, :].astype(F32)
    if tail_ref:
        own, far = own_ref[rows:, :].astype(F32), far_ref[rows:, :].astype(F32)
        near, diagonal = near_ref[rows:, :].astype(F32), diagonal_ref[rows:, :].astype(F32)
        tail_ref[0][...] = 0.5 * ((own + near) + (far + diagonal))


def join_attn_kernel(own_ref, far_ref, near_ref, diagonal_ref, *out_refs):
    h = lax.axis_index("height")
    rows = out_refs[0].shape[0]
    for first, second, index in ((own_ref, far_ref, h), (near_ref, diagonal_ref, h ^ 1)):
        for position in range(2):
            lane, other = position * BLK, (1 - position) * BLK
            column = pl.multiple_of(BLK * (index ^ (2 * position)), BLK)
            for number, dst in enumerate(out_refs):
                at = number * rows
                dst[:, pl.ds(column, BLK)] = first[at : at + rows, lane : lane + BLK].astype(
                    F32
                ) + second[at : at + rows, other : other + BLK].astype(F32)


def unpack_kernel(bucket_ref, out_own, out_away, grad_own, grad_away, out_ref, grad_ref):
    h, home, away = place(bucket_ref)
    for own, received, dst in ((out_own, out_away, out_ref), (grad_own, grad_away, grad_ref)):
        channels = dst.shape[3]
        for facts, src, wide_rows in ((away, received, 4), (home, own, 6)):
            image, tall, stride, width = facts

            @pl.when(tall)
            def _():
                for row in range(6):
                    dst[image, row, 0:16, :] = src[16 * row : 16 * row + 16, :]
                    dst[image, row, 16:32, :] = jnp.zeros((16, channels), dst.dtype)

            @pl.when(jnp.logical_not(tall))
            def _():
                for row in range(wide_rows):
                    dst[image, row] = src[32 * row : 32 * row + 32, :]
                for row in range(wide_rows, 6):
                    dst[image, row] = jnp.zeros((32, channels), dst.dtype)

            if wide_rows == 4:

                @pl.when(jnp.logical_not(tall) & (h == 3))
                def _():
                    for row in range(6):
                        dst[image, row] = jnp.zeros((32, channels), dst.dtype)


def call(kernel, name, outs, scratch, vmem, *operands, smem=1, any_from=99):
    specs = [SM] * smem + [VM] * (len(operands) - smem)
    specs = [HB if i >= any_from else spec for i, spec in enumerate(specs)]
    return pl.pallas_call(
        kernel,
        name=name,
        out_shape=[jax.ShapeDtypeStruct(shape, dtype) for shape, dtype in outs],
        in_specs=specs,
        out_specs=[SM if dtype == jnp.int32 else VM for shape, dtype in outs],
        scratch_shapes=[
            pltpu.SemaphoreType.DMA(shape) if dtype is None else pltpu.VMEM(shape, dtype)
            for shape, dtype in scratch
        ],
        compiler_params=pltpu.CompilerParams(vmem_limit_bytes=vmem << 20),
        cost_estimate=pl.CostEstimate(
            flops=LENGTH.get(name, 1) * RATE, bytes_accessed=1024, transcendentals=0
        ),
    )(*operands)


def on_device(
    inputs,
    bucket,
    norm1_gain,
    norm1_shift,
    conv1_weight,
    conv1_bias,
    norm2_gain,
    norm2_shift,
    conv2_weight,
    conv2_bias,
    norm3_gain,
    norm3_shift,
    query_weight,
    query_bias,
    key_weight,
    value_weight,
    value_bias,
    proj_weight,
    proj_bias,
    cotangent,
):
    C = inputs.shape[-1]
    batches = lax.axis_size("batch")
    bits = batches.bit_length() - 1
    shard_rows = 9 * C // batches
    small_rows = C // batches

    def to_core(v):
        return lax.ppermute(v, "height", [(i, i ^ 1) for i in range(4)])

    def to_chip(v):
        return lax.ppermute(v, "height", [(i, i ^ 2) for i in range(4)])

    def to_batch(v, change):
        return lax.ppermute(v, "batch", [(i, i ^ change) for i in range(batches)])

    def after(v, *others):
        return lax.optimization_barrier((v,) + others)[0]

    img16 = ((PIX, C), BF16)
    img32 = ((PIX, C), F32)
    rows8 = ((8, C), F32)
    block = ((PIX, BLK), BF16)
    turned = ((C, PIX), BF16)
    half = ((C // 2, PIX), BF16)
    shifts = ((3, PIX + 2 * PAD, C), BF16)

    kinds, away_x, home_x, away_c, home_c = call(
        pack_kernel, "pack",
        [((2,), jnp.int32), ((128, C), BF16), ((192, C), BF16), ((128, C), BF16), ((192, C), BF16)],
        [((24,), None)], 8, bucket, inputs, cotangent, any_from=1,
    )
    vecs = jnp.stack(
        [
            norm1_gain, norm1_shift, conv1_bias, norm2_gain, norm2_shift, conv2_bias,
            norm3_gain, norm3_shift, query_bias, value_bias, proj_bias,
        ]
    )
    recv_x = to_chip(away_x)
    core_x = to_core(home_x)
    recv_c = to_chip(away_c)
    core_c = to_core(home_c)
    core_recv_x = to_core(recv_x)
    core_recv_c = to_core(recv_c)

    image, conv, act2, stats, act1_t, act2_t, send1_t, send2_t = call(
        first_kernel, "first",
        [img16, img32, img16, rows8, turned, turned, half, half],
        [shifts], 24,
        kinds, home_x, core_x, recv_x, core_recv_x, vecs, conv1_weight,
    )
    half_t = [to_chip(v) for v in (send1_t, send2_t)]
    core_half_t = [to_core(v) for v in half_t]

    attn_out = ((batches // 2, 4 * small_rows, 2 * BLK), BF16)
    out_own, out_send, grad2, grad_middle, attn_keep, attn_send, vec_a, block2, block2_send = call(
        second_kernel, "second",
        [((192, C), BF16), ((128, C), BF16), img16, img32, attn_out, attn_out, rows8, block, block],
        [shifts, img16, img32, ((PIX, 4 * C), BF16), ((C, 8 * BLK), F32)], 32,
        kinds, image, act2, home_c, core_c, recv_c, core_recv_c, vecs,
        conv2_weight, query_weight, key_weight, value_weight, proj_weight,
    )
    block2_away = to_chip(block2_send)
    out_away = to_chip(out_send)
    attn_got = to_batch(attn_send, 1)

    grad1, block1, block1_send, vec_b = call(
        third_kernel, "third",
        [img16, block, block, rows8],
        [shifts, img32], 24,
        kinds, grad2, conv, stats, vecs, conv2_weight,
    )
    block1_away = to_chip(block1_send)

    def weight_grad(name, act_t, index, own, away, *tail):
        rows = shard_rows + (VECS if tail else 0)
        return call(
            functools.partial(weight_kernel, tail=len(tail)), name,
            [((batches // 2, rows, BLK), BF16)] * 2,
            [((C, 2 * PIX), BF16), ((2 * PIX, 9 * BLK), BF16), ((3, PIX + 2 * PAD, BLK), BF16),
             ((9 * C, BLK), F32)],
            24, kinds, act_t, half_t[index], core_half_t[index], own, away, *tail,
        )

    keep2, send2 = weight_grad("weight2", act2_t, 1, after(block2, block1), block2_away)
    got2 = to_batch(send2, 1)

    grad_own, grad_send, vec_c = call(
        fourth_kernel, "fourth",
        [((192, C), BF16), ((128, C), BF16), ((batches, VECS, BLK), F32)],
        [shifts, img32, img16, ((VECS, C), F32)], 24,
        kinds, after(grad1, send2), image, stats, grad_middle, vecs, conv1_weight, vec_a, vec_b,
    )
    grad_away = to_chip(grad_send)
    keep1, send1 = weight_grad("weight1", act1_t, 0, block1, block1_away, vec_c)
    got1 = to_batch(send1, 1)

    def scatter(name, keep, got):
        bit = 1
        while bit < bits:
            width = min(2, bits - bit)
            ways = 1 << width
            shape = (keep.shape[0] // ways,) + keep.shape[1:]
            parts = call(
                functools.partial(route_kernel, bit), name + str(bit),
                [(shape, BF16)] * ways, [], 16, keep, got, smem=0,
            )
            got = [to_batch(parts[j], j << bit) for j in range(1, ways)]
            bit += width
            if bit < bits:
                keep = parts[0]
                got = functools.reduce(lambda a, b: a + b, [g.astype(F32) for g in got]).astype(BF16)
            else:
                added = parts[0].astype(F32)
                for g in got:
                    added = added + g.astype(F32)
                return added.astype(BF16)[0]

    def gather(shard):
        far = to_chip(shard)
        near = to_core(shard)
        return shard, far, near, to_core(far)

    attn_parts = gather(scatter("routea", after(attn_keep, send1), attn_got))
    parts2 = gather(scatter("routeb", keep2, got2))
    parts1 = gather(scatter("routec", keep1, got1))
    small = call(
        join_attn_kernel, "joina", [((small_rows, C), F32)] * 4, [], 8, *attn_parts, smem=0
    )
    (whole2,) = call(join_kernel, "joinb", [((shard_rows, C), F32)], [], 8, *parts2, smem=0)
    whole1, sums = call(
        join_kernel, "joinc", [((shard_rows, C), F32), ((VECS, BLK), F32)], [], 8, *parts1, smem=0
    )
    v = [sums[i, :small_rows] for i in range(11)]

    outputs, input_grad = call(
        unpack_kernel, "unpack",
        [(inputs.shape, BF16)] * 2, [], 8,
        kinds, out_own, out_away, grad_own, grad_away,
    )
    return (
        outputs, input_grad,
        v[9], v[10], whole1, v[8],
        v[6], v[7], whole2, v[5],
        v[0], v[1],
        small[0], v[2], small[1], small[2], v[3], small[3], v[4],
    )


def solution(mesh):
    image = P("batch", "height", None, None)
    vector = P("batch")
    matrix = P("batch", None)
    return jax.shard_map(
        on_device,
        mesh=mesh,
        in_specs=(image, vector) + (P(),) * 17 + (image,),
        out_specs=(
            image, image,
            vector, vector, matrix, vector,
            vector, vector, matrix, vector,
            vector, vector,
            matrix, vector, matrix, matrix, vector, matrix, vector,
        ),
        check_vma=False,
    )
```

```python
import functools

import jax
import jax.numpy as jnp
from jax import lax
from jax.experimental import pallas as pl
from jax.experimental.pallas import tpu as pltpu
from jax.sharding import PartitionSpec as P

GROUPS = 32
UNIT = 8
PIX = 512
PAD = 32
BLK = 128
F32 = jnp.float32
BF16 = jnp.bfloat16
epsilon = 1e-05

VM = pl.BlockSpec(memory_space=pltpu.VMEM)
SM = pl.BlockSpec(memory_space=pltpu.SMEM)
HB = pl.BlockSpec(memory_space=pltpu.HBM)
RATE = 1 << 30
LENGTH = {
    "pack": 10, "stack": 10, "first": 8, "second": 30, "third": 20, "fourth": 0.02, "weight2": 0.02, "weight1": 0.02,
}


def place(bucket_ref):
    h = lax.axis_index("height")
    upper = lax.div(h, 2)
    tall_first = bucket_ref[0] == 1
    tall_image = jnp.where(tall_first, 0, 1)
    home = jnp.where(upper == 1, tall_image, 1 - tall_image)
    away = 1 - home

    def facts(image):
        kind = bucket_ref[image]
        tall = kind == 1
        stride = jnp.where(tall, 2 * UNIT, 4 * UNIT)
        width = jnp.where(kind == 0, 3 * UNIT, stride)
        return (image, tall, stride, width)

    return h, facts(home), facts(away)


def pixel_col(stride, lanes=1):
    rows = lax.broadcasted_iota(jnp.int32, (PIX, lanes), 0)
    return rows, rows & (stride - 1)


def pixel_mask(facts):
    unused, tall, stride, width = facts
    rows, cols = pixel_col(stride)
    limit = jnp.where(tall, 6 * UNIT * UNIT, 8 * UNIT * UNIT)
    mask = jnp.where((cols < width) & (rows < limit), 1.0, 0.0).astype(F32)
    size = jnp.where(tall | (width == 3 * UNIT), 6 * UNIT * UNIT, 8 * UNIT * UNIT)
    return mask, size.astype(F32)


def group_total(row):
    channels = row.shape[-1]
    lane = lax.broadcasted_iota(jnp.int32, row.shape, 1)
    step = 1
    while step < channels // GROUPS:
        up = pltpu.roll(row, channels - step, 1)
        down = pltpu.roll(row, step, 1)
        row = row + jnp.where((lane & step) == 0, up, down)
        step *= 2
    return row


def total(values):
    return jnp.sum(values, axis=0, keepdims=True)


def wide_total(row):
    return group_total(jnp.broadcast_to(row, (8, row.shape[-1])))[0:1]


def norm_stats(values, mask, group_size):
    mean = wide_total(total(values)) / group_size
    centered = (values - mean) * mask
    variance = wide_total(total(centered * centered)) / group_size
    return mean, lax.rsqrt(variance + epsilon)


def silu_norm(values, mean, inverse, gain, shift, mask):
    scale = 0.5 * inverse * gain
    half = values * scale + (0.5 * shift - mean * scale)
    return (half + half * jnp.tanh(half)) * mask


def norm_back(grad, normal, inverse, mask, group_size, gain):
    plain_row = total(grad)
    cross_row = total(grad * normal)
    plain = wide_total(plain_row * gain) / group_size
    cross = wide_total(cross_row * gain) / group_size
    grad_in = grad * (inverse * gain) - mask * (plain * inverse + normal * (cross * inverse))
    return grad_in, cross_row, plain_row


def silu_slope(u):
    half = 0.5 * u
    t = jnp.tanh(half)
    return (0.5 + 0.5 * t) * (1.0 + half * (1.0 - t))


def mm(a, b):
    return jnp.dot(a, b, preferred_element_type=F32)


def mm_nt(a, b):
    return lax.dot_general(a, b, (((1,), (1,)), ((), ())), preferred_element_type=F32)


def mm_tn(a, b):
    return lax.dot_general(a, b, (((0,), (0,)), ((), ())), preferred_element_type=F32)


def fill_shifts(shift_ref, values, stride):
    unused, cols = pixel_col(stride)
    lanes = values.shape[1]
    zeros = jnp.zeros((PAD, lanes), BF16)
    for q in range(3):
        shift_ref[q, 0:PAD, :] = zeros
        shift_ref[q, PAD + PIX : 2 * PAD + PIX, :] = zeros
    left = jnp.where(cols == 0, 0.0, pltpu.roll(values, 1, 0))
    right = jnp.where(cols == stride - 1, 0.0, pltpu.roll(values, PIX - 1, 0))
    shift_ref[0, PAD : PAD + PIX, :] = left.astype(BF16)
    shift_ref[1, PAD : PAD + PIX, :] = values.astype(BF16)
    shift_ref[2, PAD : PAD + PIX, :] = right.astype(BF16)


def tap(shift_ref, p, q, stride, first=0, count=PIX):
    start = pl.multiple_of(PAD + first + (p - 1) * stride, 16)
    return shift_ref[q, pl.ds(start, count), :]


def conv_forward(shift_ref, weight_ref, stride, out_ref, tile=256):
    for first in range(0, PIX, tile):
        stacked = jnp.concatenate(
            [tap(shift_ref, p, q, stride, first, tile) for p in range(3) for q in range(3)], axis=1
        )
        out_ref[first : first + tile, :] = mm(stacked, weight_ref[...])


def conv_backward(shift_ref, weight_ref, stride, out_ref, tile=256):
    channels = weight_ref.shape[1]
    for first in range(0, PIX, tile):
        acc = None
        for p in range(3):
            for q in range(3):
                row = (8 - (3 * p + q)) * channels
                part = mm_nt(
                    tap(shift_ref, p, q, stride, first, tile), weight_ref[row : row + channels, :]
                )
                acc = part if acc is None else acc + part
        out_ref[first : first + tile, :] = acc


def assemble(out_ref, facts, h, pieces):
    unused, tall, stride, width = facts
    own, partner, received, partner_received = pieces
    other = h ^ 1

    @pl.when(tall)
    def _():
        for ref, index in (
            (own, h),
            (partner, other),
            (received, h ^ 2),
            (partner_received, other ^ 2),
        ):
            out_ref[pl.ds(pl.multiple_of(96 * index, 16), 96), :] = ref[0:96, :]
        out_ref[384:512, :] = jnp.zeros((128, out_ref.shape[1]), out_ref.dtype)

    @pl.when(jnp.logical_not(tall))
    def _():
        low = h & 1
        out_ref[pl.ds(pl.multiple_of(192 * low, 16), 192), :] = own[...]
        out_ref[pl.ds(pl.multiple_of(192 * (1 - low), 16), 192), :] = partner[...]

        @pl.when(low == 0)
        def _():
            out_ref[384:512, :] = received[...]

        @pl.when(low == 1)
        def _():
            out_ref[384:512, :] = partner_received[...]


def split_out(full_ref, facts, h, own_ref, send_ref):
    unused, tall, stride, width = facts
    send_h = h ^ 2

    @pl.when(tall)
    def _():
        own_ref[0:96, :] = full_ref[pl.ds(pl.multiple_of(96 * h, 16), 96), :]
        own_ref[96:192, :] = jnp.zeros((96, own_ref.shape[1]), own_ref.dtype)
        send_ref[0:96, :] = full_ref[pl.ds(pl.multiple_of(96 * send_h, 16), 96), :]
        send_ref[96:128, :] = jnp.zeros((32, own_ref.shape[1]), own_ref.dtype)

    @pl.when(jnp.logical_not(tall))
    def _():
        own_ref[...] = full_ref[pl.ds(pl.multiple_of(192 * (h & 1), 16), 192), :]
        send_ref[...] = full_ref[384:512, :]


GAIN1, SHIFT1, BIAS1, GAIN2, SHIFT2, BIAS2, GAIN3, SHIFT3, QB, VB, PB = range(11)
VECS = 16


def vec(vec_ref, index):
    return vec_ref[index : index + 1, :]


def pack_kernel(
    bucket_hbm, x_ref, cot_ref, kinds, away_x, home_x, away_c, home_c, bucket_ref, bucket_sem, sems
):
    copy = pltpu.make_async_copy(bucket_hbm, bucket_ref, bucket_sem.at[0])
    copy.start()
    copy.wait()
    h, home, away = place(bucket_ref)

    def each(act):
        slot = 0
        for src, away_ref, home_ref in ((x_ref, away_x, home_x), (cot_ref, away_c, home_c)):
            for facts, dst, wide_rows in ((away, away_ref, 4), (home, home_ref, 6)):
                image, tall, stride, width = facts

                @pl.when(tall)
                def _():
                    for row in range(6):
                        act(
                            src.at[image, row, pl.ds(0, 16), :],
                            dst.at[pl.ds(16 * row, 16), :],
                            sems.at[slot + row],
                        )

                @pl.when(jnp.logical_not(tall))
                def _():
                    for row in range(wide_rows):
                        act(src.at[image, row], dst.at[pl.ds(32 * row, 32), :], sems.at[slot + row])

                slot += 6

    each(lambda a, b, sem: pltpu.make_async_copy(a, b, sem).start())
    kinds[0] = bucket_ref[0]
    kinds[1] = bucket_ref[1]
    each(lambda a, b, sem: pltpu.make_async_copy(a, b, sem).wait())


def stack_kernel(*refs):
    out_ref = refs[-1]
    for index, ref in enumerate(refs[:-1]):
        out_ref[index : index + 1, :] = ref[...]
    out_ref[len(refs) - 1 :, :] = jnp.zeros((VECS - len(refs) + 1, out_ref.shape[1]), F32)


def first_kernel(
    bucket_ref, own, partner, received, partner_received, vecs, weight1,
    image_ref, conv_ref, act2_ref, stats_ref, act1_t, act2_t, send_t,
    shift_ref,
):
    h, home, away = place(bucket_ref)
    stride = home[2]
    mask, pixels = pixel_mask(home)
    channels = vecs.shape[1]
    group_size = pixels * (channels // GROUPS)
    assemble(image_ref, home, h, (own, partner, received, partner_received))
    values = image_ref[...].astype(F32) * mask
    mean1, inverse1 = norm_stats(values, mask, group_size)
    act = silu_norm(values, mean1, inverse1, vec(vecs, GAIN1), vec(vecs, SHIFT1), mask)
    fill_shifts(shift_ref, act, stride)
    act1_t[...] = act.astype(BF16).T
    conv_forward(shift_ref, weight1, stride, conv_ref)
    values = (conv_ref[...] + vec(vecs, BIAS1)) * mask
    conv_ref[...] = values
    mean2, inverse2 = norm_stats(values, mask, group_size)
    act = silu_norm(values, mean2, inverse2, vec(vecs, GAIN2), vec(vecs, SHIFT2), mask)
    act = act.astype(BF16)
    act2_ref[...] = act
    act2_t[...] = act.T
    half = pl.multiple_of((h & 1) * (channels // 2), 16)
    send_t[0] = act1_t[pl.ds(half, channels // 2), :]
    send_t[1] = act2_t[pl.ds(half, channels // 2), :]
    stats_ref[0:1, :] = mean1
    stats_ref[1:2, :] = inverse1
    stats_ref[2:3, :] = mean2
    stats_ref[3:4, :] = inverse2
    stats_ref[4:8, :] = jnp.zeros((4, channels), F32)


def second_kernel(
    bucket_ref, image_ref, act2_ref, own, partner, received, partner_received, vecs,
    weight2, wq, wk, wv, wp,
    out_own, out_send, grad2_ref, grad_middle_ref, attn_keep, attn_send, vec_ref,
    block_keep, block_send,
    shift_ref, full_ref, middle_ref, grads_ref, sum_ref,
):
    h, home, away = place(bucket_ref)
    stride = home[2]
    mask, pixels = pixel_mask(home)
    channels = vecs.shape[1]
    group_size = pixels * (channels // GROUPS)
    scaling = channels ** (-0.5)
    fill_shifts(shift_ref, act2_ref[...].astype(F32), stride)
    conv_forward(shift_ref, weight2, stride, middle_ref)
    middle = mask * (image_ref[...].astype(F32) + (middle_ref[...] + vec(vecs, BIAS2)))
    middle_ref[...] = middle
    mean3, inverse3 = norm_stats(middle, mask, group_size)
    normal = (middle - mean3) * inverse3
    normed = (normal * vec(vecs, GAIN3) + vec(vecs, SHIFT3)).astype(BF16)
    wide = jnp.concatenate([wq[...], wk[...], wv[...]], axis=1)
    joint = mm(normed, wide)
    queries = (joint[:, 0:channels] + vec(vecs, QB)).astype(BF16)
    keys = joint[:, channels : 2 * channels].astype(BF16)
    values = (joint[:, 2 * channels :] + vec(vecs, VB)).astype(BF16)
    lanes = lax.broadcasted_iota(jnp.int32, (1, PIX), 1)
    key_cols = lanes & (stride - 1)
    key_valid = (key_cols < home[3]) & (lanes < jnp.where(home[1], 384, 512))
    scores = jnp.where(key_valid, mm_nt(queries, keys) * scaling, -1000000000.0)
    raised = jnp.exp(scores - jnp.max(scores, axis=1, keepdims=True))
    soft = raised * (1.0 / jnp.sum(raised, axis=1, keepdims=True))
    soft16 = soft.astype(BF16)
    mixed = mm(soft16, values).astype(BF16)
    projected = mm(mixed, wp[...]) + vec(vecs, PB)
    full_ref[...] = (mask * (middle_ref[...] + projected)).astype(BF16)
    split_out(full_ref, home, h, out_own, out_send)

    assemble(full_ref, home, h, (own, partner, received, partner_received))
    grad_top = full_ref[...].astype(F32) * mask
    grad_rows = grad_top.astype(BF16)
    grad_mixed = mm_nt(grad_rows, wp[...]).astype(BF16)
    grad_soft = mm_nt(grad_mixed, values)
    grad_values = mm_tn(soft16, grad_mixed).astype(BF16)
    grad_scores = soft * (grad_soft - jnp.sum(soft * grad_soft, axis=1, keepdims=True))
    grad_scores = grad_scores.astype(BF16)
    grad_queries = (mm(grad_scores, keys) * scaling).astype(BF16)
    grad_keys = (mm_tn(grad_scores, queries) * scaling).astype(BF16)
    grads_ref[:, 0:channels] = grad_queries
    grads_ref[:, channels : 2 * channels] = grad_keys
    grads_ref[:, 2 * channels : 3 * channels] = grad_values
    grads_ref[:, 3 * channels : 4 * channels] = grad_rows
    grad_normed = mm_nt(grads_ref[:, 0 : 3 * channels], wide)
    grad_in, gain_grad, shift_grad = norm_back(
        grad_normed, normal, inverse3, mask, group_size, vec(vecs, GAIN3)
    )
    grad_middle = mask * (grad_top + grad_in)
    grad_middle_ref[...] = grad_middle
    grad2 = grad_middle.astype(BF16)
    grad2_ref[...] = grad2
    vec_ref[0:1, :] = gain_grad
    vec_ref[1:2, :] = shift_grad
    vec_ref[2:3, :] = total(grad_queries.astype(F32))
    vec_ref[3:4, :] = total(grad_values.astype(F32))
    vec_ref[4:5, :] = total(grad_top)
    vec_ref[5:6, :] = total(grad2.astype(F32))
    vec_ref[6:8, :] = jnp.zeros((2, channels), F32)

    keep_at = pl.multiple_of(BLK * h, BLK)
    send_at = pl.multiple_of(BLK * (h ^ 2), BLK)
    block_keep[...] = grad2_ref[:, pl.ds(keep_at, BLK)]
    block_send[...] = grad2_ref[:, pl.ds(send_at, BLK)]

    def blocks(index):
        start = index * channels
        return [
            grads_ref[:, pl.ds(pl.multiple_of(start + BLK * h, BLK), BLK)],
            grads_ref[:, pl.ds(pl.multiple_of(start + BLK * (h ^ 2), BLK), BLK)],
        ]

    sum_ref[:, 0 : 6 * BLK] = mm_tn(normed, jnp.concatenate(blocks(0) + blocks(1) + blocks(2), axis=1))
    sum_ref[:, 6 * BLK : 8 * BLK] = mm_tn(mixed, jnp.concatenate(blocks(3), axis=1))
    mine = lax.axis_index("batch") & 1
    pairs = attn_keep.shape[0]
    rows = channels // (2 * pairs)
    for pair in range(pairs):
        for dst, which in ((attn_keep, mine), (attn_send, 1 - mine)):
            part = sum_ref[pl.ds(pl.multiple_of((2 * pair + which) * rows, 8), rows), :].astype(BF16)
            for index in range(4):
                dst[pair, index * rows : (index + 1) * rows, :] = part[:, index * 2 * BLK : (index + 1) * 2 * BLK]


def third_kernel(
    bucket_ref, grad2_ref, conv_ref, stats_ref, vecs, weight2,
    grad1_ref, block_keep, block_send, vec_ref,
    shift_ref, acc_ref,
):
    h, home, away = place(bucket_ref)
    stride = home[2]
    mask, pixels = pixel_mask(home)
    channels = vecs.shape[1]
    group_size = pixels * (channels // GROUPS)
    fill_shifts(shift_ref, grad2_ref[...].astype(F32), stride)
    conv_backward(shift_ref, weight2, stride, acc_ref)
    inverse = stats_ref[3:4, :]
    normal = (conv_ref[...] - stats_ref[2:3, :]) * inverse
    u = normal * vec(vecs, GAIN2) + vec(vecs, SHIFT2)
    grad = mask * acc_ref[...] * silu_slope(u)
    grad_in, gain_grad, shift_grad = norm_back(
        grad, normal, inverse, mask, group_size, vec(vecs, GAIN2)
    )
    grad1 = grad_in.astype(BF16)
    grad1_ref[...] = grad1
    vec_ref[0:1, :] = gain_grad
    vec_ref[1:2, :] = shift_grad
    vec_ref[2:3, :] = total(grad1.astype(F32))
    vec_ref[3:8, :] = jnp.zeros((5, channels), F32)
    block_keep[...] = grad1_ref[:, pl.ds(pl.multiple_of(BLK * h, BLK), BLK)]
    block_send[...] = grad1_ref[:, pl.ds(pl.multiple_of(BLK * (h ^ 2), BLK), BLK)]


def fourth_kernel(
    bucket_ref, grad1_ref, image_ref, stats_ref, grad_middle_ref, vecs, weight1, vec_a, vec_b,
    grad_own, grad_send, vec_out,
    shift_ref, acc_ref, full_ref, vec_ref,
):
    h, home, away = place(bucket_ref)
    stride = home[2]
    mask, pixels = pixel_mask(home)
    channels = vecs.shape[1]
    group_size = pixels * (channels // GROUPS)
    fill_shifts(shift_ref, grad1_ref[...].astype(F32), stride)
    conv_backward(shift_ref, weight1, stride, acc_ref)
    inverse = stats_ref[1:2, :]
    normal = (image_ref[...].astype(F32) * mask - stats_ref[0:1, :]) * inverse
    u = normal * vec(vecs, GAIN1) + vec(vecs, SHIFT1)
    grad = mask * acc_ref[...] * silu_slope(u)
    grad_in, gain_grad, shift_grad = norm_back(
        grad, normal, inverse, mask, group_size, vec(vecs, GAIN1)
    )
    full_ref[...] = (mask * (grad_middle_ref[...] + grad_in)).astype(BF16)
    split_out(full_ref, home, h, grad_own, grad_send)
    vec_ref[0:6, :] = vec_a[0:6, :]
    vec_ref[6:9, :] = vec_b[0:3, :]
    vec_ref[9:10, :] = gain_grad
    vec_ref[10:11, :] = shift_grad
    vec_ref[11:VECS, :] = jnp.zeros((VECS - 11, channels), F32)
    batches = vec_out.shape[0]
    rows = channels // batches
    for shard in range(batches):
        start = shard * rows
        tile = start // BLK * BLK
        part = vec_ref[:, tile : tile + BLK]
        if start > tile:
            part = pltpu.roll(part, BLK - (start - tile), 1)
        vec_out[shard] = part


def weight_kernel(
    bucket_ref, act_t, half_t, partner_half_t, block_own, block_away, *rest, layer, tail
):
    vec_in = rest[0] if tail else None
    keep_ref, send_ref, left_ref, right_ref, shift_ref, sum_ref = rest[tail:]
    h, home, away = place(bucket_ref)
    channels = act_t.shape[0]
    half = channels // 2
    left_ref[:, 0:PIX] = act_t[...]
    left_ref[pl.ds(pl.multiple_of((h & 1) * half, 16), half), PIX : 2 * PIX] = half_t[layer]
    left_ref[pl.ds(pl.multiple_of((1 - (h & 1)) * half, 16), half), PIX : 2 * PIX] = (
        partner_half_t[layer]
    )
    for index, (facts, block) in enumerate(((home, block_own), (away, block_away))):
        stride = facts[2]
        fill_shifts(shift_ref, block[...].astype(F32), stride)
        for p in range(3):
            for q in range(3):
                column = (3 * p + q) * BLK
                right_ref[index * PIX : (index + 1) * PIX, column : column + BLK] = tap(
                    shift_ref, 2 - p, 2 - q, stride
                )
    joint = mm(left_ref[...], right_ref[...])
    for t in range(9):
        sum_ref[t * channels : (t + 1) * channels, :] = joint[:, t * BLK : (t + 1) * BLK]
    mine = lax.axis_index("batch") & 1
    pairs = keep_ref.shape[0]
    rows = 9 * channels // (2 * pairs)
    for pair in range(pairs):
        for dst, which in ((keep_ref, mine), (send_ref, 1 - mine)):
            shard = 2 * pair + which
            dst[pair, 0:rows, :] = sum_ref[pl.ds(pl.multiple_of(shard * rows, 8), rows), :].astype(BF16)
            if tail:
                dst[pair, rows : rows + VECS, :] = vec_in[shard].astype(BF16)


def route_kernel(bit, keep_ref, got_ref, own_ref, *out_refs):
    group = (lax.axis_index("batch") >> bit) & (len(out_refs))
    count = own_ref.shape[0]
    for step, dst in enumerate((own_ref,) + out_refs):
        which = group ^ step
        for index in range(count):
            at = index * (len(out_refs) + 1) + which
            dst[index] = (keep_ref[at].astype(F32) + got_ref[at].astype(F32)).astype(BF16)


def join_kernel(own_ref, far_ref, near_ref, diagonal_ref, out_ref, *tail_ref):
    h = lax.axis_index("height")
    rows = out_ref.shape[0]
    for ref, index in ((own_ref, h), (far_ref, h ^ 2), (near_ref, h ^ 1), (diagonal_ref, h ^ 3)):
        out_ref[:, pl.ds(pl.multiple_of(BLK * index, BLK), BLK)] = ref[0:rows, :].astype(F32)
    if tail_ref:
        own, far = own_ref[rows:, :].astype(F32), far_ref[rows:, :].astype(F32)
        near, diagonal = near_ref[rows:, :].astype(F32), diagonal_ref[rows:, :].astype(F32)
        tail_ref[0][...] = 0.5 * ((own + near) + (far + diagonal))


def join_attn_kernel(own_ref, far_ref, near_ref, diagonal_ref, *out_refs):
    h = lax.axis_index("height")
    rows = out_refs[0].shape[0]
    for first, second, index in ((own_ref, far_ref, h), (near_ref, diagonal_ref, h ^ 1)):
        for position in range(2):
            lane, other = position * BLK, (1 - position) * BLK
            column = pl.multiple_of(BLK * (index ^ (2 * position)), BLK)
            for number, dst in enumerate(out_refs):
                at = number * rows
                dst[:, pl.ds(column, BLK)] = first[at : at + rows, lane : lane + BLK].astype(
                    F32
                ) + second[at : at + rows, other : other + BLK].astype(F32)


def unpack_kernel(bucket_ref, out_own, out_away, grad_own, grad_away, out_ref, grad_ref):
    h, home, away = place(bucket_ref)
    for own, received, dst in ((out_own, out_away, out_ref), (grad_own, grad_away, grad_ref)):
        channels = dst.shape[3]
        for facts, src, wide_rows in ((away, received, 4), (home, own, 6)):
            image, tall, stride, width = facts

            @pl.when(tall)
            def _():
                for row in range(6):
                    dst[image, row, 0:16, :] = src[16 * row : 16 * row + 16, :]
                    dst[image, row, 16:32, :] = jnp.zeros((16, channels), dst.dtype)

            @pl.when(jnp.logical_not(tall))
            def _():
                for row in range(wide_rows):
                    dst[image, row] = src[32 * row : 32 * row + 32, :]
                for row in range(wide_rows, 6):
                    dst[image, row] = jnp.zeros((32, channels), dst.dtype)

            if wide_rows == 4:

                @pl.when(jnp.logical_not(tall) & (h == 3))
                def _():
                    for row in range(6):
                        dst[image, row] = jnp.zeros((32, channels), dst.dtype)


def call(kernel, name, outs, scratch, vmem, *operands, smem=1, any_from=99):
    specs = [SM] * smem + [VM] * (len(operands) - smem)
    specs = [HB if i >= any_from else spec for i, spec in enumerate(specs)]
    return pl.pallas_call(
        kernel,
        name=name,
        out_shape=[jax.ShapeDtypeStruct(shape, dtype) for shape, dtype in outs],
        in_specs=specs,
        out_specs=[SM if dtype == jnp.int32 else VM for shape, dtype in outs],
        scratch_shapes=[
            pltpu.SemaphoreType.DMA(shape)
            if dtype is None
            else (pltpu.SMEM if dtype == jnp.int32 else pltpu.VMEM)(shape, dtype)
            for shape, dtype in scratch
        ],
        compiler_params=pltpu.CompilerParams(vmem_limit_bytes=vmem << 20),
        cost_estimate=pl.CostEstimate(
            flops=int(LENGTH.get(name, 1) * RATE), bytes_accessed=1024, transcendentals=0
        ),
    )(*operands)


def on_device(
    inputs,
    bucket,
    norm1_gain,
    norm1_shift,
    conv1_weight,
    conv1_bias,
    norm2_gain,
    norm2_shift,
    conv2_weight,
    conv2_bias,
    norm3_gain,
    norm3_shift,
    query_weight,
    query_bias,
    key_weight,
    value_weight,
    value_bias,
    proj_weight,
    proj_bias,
    cotangent,
):
    C = inputs.shape[-1]
    batches = lax.axis_size("batch")
    bits = batches.bit_length() - 1
    shard_rows = 9 * C // batches
    small_rows = C // batches

    def row(v):
        return v.reshape(1, C)

    def to_core(v):
        return lax.ppermute(v, "height", [(i, i ^ 1) for i in range(4)])

    def to_chip(v):
        return lax.ppermute(v, "height", [(i, i ^ 2) for i in range(4)])

    def to_batch(v, change):
        return lax.ppermute(v, "batch", [(i, i ^ change) for i in range(batches)])

    def after(v, *others):
        return lax.optimization_barrier((v,) + others)[0]

    img16 = ((PIX, C), BF16)
    img32 = ((PIX, C), F32)
    rows8 = ((8, C), F32)
    block = ((PIX, BLK), BF16)
    turned = ((C, PIX), BF16)
    shifts = ((3, PIX + 2 * PAD, C), BF16)

    kinds, away_x, home_x, away_c, home_c = call(
        pack_kernel, "pack",
        [((2,), jnp.int32), ((128, C), BF16), ((192, C), BF16), ((128, C), BF16), ((192, C), BF16)],
        [((2,), jnp.int32), ((1,), None), ((24,), None)], 54, bucket, inputs, cotangent,
        smem=0, any_from=0,
    )
    vectors = (
        norm1_gain, norm1_shift, conv1_bias, norm2_gain, norm2_shift, conv2_bias,
        norm3_gain, norm3_shift, query_bias, value_bias, proj_bias,
    )
    (vecs,) = call(
        stack_kernel, "stack", [((VECS, C), F32)], [], 8,
        after(row(vectors[0]), away_x), *[row(v) for v in vectors[1:]], smem=0,
    )
    recv_x = to_chip(away_x)
    core_x = to_core(home_x)
    recv_x = after(recv_x, vecs)
    recv_c = to_chip(after(away_c, recv_x))
    core_c = to_core(home_c)
    core_recv_x = to_core(recv_x)
    core_recv_c = lax.ppermute(after(away_c, recv_x), "height", [(i, i ^ 3) for i in range(4)])

    image, conv, act2, stats, act1_t, act2_t, send_t = call(
        first_kernel, "first",
        [img16, img32, img16, rows8, turned, turned, ((2, C // 2, PIX), BF16)],
        [shifts], 24,
        kinds, home_x, core_x, recv_x, core_recv_x, vecs, conv1_weight,
    )
    half_t = to_chip(send_t)
    core_half_t = to_core(half_t)

    attn_out = ((batches // 2, 4 * small_rows, 2 * BLK), BF16)
    out_own, out_send, grad2, grad_middle, attn_keep, attn_send, vec_a, block2, block2_send = call(
        second_kernel, "second",
        [((192, C), BF16), ((128, C), BF16), img16, img32, attn_out, attn_out, rows8, block, block],
        [shifts, img16, img32, ((PIX, 4 * C), BF16), ((C, 8 * BLK), F32)], 32,
        kinds, image, act2, home_c, core_c, recv_c, core_recv_c, vecs,
        conv2_weight, query_weight, key_weight, value_weight, proj_weight,
    )
    block2_away = to_chip(block2_send)
    out_away = to_chip(out_send)
    attn_got = to_batch(attn_send, 1)

    grad1, block1, block1_send, vec_b = call(
        third_kernel, "third",
        [img16, block, block, rows8],
        [shifts, img32], 24,
        kinds, grad2, conv, stats, vecs, conv2_weight,
    )
    block1_away = to_chip(block1_send)

    def weight_grad(name, act_t, index, own, away, *tail):
        rows = shard_rows + (VECS if tail else 0)
        return call(
            functools.partial(weight_kernel, layer=index, tail=len(tail)), name,
            [((batches // 2, rows, BLK), BF16)] * 2,
            [((C, 2 * PIX), BF16), ((2 * PIX, 9 * BLK), BF16), ((3, PIX + 2 * PAD, BLK), BF16),
             ((9 * C, BLK), F32)],
            24, kinds, act_t, half_t, core_half_t, own, away, *tail,
        )

    keep2, send2 = weight_grad("weight2", act2_t, 1, after(block2, block1), block2_away)
    got2 = to_batch(send2, 1)

    grad_own, grad_send, vec_c = call(
        fourth_kernel, "fourth",
        [((192, C), BF16), ((128, C), BF16), ((batches, VECS, BLK), F32)],
        [shifts, img32, img16, ((VECS, C), F32)], 24,
        kinds, after(grad1, send2), image, stats, grad_middle, vecs, conv1_weight, vec_a, vec_b,
    )
    grad_away = to_chip(grad_send)
    keep1, send1 = weight_grad("weight1", act1_t, 0, block1, block1_away, vec_c)
    got1 = to_batch(send1, 1)

    def scatter(name, keep, got):
        bit = 1
        while bit < bits:
            width = min(2, bits - bit)
            ways = 1 << width
            shape = (keep.shape[0] // ways,) + keep.shape[1:]
            parts = call(
                functools.partial(route_kernel, bit), name + str(bit),
                [(shape, BF16)] * ways, [], 16, keep, got, smem=0,
            )
            got = [to_batch(parts[j], j << bit) for j in range(1, ways)]
            bit += width
            if bit < bits:
                keep = parts[0]
                got = functools.reduce(lambda a, b: a + b, [g.astype(F32) for g in got]).astype(BF16)
            else:
                added = parts[0].astype(F32)
                for g in got:
                    added = added + g.astype(F32)
                return added.astype(BF16)[0]

    def gather(shard):
        far = to_chip(shard)
        near = to_core(shard)
        return shard, far, near, to_core(far)

    attn_parts = gather(scatter("routea", after(attn_keep, send1), attn_got))
    parts2 = gather(scatter("routeb", keep2, got2))
    small = call(
        join_attn_kernel, "joina", [((small_rows, C), F32)] * 4, [], 8, *attn_parts, smem=0
    )
    (whole2,) = call(join_kernel, "joinb", [((shard_rows, C), F32)], [], 8, *parts2, smem=0)
    outputs, input_grad = call(
        unpack_kernel, "unpack",
        [(inputs.shape, BF16)] * 2, [], 8,
        kinds, out_own, out_away, grad_own, grad_away,
    )
    shard1 = scatter("routec", keep1, got1)
    parts1 = gather(after(shard1, whole2, small[0], outputs))
    whole1, sums = call(
        join_kernel, "joinc", [((shard_rows, C), F32), ((VECS, BLK), F32)], [], 8, *parts1, smem=0
    )
    v = [sums[i, :small_rows] for i in range(11)]

    return (
        outputs, input_grad,
        v[9], v[10], whole1, v[8],
        v[6], v[7], whole2, v[5],
        v[0], v[1],
        small[0], v[2], small[1], small[2], v[3], small[3], v[4],
    )


def solution(mesh):
    image = P("batch", "height", None, None)
    vector = P("batch")
    matrix = P("batch", None)
    return jax.shard_map(
        on_device,
        mesh=mesh,
        in_specs=(image, vector) + (P(),) * 17 + (image,),
        out_specs=(
            image, image,
            vector, vector, matrix, vector,
            vector, vector, matrix, vector,
            vector, vector,
            matrix, vector, matrix, matrix, vector, matrix, vector,
        ),
        check_vma=False,
    )
```

```python
import functools

import jax
import jax.numpy as jnp
from jax import lax
from jax.experimental import pallas as pl
from jax.experimental.pallas import tpu as pltpu
from jax.sharding import PartitionSpec as P

GROUPS = 32
UNIT = 8
PIX = 512
PAD = 32
BLK = 128
F32 = jnp.float32
BF16 = jnp.bfloat16
epsilon = 1e-05

VM = pl.BlockSpec(memory_space=pltpu.VMEM)
SM = pl.BlockSpec(memory_space=pltpu.SMEM)
HB = pl.BlockSpec(memory_space=pltpu.HBM)
RATE = 1 << 30
LENGTH = {
    "pack": 10, "stack": 10, "first": 0.02, "second": 30, "third": 20, "fourth": 0.02, "weight2": 1, "weight1": 0.02,
}


def place(bucket_ref):
    h = lax.axis_index("height")
    upper = lax.div(h, 2)
    tall_first = bucket_ref[0] == 1
    tall_image = jnp.where(tall_first, 0, 1)
    home = jnp.where(upper == 1, tall_image, 1 - tall_image)
    away = 1 - home

    def facts(image):
        kind = bucket_ref[image]
        tall = kind == 1
        stride = jnp.where(tall, 2 * UNIT, 4 * UNIT)
        width = jnp.where(kind == 0, 3 * UNIT, stride)
        return (image, tall, stride, width)

    return h, facts(home), facts(away)


def pixel_col(stride, lanes=1):
    rows = lax.broadcasted_iota(jnp.int32, (PIX, lanes), 0)
    return rows, rows & (stride - 1)


def pixel_mask(facts):
    unused, tall, stride, width = facts
    rows, cols = pixel_col(stride)
    limit = jnp.where(tall, 6 * UNIT * UNIT, 8 * UNIT * UNIT)
    mask = jnp.where((cols < width) & (rows < limit), 1.0, 0.0).astype(F32)
    size = jnp.where(tall | (width == 3 * UNIT), 6 * UNIT * UNIT, 8 * UNIT * UNIT)
    return mask, size.astype(F32)


def group_total(row):
    channels = row.shape[-1]
    lane = lax.broadcasted_iota(jnp.int32, row.shape, 1)
    step = 1
    while step < channels // GROUPS:
        up = pltpu.roll(row, channels - step, 1)
        down = pltpu.roll(row, step, 1)
        row = row + jnp.where((lane & step) == 0, up, down)
        step *= 2
    return row


def total(values):
    return jnp.sum(values, axis=0, keepdims=True)


def wide_total(row):
    return group_total(jnp.broadcast_to(row, (8, row.shape[-1])))[0:1]


def norm_stats(values, mask, group_size):
    mean = wide_total(total(values)) / group_size
    centered = (values - mean) * mask
    variance = wide_total(total(centered * centered)) / group_size
    return mean, lax.rsqrt(variance + epsilon)


def silu_norm(values, mean, inverse, gain, shift, mask):
    scale = 0.5 * inverse * gain
    half = values * scale + (0.5 * shift - mean * scale)
    return (half + half * jnp.tanh(half)) * mask


def norm_back(grad, normal, inverse, mask, group_size, gain):
    plain_row = total(grad)
    cross_row = total(grad * normal)
    plain = wide_total(plain_row * gain) / group_size
    cross = wide_total(cross_row * gain) / group_size
    grad_in = grad * (inverse * gain) - mask * (plain * inverse + normal * (cross * inverse))
    return grad_in, cross_row, plain_row


def silu_slope(u):
    half = 0.5 * u
    t = jnp.tanh(half)
    return (0.5 + 0.5 * t) * (1.0 + half * (1.0 - t))


def mm(a, b):
    return jnp.dot(a, b, preferred_element_type=F32)


def mm_nt(a, b):
    return lax.dot_general(a, b, (((1,), (1,)), ((), ())), preferred_element_type=F32)


def mm_tn(a, b):
    return lax.dot_general(a, b, (((0,), (0,)), ((), ())), preferred_element_type=F32)


def fill_shifts(shift_ref, values, stride):
    unused, cols = pixel_col(stride)
    lanes = values.shape[1]
    zeros = jnp.zeros((PAD, lanes), BF16)
    for q in range(3):
        shift_ref[q, 0:PAD, :] = zeros
        shift_ref[q, PAD + PIX : 2 * PAD + PIX, :] = zeros
    left = jnp.where(cols == 0, 0.0, pltpu.roll(values, 1, 0))
    right = jnp.where(cols == stride - 1, 0.0, pltpu.roll(values, PIX - 1, 0))
    shift_ref[0, PAD : PAD + PIX, :] = left.astype(BF16)
    shift_ref[1, PAD : PAD + PIX, :] = values.astype(BF16)
    shift_ref[2, PAD : PAD + PIX, :] = right.astype(BF16)


def tap(shift_ref, p, q, stride, first=0, count=PIX):
    start = pl.multiple_of(PAD + first + (p - 1) * stride, 16)
    return shift_ref[q, pl.ds(start, count), :]


def conv_forward(shift_ref, weight_ref, stride, out_ref, tile=256):
    for first in range(0, PIX, tile):
        stacked = jnp.concatenate(
            [tap(shift_ref, p, q, stride, first, tile) for p in range(3) for q in range(3)], axis=1
        )
        out_ref[first : first + tile, :] = mm(stacked, weight_ref[...])


def conv_backward(shift_ref, weight_ref, stride, out_ref, tile=256):
    channels = weight_ref.shape[1]
    for first in range(0, PIX, tile):
        acc = None
        for p in range(3):
            for q in range(3):
                row = (8 - (3 * p + q)) * channels
                part = mm_nt(
                    tap(shift_ref, p, q, stride, first, tile), weight_ref[row : row + channels, :]
                )
                acc = part if acc is None else acc + part
        out_ref[first : first + tile, :] = acc


def assemble(out_ref, facts, h, pieces):
    unused, tall, stride, width = facts
    own, partner, received, partner_received = pieces
    other = h ^ 1

    @pl.when(tall)
    def _():
        for ref, index in (
            (own, h),
            (partner, other),
            (received, h ^ 2),
            (partner_received, other ^ 2),
        ):
            out_ref[pl.ds(pl.multiple_of(96 * index, 16), 96), :] = ref[0:96, :]
        out_ref[384:512, :] = jnp.zeros((128, out_ref.shape[1]), out_ref.dtype)

    @pl.when(jnp.logical_not(tall))
    def _():
        low = h & 1
        out_ref[pl.ds(pl.multiple_of(192 * low, 16), 192), :] = own[...]
        out_ref[pl.ds(pl.multiple_of(192 * (1 - low), 16), 192), :] = partner[...]

        @pl.when(low == 0)
        def _():
            out_ref[384:512, :] = received[...]

        @pl.when(low == 1)
        def _():
            out_ref[384:512, :] = partner_received[...]


def split_out(full_ref, facts, h, own_ref, send_ref):
    unused, tall, stride, width = facts
    send_h = h ^ 2

    @pl.when(tall)
    def _():
        own_ref[0:96, :] = full_ref[pl.ds(pl.multiple_of(96 * h, 16), 96), :]
        own_ref[96:192, :] = jnp.zeros((96, own_ref.shape[1]), own_ref.dtype)
        send_ref[0:96, :] = full_ref[pl.ds(pl.multiple_of(96 * send_h, 16), 96), :]
        send_ref[96:128, :] = jnp.zeros((32, own_ref.shape[1]), own_ref.dtype)

    @pl.when(jnp.logical_not(tall))
    def _():
        own_ref[...] = full_ref[pl.ds(pl.multiple_of(192 * (h & 1), 16), 192), :]
        send_ref[...] = full_ref[384:512, :]


GAIN1, SHIFT1, BIAS1, GAIN2, SHIFT2, BIAS2, GAIN3, SHIFT3, QB, VB, PB = range(11)
VECS = 16


def vec(vec_ref, index):
    return vec_ref[index : index + 1, :]


def pack(src, facts, dst, wide_rows):
    image, tall, stride, width = facts

    @pl.when(tall)
    def _():
        for row in range(6):
            dst[16 * row : 16 * row + 16, :] = src[image, row, 0:16, :]
        dst[96 : dst.shape[0], :] = jnp.zeros((dst.shape[0] - 96, dst.shape[1]), dst.dtype)

    @pl.when(jnp.logical_not(tall))
    def _():
        for row in range(wide_rows):
            dst[32 * row : 32 * row + 32, :] = src[image, row]


def pack_kernel(bucket_hbm, x_hbm, kinds, away_x, home_x, bucket_ref, x_ref, sems):
    copies = (
        pltpu.make_async_copy(bucket_hbm, bucket_ref, sems.at[0]),
        pltpu.make_async_copy(x_hbm, x_ref, sems.at[1]),
    )
    for copy in copies:
        copy.start()
    for copy in copies:
        copy.wait()
    h, home, away = place(bucket_ref)
    kinds[0] = bucket_ref[0]
    kinds[1] = bucket_ref[1]
    pack(x_ref, away, away_x, 4)
    pack(x_ref, home, home_x, 6)


def stack_kernel(kinds, cot_ref, *refs):
    h, home, away = place(kinds)
    out_ref, away_c, home_c = refs[-3:]
    count = len(refs) - 3
    for index, ref in enumerate(refs[:count]):
        out_ref[index : index + 1, :] = ref[...]
    out_ref[count:, :] = jnp.zeros((VECS - count, out_ref.shape[1]), F32)
    pack(cot_ref, away, away_c, 4)
    pack(cot_ref, home, home_c, 6)


def first_kernel(
    bucket_ref, own, partner, received, partner_received, vecs, weight1,
    image_ref, conv_ref, act2_ref, stats_ref, act1_t, act2_t, send_t,
    shift_ref,
):
    h, home, away = place(bucket_ref)
    stride = home[2]
    mask, pixels = pixel_mask(home)
    channels = vecs.shape[1]
    group_size = pixels * (channels // GROUPS)
    assemble(image_ref, home, h, (own, partner, received, partner_received))
    values = image_ref[...].astype(F32) * mask
    mean1, inverse1 = norm_stats(values, mask, group_size)
    act = silu_norm(values, mean1, inverse1, vec(vecs, GAIN1), vec(vecs, SHIFT1), mask)
    fill_shifts(shift_ref, act, stride)
    act1_t[...] = act.astype(BF16).T
    conv_forward(shift_ref, weight1, stride, conv_ref)
    values = (conv_ref[...] + vec(vecs, BIAS1)) * mask
    conv_ref[...] = values
    mean2, inverse2 = norm_stats(values, mask, group_size)
    act = silu_norm(values, mean2, inverse2, vec(vecs, GAIN2), vec(vecs, SHIFT2), mask)
    act = act.astype(BF16)
    act2_ref[...] = act
    act2_t[...] = act.T
    half = pl.multiple_of((h & 1) * (channels // 2), 16)
    send_t[0] = act1_t[pl.ds(half, channels // 2), :]
    send_t[1] = act2_t[pl.ds(half, channels // 2), :]
    stats_ref[0:1, :] = mean1
    stats_ref[1:2, :] = inverse1
    stats_ref[2:3, :] = mean2
    stats_ref[3:4, :] = inverse2
    stats_ref[4:8, :] = jnp.zeros((4, channels), F32)


def second_kernel(
    bucket_ref, image_ref, act2_ref, own, partner, received, partner_received, vecs,
    weight2, wq, wk, wv, wp,
    middle_ref, mixed_ref, grad2_ref, grad_middle_ref, attn_keep, attn_send, vec_ref,
    block_keep, block_send,
    shift_ref, full_ref, grads_ref, sum_ref,
):
    h, home, away = place(bucket_ref)
    stride = home[2]
    mask, pixels = pixel_mask(home)
    channels = vecs.shape[1]
    group_size = pixels * (channels // GROUPS)
    scaling = channels ** (-0.5)
    fill_shifts(shift_ref, act2_ref[...].astype(F32), stride)
    conv_forward(shift_ref, weight2, stride, middle_ref)
    middle = mask * (image_ref[...].astype(F32) + (middle_ref[...] + vec(vecs, BIAS2)))
    middle_ref[...] = middle
    mean3, inverse3 = norm_stats(middle, mask, group_size)
    normal = (middle - mean3) * inverse3
    normed = (normal * vec(vecs, GAIN3) + vec(vecs, SHIFT3)).astype(BF16)
    wide = jnp.concatenate([wq[...], wk[...], wv[...]], axis=1)
    joint = mm(normed, wide)
    queries = (joint[:, 0:channels] + vec(vecs, QB)).astype(BF16)
    keys = joint[:, channels : 2 * channels].astype(BF16)
    values = (joint[:, 2 * channels :] + vec(vecs, VB)).astype(BF16)
    lanes = lax.broadcasted_iota(jnp.int32, (1, PIX), 1)
    key_cols = lanes & (stride - 1)
    key_valid = (key_cols < home[3]) & (lanes < jnp.where(home[1], 384, 512))
    scores = jnp.where(key_valid, mm_nt(queries, keys) * scaling, -1000000000.0)
    raised = jnp.exp(scores - jnp.max(scores, axis=1, keepdims=True))
    soft = raised * (1.0 / jnp.sum(raised, axis=1, keepdims=True))
    soft16 = soft.astype(BF16)
    mixed = mm(soft16, values).astype(BF16)
    mixed_ref[...] = mixed

    assemble(full_ref, home, h, (own, partner, received, partner_received))
    grad_top = full_ref[...].astype(F32) * mask
    grad_rows = grad_top.astype(BF16)
    grad_mixed = mm_nt(grad_rows, wp[...]).astype(BF16)
    grad_soft = mm_nt(grad_mixed, values)
    grad_values = mm_tn(soft16, grad_mixed).astype(BF16)
    grad_scores = soft * (grad_soft - jnp.sum(soft * grad_soft, axis=1, keepdims=True))
    grad_scores = grad_scores.astype(BF16)
    grad_queries = (mm(grad_scores, keys) * scaling).astype(BF16)
    grad_keys = (mm_tn(grad_scores, queries) * scaling).astype(BF16)
    grads_ref[:, 0:channels] = grad_queries
    grads_ref[:, channels : 2 * channels] = grad_keys
    grads_ref[:, 2 * channels : 3 * channels] = grad_values
    grads_ref[:, 3 * channels : 4 * channels] = grad_rows
    grad_normed = mm_nt(grads_ref[:, 0 : 3 * channels], wide)
    grad_in, gain_grad, shift_grad = norm_back(
        grad_normed, normal, inverse3, mask, group_size, vec(vecs, GAIN3)
    )
    grad_middle = mask * (grad_top + grad_in)
    grad_middle_ref[...] = grad_middle
    grad2 = grad_middle.astype(BF16)
    grad2_ref[...] = grad2
    vec_ref[0:1, :] = gain_grad
    vec_ref[1:2, :] = shift_grad
    vec_ref[2:3, :] = total(grad_queries.astype(F32))
    vec_ref[3:4, :] = total(grad_values.astype(F32))
    vec_ref[4:5, :] = total(grad_top)
    vec_ref[5:6, :] = total(grad2.astype(F32))
    vec_ref[6:8, :] = jnp.zeros((2, channels), F32)

    keep_at = pl.multiple_of(BLK * h, BLK)
    send_at = pl.multiple_of(BLK * (h ^ 2), BLK)
    block_keep[...] = grad2_ref[:, pl.ds(keep_at, BLK)]
    block_send[...] = grad2_ref[:, pl.ds(send_at, BLK)]

    def blocks(index):
        start = index * channels
        return [
            grads_ref[:, pl.ds(pl.multiple_of(start + BLK * h, BLK), BLK)],
            grads_ref[:, pl.ds(pl.multiple_of(start + BLK * (h ^ 2), BLK), BLK)],
        ]

    sum_ref[:, 0 : 6 * BLK] = mm_tn(normed, jnp.concatenate(blocks(0) + blocks(1) + blocks(2), axis=1))
    sum_ref[:, 6 * BLK : 8 * BLK] = mm_tn(mixed, jnp.concatenate(blocks(3), axis=1))
    mine = lax.axis_index("batch") & 1
    pairs = attn_keep.shape[0]
    rows = channels // (2 * pairs)
    for pair in range(pairs):
        for dst, which in ((attn_keep, mine), (attn_send, 1 - mine)):
            part = sum_ref[pl.ds(pl.multiple_of((2 * pair + which) * rows, 8), rows), :].astype(BF16)
            for index in range(4):
                dst[pair, index * rows : (index + 1) * rows, :] = part[:, index * 2 * BLK : (index + 1) * 2 * BLK]


def third_kernel(
    bucket_ref, grad2_ref, conv_ref, stats_ref, vecs, weight2,
    grad1_ref, block_keep, block_send, vec_ref,
    shift_ref, acc_ref,
):
    h, home, away = place(bucket_ref)
    stride = home[2]
    mask, pixels = pixel_mask(home)
    channels = vecs.shape[1]
    group_size = pixels * (channels // GROUPS)
    fill_shifts(shift_ref, grad2_ref[...].astype(F32), stride)
    conv_backward(shift_ref, weight2, stride, acc_ref)
    inverse = stats_ref[3:4, :]
    normal = (conv_ref[...] - stats_ref[2:3, :]) * inverse
    u = normal * vec(vecs, GAIN2) + vec(vecs, SHIFT2)
    grad = mask * acc_ref[...] * silu_slope(u)
    grad_in, gain_grad, shift_grad = norm_back(
        grad, normal, inverse, mask, group_size, vec(vecs, GAIN2)
    )
    grad1 = grad_in.astype(BF16)
    grad1_ref[...] = grad1
    vec_ref[0:1, :] = gain_grad
    vec_ref[1:2, :] = shift_grad
    vec_ref[2:3, :] = total(grad1.astype(F32))
    vec_ref[3:8, :] = jnp.zeros((5, channels), F32)
    block_keep[...] = grad1_ref[:, pl.ds(pl.multiple_of(BLK * h, BLK), BLK)]
    block_send[...] = grad1_ref[:, pl.ds(pl.multiple_of(BLK * (h ^ 2), BLK), BLK)]


def fourth_kernel(
    bucket_ref, grad1_ref, image_ref, stats_ref, grad_middle_ref, middle_ref, mixed_ref, vecs,
    weight1, wp, vec_a, vec_b,
    out_own, grad_own, send_ref, vec_keep, vec_send,
    shift_ref, acc_ref, full_ref, vec_ref,
):
    h, home, away = place(bucket_ref)
    stride = home[2]
    mask, pixels = pixel_mask(home)
    channels = vecs.shape[1]
    group_size = pixels * (channels // GROUPS)
    projected = mm(mixed_ref[...], wp[...]) + vec(vecs, PB)
    full_ref[...] = (mask * (middle_ref[...] + projected)).astype(BF16)
    split_out(full_ref, home, h, out_own, send_ref.at[0])
    fill_shifts(shift_ref, grad1_ref[...].astype(F32), stride)
    conv_backward(shift_ref, weight1, stride, acc_ref)
    inverse = stats_ref[1:2, :]
    normal = (image_ref[...].astype(F32) * mask - stats_ref[0:1, :]) * inverse
    u = normal * vec(vecs, GAIN1) + vec(vecs, SHIFT1)
    grad = mask * acc_ref[...] * silu_slope(u)
    grad_in, gain_grad, shift_grad = norm_back(
        grad, normal, inverse, mask, group_size, vec(vecs, GAIN1)
    )
    full_ref[...] = (mask * (grad_middle_ref[...] + grad_in)).astype(BF16)
    split_out(full_ref, home, h, grad_own, send_ref.at[1])
    vec_ref[0:6, :] = vec_a[0:6, :]
    vec_ref[6:9, :] = vec_b[0:3, :]
    vec_ref[9:10, :] = gain_grad
    vec_ref[10:11, :] = shift_grad
    vec_ref[11:VECS, :] = jnp.zeros((VECS - 11, channels), F32)
    pairs = vec_keep.shape[0]
    rows = channels // (2 * pairs)
    mine = (lax.axis_index("batch") & 1) == 1
    for pair in range(pairs):
        parts = []
        for shard in (2 * pair, 2 * pair + 1):
            start = shard * rows
            tile = start // BLK * BLK
            part = vec_ref[:, tile : tile + BLK]
            parts.append(part if start == tile else pltpu.roll(part, BLK - (start - tile), 1))
        vec_keep[pair] = jnp.where(mine, parts[1], parts[0]).astype(BF16)
        vec_send[pair] = jnp.where(mine, parts[0], parts[1]).astype(BF16)


def weight_kernel(
    bucket_ref, act_t, half_t, partner_half_t, block_own, block_away,
    keep_ref, send_ref, left_ref, right_ref, shift_ref, sum_ref, *, layer,
):
    h, home, away = place(bucket_ref)
    channels = act_t.shape[0]
    half = channels // 2
    left_ref[:, 0:PIX] = act_t[...]
    left_ref[pl.ds(pl.multiple_of((h & 1) * half, 16), half), PIX : 2 * PIX] = half_t[layer]
    left_ref[pl.ds(pl.multiple_of((1 - (h & 1)) * half, 16), half), PIX : 2 * PIX] = (
        partner_half_t[layer]
    )
    for index, (facts, block) in enumerate(((home, block_own), (away, block_away))):
        stride = facts[2]
        fill_shifts(shift_ref, block[...].astype(F32), stride)
        for p in range(3):
            for q in range(3):
                column = (3 * p + q) * BLK
                right_ref[index * PIX : (index + 1) * PIX, column : column + BLK] = tap(
                    shift_ref, 2 - p, 2 - q, stride
                )
    joint = mm(left_ref[...], right_ref[...])
    for t in range(9):
        sum_ref[t * channels : (t + 1) * channels, :] = joint[:, t * BLK : (t + 1) * BLK]
    mine = lax.axis_index("batch") & 1
    pairs = keep_ref.shape[0]
    rows = 9 * channels // (2 * pairs)
    for pair in range(pairs):
        for dst, which in ((keep_ref, mine), (send_ref, 1 - mine)):
            shard = 2 * pair + which
            dst[pair] = sum_ref[pl.ds(pl.multiple_of(shard * rows, 8), rows), :].astype(BF16)


def route_kernel(*refs, bit, ways):
    group = (lax.axis_index("batch") >> bit) & (ways - 1)
    outs = refs[len(refs) - ways :]
    count = outs[0].shape[0]
    first = 0
    for keep_ref, got_ref in zip(refs[0 : len(refs) - ways : 2], refs[1 : len(refs) - ways : 2]):
        rows = keep_ref.shape[1]
        for step, dst in enumerate(outs):
            which = group ^ step
            for index in range(count):
                at = index * ways + which
                dst[index, first : first + rows, :] = (
                    keep_ref[at].astype(F32) + got_ref[at].astype(F32)
                ).astype(BF16)
        first += rows


def join_kernel(own_ref, far_ref, near_ref, diagonal_ref, out_ref, *tail_ref):
    h = lax.axis_index("height")
    rows = out_ref.shape[0]
    for ref, index in ((own_ref, h), (far_ref, h ^ 2), (near_ref, h ^ 1), (diagonal_ref, h ^ 3)):
        out_ref[:, pl.ds(pl.multiple_of(BLK * index, BLK), BLK)] = ref[0:rows, :].astype(F32)
    if tail_ref:
        own, far = own_ref[rows:, :].astype(F32), far_ref[rows:, :].astype(F32)
        near, diagonal = near_ref[rows:, :].astype(F32), diagonal_ref[rows:, :].astype(F32)
        sums = 0.5 * ((own + near) + (far + diagonal))
        for index, dst in enumerate(tail_ref):
            dst[...] = sums[index : index + 1, 0 : dst.shape[1]]


def join_attn_kernel(own_ref, far_ref, near_ref, diagonal_ref, *out_refs):
    h = lax.axis_index("height")
    rows = out_refs[0].shape[0]
    for first, second, index in ((own_ref, far_ref, h), (near_ref, diagonal_ref, h ^ 1)):
        for position in range(2):
            lane, other = position * BLK, (1 - position) * BLK
            column = pl.multiple_of(BLK * (index ^ (2 * position)), BLK)
            for number, dst in enumerate(out_refs):
                at = number * rows
                dst[:, pl.ds(column, BLK)] = first[at : at + rows, lane : lane + BLK].astype(
                    F32
                ) + second[at : at + rows, other : other + BLK].astype(F32)


def unpack_kernel(bucket_ref, out_own, grad_own, away_ref, out_ref, grad_ref):
    h, home, away = place(bucket_ref)
    for own, received, dst in (
        (out_own, away_ref.at[0], out_ref),
        (grad_own, away_ref.at[1], grad_ref),
    ):
        channels = dst.shape[3]
        for facts, src, wide_rows in ((away, received, 4), (home, own, 6)):
            image, tall, stride, width = facts

            @pl.when(tall)
            def _():
                for row in range(6):
                    dst[image, row, 0:16, :] = src[16 * row : 16 * row + 16, :]
                    dst[image, row, 16:32, :] = jnp.zeros((16, channels), dst.dtype)

            @pl.when(jnp.logical_not(tall))
            def _():
                for row in range(wide_rows):
                    dst[image, row] = src[32 * row : 32 * row + 32, :]
                for row in range(wide_rows, 6):
                    dst[image, row] = jnp.zeros((32, channels), dst.dtype)

            if wide_rows == 4:

                @pl.when(jnp.logical_not(tall) & (h == 3))
                def _():
                    for row in range(6):
                        dst[image, row] = jnp.zeros((32, channels), dst.dtype)


def call(kernel, name, outs, scratch, vmem, *operands, smem=1, any_from=99):
    specs = [SM] * smem + [VM] * (len(operands) - smem)
    specs = [HB if i >= any_from else spec for i, spec in enumerate(specs)]
    return pl.pallas_call(
        kernel,
        name=name,
        out_shape=[jax.ShapeDtypeStruct(shape, dtype) for shape, dtype in outs],
        in_specs=specs,
        out_specs=[SM if dtype == jnp.int32 else VM for shape, dtype in outs],
        scratch_shapes=[
            pltpu.SemaphoreType.DMA(shape)
            if dtype is None
            else (pltpu.SMEM if dtype == jnp.int32 else pltpu.VMEM)(shape, dtype)
            for shape, dtype in scratch
        ],
        compiler_params=pltpu.CompilerParams(vmem_limit_bytes=vmem << 20),
        cost_estimate=pl.CostEstimate(
            flops=int(LENGTH.get(name, 0.02) * RATE), bytes_accessed=1024, transcendentals=0
        ),
    )(*operands)


def on_device(
    inputs,
    bucket,
    norm1_gain,
    norm1_shift,
    conv1_weight,
    conv1_bias,
    norm2_gain,
    norm2_shift,
    conv2_weight,
    conv2_bias,
    norm3_gain,
    norm3_shift,
    query_weight,
    query_bias,
    key_weight,
    value_weight,
    value_bias,
    proj_weight,
    proj_bias,
    cotangent,
):
    C = inputs.shape[-1]
    batches = lax.axis_size("batch")
    bits = batches.bit_length() - 1
    shard_rows = 9 * C // batches
    small_rows = C // batches

    def row(v):
        return v.reshape(1, C)

    def to_core(v):
        return lax.ppermute(v, "height", [(i, i ^ 1) for i in range(4)])

    def to_chip(v):
        return lax.ppermute(v, "height", [(i, i ^ 2) for i in range(4)])

    def to_batch(v, change):
        return lax.ppermute(v, "batch", [(i, i ^ change) for i in range(batches)])

    def after(v, *others):
        return lax.optimization_barrier((v,) + others)[0]

    img16 = ((PIX, C), BF16)
    img32 = ((PIX, C), F32)
    rows8 = ((8, C), F32)
    block = ((PIX, BLK), BF16)
    turned = ((C, PIX), BF16)
    shifts = ((3, PIX + 2 * PAD, C), BF16)

    kinds, away_x, home_x = call(
        pack_kernel, "pack",
        [((2,), jnp.int32), ((128, C), BF16), ((192, C), BF16)],
        [((2,), jnp.int32), (inputs.shape, BF16), ((2,), None)], 54, bucket, inputs,
        smem=0, any_from=0,
    )
    vectors = (
        norm1_gain, norm1_shift, conv1_bias, norm2_gain, norm2_shift, conv2_bias,
        norm3_gain, norm3_shift, query_bias, value_bias, proj_bias,
    )
    recv_x = to_chip(away_x)
    core_x = to_core(home_x)
    vecs, away_c, home_c = call(
        stack_kernel, "stack", [((VECS, C), F32), ((128, C), BF16), ((192, C), BF16)], [], 8,
        kinds, cotangent, *[row(v) for v in vectors],
    )
    recv_c = to_chip(away_c)
    core_c = to_core(home_c)
    core_recv_c = lax.ppermute(away_c, "height", [(i, i ^ 3) for i in range(4)])
    core_recv_x = to_core(after(recv_x, vecs))

    image, conv, act2, stats, act1_t, act2_t, send_t = call(
        first_kernel, "first",
        [img16, img32, img16, rows8, turned, turned, ((2, C // 2, PIX), BF16)],
        [shifts], 24,
        kinds, home_x, core_x, recv_x, core_recv_x, vecs, conv1_weight,
    )
    half_t = to_chip(send_t)
    core_half_t = to_core(half_t)

    attn_out = ((batches // 2, 4 * small_rows, 2 * BLK), BF16)
    middle, mixed, grad2, grad_middle, attn_keep, attn_send, vec_a, block2, block2_send = call(
        second_kernel, "second",
        [img32, img16, img16, img32, attn_out, attn_out, rows8, block, block],
        [shifts, img16, ((PIX, 4 * C), BF16), ((C, 8 * BLK), F32)], 32,
        kinds, image, act2, home_c, core_c, recv_c, core_recv_c, vecs,
        conv2_weight, query_weight, key_weight, value_weight, proj_weight,
    )
    block2_away = to_chip(block2_send)
    attn_got = to_batch(attn_send, 1)

    grad1, block1, block1_send, vec_b = call(
        third_kernel, "third",
        [img16, block, block, rows8],
        [shifts, img32], 24,
        kinds, grad2, conv, stats, vecs, conv2_weight,
    )
    block1_away = to_chip(block1_send)

    def weight_grad(name, act_t, index, own, away):
        return call(
            functools.partial(weight_kernel, layer=index), name,
            [((batches // 2, shard_rows, BLK), BF16)] * 2,
            [((C, 2 * PIX), BF16), ((2 * PIX, 9 * BLK), BF16), ((3, PIX + 2 * PAD, BLK), BF16),
             ((9 * C, BLK), F32)],
            24, kinds, act_t, half_t, core_half_t, own, away,
        )

    keep2, send2 = weight_grad("weight2", act2_t, 1, after(block2, block1), block2_away)
    got2 = to_batch(send2, 1)

    def scatter(name, *pairs):
        bit = 1
        while True:
            width = min(2, bits - bit)
            ways = 1 << width
            count = pairs[0].shape[0] // ways
            rows = sum(v.shape[1] for v in pairs[::2])
            parts = call(
                functools.partial(route_kernel, bit=bit, ways=ways), name + str(bit),
                [((count, rows, pairs[0].shape[2]), BF16)] * ways, [], 16, *pairs, smem=0,
            )
            got = [to_batch(parts[j], j << bit) for j in range(1, ways)]
            bit += width
            added = functools.reduce(lambda a, b: a + b, [g.astype(F32) for g in got])
            if bit == bits:
                return parts, (added + parts[0].astype(F32)).astype(BF16)[0]
            pairs = (parts[0], added.astype(BF16))

    def gather(shard):
        far = to_chip(shard)
        near = to_core(shard)
        return shard, far, near, to_core(far)

    routed_a, shard_a = scatter("routea", after(attn_keep, send2), attn_got)
    keep1, send1 = weight_grad("weight1", act1_t, 0, after(block1, *routed_a), block1_away)
    got1 = to_batch(send1, 1)

    out_own, grad_own, image_send, vec_keep, vec_send = call(
        fourth_kernel, "fourth",
        [((192, C), BF16), ((192, C), BF16), ((2, 128, C), BF16),
         ((batches // 2, VECS, BLK), BF16), ((batches // 2, VECS, BLK), BF16)],
        [shifts, img32, img16, ((VECS, C), F32)], 24,
        kinds, after(grad1, send1), image, stats, grad_middle, middle, mixed, vecs,
        conv1_weight, proj_weight, vec_a, vec_b,
    )
    image_away = to_chip(image_send)
    vec_got = to_batch(vec_send, 1)

    routed_b, shard_b = scatter("routeb", after(keep2, shard_a, vec_keep), got2)
    parts_a = gather(after(shard_a, *routed_b))
    small = call(
        join_attn_kernel, "joina", [((small_rows, C), F32)] * 4, [], 8, *parts_a, smem=0
    )
    outputs, input_grad = call(
        unpack_kernel, "unpack",
        [(inputs.shape, BF16)] * 2, [], 8,
        kinds, out_own, grad_own, after(image_away, *routed_b),
    )
    routed_c, shard_c = scatter(
        "routec", after(keep1, shard_b), got1, vec_keep, vec_got
    )
    (whole2,) = call(join_kernel, "joinb", [((shard_rows, C), F32)], [], 8, *gather(shard_b), smem=0)
    whole1, *sums = call(
        join_kernel, "joinc", [((shard_rows, C), F32)] + [((1, small_rows), F32)] * 11, [], 8,
        *gather(after(shard_c, whole2, small[0], outputs)), smem=0,
    )
    v = [row.reshape(small_rows) for row in sums]

    return (
        outputs, input_grad,
        v[9], v[10], whole1, v[8],
        v[6], v[7], whole2, v[5],
        v[0], v[1],
        small[0], v[2], small[1], small[2], v[3], small[3], v[4],
    )


def solution(mesh):
    image = P("batch", "height", None, None)
    vector = P("batch")
    matrix = P("batch", None)
    return jax.shard_map(
        on_device,
        mesh=mesh,
        in_specs=(image, vector) + (P(),) * 17 + (image,),
        out_specs=(
            image, image,
            vector, vector, matrix, vector,
            vector, vector, matrix, vector,
            vector, vector,
            matrix, vector, matrix, matrix, vector, matrix, vector,
        ),
        check_vma=False,
    )
```

```python
import functools

import jax
import jax.numpy as jnp
from jax import lax
from jax.experimental import pallas as pl
from jax.experimental.pallas import tpu as pltpu
from jax.sharding import PartitionSpec as P

GROUPS = 32
UNIT = 8
PIX = 512
PAD = 32
BLK = 128
F32 = jnp.float32
BF16 = jnp.bfloat16
epsilon = 1e-05

VM = pl.BlockSpec(memory_space=pltpu.VMEM)
SM = pl.BlockSpec(memory_space=pltpu.SMEM)
HB = pl.BlockSpec(memory_space=pltpu.HBM)
RATE = 1 << 30
LENGTH = {
    "pack": 10, "stack": 10, "first": 0.02, "second": 30, "third": 20, "fourth": 10, "weight2": 1, "weight1": 3,
}


def place(bucket_ref):
    h = lax.axis_index("height")
    upper = lax.div(h, 2)
    tall_first = bucket_ref[0] == 1
    tall_image = jnp.where(tall_first, 0, 1)
    home = jnp.where(upper == 1, tall_image, 1 - tall_image)
    away = 1 - home

    def facts(image):
        kind = bucket_ref[image]
        tall = kind == 1
        stride = jnp.where(tall, 2 * UNIT, 4 * UNIT)
        width = jnp.where(kind == 0, 3 * UNIT, stride)
        return (image, tall, stride, width)

    return h, facts(home), facts(away)


def pixel_col(stride, lanes=1):
    rows = lax.broadcasted_iota(jnp.int32, (PIX, lanes), 0)
    return rows, rows & (stride - 1)


def pixel_mask(facts):
    unused, tall, stride, width = facts
    rows, cols = pixel_col(stride)
    limit = jnp.where(tall, 6 * UNIT * UNIT, 8 * UNIT * UNIT)
    mask = jnp.where((cols < width) & (rows < limit), 1.0, 0.0).astype(F32)
    size = jnp.where(tall | (width == 3 * UNIT), 6 * UNIT * UNIT, 8 * UNIT * UNIT)
    return mask, size.astype(F32)


def group_total(rows):
    members = rows.shape[1] // GROUPS
    lane = lax.broadcasted_iota(jnp.int32, (rows.shape[0], BLK), 1)
    tiles = []
    for tile in range(rows.shape[1] // BLK):
        part = rows[:, tile * BLK : (tile + 1) * BLK]
        step = 1
        while step < members:
            place_in_four = (lane // step) & 3
            added = part
            for d in (1, 2, 3):
                up = pltpu.roll(part, BLK - d * step, 1)
                down = pltpu.roll(part, (4 - d) * step, 1)
                added = added + jnp.where(place_in_four + d < 4, up, down)
            part = added
            step *= 4
        tiles.append(part)
    return jnp.concatenate(tiles, axis=1)


def total(values):
    return jnp.sum(values, axis=0, keepdims=True)


def wide_total(*rows):
    stacked = jnp.concatenate(list(rows) + [rows[0]] * (8 - len(rows)), axis=0)
    sums = group_total(stacked)
    return [sums[i : i + 1] for i in range(len(rows))]


def norm_stats(values, mask, group_size):
    mean = wide_total(total(values))[0] / group_size
    centered = (values - mean) * mask
    variance = wide_total(total(centered * centered))[0] / group_size
    return mean, lax.rsqrt(variance + epsilon)


def silu_norm(values, mean, inverse, gain, shift, mask):
    scale = 0.5 * inverse * gain
    half = values * scale + (0.5 * shift - mean * scale)
    return (half + half * jnp.tanh(half)) * mask


def norm_back(grad, normal, inverse, mask, group_size, gain):
    plain_row = total(grad)
    cross_row = total(grad * normal)
    plain, cross = [v / group_size for v in wide_total(plain_row * gain, cross_row * gain)]
    grad_in = grad * (inverse * gain) - mask * (plain * inverse + normal * (cross * inverse))
    return grad_in, cross_row, plain_row


def silu_slope(u):
    half = 0.5 * u
    t = jnp.tanh(half)
    return (0.5 + 0.5 * t) * (1.0 + half * (1.0 - t))


def mm(a, b):
    return jnp.dot(a, b, preferred_element_type=F32)


def mm_nt(a, b):
    return lax.dot_general(a, b, (((1,), (1,)), ((), ())), preferred_element_type=F32)


def mm_tn(a, b):
    return lax.dot_general(a, b, (((0,), (0,)), ((), ())), preferred_element_type=F32)


def fill_shifts(shift_ref, values, stride):
    unused, cols = pixel_col(stride)
    lanes = values.shape[1]
    zeros = jnp.zeros((PAD, lanes), BF16)
    for q in range(3):
        shift_ref[q, 0:PAD, :] = zeros
        shift_ref[q, PAD + PIX : 2 * PAD + PIX, :] = zeros
    left = jnp.where(cols == 0, 0.0, pltpu.roll(values, 1, 0))
    right = jnp.where(cols == stride - 1, 0.0, pltpu.roll(values, PIX - 1, 0))
    shift_ref[0, PAD : PAD + PIX, :] = left.astype(BF16)
    shift_ref[1, PAD : PAD + PIX, :] = values.astype(BF16)
    shift_ref[2, PAD : PAD + PIX, :] = right.astype(BF16)


def tap(shift_ref, p, q, stride, first=0, count=PIX):
    start = pl.multiple_of(PAD + first + (p - 1) * stride, 16)
    return shift_ref[q, pl.ds(start, count), :]


def conv_forward(shift_ref, weight_ref, stride, out_ref, tile=256):
    for first in range(0, PIX, tile):
        stacked = jnp.concatenate(
            [tap(shift_ref, p, q, stride, first, tile) for p in range(3) for q in range(3)], axis=1
        )
        out_ref[first : first + tile, :] = mm(stacked, weight_ref[...])


def conv_backward(shift_ref, weight_ref, stride, out_ref, tile=256):
    channels = weight_ref.shape[1]
    for first in range(0, PIX, tile):
        acc = None
        for p in range(3):
            for q in range(3):
                row = (8 - (3 * p + q)) * channels
                part = mm_nt(
                    tap(shift_ref, p, q, stride, first, tile), weight_ref[row : row + channels, :]
                )
                acc = part if acc is None else acc + part
        out_ref[first : first + tile, :] = acc


def assemble(out_ref, facts, h, pieces):
    unused, tall, stride, width = facts
    own, partner, received, partner_received = pieces
    other = h ^ 1

    @pl.when(tall)
    def _():
        for ref, index in (
            (own, h),
            (partner, other),
            (received, h ^ 2),
            (partner_received, other ^ 2),
        ):
            out_ref[pl.ds(pl.multiple_of(96 * index, 16), 96), :] = ref[0:96, :]
        out_ref[384:512, :] = jnp.zeros((128, out_ref.shape[1]), out_ref.dtype)

    @pl.when(jnp.logical_not(tall))
    def _():
        low = h & 1
        out_ref[pl.ds(pl.multiple_of(192 * low, 16), 192), :] = own[...]
        out_ref[pl.ds(pl.multiple_of(192 * (1 - low), 16), 192), :] = partner[...]

        @pl.when(low == 0)
        def _():
            out_ref[384:512, :] = received[0:128, :]

        @pl.when(low == 1)
        def _():
            out_ref[384:512, :] = partner_received[0:128, :]


def split_out(full_ref, facts, h, own_ref, send_ref):
    unused, tall, stride, width = facts
    send_h = h ^ 2

    @pl.when(tall)
    def _():
        own_ref[0:96, :] = full_ref[pl.ds(pl.multiple_of(96 * h, 16), 96), :]
        own_ref[96:192, :] = jnp.zeros((96, own_ref.shape[1]), own_ref.dtype)
        send_ref[0:96, :] = full_ref[pl.ds(pl.multiple_of(96 * send_h, 16), 96), :]
        send_ref[96:128, :] = jnp.zeros((32, own_ref.shape[1]), own_ref.dtype)

    @pl.when(jnp.logical_not(tall))
    def _():
        own_ref[...] = full_ref[pl.ds(pl.multiple_of(192 * (h & 1), 16), 192), :]
        send_ref[...] = full_ref[384:512, :]


GAIN1, SHIFT1, BIAS1, GAIN2, SHIFT2, BIAS2, GAIN3, SHIFT3, QB, VB, PB = range(11)
VECS = 16


def vec(vec_ref, index):
    return vec_ref[index : index + 1, :]


def pack(src, facts, dst, wide_rows):
    image, tall, stride, width = facts

    @pl.when(tall)
    def _():
        for row in range(6):
            dst[16 * row : 16 * row + 16, :] = src[image, row, 0:16, :]
        dst[96 : dst.shape[0], :] = jnp.zeros((dst.shape[0] - 96, dst.shape[1]), dst.dtype)

    @pl.when(jnp.logical_not(tall))
    def _():
        for row in range(wide_rows):
            dst[32 * row : 32 * row + 32, :] = src[image, row]


def pack_kernel(bucket_hbm, x_hbm, kinds, away_x, home_x, bucket_ref, x_ref, sems):
    copies = (
        pltpu.make_async_copy(bucket_hbm, bucket_ref, sems.at[0]),
        pltpu.make_async_copy(x_hbm, x_ref, sems.at[1]),
    )
    for copy in copies:
        copy.start()
    for copy in copies:
        copy.wait()
    h, home, away = place(bucket_ref)
    kinds[0] = bucket_ref[0]
    kinds[1] = bucket_ref[1]
    pack(x_ref, away, away_x, 4)
    pack(x_ref, home, home_x, 6)


def stack_kernel(kinds, cot_ref, *refs):
    h, home, away = place(kinds)
    out_ref, away_c, home_c = refs[-3:]
    count = len(refs) - 3
    for index, ref in enumerate(refs[:count]):
        out_ref[index : index + 1, :] = ref[...]
    out_ref[count:, :] = jnp.zeros((VECS - count, out_ref.shape[1]), F32)
    pack(cot_ref, away, away_c, 4)
    pack(cot_ref, home, home_c, 6)


def first_kernel(
    bucket_ref, own, partner, received, partner_received, vecs, weight1,
    image_ref, conv_ref, act2_ref, stats_ref, act1_t, act2_t, send_t,
    shift_ref,
):
    h, home, away = place(bucket_ref)
    stride = home[2]
    mask, pixels = pixel_mask(home)
    channels = vecs.shape[1]
    group_size = pixels * (channels // GROUPS)
    assemble(image_ref, home, h, (own, partner, received, partner_received))
    values = image_ref[...].astype(F32) * mask
    mean1, inverse1 = norm_stats(values, mask, group_size)
    act = silu_norm(values, mean1, inverse1, vec(vecs, GAIN1), vec(vecs, SHIFT1), mask)
    fill_shifts(shift_ref, act, stride)
    act1_t[...] = act.astype(BF16).T
    conv_forward(shift_ref, weight1, stride, conv_ref)
    values = (conv_ref[...] + vec(vecs, BIAS1)) * mask
    conv_ref[...] = values
    mean2, inverse2 = norm_stats(values, mask, group_size)
    act = silu_norm(values, mean2, inverse2, vec(vecs, GAIN2), vec(vecs, SHIFT2), mask)
    act = act.astype(BF16)
    act2_ref[...] = act
    act2_t[...] = act.T
    half = pl.multiple_of((h & 1) * (channels // 2), 16)
    send_t[0] = act1_t[pl.ds(half, channels // 2), :]
    send_t[1] = act2_t[pl.ds(half, channels // 2), :]
    stats_ref[0:1, :] = mean1
    stats_ref[1:2, :] = inverse1
    stats_ref[2:3, :] = mean2
    stats_ref[3:4, :] = inverse2
    stats_ref[4:8, :] = jnp.zeros((4, channels), F32)


def second_kernel(
    bucket_ref, image_ref, act2_ref, own, partner, received, partner_received, vecs,
    weight2, wq, wk, wv, wp,
    middle_ref, mixed_ref, grad2_ref, grad_middle_ref, attn_keep, attn_send, vec_ref,
    block_keep, block_send,
    shift_ref, full_ref, grads_ref, sum_ref,
):
    h, home, away = place(bucket_ref)
    stride = home[2]
    mask, pixels = pixel_mask(home)
    channels = vecs.shape[1]
    group_size = pixels * (channels // GROUPS)
    scaling = channels ** (-0.5)
    assemble(full_ref, home, h, (own, partner, received, partner_received))
    fill_shifts(shift_ref, act2_ref[...].astype(F32), stride)
    conv_forward(shift_ref, weight2, stride, middle_ref)
    middle = mask * (image_ref[...].astype(F32) + (middle_ref[...] + vec(vecs, BIAS2)))
    middle_ref[...] = middle
    mean3, inverse3 = norm_stats(middle, mask, group_size)
    normal = (middle - mean3) * inverse3
    normed = (normal * vec(vecs, GAIN3) + vec(vecs, SHIFT3)).astype(BF16)
    wide = jnp.concatenate([wq[...], wk[...], wv[...]], axis=1)
    joint = mm(normed, wide)
    queries = (joint[:, 0:channels] + vec(vecs, QB)).astype(BF16)
    keys = joint[:, channels : 2 * channels].astype(BF16)
    values = (joint[:, 2 * channels :] + vec(vecs, VB)).astype(BF16)
    lanes = lax.broadcasted_iota(jnp.int32, (1, PIX), 1)
    key_cols = lanes & (stride - 1)
    key_valid = (key_cols < home[3]) & (lanes < jnp.where(home[1], 384, 512))
    scores = jnp.where(key_valid, mm_nt(queries, keys) * scaling, -1000000000.0)
    grad_top = full_ref[...].astype(F32) * mask
    grad_rows = grad_top.astype(BF16)
    grad_mixed = mm_nt(grad_rows, wp[...]).astype(BF16)
    grad_soft = mm_nt(grad_mixed, values)
    raised = jnp.exp(scores - jnp.max(scores, axis=1, keepdims=True))
    soft = raised * (1.0 / jnp.sum(raised, axis=1, keepdims=True))
    soft16 = soft.astype(BF16)
    mixed = mm(soft16, values).astype(BF16)
    mixed_ref[...] = mixed

    grad_values = mm_tn(soft16, grad_mixed).astype(BF16)
    grad_scores = soft * (grad_soft - jnp.sum(soft * grad_soft, axis=1, keepdims=True))
    grad_scores = grad_scores.astype(BF16)
    grad_queries = (mm(grad_scores, keys) * scaling).astype(BF16)
    grad_keys = (mm_tn(grad_scores, queries) * scaling).astype(BF16)
    grads_ref[:, 0:channels] = grad_queries
    grads_ref[:, channels : 2 * channels] = grad_keys
    grads_ref[:, 2 * channels : 3 * channels] = grad_values
    grads_ref[:, 3 * channels : 4 * channels] = grad_rows
    grad_normed = mm_nt(grads_ref[:, 0 : 3 * channels], wide)
    grad_in, gain_grad, shift_grad = norm_back(
        grad_normed, normal, inverse3, mask, group_size, vec(vecs, GAIN3)
    )
    grad_middle = mask * (grad_top + grad_in)
    grad_middle_ref[...] = grad_middle
    grad2 = grad_middle.astype(BF16)
    grad2_ref[...] = grad2
    vec_ref[0:1, :] = gain_grad
    vec_ref[1:2, :] = shift_grad
    vec_ref[2:3, :] = total(grad_queries.astype(F32))
    vec_ref[3:4, :] = total(grad_values.astype(F32))
    vec_ref[4:5, :] = total(grad_top)
    vec_ref[5:6, :] = total(grad2.astype(F32))
    vec_ref[6:8, :] = jnp.zeros((2, channels), F32)

    keep_at = pl.multiple_of(BLK * h, BLK)
    send_at = pl.multiple_of(BLK * (h ^ 2), BLK)
    block_keep[...] = grad2_ref[:, pl.ds(keep_at, BLK)]
    block_send[...] = grad2_ref[:, pl.ds(send_at, BLK)]

    def blocks(index):
        start = index * channels
        return [
            grads_ref[:, pl.ds(pl.multiple_of(start + BLK * h, BLK), BLK)],
            grads_ref[:, pl.ds(pl.multiple_of(start + BLK * (h ^ 2), BLK), BLK)],
        ]

    sum_ref[:, 0 : 6 * BLK] = mm_tn(normed, jnp.concatenate(blocks(0) + blocks(1) + blocks(2), axis=1))
    sum_ref[:, 6 * BLK : 8 * BLK] = mm_tn(mixed, jnp.concatenate(blocks(3), axis=1))
    shards = attn_keep.shape[0]
    rows = channels // shards
    for shard in range(shards):
        part = sum_ref[shard * rows : (shard + 1) * rows, :].astype(BF16)
        for index in range(4):
            at = index * 2 * BLK
            attn_keep[shard, index * rows : (index + 1) * rows, :] = part[:, at : at + BLK]
            attn_send[shard, index * rows : (index + 1) * rows, :] = part[:, at + BLK : at + 2 * BLK]


def third_kernel(
    bucket_ref, grad2_ref, conv_ref, stats_ref, vecs, weight2,
    grad1_ref, block_keep, block_send, vec_ref,
    shift_ref, acc_ref,
):
    h, home, away = place(bucket_ref)
    stride = home[2]
    mask, pixels = pixel_mask(home)
    channels = vecs.shape[1]
    group_size = pixels * (channels // GROUPS)
    fill_shifts(shift_ref, grad2_ref[...].astype(F32), stride)
    conv_backward(shift_ref, weight2, stride, acc_ref)
    inverse = stats_ref[3:4, :]
    normal = (conv_ref[...] - stats_ref[2:3, :]) * inverse
    u = normal * vec(vecs, GAIN2) + vec(vecs, SHIFT2)
    grad = mask * acc_ref[...] * silu_slope(u)
    grad_in, gain_grad, shift_grad = norm_back(
        grad, normal, inverse, mask, group_size, vec(vecs, GAIN2)
    )
    grad1 = grad_in.astype(BF16)
    grad1_ref[...] = grad1
    vec_ref[0:1, :] = gain_grad
    vec_ref[1:2, :] = shift_grad
    vec_ref[2:3, :] = total(grad1.astype(F32))
    vec_ref[3:8, :] = jnp.zeros((5, channels), F32)
    block_keep[...] = grad1_ref[:, pl.ds(pl.multiple_of(BLK * h, BLK), BLK)]
    block_send[...] = grad1_ref[:, pl.ds(pl.multiple_of(BLK * (h ^ 2), BLK), BLK)]


def fourth_kernel(
    bucket_ref, grad1_ref, image_ref, stats_ref, grad_middle_ref, middle_ref, mixed_ref, vecs,
    weight1, wp, vec_a, vec_b,
    out_own, grad_own, send_ref, vec_keep, vec_send,
    shift_ref, acc_ref, full_ref, vec_ref,
):
    h, home, away = place(bucket_ref)
    stride = home[2]
    mask, pixels = pixel_mask(home)
    channels = vecs.shape[1]
    group_size = pixels * (channels // GROUPS)
    projected = mm(mixed_ref[...], wp[...]) + vec(vecs, PB)
    full_ref[...] = (mask * (middle_ref[...] + projected)).astype(BF16)
    split_out(full_ref, home, h, out_own, send_ref.at[0])
    fill_shifts(shift_ref, grad1_ref[...].astype(F32), stride)
    conv_backward(shift_ref, weight1, stride, acc_ref)
    inverse = stats_ref[1:2, :]
    normal = (image_ref[...].astype(F32) * mask - stats_ref[0:1, :]) * inverse
    u = normal * vec(vecs, GAIN1) + vec(vecs, SHIFT1)
    grad = mask * acc_ref[...] * silu_slope(u)
    grad_in, gain_grad, shift_grad = norm_back(
        grad, normal, inverse, mask, group_size, vec(vecs, GAIN1)
    )
    full_ref[...] = (mask * (grad_middle_ref[...] + grad_in)).astype(BF16)
    split_out(full_ref, home, h, grad_own, send_ref.at[1])
    vec_ref[0:6, :] = vec_a[0:6, :]
    vec_ref[6:9, :] = vec_b[0:3, :]
    vec_ref[9:10, :] = gain_grad
    vec_ref[10:11, :] = shift_grad
    vec_ref[11:VECS, :] = jnp.zeros((VECS - 11, channels), F32)
    pairs = vec_keep.shape[0]
    rows = channels // (2 * pairs)
    mine = (lax.axis_index("batch") & 1) == 1
    for pair in range(pairs):
        parts = []
        for shard in (2 * pair, 2 * pair + 1):
            start = shard * rows
            tile = start // BLK * BLK
            part = vec_ref[:, tile : tile + BLK]
            parts.append(part if start == tile else pltpu.roll(part, BLK - (start - tile), 1))
        vec_keep[pair] = jnp.where(mine, parts[1], parts[0]).astype(BF16)
        vec_send[pair] = jnp.where(mine, parts[0], parts[1]).astype(BF16)


def weight_kernel(
    bucket_ref, act_t, half_t, partner_half_t, block_own, block_away,
    keep_ref, send_ref, left_ref, right_ref, shift_ref, sum_ref, *, layer,
):
    h, home, away = place(bucket_ref)
    channels = act_t.shape[0]
    half = channels // 2
    left_ref[:, 0:PIX] = act_t[...]
    left_ref[pl.ds(pl.multiple_of((h & 1) * half, 16), half), PIX : 2 * PIX] = half_t[layer]
    left_ref[pl.ds(pl.multiple_of((1 - (h & 1)) * half, 16), half), PIX : 2 * PIX] = (
        partner_half_t[layer]
    )
    for index, (facts, block) in enumerate(((home, block_own), (away, block_away))):
        stride = facts[2]
        fill_shifts(shift_ref, block[...].astype(F32), stride)
        for p in range(3):
            for q in range(3):
                column = (3 * p + q) * BLK
                right_ref[index * PIX : (index + 1) * PIX, column : column + BLK] = tap(
                    shift_ref, 2 - p, 2 - q, stride
                )
    joint = mm(left_ref[...], right_ref[...])
    for t in range(9):
        sum_ref[t * channels : (t + 1) * channels, :] = joint[:, t * BLK : (t + 1) * BLK]
    mine = lax.axis_index("batch") & 1
    pairs = keep_ref.shape[0]
    rows = 9 * channels // (2 * pairs)
    for pair in range(pairs):
        for dst, which in ((keep_ref, mine), (send_ref, 1 - mine)):
            shard = 2 * pair + which
            dst[pair] = sum_ref[pl.ds(pl.multiple_of(shard * rows, 8), rows), :].astype(BF16)


def route_kernel(*refs, bit, ways, low):
    group = (lax.axis_index("batch") >> bit) & (ways - 1)
    ins, outs = refs[: len(refs) - ways], refs[len(refs) - ways :]
    first = 0
    for keep_ref, got_ref in zip(ins[::2], ins[1::2]):
        rows = keep_ref.shape[1]
        for step, dst in enumerate(outs):
            which = group ^ step
            for index in range(dst.shape[0]):
                at = (index // low * ways + which) * low + index % low
                dst[index, first : first + rows, :] = (
                    keep_ref[at].astype(F32) + got_ref[at].astype(F32)
                ).astype(BF16)
        first += rows


def total_of(refs):
    added = refs[0].astype(F32)
    for ref in refs[1:]:
        added = added + ref.astype(F32)
    return added


def half_kernel(*refs):
    mine = lax.axis_index("batch") & 1
    for dst, which in zip(refs[-2:], (mine, 1 - mine)):
        dst[...] = total_of([ref[which] for ref in refs[:-2]]).astype(BF16)


def sum_kernel(*refs, count):
    out_ref = refs[-1]
    rows = refs[0].shape[1]
    out_ref[0:rows, :] = total_of([ref[0] for ref in refs[:count]]).astype(BF16)
    if count < len(refs) - 1:
        out_ref[rows:, :] = total_of([ref[...] for ref in refs[count:-1]]).astype(BF16)


def join_kernel(own_ref, far_ref, near_ref, diagonal_ref, *out_refs):
    h = lax.axis_index("height")
    first = 0
    for dst in [ref for ref in out_refs if ref.shape[0] > 1]:
        rows = dst.shape[0]
        for ref, index in ((own_ref, h), (far_ref, h ^ 2), (near_ref, h ^ 1), (diagonal_ref, h ^ 3)):
            dst[:, pl.ds(pl.multiple_of(BLK * index, BLK), BLK)] = ref[first : first + rows, :].astype(F32)
        first += rows
    if own_ref.shape[0] > first:
        own, far = own_ref[first:, :].astype(F32), far_ref[first:, :].astype(F32)
        near, diagonal = near_ref[first:, :].astype(F32), diagonal_ref[first:, :].astype(F32)
        sums = 0.5 * ((own + near) + (far + diagonal))
        for index, dst in enumerate([ref for ref in out_refs if ref.shape[0] == 1]):
            dst[...] = sums[index : index + 1, 0 : dst.shape[1]]


def unpack_kernel(bucket_ref, out_own, grad_own, away_ref, out_ref, grad_ref):
    h, home, away = place(bucket_ref)
    for own, received, dst in (
        (out_own, away_ref.at[0], out_ref),
        (grad_own, away_ref.at[1], grad_ref),
    ):
        channels = dst.shape[3]
        for facts, src, wide_rows in ((away, received, 4), (home, own, 6)):
            image, tall, stride, width = facts

            @pl.when(tall)
            def _():
                for row in range(6):
                    dst[image, row, 0:16, :] = src[16 * row : 16 * row + 16, :]
                    dst[image, row, 16:32, :] = jnp.zeros((16, channels), dst.dtype)

            @pl.when(jnp.logical_not(tall))
            def _():
                for row in range(wide_rows):
                    dst[image, row] = src[32 * row : 32 * row + 32, :]
                for row in range(wide_rows, 6):
                    dst[image, row] = jnp.zeros((32, channels), dst.dtype)

            if wide_rows == 4:

                @pl.when(jnp.logical_not(tall) & (h == 3))
                def _():
                    for row in range(6):
                        dst[image, row] = jnp.zeros((32, channels), dst.dtype)


def call(kernel, name, outs, scratch, vmem, *operands, smem=1, any_from=99):
    specs = [SM] * smem + [VM] * (len(operands) - smem)
    specs = [HB if i >= any_from else spec for i, spec in enumerate(specs)]
    return pl.pallas_call(
        kernel,
        name=name,
        out_shape=[jax.ShapeDtypeStruct(shape, dtype) for shape, dtype in outs],
        in_specs=specs,
        out_specs=[SM if dtype == jnp.int32 else VM for shape, dtype in outs],
        scratch_shapes=[
            pltpu.SemaphoreType.DMA(shape)
            if dtype is None
            else (pltpu.SMEM if dtype == jnp.int32 else pltpu.VMEM)(shape, dtype)
            for shape, dtype in scratch
        ],
        compiler_params=pltpu.CompilerParams(vmem_limit_bytes=vmem << 20),
        cost_estimate=pl.CostEstimate(
            flops=int(LENGTH.get(name, 0.02) * RATE), bytes_accessed=1024, transcendentals=0
        ),
    )(*operands)


def on_device(
    inputs,
    bucket,
    norm1_gain,
    norm1_shift,
    conv1_weight,
    conv1_bias,
    norm2_gain,
    norm2_shift,
    conv2_weight,
    conv2_bias,
    norm3_gain,
    norm3_shift,
    query_weight,
    query_bias,
    key_weight,
    value_weight,
    value_bias,
    proj_weight,
    proj_bias,
    cotangent,
):
    C = inputs.shape[-1]
    batches = lax.axis_size("batch")
    bits = batches.bit_length() - 1
    shard_rows = 9 * C // batches
    small_rows = C // batches

    def row(v):
        return v.reshape(1, C)

    def to_core(v):
        return lax.ppermute(v, "height", [(i, i ^ 1) for i in range(4)])

    def to_chip(v):
        return lax.ppermute(v, "height", [(i, i ^ 2) for i in range(4)])

    def to_batch(v, change):
        return lax.ppermute(v, "batch", [(i, i ^ change) for i in range(batches)])

    def after(v, *others):
        return lax.optimization_barrier((v,) + others)[0]

    img16 = ((PIX, C), BF16)
    img32 = ((PIX, C), F32)
    rows8 = ((8, C), F32)
    block = ((PIX, BLK), BF16)
    turned = ((C, PIX), BF16)
    shifts = ((3, PIX + 2 * PAD, C), BF16)

    kinds, away_x, home_x = call(
        pack_kernel, "pack",
        [((2,), jnp.int32), ((128, C), BF16), ((192, C), BF16)],
        [((2,), jnp.int32), (inputs.shape, BF16), ((2,), None)], 54, bucket, inputs,
        smem=0, any_from=0,
    )
    vectors = (
        norm1_gain, norm1_shift, conv1_bias, norm2_gain, norm2_shift, conv2_bias,
        norm3_gain, norm3_shift, query_bias, value_bias, proj_bias,
    )
    recv_x = to_chip(away_x)
    core_x = to_core(home_x)
    vecs, away_c, home_c = call(
        stack_kernel, "stack", [((VECS, C), F32), ((160, C), BF16), ((192, C), BF16)], [], 8,
        kinds, cotangent, *[row(v) for v in vectors],
    )
    recv_c = to_chip(away_c)
    core_c = to_core(home_c)
    core_recv_c = lax.ppermute(away_c, "height", [(i, i ^ 3) for i in range(4)])
    core_recv_x = to_core(after(recv_x, vecs))

    image, conv, act2, stats, act1_t, act2_t, send_t = call(
        first_kernel, "first",
        [img16, img32, img16, rows8, turned, turned, ((2, C // 2, PIX), BF16)],
        [shifts], 14,
        kinds, home_x, core_x, recv_x, core_recv_x, vecs, conv1_weight,
    )
    half_t = to_chip(send_t)
    core_half_t = to_core(half_t)

    attn_out = ((batches, 4 * small_rows, BLK), BF16)
    middle, mixed, grad2, grad_middle, attn_keep, attn_send, vec_a, block2, block2_send = call(
        second_kernel, "second",
        [img32, img16, img16, img32, attn_out, attn_out, rows8, block, block],
        [shifts, img16, ((PIX, 4 * C), BF16), ((C, 8 * BLK), F32)], 24,
        kinds, image, act2, home_c, core_c, recv_c, core_recv_c, vecs,
        conv2_weight, query_weight, key_weight, value_weight, proj_weight,
    )
    block2_away = to_chip(block2_send)
    attn_got = to_chip(attn_send)

    grad1, block1, block1_send, vec_b = call(
        third_kernel, "third",
        [img16, block, block, rows8],
        [shifts, img32], 14,
        kinds, grad2, conv, stats, vecs, conv2_weight,
    )
    block1_away = to_chip(block1_send)

    def weight_grad(name, act_t, index, own, away):
        return call(
            functools.partial(weight_kernel, layer=index), name,
            [((batches // 2, shard_rows, BLK), BF16)] * 2,
            [((C, 2 * PIX), BF16), ((2 * PIX, 9 * BLK), BF16), ((3, PIX + 2 * PAD, BLK), BF16),
             ((9 * C, BLK), F32)],
            18, kinds, act_t, half_t, core_half_t, own, away,
        )

    keep2, send2 = weight_grad("weight2", act2_t, 1, after(block2, block1), block2_away)
    got2 = to_batch(send2, 1)

    def spread(name, bit, low, *pairs):
        ways = 1 << min(2, bits - bit)
        count = pairs[0].shape[0] // ways
        rows = sum(v.shape[1] for v in pairs[::2])
        parts = call(
            functools.partial(route_kernel, bit=bit, ways=ways, low=low), name + str(bit),
            [((count, rows, BLK), BF16)] * ways, [], 16, *pairs, smem=0,
        )
        return parts, [to_batch(parts[j], j << bit) for j in range(1, ways)]

    def rest(name, low, parts, got):
        for bit in range(3, bits, 2):
            added = total_of([parts[0]] + got).astype(BF16)
            parts, got = spread(name, bit, low, added, jnp.zeros_like(added))
        return [parts[0]] + got

    def finish(name, arrays, *others):
        rows = arrays[0].shape[1] + (others[0].shape[0] if others else 0)
        return call(
            functools.partial(sum_kernel, count=len(arrays)), name, [((rows, BLK), BF16)], [], 8,
            *arrays, *others, smem=0,
        )[0]

    def gather(shard):
        far = to_chip(shard)
        near = to_core(shard)
        return shard, far, near, to_core(far)

    parts_a, got_a = spread("routea", 1, 2, after(attn_keep, send2), attn_got)
    keep1, send1 = weight_grad("weight1", act1_t, 0, after(block1, *parts_a), block1_away)
    got1 = to_batch(send1, 1)
    parts_b, got_b = spread("routeb", 1, 1, after(keep2, send1), got2)

    out_own, grad_own, image_send, vec_keep, vec_send = call(
        fourth_kernel, "fourth",
        [((192, C), BF16), ((192, C), BF16), ((2, 128, C), BF16),
         ((batches // 2, VECS, BLK), BF16), ((batches // 2, VECS, BLK), BF16)],
        [shifts, img32, img16, ((VECS, C), F32)], 14,
        kinds, after(grad1, *parts_b), image, stats, grad_middle, middle, mixed, vecs,
        conv1_weight, proj_weight, vec_a, vec_b,
    )
    image_away = to_chip(image_send)
    vec_got = to_batch(vec_send, 1)

    attn_mine, attn_other = call(
        half_kernel, "halfa", [((4 * small_rows, BLK), BF16)] * 2, [], 8,
        *rest("routea", 2, parts_a, [after(g, parts_b[0]) for g in got_a]), smem=0,
    )
    attn_far = to_batch(attn_other, 1)
    shard_b = finish("sumb", rest("routeb", 1, parts_b, got_b), attn_mine, attn_far)
    parts_c, got_c = spread("routec", 1, 1, after(keep1, shard_b), got1, vec_keep, vec_got)
    shard_b = after(shard_b, *parts_c)
    gathered_b = gather(shard_b)
    outputs, input_grad = call(
        unpack_kernel, "unpack",
        [(inputs.shape, BF16)] * 2, [], 8,
        kinds, out_own, grad_own, after(image_away, *parts_c),
    )
    shard_c = finish("sumc", rest("routec", 1, parts_c, got_c))
    whole2, *small = call(
        join_kernel, "joinb", [((shard_rows, C), F32)] + [((small_rows, C), F32)] * 4, [], 8,
        after(gathered_b[0], shard_c), *gathered_b[1:], smem=0,
    )
    gathered_c = gather(after(shard_c, outputs))
    whole1, *sums = call(
        join_kernel, "joinc", [((shard_rows, C), F32)] + [((1, small_rows), F32)] * 11, [], 8,
        after(gathered_c[0], whole2), *gathered_c[1:], smem=0,
    )
    v = [row.reshape(small_rows) for row in sums]

    return (
        outputs, input_grad,
        v[9], v[10], whole1, v[8],
        v[6], v[7], whole2, v[5],
        v[0], v[1],
        small[0], v[2], small[1], small[2], v[3], small[3], v[4],
    )


def solution(mesh):
    image = P("batch", "height", None, None)
    vector = P("batch")
    matrix = P("batch", None)
    return jax.shard_map(
        on_device,
        mesh=mesh,
        in_specs=(image, vector) + (P(),) * 17 + (image,),
        out_specs=(
            image, image,
            vector, vector, matrix, vector,
            vector, vector, matrix, vector,
            vector, vector,
            matrix, vector, matrix, matrix, vector, matrix, vector,
        ),
        check_vma=False,
    )
```

```python
import functools

import jax
import jax.numpy as jnp
from jax import lax
from jax.experimental import pallas as pl
from jax.experimental.pallas import tpu as pltpu
from jax.sharding import PartitionSpec as P

GROUPS = 32
UNIT = 8
PIX = 512
PAD = 32
BLK = 128
F32 = jnp.float32
BF16 = jnp.bfloat16
epsilon = 1e-05

VM = pl.BlockSpec(memory_space=pltpu.VMEM)
SM = pl.BlockSpec(memory_space=pltpu.SMEM)
HB = pl.BlockSpec(memory_space=pltpu.HBM)
RATE = 1 << 30
LENGTH = {
    "pack": 10, "stack": 10, "first": 0.02, "second": 30, "third": 20, "fourth": 10, "weight2": 1, "weight1": 0.02, "routeb1": 20, "unpack": 5,
}


def place(bucket_ref):
    h = lax.axis_index("height")
    upper = lax.div(h, 2)
    tall_first = bucket_ref[0] == 1
    tall_image = jnp.where(tall_first, 0, 1)
    home = jnp.where(upper == 1, tall_image, 1 - tall_image)
    away = 1 - home

    def facts(image):
        kind = bucket_ref[image]
        tall = kind == 1
        stride = jnp.where(tall, 2 * UNIT, 4 * UNIT)
        width = jnp.where(kind == 0, 3 * UNIT, stride)
        return (image, tall, stride, width)

    return h, facts(home), facts(away)


def pixel_col(stride, lanes=1):
    rows = lax.broadcasted_iota(jnp.int32, (PIX, lanes), 0)
    return rows, rows & (stride - 1)


def pixel_mask(facts):
    unused, tall, stride, width = facts
    rows, cols = pixel_col(stride)
    limit = jnp.where(tall, 6 * UNIT * UNIT, 8 * UNIT * UNIT)
    mask = jnp.where((cols < width) & (rows < limit), 1.0, 0.0).astype(F32)
    size = jnp.where(tall | (width == 3 * UNIT), 6 * UNIT * UNIT, 8 * UNIT * UNIT)
    return mask, size.astype(F32)


def group_total(rows):
    members = rows.shape[1] // GROUPS
    lane = lax.broadcasted_iota(jnp.int32, (rows.shape[0], BLK), 1)
    tiles = []
    for tile in range(rows.shape[1] // BLK):
        part = rows[:, tile * BLK : (tile + 1) * BLK]
        step = 1
        while step < members:
            place_in_four = (lane // step) & 3
            added = part
            for d in (1, 2, 3):
                up = pltpu.roll(part, BLK - d * step, 1)
                down = pltpu.roll(part, (4 - d) * step, 1)
                added = added + jnp.where(place_in_four + d < 4, up, down)
            part = added
            step *= 4
        tiles.append(part)
    return jnp.concatenate(tiles, axis=1)


def total(values):
    return jnp.sum(values, axis=0, keepdims=True)


def wide_total(*rows):
    stacked = jnp.concatenate(list(rows) + [rows[0]] * (8 - len(rows)), axis=0)
    sums = group_total(stacked)
    return [sums[i : i + 1] for i in range(len(rows))]


def norm_stats(values, mask, group_size):
    mean = wide_total(total(values))[0] / group_size
    centered = (values - mean) * mask
    variance = wide_total(total(centered * centered))[0] / group_size
    return mean, lax.rsqrt(variance + epsilon)


def silu_norm(values, mean, inverse, gain, shift, mask):
    scale = 0.5 * inverse * gain
    half = values * scale + (0.5 * shift - mean * scale)
    return (half + half * jnp.tanh(half)) * mask


def norm_back(grad, normal, inverse, mask, group_size, gain):
    plain_row = total(grad)
    cross_row = total(grad * normal)
    plain, cross = [v / group_size for v in wide_total(plain_row * gain, cross_row * gain)]
    grad_in = grad * (inverse * gain) - mask * (plain * inverse + normal * (cross * inverse))
    return grad_in, cross_row, plain_row


def silu_slope(u):
    half = 0.5 * u
    t = jnp.tanh(half)
    return (0.5 + 0.5 * t) * (1.0 + half * (1.0 - t))


def mm(a, b):
    return jnp.dot(a, b, preferred_element_type=F32)


def mm_nt(a, b):
    return lax.dot_general(a, b, (((1,), (1,)), ((), ())), preferred_element_type=F32)


def mm_tn(a, b):
    return lax.dot_general(a, b, (((0,), (0,)), ((), ())), preferred_element_type=F32)


def fill_shifts(shift_ref, values, stride):
    unused, cols = pixel_col(stride)
    lanes = values.shape[1]
    zeros = jnp.zeros((PAD, lanes), BF16)
    for q in range(3):
        shift_ref[q, 0:PAD, :] = zeros
        shift_ref[q, PAD + PIX : 2 * PAD + PIX, :] = zeros
    left = jnp.where(cols == 0, 0.0, pltpu.roll(values, 1, 0))
    right = jnp.where(cols == stride - 1, 0.0, pltpu.roll(values, PIX - 1, 0))
    shift_ref[0, PAD : PAD + PIX, :] = left.astype(BF16)
    shift_ref[1, PAD : PAD + PIX, :] = values.astype(BF16)
    shift_ref[2, PAD : PAD + PIX, :] = right.astype(BF16)


def tap(shift_ref, p, q, stride, first=0, count=PIX):
    start = pl.multiple_of(PAD + first + (p - 1) * stride, 16)
    return shift_ref[q, pl.ds(start, count), :]


def conv_forward(shift_ref, weight_ref, stride, out_ref, tile=256):
    for first in range(0, PIX, tile):
        stacked = jnp.concatenate(
            [tap(shift_ref, p, q, stride, first, tile) for p in range(3) for q in range(3)], axis=1
        )
        out_ref[first : first + tile, :] = mm(stacked, weight_ref[...])


def conv_backward(shift_ref, weight_ref, stride, out_ref, tile=256):
    channels = weight_ref.shape[1]
    for first in range(0, PIX, tile):
        acc = None
        for p in range(3):
            for q in range(3):
                row = (8 - (3 * p + q)) * channels
                part = mm_nt(
                    tap(shift_ref, p, q, stride, first, tile), weight_ref[row : row + channels, :]
                )
                acc = part if acc is None else acc + part
        out_ref[first : first + tile, :] = acc


def assemble(out_ref, facts, h, pieces):
    unused, tall, stride, width = facts
    own, partner, received, partner_received = pieces
    other = h ^ 1

    @pl.when(tall)
    def _():
        for ref, index in (
            (own, h),
            (partner, other),
            (received, h ^ 2),
            (partner_received, other ^ 2),
        ):
            out_ref[pl.ds(pl.multiple_of(96 * index, 16), 96), :] = ref[0:96, :]
        out_ref[384:512, :] = jnp.zeros((128, out_ref.shape[1]), out_ref.dtype)

    @pl.when(jnp.logical_not(tall))
    def _():
        low = h & 1
        out_ref[pl.ds(pl.multiple_of(192 * low, 16), 192), :] = own[...]
        out_ref[pl.ds(pl.multiple_of(192 * (1 - low), 16), 192), :] = partner[...]

        @pl.when(low == 0)
        def _():
            out_ref[384:512, :] = received[0:128, :]

        @pl.when(low == 1)
        def _():
            out_ref[384:512, :] = partner_received[0:128, :]


def split_out(full_ref, facts, h, own_ref, send_ref):
    unused, tall, stride, width = facts
    send_h = h ^ 2

    @pl.when(tall)
    def _():
        own_ref[0:96, :] = full_ref[pl.ds(pl.multiple_of(96 * h, 16), 96), :]
        own_ref[96:192, :] = jnp.zeros((96, own_ref.shape[1]), own_ref.dtype)
        send_ref[0:96, :] = full_ref[pl.ds(pl.multiple_of(96 * send_h, 16), 96), :]
        send_ref[96:128, :] = jnp.zeros((32, own_ref.shape[1]), own_ref.dtype)

    @pl.when(jnp.logical_not(tall))
    def _():
        own_ref[...] = full_ref[pl.ds(pl.multiple_of(192 * (h & 1), 16), 192), :]
        send_ref[...] = full_ref[384:512, :]


GAIN1, SHIFT1, BIAS1, GAIN2, SHIFT2, BIAS2, GAIN3, SHIFT3, QB, VB, PB = range(11)
VECS = 16


def vec(vec_ref, index):
    return vec_ref[index : index + 1, :]


def pack(src, facts, dst, wide_rows):
    image, tall, stride, width = facts

    @pl.when(tall)
    def _():
        for row in range(6):
            dst[16 * row : 16 * row + 16, :] = src[image, row, 0:16, :]
        dst[96 : dst.shape[0], :] = jnp.zeros((dst.shape[0] - 96, dst.shape[1]), dst.dtype)

    @pl.when(jnp.logical_not(tall))
    def _():
        for row in range(wide_rows):
            dst[32 * row : 32 * row + 32, :] = src[image, row]


def pack_kernel(bucket_hbm, x_hbm, kinds, away_x, home_x, bucket_ref, x_ref, sems):
    copies = (
        pltpu.make_async_copy(bucket_hbm, bucket_ref, sems.at[0]),
        pltpu.make_async_copy(x_hbm, x_ref, sems.at[1]),
    )
    for copy in copies:
        copy.start()
    for copy in copies:
        copy.wait()
    h, home, away = place(bucket_ref)
    kinds[0] = bucket_ref[0]
    kinds[1] = bucket_ref[1]
    pack(x_ref, away, away_x, 4)
    pack(x_ref, home, home_x, 6)


def stack_kernel(kinds, cot_ref, *refs):
    h, home, away = place(kinds)
    out_ref, away_c, home_c = refs[-3:]
    count = len(refs) - 3
    for index, ref in enumerate(refs[:count]):
        out_ref[index : index + 1, :] = ref[...]
    out_ref[count:, :] = jnp.zeros((VECS - count, out_ref.shape[1]), F32)
    pack(cot_ref, away, away_c, 4)
    pack(cot_ref, home, home_c, 6)


def first_kernel(
    bucket_ref, own, partner, received, partner_received, vecs, weight1,
    image_ref, conv_ref, act2_ref, stats_ref, act1_t, act2_t, send_t,
    shift_ref,
):
    h, home, away = place(bucket_ref)
    stride = home[2]
    mask, pixels = pixel_mask(home)
    channels = vecs.shape[1]
    group_size = pixels * (channels // GROUPS)
    assemble(image_ref, home, h, (own, partner, received, partner_received))
    values = image_ref[...].astype(F32) * mask
    mean1, inverse1 = norm_stats(values, mask, group_size)
    act = silu_norm(values, mean1, inverse1, vec(vecs, GAIN1), vec(vecs, SHIFT1), mask)
    fill_shifts(shift_ref, act, stride)
    act1_t[...] = act.astype(BF16).T
    conv_forward(shift_ref, weight1, stride, conv_ref)
    values = (conv_ref[...] + vec(vecs, BIAS1)) * mask
    conv_ref[...] = values
    mean2, inverse2 = norm_stats(values, mask, group_size)
    act = silu_norm(values, mean2, inverse2, vec(vecs, GAIN2), vec(vecs, SHIFT2), mask)
    act = act.astype(BF16)
    act2_ref[...] = act
    act2_t[...] = act.T
    half = pl.multiple_of((h & 1) * (channels // 2), 16)
    send_t[0] = act1_t[pl.ds(half, channels // 2), :]
    send_t[1] = act2_t[pl.ds(half, channels // 2), :]
    stats_ref[0:1, :] = mean1
    stats_ref[1:2, :] = inverse1
    stats_ref[2:3, :] = mean2
    stats_ref[3:4, :] = inverse2
    stats_ref[4:8, :] = jnp.zeros((4, channels), F32)


def second_kernel(
    bucket_ref, image_ref, act2_ref, own, partner, received, partner_received, vecs,
    weight2, wq, wk, wv, wp,
    middle_ref, mixed_ref, grad2_ref, grad_middle_ref, attn_keep, attn_send, vec_ref,
    block_keep, block_send,
    shift_ref, full_ref, grads_ref, sum_ref,
):
    h, home, away = place(bucket_ref)
    stride = home[2]
    mask, pixels = pixel_mask(home)
    channels = vecs.shape[1]
    group_size = pixels * (channels // GROUPS)
    scaling = channels ** (-0.5)
    assemble(full_ref, home, h, (own, partner, received, partner_received))
    fill_shifts(shift_ref, act2_ref[...].astype(F32), stride)
    conv_forward(shift_ref, weight2, stride, middle_ref)
    middle = mask * (image_ref[...].astype(F32) + (middle_ref[...] + vec(vecs, BIAS2)))
    middle_ref[...] = middle
    mean3, inverse3 = norm_stats(middle, mask, group_size)
    normal = (middle - mean3) * inverse3
    normed = (normal * vec(vecs, GAIN3) + vec(vecs, SHIFT3)).astype(BF16)
    wide = jnp.concatenate([wq[...], wk[...], wv[...]], axis=1)
    joint = mm(normed, wide)
    queries = (joint[:, 0:channels] + vec(vecs, QB)).astype(BF16)
    keys = joint[:, channels : 2 * channels].astype(BF16)
    values = (joint[:, 2 * channels :] + vec(vecs, VB)).astype(BF16)
    lanes = lax.broadcasted_iota(jnp.int32, (1, PIX), 1)
    key_cols = lanes & (stride - 1)
    key_valid = (key_cols < home[3]) & (lanes < jnp.where(home[1], 384, 512))
    scores = jnp.where(key_valid, mm_nt(queries, keys) * scaling, -1000000000.0)
    grad_top = full_ref[...].astype(F32) * mask
    grad_rows = grad_top.astype(BF16)
    grad_mixed = mm_nt(grad_rows, wp[...]).astype(BF16)
    grad_soft = mm_nt(grad_mixed, values)
    raised = jnp.exp(scores - jnp.max(scores, axis=1, keepdims=True))
    soft = raised * (1.0 / jnp.sum(raised, axis=1, keepdims=True))
    soft16 = soft.astype(BF16)
    mixed = mm(soft16, values).astype(BF16)
    mixed_ref[...] = mixed

    grad_values = mm_tn(soft16, grad_mixed).astype(BF16)
    grad_scores = soft * (grad_soft - jnp.sum(soft * grad_soft, axis=1, keepdims=True))
    grad_scores = grad_scores.astype(BF16)
    grad_queries = (mm(grad_scores, keys) * scaling).astype(BF16)
    grad_keys = (mm_tn(grad_scores, queries) * scaling).astype(BF16)
    grads_ref[:, 0:channels] = grad_queries
    grads_ref[:, channels : 2 * channels] = grad_keys
    grads_ref[:, 2 * channels : 3 * channels] = grad_values
    grads_ref[:, 3 * channels : 4 * channels] = grad_rows
    grad_normed = mm_nt(grads_ref[:, 0 : 3 * channels], wide)
    grad_in, gain_grad, shift_grad = norm_back(
        grad_normed, normal, inverse3, mask, group_size, vec(vecs, GAIN3)
    )
    grad_middle = mask * (grad_top + grad_in)
    grad_middle_ref[...] = grad_middle
    grad2 = grad_middle.astype(BF16)
    grad2_ref[...] = grad2
    vec_ref[0:1, :] = gain_grad
    vec_ref[1:2, :] = shift_grad
    vec_ref[2:3, :] = total(grad_queries.astype(F32))
    vec_ref[3:4, :] = total(grad_values.astype(F32))
    vec_ref[4:5, :] = total(grad_top)
    vec_ref[5:6, :] = total(grad2.astype(F32))
    vec_ref[6:8, :] = jnp.zeros((2, channels), F32)

    keep_at = pl.multiple_of(BLK * h, BLK)
    send_at = pl.multiple_of(BLK * (h ^ 2), BLK)
    block_keep[...] = grad2_ref[:, pl.ds(keep_at, BLK)]
    block_send[...] = grad2_ref[:, pl.ds(send_at, BLK)]

    def blocks(index):
        start = index * channels
        return [
            grads_ref[:, pl.ds(pl.multiple_of(start + BLK * h, BLK), BLK)],
            grads_ref[:, pl.ds(pl.multiple_of(start + BLK * (h ^ 2), BLK), BLK)],
        ]

    sum_ref[:, 0 : 6 * BLK] = mm_tn(normed, jnp.concatenate(blocks(0) + blocks(1) + blocks(2), axis=1))
    sum_ref[:, 6 * BLK : 8 * BLK] = mm_tn(mixed, jnp.concatenate(blocks(3), axis=1))
    mine = lax.axis_index("batch") & 1
    pairs = attn_keep.shape[0]
    rows = channels // (2 * pairs)
    for pair in range(pairs):
        for dst, which in ((attn_keep, mine), (attn_send, 1 - mine)):
            part = sum_ref[pl.ds(pl.multiple_of((2 * pair + which) * rows, 8), rows), :].astype(BF16)
            for index in range(4):
                at = index * 2 * BLK
                dst[pair, index * rows : (index + 1) * rows, :] = part[:, at : at + 2 * BLK]


def third_kernel(
    bucket_ref, grad2_ref, conv_ref, stats_ref, vecs, weight2,
    grad1_ref, block_keep, block_send, vec_ref,
    shift_ref, acc_ref,
):
    h, home, away = place(bucket_ref)
    stride = home[2]
    mask, pixels = pixel_mask(home)
    channels = vecs.shape[1]
    group_size = pixels * (channels // GROUPS)
    fill_shifts(shift_ref, grad2_ref[...].astype(F32), stride)
    conv_backward(shift_ref, weight2, stride, acc_ref)
    inverse = stats_ref[3:4, :]
    normal = (conv_ref[...] - stats_ref[2:3, :]) * inverse
    u = normal * vec(vecs, GAIN2) + vec(vecs, SHIFT2)
    grad = mask * acc_ref[...] * silu_slope(u)
    grad_in, gain_grad, shift_grad = norm_back(
        grad, normal, inverse, mask, group_size, vec(vecs, GAIN2)
    )
    grad1 = grad_in.astype(BF16)
    grad1_ref[...] = grad1
    vec_ref[0:1, :] = gain_grad
    vec_ref[1:2, :] = shift_grad
    vec_ref[2:3, :] = total(grad1.astype(F32))
    vec_ref[3:8, :] = jnp.zeros((5, channels), F32)
    block_keep[...] = grad1_ref[:, pl.ds(pl.multiple_of(BLK * h, BLK), BLK)]
    block_send[...] = grad1_ref[:, pl.ds(pl.multiple_of(BLK * (h ^ 2), BLK), BLK)]


def fourth_kernel(
    bucket_ref, grad1_ref, image_ref, stats_ref, grad_middle_ref, middle_ref, mixed_ref, vecs,
    weight1, wp, vec_a, vec_b,
    out_own, grad_own, send_ref, vec_out,
    shift_ref, acc_ref, full_ref, vec_ref,
):
    h, home, away = place(bucket_ref)
    stride = home[2]
    mask, pixels = pixel_mask(home)
    channels = vecs.shape[1]
    group_size = pixels * (channels // GROUPS)
    projected = mm(mixed_ref[...], wp[...]) + vec(vecs, PB)
    full_ref[...] = (mask * (middle_ref[...] + projected)).astype(BF16)
    split_out(full_ref, home, h, out_own, send_ref.at[0])
    fill_shifts(shift_ref, grad1_ref[...].astype(F32), stride)
    conv_backward(shift_ref, weight1, stride, acc_ref)
    inverse = stats_ref[1:2, :]
    normal = (image_ref[...].astype(F32) * mask - stats_ref[0:1, :]) * inverse
    u = normal * vec(vecs, GAIN1) + vec(vecs, SHIFT1)
    grad = mask * acc_ref[...] * silu_slope(u)
    grad_in, gain_grad, shift_grad = norm_back(
        grad, normal, inverse, mask, group_size, vec(vecs, GAIN1)
    )
    full_ref[...] = (mask * (grad_middle_ref[...] + grad_in)).astype(BF16)
    split_out(full_ref, home, h, grad_own, send_ref.at[1])
    vec_ref[0:6, :] = vec_a[0:6, :]
    vec_ref[6:9, :] = vec_b[0:3, :]
    vec_ref[9:10, :] = gain_grad
    vec_ref[10:11, :] = shift_grad
    vec_ref[11:VECS, :] = jnp.zeros((VECS - 11, channels), F32)
    shards = vec_out.shape[0]
    rows = channels // shards
    for shard in range(shards):
        start = shard * rows
        tile = start // BLK * BLK
        part = vec_ref[:, tile : tile + BLK]
        vec_out[shard] = part if start == tile else pltpu.roll(part, BLK - (start - tile), 1)


def weight_kernel(
    bucket_ref, act_t, half_t, partner_half_t, block_own, block_away,
    *rest, layer,
):
    vec_ref = rest[0] if len(rest) == 7 else None
    keep_ref, send_ref, left_ref, right_ref, shift_ref, sum_ref = rest[-6:]
    h, home, away = place(bucket_ref)
    channels = act_t.shape[0]
    half = channels // 2
    left_ref[:, 0:PIX] = act_t[...]
    left_ref[pl.ds(pl.multiple_of((h & 1) * half, 16), half), PIX : 2 * PIX] = half_t[layer]
    left_ref[pl.ds(pl.multiple_of((1 - (h & 1)) * half, 16), half), PIX : 2 * PIX] = (
        partner_half_t[layer]
    )
    for index, (facts, block) in enumerate(((home, block_own), (away, block_away))):
        stride = facts[2]
        fill_shifts(shift_ref, block[...].astype(F32), stride)
        for p in range(3):
            for q in range(3):
                column = (3 * p + q) * BLK
                right_ref[index * PIX : (index + 1) * PIX, column : column + BLK] = tap(
                    shift_ref, 2 - p, 2 - q, stride
                )
    joint = mm(left_ref[...], right_ref[...])
    for t in range(9):
        sum_ref[t * channels : (t + 1) * channels, :] = joint[:, t * BLK : (t + 1) * BLK]
    mine = lax.axis_index("batch") & 1
    pairs = keep_ref.shape[0]
    rows = 9 * channels // (2 * pairs)
    for pair in range(pairs):
        for dst, which in ((keep_ref, mine), (send_ref, 1 - mine)):
            shard = 2 * pair + which
            dst[pair, 0:rows, :] = sum_ref[pl.ds(pl.multiple_of(shard * rows, 8), rows), :].astype(BF16)
            if vec_ref is not None:
                dst[pair, rows : rows + VECS, :] = vec_ref[shard].astype(BF16)


def route_kernel(*refs, bit, ways):
    group = (lax.axis_index("batch") >> bit) & (ways - 1)
    ins, outs = refs[: len(refs) - ways], refs[len(refs) - ways :]
    first = 0
    for keep_ref, got_ref in zip(ins[::2], ins[1::2]):
        rows = keep_ref.shape[1]
        for step, dst in enumerate(outs):
            which = group ^ step
            for index in range(dst.shape[0]):
                at = index * ways + which
                dst[index, first : first + rows, :] = (
                    keep_ref[at].astype(F32) + got_ref[at].astype(F32)
                ).astype(BF16)
        first += rows


def total_of(refs):
    added = refs[0].astype(F32)
    for ref in refs[1:]:
        added = added + ref.astype(F32)
    return added


def sum_kernel(*refs):
    refs[-1][...] = total_of([ref[0] for ref in refs[:-1]]).astype(BF16)


def join_kernel(own_ref, far_ref, near_ref, diagonal_ref, *out_refs):
    h = lax.axis_index("height")
    first = 0
    for dst in [ref for ref in out_refs if ref.shape[0] > 1]:
        rows = dst.shape[0]
        for ref, index in ((own_ref, h), (far_ref, h ^ 2), (near_ref, h ^ 1), (diagonal_ref, h ^ 3)):
            dst[:, pl.ds(pl.multiple_of(BLK * index, BLK), BLK)] = ref[first : first + rows, :].astype(F32)
        first += rows
    if own_ref.shape[0] > first:
        own, far = own_ref[first:, :].astype(F32), far_ref[first:, :].astype(F32)
        near, diagonal = near_ref[first:, :].astype(F32), diagonal_ref[first:, :].astype(F32)
        sums = 0.5 * ((own + near) + (far + diagonal))
        for index, dst in enumerate([ref for ref in out_refs if ref.shape[0] == 1]):
            dst[...] = sums[index : index + 1, 0 : dst.shape[1]]


def join_attn_kernel(own_ref, far_ref, near_ref, diagonal_ref, *out_refs):
    h = lax.axis_index("height")
    rows = out_refs[0].shape[0]
    for first, second, index in ((own_ref, far_ref, h), (near_ref, diagonal_ref, h ^ 1)):
        for position in range(2):
            lane, other = position * BLK, (1 - position) * BLK
            column = pl.multiple_of(BLK * (index ^ (2 * position)), BLK)
            for number, dst in enumerate(out_refs):
                at = number * rows
                dst[:, pl.ds(column, BLK)] = first[at : at + rows, lane : lane + BLK].astype(
                    F32
                ) + second[at : at + rows, other : other + BLK].astype(F32)


def unpack_kernel(bucket_ref, out_own, grad_own, away_ref, out_ref, grad_ref):
    h, home, away = place(bucket_ref)
    for own, received, dst in (
        (out_own, away_ref.at[0], out_ref),
        (grad_own, away_ref.at[1], grad_ref),
    ):
        channels = dst.shape[3]
        for facts, src, wide_rows in ((away, received, 4), (home, own, 6)):
            image, tall, stride, width = facts

            @pl.when(tall)
            def _():
                for row in range(6):
                    dst[image, row, 0:16, :] = src[16 * row : 16 * row + 16, :]
                    dst[image, row, 16:32, :] = jnp.zeros((16, channels), dst.dtype)

            @pl.when(jnp.logical_not(tall))
            def _():
                for row in range(wide_rows):
                    dst[image, row] = src[32 * row : 32 * row + 32, :]
                for row in range(wide_rows, 6):
                    dst[image, row] = jnp.zeros((32, channels), dst.dtype)

            if wide_rows == 4:

                @pl.when(jnp.logical_not(tall) & (h == 3))
                def _():
                    for row in range(6):
                        dst[image, row] = jnp.zeros((32, channels), dst.dtype)


def call(kernel, name, outs, scratch, vmem, *operands, smem=1, any_from=99):
    specs = [SM] * smem + [VM] * (len(operands) - smem)
    specs = [HB if i >= any_from else spec for i, spec in enumerate(specs)]
    return pl.pallas_call(
        kernel,
        name=name,
        out_shape=[jax.ShapeDtypeStruct(shape, dtype) for shape, dtype in outs],
        in_specs=specs,
        out_specs=[SM if dtype == jnp.int32 else VM for shape, dtype in outs],
        scratch_shapes=[
            pltpu.SemaphoreType.DMA(shape)
            if dtype is None
            else (pltpu.SMEM if dtype == jnp.int32 else pltpu.VMEM)(shape, dtype)
            for shape, dtype in scratch
        ],
        compiler_params=pltpu.CompilerParams(vmem_limit_bytes=vmem << 20),
        cost_estimate=pl.CostEstimate(
            flops=int(LENGTH.get(name, 0.02) * RATE), bytes_accessed=1024, transcendentals=0
        ),
    )(*operands)


def on_device(
    inputs,
    bucket,
    norm1_gain,
    norm1_shift,
    conv1_weight,
    conv1_bias,
    norm2_gain,
    norm2_shift,
    conv2_weight,
    conv2_bias,
    norm3_gain,
    norm3_shift,
    query_weight,
    query_bias,
    key_weight,
    value_weight,
    value_bias,
    proj_weight,
    proj_bias,
    cotangent,
):
    C = inputs.shape[-1]
    batches = lax.axis_size("batch")
    bits = batches.bit_length() - 1
    shard_rows = 9 * C // batches
    small_rows = C // batches

    def row(v):
        return v.reshape(1, C)

    def to_core(v):
        return lax.ppermute(v, "height", [(i, i ^ 1) for i in range(4)])

    def to_chip(v):
        return lax.ppermute(v, "height", [(i, i ^ 2) for i in range(4)])

    def to_batch(v, change):
        return lax.ppermute(v, "batch", [(i, i ^ change) for i in range(batches)])

    def after(v, *others):
        return lax.optimization_barrier((v,) + others)[0]

    img16 = ((PIX, C), BF16)
    img32 = ((PIX, C), F32)
    rows8 = ((8, C), F32)
    block = ((PIX, BLK), BF16)
    turned = ((C, PIX), BF16)
    shifts = ((3, PIX + 2 * PAD, C), BF16)

    kinds, away_x, home_x = call(
        pack_kernel, "pack",
        [((2,), jnp.int32), ((128, C), BF16), ((192, C), BF16)],
        [((2,), jnp.int32), (inputs.shape, BF16), ((2,), None)], 54, bucket, inputs,
        smem=0, any_from=0,
    )
    vectors = (
        norm1_gain, norm1_shift, conv1_bias, norm2_gain, norm2_shift, conv2_bias,
        norm3_gain, norm3_shift, query_bias, value_bias, proj_bias,
    )
    recv_x = to_chip(away_x)
    core_x = to_core(home_x)
    vecs, away_c, home_c = call(
        stack_kernel, "stack", [((VECS, C), F32), ((160, C), BF16), ((192, C), BF16)], [], 8,
        kinds, cotangent, *[row(v) for v in vectors],
    )
    recv_c = to_chip(away_c)
    core_c = to_core(home_c)
    core_recv_c = lax.ppermute(away_c, "height", [(i, i ^ 3) for i in range(4)])
    core_recv_x = to_core(after(recv_x, vecs))

    image, conv, act2, stats, act1_t, act2_t, send_t = call(
        first_kernel, "first",
        [img16, img32, img16, rows8, turned, turned, ((2, C // 2, PIX), BF16)],
        [shifts], 14,
        kinds, home_x, core_x, recv_x, core_recv_x, vecs, conv1_weight,
    )
    half_t = to_chip(send_t)
    core_half_t = to_core(half_t)

    attn_out = ((batches // 2, 4 * small_rows, 2 * BLK), BF16)
    middle, mixed, grad2, grad_middle, attn_keep, attn_send, vec_a, block2, block2_send = call(
        second_kernel, "second",
        [img32, img16, img16, img32, attn_out, attn_out, rows8, block, block],
        [shifts, img16, ((PIX, 4 * C), BF16), ((C, 8 * BLK), F32)], 24,
        kinds, image, act2, home_c, core_c, recv_c, core_recv_c, vecs,
        conv2_weight, query_weight, key_weight, value_weight, proj_weight,
    )
    block2_away = to_chip(block2_send)
    attn_got = to_batch(attn_send, 1)

    grad1, block1, block1_send, vec_b = call(
        third_kernel, "third",
        [img16, block, block, rows8],
        [shifts, img32], 14,
        kinds, grad2, conv, stats, vecs, conv2_weight,
    )
    block1_away = to_chip(block1_send)

    def weight_grad(name, act_t, index, own, away, *vec):
        rows = shard_rows + (VECS if vec else 0)
        return call(
            functools.partial(weight_kernel, layer=index), name,
            [((batches // 2, rows, BLK), BF16)] * 2,
            [((C, 2 * PIX), BF16), ((2 * PIX, 9 * BLK), BF16), ((3, PIX + 2 * PAD, BLK), BF16),
             ((9 * C, BLK), F32)],
            18, kinds, act_t, half_t, core_half_t, own, away, *vec,
        )

    keep2, send2 = weight_grad("weight2", act2_t, 1, after(block2, block1), block2_away)
    got2 = to_batch(send2, 1)

    def spread(name, bit, *pairs, behind=()):
        ways = 1 << min(2, bits - bit)
        shape = (pairs[0].shape[0] // ways, sum(v.shape[1] for v in pairs[::2]), pairs[0].shape[2])
        parts = call(
            functools.partial(route_kernel, bit=bit, ways=ways), name + str(bit),
            [(shape, BF16)] * ways, [], 16, *pairs, smem=0,
        )
        return parts, [to_batch(after(parts[j], *behind), j << bit) for j in range(1, ways)]

    def finish(name, parts, got):
        for bit in range(3, bits, 2):
            added = total_of([parts[0]] + got).astype(BF16)
            parts, got = spread(name, bit, added, jnp.zeros_like(added))
        return call(
            sum_kernel, "sum" + name, [(parts[0].shape[1:], BF16)], [], 8, parts[0], *got, smem=0
        )[0]

    def gather(shard, *between):
        far = to_chip(shard)
        near = to_core(shard)
        return shard, far, near, to_core(after(far, *between))

    parts_a, got_a = spread("routea", 1, after(attn_keep, send2), attn_got)
    out_own, grad_own, image_send, vec_c = call(
        fourth_kernel, "fourth",
        [((192, C), BF16), ((192, C), BF16), ((2, 128, C), BF16), ((batches, VECS, BLK), F32)],
        [shifts, img32, img16, ((VECS, C), F32)], 14,
        kinds, after(grad1, *parts_a), image, stats, grad_middle, middle, mixed, vecs,
        conv1_weight, proj_weight, vec_a, vec_b,
    )
    image_away = to_chip(image_send)
    keep1, send1 = weight_grad("weight1", act1_t, 0, block1, block1_away, vec_c)
    got1 = to_batch(send1, 1)
    shard_a = finish("routea", parts_a, [after(g, vec_c) for g in got_a])
    parts_b, got_b = spread("routeb", 1, after(keep2, send1, shard_a), got2)
    gathered_a = gather(shard_a)
    outputs, input_grad = call(
        unpack_kernel, "unpack",
        [(inputs.shape, BF16)] * 2, [], 8,
        kinds, out_own, grad_own, after(image_away, parts_b[0]),
    )
    parts_c, got_c = spread("routec", 1, after(keep1, outputs), got1, behind=got_b)
    shard_b = finish("routeb", parts_b, [after(g, parts_c[0]) for g in got_b])
    gathered_b = gather(shard_b)
    shard_c = finish(
        "routec", parts_c, [after(g, gathered_b[1], gathered_a[1]) for g in got_c]
    )
    small = call(
        join_attn_kernel, "joina", [((small_rows, C), F32)] * 4, [], 8,
        after(gathered_a[0], shard_c), *gathered_a[1:], smem=0,
    )
    (whole2,) = call(
        join_kernel, "joinb", [((shard_rows, C), F32)], [], 8,
        after(gathered_b[0], shard_c), *gathered_b[1:], smem=0,
    )
    gathered_c = gather(shard_c, whole2, *small)
    whole1, *sums = call(
        join_kernel, "joinc", [((shard_rows, C), F32)] + [((1, small_rows), F32)] * 11, [], 8,
        *gathered_c, smem=0,
    )
    v = [row.reshape(small_rows) for row in sums]

    return (
        outputs, input_grad,
        v[9], v[10], whole1, v[8],
        v[6], v[7], whole2, v[5],
        v[0], v[1],
        small[0], v[2], small[1], small[2], v[3], small[3], v[4],
    )


def solution(mesh):
    image = P("batch", "height", None, None)
    vector = P("batch")
    matrix = P("batch", None)
    return jax.shard_map(
        on_device,
        mesh=mesh,
        in_specs=(image, vector) + (P(),) * 17 + (image,),
        out_specs=(
            image, image,
            vector, vector, matrix, vector,
            vector, vector, matrix, vector,
            vector, vector,
            matrix, vector, matrix, matrix, vector, matrix, vector,
        ),
        check_vma=False,
    )
```

```python
import functools

import jax
import jax.numpy as jnp
from jax import lax
from jax.experimental import pallas as pl
from jax.experimental.pallas import tpu as pltpu
from jax.sharding import PartitionSpec as P

GROUPS = 32
UNIT = 8
PIX = 512
PAD = 32
BLK = 128
F32 = jnp.float32
BF16 = jnp.bfloat16
epsilon = 1e-05

VM = pl.BlockSpec(memory_space=pltpu.VMEM)
SM = pl.BlockSpec(memory_space=pltpu.SMEM)
HB = pl.BlockSpec(memory_space=pltpu.HBM)
RATE = 1 << 30
LENGTH = {
    "pack": 10, "stack": 10, "first": 0.02, "second": 30, "third": 20, "fourth": 10, "weight2": 1, "weight1": 3, "routeb1": 20,
}


def place(bucket_ref):
    h = lax.axis_index("height")
    upper = lax.div(h, 2)
    tall_first = bucket_ref[0] == 1
    tall_image = jnp.where(tall_first, 0, 1)
    home = jnp.where(upper == 1, tall_image, 1 - tall_image)
    away = 1 - home

    def facts(image):
        kind = bucket_ref[image]
        tall = kind == 1
        stride = jnp.where(tall, 2 * UNIT, 4 * UNIT)
        width = jnp.where(kind == 0, 3 * UNIT, stride)
        return (image, tall, stride, width)

    return h, facts(home), facts(away)


def pixel_col(stride, lanes=1):
    rows = lax.broadcasted_iota(jnp.int32, (PIX, lanes), 0)
    return rows, rows & (stride - 1)


def pixel_mask(facts):
    unused, tall, stride, width = facts
    rows, cols = pixel_col(stride)
    limit = jnp.where(tall, 6 * UNIT * UNIT, 8 * UNIT * UNIT)
    mask = jnp.where((cols < width) & (rows < limit), 1.0, 0.0).astype(F32)
    size = jnp.where(tall | (width == 3 * UNIT), 6 * UNIT * UNIT, 8 * UNIT * UNIT)
    return mask, size.astype(F32)


def group_total(rows):
    members = rows.shape[1] // GROUPS
    lane = lax.broadcasted_iota(jnp.int32, (rows.shape[0], BLK), 1)
    tiles = []
    for tile in range(rows.shape[1] // BLK):
        part = rows[:, tile * BLK : (tile + 1) * BLK]
        step = 1
        while step < members:
            place_in_four = (lane // step) & 3
            added = part
            for d in (1, 2, 3):
                up = pltpu.roll(part, BLK - d * step, 1)
                down = pltpu.roll(part, (4 - d) * step, 1)
                added = added + jnp.where(place_in_four + d < 4, up, down)
            part = added
            step *= 4
        tiles.append(part)
    return jnp.concatenate(tiles, axis=1)


def total(values):
    return jnp.sum(values, axis=0, keepdims=True)


def wide_total(*rows):
    stacked = jnp.concatenate(list(rows) + [rows[0]] * (8 - len(rows)), axis=0)
    sums = group_total(stacked)
    return [sums[i : i + 1] for i in range(len(rows))]


def norm_stats(values, mask, group_size):
    mean = wide_total(total(values))[0] / group_size
    centered = (values - mean) * mask
    variance = wide_total(total(centered * centered))[0] / group_size
    return mean, lax.rsqrt(variance + epsilon)


def silu_norm(values, mean, inverse, gain, shift, mask):
    scale = 0.5 * inverse * gain
    half = values * scale + (0.5 * shift - mean * scale)
    return (half + half * jnp.tanh(half)) * mask


def norm_back(grad, normal, inverse, mask, group_size, gain):
    plain_row = total(grad)
    cross_row = total(grad * normal)
    plain, cross = [v / group_size for v in wide_total(plain_row * gain, cross_row * gain)]
    grad_in = grad * (inverse * gain) - mask * (plain * inverse + normal * (cross * inverse))
    return grad_in, cross_row, plain_row


def silu_slope(u):
    half = 0.5 * u
    t = jnp.tanh(half)
    return (0.5 + 0.5 * t) * (1.0 + half * (1.0 - t))


def mm(a, b):
    return jnp.dot(a, b, preferred_element_type=F32)


def mm_nt(a, b):
    return lax.dot_general(a, b, (((1,), (1,)), ((), ())), preferred_element_type=F32)


def mm_tn(a, b):
    return lax.dot_general(a, b, (((0,), (0,)), ((), ())), preferred_element_type=F32)


def fill_shifts(shift_ref, values, stride):
    unused, cols = pixel_col(stride)
    lanes = values.shape[1]
    zeros = jnp.zeros((PAD, lanes), BF16)
    for q in range(3):
        shift_ref[q, 0:PAD, :] = zeros
        shift_ref[q, PAD + PIX : 2 * PAD + PIX, :] = zeros
    left = jnp.where(cols == 0, 0.0, pltpu.roll(values, 1, 0))
    right = jnp.where(cols == stride - 1, 0.0, pltpu.roll(values, PIX - 1, 0))
    shift_ref[0, PAD : PAD + PIX, :] = left.astype(BF16)
    shift_ref[1, PAD : PAD + PIX, :] = values.astype(BF16)
    shift_ref[2, PAD : PAD + PIX, :] = right.astype(BF16)


def tap(shift_ref, p, q, stride, first=0, count=PIX):
    start = pl.multiple_of(PAD + first + (p - 1) * stride, 16)
    return shift_ref[q, pl.ds(start, count), :]


def conv_forward(shift_ref, weight_ref, stride, out_ref, tile=256):
    for first in range(0, PIX, tile):
        stacked = jnp.concatenate(
            [tap(shift_ref, p, q, stride, first, tile) for p in range(3) for q in range(3)], axis=1
        )
        out_ref[first : first + tile, :] = mm(stacked, weight_ref[...])


def conv_backward(shift_ref, weight_ref, stride, out_ref, tile=256):
    channels = weight_ref.shape[1]
    for first in range(0, PIX, tile):
        acc = None
        for p in range(3):
            for q in range(3):
                row = (8 - (3 * p + q)) * channels
                part = mm_nt(
                    tap(shift_ref, p, q, stride, first, tile), weight_ref[row : row + channels, :]
                )
                acc = part if acc is None else acc + part
        out_ref[first : first + tile, :] = acc


def assemble(out_ref, facts, h, pieces):
    unused, tall, stride, width = facts
    own, partner, received, partner_received = pieces
    other = h ^ 1

    @pl.when(tall)
    def _():
        for ref, index in (
            (own, h),
            (partner, other),
            (received, h ^ 2),
            (partner_received, other ^ 2),
        ):
            out_ref[pl.ds(pl.multiple_of(96 * index, 16), 96), :] = ref[0:96, :]
        out_ref[384:512, :] = jnp.zeros((128, out_ref.shape[1]), out_ref.dtype)

    @pl.when(jnp.logical_not(tall))
    def _():
        low = h & 1
        out_ref[pl.ds(pl.multiple_of(192 * low, 16), 192), :] = own[...]
        out_ref[pl.ds(pl.multiple_of(192 * (1 - low), 16), 192), :] = partner[...]

        @pl.when(low == 0)
        def _():
            out_ref[384:512, :] = received[0:128, :]

        @pl.when(low == 1)
        def _():
            out_ref[384:512, :] = partner_received[0:128, :]


def split_out(full_ref, facts, h, own_ref, send_ref):
    unused, tall, stride, width = facts
    send_h = h ^ 2

    @pl.when(tall)
    def _():
        own_ref[0:96, :] = full_ref[pl.ds(pl.multiple_of(96 * h, 16), 96), :]
        own_ref[96:192, :] = jnp.zeros((96, own_ref.shape[1]), own_ref.dtype)
        send_ref[0:96, :] = full_ref[pl.ds(pl.multiple_of(96 * send_h, 16), 96), :]
        send_ref[96:128, :] = jnp.zeros((32, own_ref.shape[1]), own_ref.dtype)

    @pl.when(jnp.logical_not(tall))
    def _():
        own_ref[...] = full_ref[pl.ds(pl.multiple_of(192 * (h & 1), 16), 192), :]
        send_ref[...] = full_ref[384:512, :]


GAIN1, SHIFT1, BIAS1, GAIN2, SHIFT2, BIAS2, GAIN3, SHIFT3, QB, VB, PB = range(11)
VECS = 16


def vec(vec_ref, index):
    return vec_ref[index : index + 1, :]


def pack(src, facts, dst, wide_rows):
    image, tall, stride, width = facts

    @pl.when(tall)
    def _():
        for row in range(6):
            dst[16 * row : 16 * row + 16, :] = src[image, row, 0:16, :]
        dst[96 : dst.shape[0], :] = jnp.zeros((dst.shape[0] - 96, dst.shape[1]), dst.dtype)

    @pl.when(jnp.logical_not(tall))
    def _():
        for row in range(wide_rows):
            dst[32 * row : 32 * row + 32, :] = src[image, row]


def pack_kernel(bucket_hbm, x_hbm, kinds, away_x, home_x, bucket_ref, x_ref, sems):
    copies = (
        pltpu.make_async_copy(bucket_hbm, bucket_ref, sems.at[0]),
        pltpu.make_async_copy(x_hbm, x_ref, sems.at[1]),
    )
    for copy in copies:
        copy.start()
    for copy in copies:
        copy.wait()
    h, home, away = place(bucket_ref)
    kinds[0] = bucket_ref[0]
    kinds[1] = bucket_ref[1]
    pack(x_ref, away, away_x, 4)
    pack(x_ref, home, home_x, 6)


def stack_kernel(kinds, cot_ref, *refs):
    h, home, away = place(kinds)
    out_ref, away_c, home_c = refs[-3:]
    count = len(refs) - 3
    for index, ref in enumerate(refs[:count]):
        out_ref[index : index + 1, :] = ref[...]
    out_ref[count:, :] = jnp.zeros((VECS - count, out_ref.shape[1]), F32)
    pack(cot_ref, away, away_c, 4)
    pack(cot_ref, home, home_c, 6)


def first_kernel(
    bucket_ref, own, partner, received, partner_received, vecs, weight1,
    image_ref, conv_ref, act2_ref, stats_ref, act1_t, act2_t, send_t,
    shift_ref,
):
    h, home, away = place(bucket_ref)
    stride = home[2]
    mask, pixels = pixel_mask(home)
    channels = vecs.shape[1]
    group_size = pixels * (channels // GROUPS)
    assemble(image_ref, home, h, (own, partner, received, partner_received))
    values = image_ref[...].astype(F32) * mask
    mean1, inverse1 = norm_stats(values, mask, group_size)
    act = silu_norm(values, mean1, inverse1, vec(vecs, GAIN1), vec(vecs, SHIFT1), mask)
    fill_shifts(shift_ref, act, stride)
    act1_t[...] = act.astype(BF16).T
    conv_forward(shift_ref, weight1, stride, conv_ref)
    values = (conv_ref[...] + vec(vecs, BIAS1)) * mask
    conv_ref[...] = values
    mean2, inverse2 = norm_stats(values, mask, group_size)
    act = silu_norm(values, mean2, inverse2, vec(vecs, GAIN2), vec(vecs, SHIFT2), mask)
    act = act.astype(BF16)
    act2_ref[...] = act
    act2_t[...] = act.T
    half = pl.multiple_of((h & 1) * (channels // 2), 16)
    send_t[0] = act1_t[pl.ds(half, channels // 2), :]
    send_t[1] = act2_t[pl.ds(half, channels // 2), :]
    stats_ref[0:1, :] = mean1
    stats_ref[1:2, :] = inverse1
    stats_ref[2:3, :] = mean2
    stats_ref[3:4, :] = inverse2
    stats_ref[4:8, :] = jnp.zeros((4, channels), F32)


def second_kernel(
    bucket_ref, image_ref, act2_ref, own, partner, received, partner_received, vecs,
    weight2, wq, wk, wv, wp,
    middle_ref, mixed_ref, grad2_ref, grad_middle_ref, attn_keep, attn_send, vec_ref,
    block_keep, block_send,
    shift_ref, full_ref, grads_ref, sum_ref,
):
    h, home, away = place(bucket_ref)
    stride = home[2]
    mask, pixels = pixel_mask(home)
    channels = vecs.shape[1]
    group_size = pixels * (channels // GROUPS)
    scaling = channels ** (-0.5)
    assemble(full_ref, home, h, (own, partner, received, partner_received))
    fill_shifts(shift_ref, act2_ref[...].astype(F32), stride)
    conv_forward(shift_ref, weight2, stride, middle_ref)
    middle = mask * (image_ref[...].astype(F32) + (middle_ref[...] + vec(vecs, BIAS2)))
    middle_ref[...] = middle
    mean3, inverse3 = norm_stats(middle, mask, group_size)
    normal = (middle - mean3) * inverse3
    normed = (normal * vec(vecs, GAIN3) + vec(vecs, SHIFT3)).astype(BF16)
    wide = jnp.concatenate([wq[...], wk[...], wv[...]], axis=1)
    joint = mm(normed, wide)
    queries = (joint[:, 0:channels] + vec(vecs, QB)).astype(BF16)
    keys = joint[:, channels : 2 * channels].astype(BF16)
    values = (joint[:, 2 * channels :] + vec(vecs, VB)).astype(BF16)
    lanes = lax.broadcasted_iota(jnp.int32, (1, PIX), 1)
    key_cols = lanes & (stride - 1)
    key_valid = (key_cols < home[3]) & (lanes < jnp.where(home[1], 384, 512))
    scores = jnp.where(key_valid, mm_nt(queries, keys) * scaling, -1000000000.0)
    grad_top = full_ref[...].astype(F32) * mask
    grad_rows = grad_top.astype(BF16)
    grad_mixed = mm_nt(grad_rows, wp[...]).astype(BF16)
    grad_soft = mm_nt(grad_mixed, values)
    raised = jnp.exp(scores - jnp.max(scores, axis=1, keepdims=True))
    soft = raised * (1.0 / jnp.sum(raised, axis=1, keepdims=True))
    soft16 = soft.astype(BF16)
    mixed = mm(soft16, values).astype(BF16)
    mixed_ref[...] = mixed

    grad_values = mm_tn(soft16, grad_mixed).astype(BF16)
    grad_scores = soft * (grad_soft - jnp.sum(soft * grad_soft, axis=1, keepdims=True))
    grad_scores = grad_scores.astype(BF16)
    grad_queries = (mm(grad_scores, keys) * scaling).astype(BF16)
    grad_keys = (mm_tn(grad_scores, queries) * scaling).astype(BF16)
    grads_ref[:, 0:channels] = grad_queries
    grads_ref[:, channels : 2 * channels] = grad_keys
    grads_ref[:, 2 * channels : 3 * channels] = grad_values
    grads_ref[:, 3 * channels : 4 * channels] = grad_rows
    grad_normed = mm_nt(grads_ref[:, 0 : 3 * channels], wide)
    grad_in, gain_grad, shift_grad = norm_back(
        grad_normed, normal, inverse3, mask, group_size, vec(vecs, GAIN3)
    )
    grad_middle = mask * (grad_top + grad_in)
    grad_middle_ref[...] = grad_middle
    grad2 = grad_middle.astype(BF16)
    grad2_ref[...] = grad2
    vec_ref[0:1, :] = gain_grad
    vec_ref[1:2, :] = shift_grad
    vec_ref[2:3, :] = total(grad_queries.astype(F32))
    vec_ref[3:4, :] = total(grad_values.astype(F32))
    vec_ref[4:5, :] = total(grad_top)
    vec_ref[5:6, :] = total(grad2.astype(F32))
    vec_ref[6:8, :] = jnp.zeros((2, channels), F32)

    keep_at = pl.multiple_of(BLK * h, BLK)
    send_at = pl.multiple_of(BLK * (h ^ 2), BLK)
    block_keep[...] = grad2_ref[:, pl.ds(keep_at, BLK)]
    block_send[...] = grad2_ref[:, pl.ds(send_at, BLK)]

    def blocks(index):
        start = index * channels
        return [
            grads_ref[:, pl.ds(pl.multiple_of(start + BLK * h, BLK), BLK)],
            grads_ref[:, pl.ds(pl.multiple_of(start + BLK * (h ^ 2), BLK), BLK)],
        ]

    sum_ref[:, 0 : 6 * BLK] = mm_tn(normed, jnp.concatenate(blocks(0) + blocks(1) + blocks(2), axis=1))
    sum_ref[:, 6 * BLK : 8 * BLK] = mm_tn(mixed, jnp.concatenate(blocks(3), axis=1))
    mine = lax.axis_index("batch") & 1
    pairs = attn_keep.shape[0]
    rows = channels // (2 * pairs)
    for pair in range(pairs):
        for dst, which in ((attn_keep, mine), (attn_send, 1 - mine)):
            part = sum_ref[pl.ds(pl.multiple_of((2 * pair + which) * rows, 8), rows), :].astype(BF16)
            for index in range(4):
                at = index * 2 * BLK
                dst[pair, index * rows : (index + 1) * rows, :] = part[:, at : at + 2 * BLK]


def third_kernel(
    bucket_ref, grad2_ref, conv_ref, stats_ref, vecs, weight2,
    grad1_ref, block_keep, block_send, vec_ref,
    shift_ref, acc_ref,
):
    h, home, away = place(bucket_ref)
    stride = home[2]
    mask, pixels = pixel_mask(home)
    channels = vecs.shape[1]
    group_size = pixels * (channels // GROUPS)
    fill_shifts(shift_ref, grad2_ref[...].astype(F32), stride)
    conv_backward(shift_ref, weight2, stride, acc_ref)
    inverse = stats_ref[3:4, :]
    normal = (conv_ref[...] - stats_ref[2:3, :]) * inverse
    u = normal * vec(vecs, GAIN2) + vec(vecs, SHIFT2)
    grad = mask * acc_ref[...] * silu_slope(u)
    grad_in, gain_grad, shift_grad = norm_back(
        grad, normal, inverse, mask, group_size, vec(vecs, GAIN2)
    )
    grad1 = grad_in.astype(BF16)
    grad1_ref[...] = grad1
    vec_ref[0:1, :] = gain_grad
    vec_ref[1:2, :] = shift_grad
    vec_ref[2:3, :] = total(grad1.astype(F32))
    vec_ref[3:8, :] = jnp.zeros((5, channels), F32)
    block_keep[...] = grad1_ref[:, pl.ds(pl.multiple_of(BLK * h, BLK), BLK)]
    block_send[...] = grad1_ref[:, pl.ds(pl.multiple_of(BLK * (h ^ 2), BLK), BLK)]


def fourth_kernel(
    bucket_ref, grad1_ref, image_ref, stats_ref, grad_middle_ref, middle_ref, mixed_ref, vecs,
    weight1, wp, vec_a, vec_b,
    out_own, grad_own, send_ref, vec_keep, vec_send,
    shift_ref, acc_ref, full_ref, vec_ref,
):
    h, home, away = place(bucket_ref)
    stride = home[2]
    mask, pixels = pixel_mask(home)
    channels = vecs.shape[1]
    group_size = pixels * (channels // GROUPS)
    projected = mm(mixed_ref[...], wp[...]) + vec(vecs, PB)
    full_ref[...] = (mask * (middle_ref[...] + projected)).astype(BF16)
    split_out(full_ref, home, h, out_own, send_ref.at[0])
    fill_shifts(shift_ref, grad1_ref[...].astype(F32), stride)
    conv_backward(shift_ref, weight1, stride, acc_ref)
    inverse = stats_ref[1:2, :]
    normal = (image_ref[...].astype(F32) * mask - stats_ref[0:1, :]) * inverse
    u = normal * vec(vecs, GAIN1) + vec(vecs, SHIFT1)
    grad = mask * acc_ref[...] * silu_slope(u)
    grad_in, gain_grad, shift_grad = norm_back(
        grad, normal, inverse, mask, group_size, vec(vecs, GAIN1)
    )
    full_ref[...] = (mask * (grad_middle_ref[...] + grad_in)).astype(BF16)
    split_out(full_ref, home, h, grad_own, send_ref.at[1])
    vec_ref[0:6, :] = vec_a[0:6, :]
    vec_ref[6:9, :] = vec_b[0:3, :]
    vec_ref[9:10, :] = gain_grad
    vec_ref[10:11, :] = shift_grad
    vec_ref[11:VECS, :] = jnp.zeros((VECS - 11, channels), F32)
    pairs = vec_keep.shape[0]
    rows = channels // (2 * pairs)
    mine = (lax.axis_index("batch") & 1) == 1
    for pair in range(pairs):
        parts = []
        for shard in (2 * pair, 2 * pair + 1):
            start = shard * rows
            tile = start // BLK * BLK
            part = vec_ref[:, tile : tile + BLK]
            parts.append(part if start == tile else pltpu.roll(part, BLK - (start - tile), 1))
        vec_keep[pair] = jnp.where(mine, parts[1], parts[0]).astype(BF16)
        vec_send[pair] = jnp.where(mine, parts[0], parts[1]).astype(BF16)


def weight_kernel(
    bucket_ref, act_t, half_t, partner_half_t, block_own, block_away,
    keep_ref, send_ref, left_ref, right_ref, shift_ref, sum_ref, *, layer,
):
    h, home, away = place(bucket_ref)
    channels = act_t.shape[0]
    half = channels // 2
    left_ref[:, 0:PIX] = act_t[...]
    left_ref[pl.ds(pl.multiple_of((h & 1) * half, 16), half), PIX : 2 * PIX] = half_t[layer]
    left_ref[pl.ds(pl.multiple_of((1 - (h & 1)) * half, 16), half), PIX : 2 * PIX] = (
        partner_half_t[layer]
    )
    for index, (facts, block) in enumerate(((home, block_own), (away, block_away))):
        stride = facts[2]
        fill_shifts(shift_ref, block[...].astype(F32), stride)
        for p in range(3):
            for q in range(3):
                column = (3 * p + q) * BLK
                right_ref[index * PIX : (index + 1) * PIX, column : column + BLK] = tap(
                    shift_ref, 2 - p, 2 - q, stride
                )
    joint = mm(left_ref[...], right_ref[...])
    for t in range(9):
        sum_ref[t * channels : (t + 1) * channels, :] = joint[:, t * BLK : (t + 1) * BLK]
    mine = lax.axis_index("batch") & 1
    pairs = keep_ref.shape[0]
    rows = 9 * channels // (2 * pairs)
    for pair in range(pairs):
        for dst, which in ((keep_ref, mine), (send_ref, 1 - mine)):
            shard = 2 * pair + which
            dst[pair] = sum_ref[pl.ds(pl.multiple_of(shard * rows, 8), rows), :].astype(BF16)


def route_kernel(keep_ref, got_ref, *outs, bit, first):
    ways = len(outs) if first == 0 else len(outs) // 2
    group = (lax.axis_index("batch") >> bit) & (ways - 1)
    rows = keep_ref.shape[1]
    for step, dst in enumerate(outs[-ways:]):
        which = group ^ step
        for index in range(dst.shape[0]):
            at = index * ways + which
            dst[index, first : first + rows, :] = (
                keep_ref[at].astype(F32) + got_ref[at].astype(F32)
            ).astype(BF16)


def total_of(refs):
    added = refs[0].astype(F32)
    for ref in refs[1:]:
        added = added + ref.astype(F32)
    return added


def sum_kernel(*refs):
    refs[-1][...] = total_of([ref[0] for ref in refs[:-1]]).astype(BF16)


def join_kernel(own_ref, far_ref, near_ref, diagonal_ref, *out_refs):
    h = lax.axis_index("height")
    first = 0
    for dst in [ref for ref in out_refs if ref.shape[0] > 1]:
        rows = dst.shape[0]
        for ref, index in ((own_ref, h), (far_ref, h ^ 2), (near_ref, h ^ 1), (diagonal_ref, h ^ 3)):
            dst[:, pl.ds(pl.multiple_of(BLK * index, BLK), BLK)] = ref[first : first + rows, :].astype(F32)
        first += rows
    if own_ref.shape[0] > first:
        own, far = own_ref[first:, :].astype(F32), far_ref[first:, :].astype(F32)
        near, diagonal = near_ref[first:, :].astype(F32), diagonal_ref[first:, :].astype(F32)
        sums = 0.5 * ((own + near) + (far + diagonal))
        for index, dst in enumerate([ref for ref in out_refs if ref.shape[0] == 1]):
            dst[...] = sums[index : index + 1, 0 : dst.shape[1]]


def join_attn_kernel(own_ref, far_ref, near_ref, diagonal_ref, *out_refs):
    h = lax.axis_index("height")
    rows = out_refs[0].shape[0]
    for first, second, index in ((own_ref, far_ref, h), (near_ref, diagonal_ref, h ^ 1)):
        for position in range(2):
            lane, other = position * BLK, (1 - position) * BLK
            column = pl.multiple_of(BLK * (index ^ (2 * position)), BLK)
            for number, dst in enumerate(out_refs):
                at = number * rows
                dst[:, pl.ds(column, BLK)] = first[at : at + rows, lane : lane + BLK].astype(
                    F32
                ) + second[at : at + rows, other : other + BLK].astype(F32)


def unpack_kernel(bucket_ref, out_own, grad_own, away_ref, out_ref, grad_ref):
    h, home, away = place(bucket_ref)
    for own, received, dst in (
        (out_own, away_ref.at[0], out_ref),
        (grad_own, away_ref.at[1], grad_ref),
    ):
        channels = dst.shape[3]
        for facts, src, wide_rows in ((away, received, 4), (home, own, 6)):
            image, tall, stride, width = facts

            @pl.when(tall)
            def _():
                for row in range(6):
                    dst[image, row, 0:16, :] = src[16 * row : 16 * row + 16, :]
                    dst[image, row, 16:32, :] = jnp.zeros((16, channels), dst.dtype)

            @pl.when(jnp.logical_not(tall))
            def _():
                for row in range(wide_rows):
                    dst[image, row] = src[32 * row : 32 * row + 32, :]
                for row in range(wide_rows, 6):
                    dst[image, row] = jnp.zeros((32, channels), dst.dtype)

            if wide_rows == 4:

                @pl.when(jnp.logical_not(tall) & (h == 3))
                def _():
                    for row in range(6):
                        dst[image, row] = jnp.zeros((32, channels), dst.dtype)


def call(kernel, name, outs, scratch, vmem, *operands, smem=1, any_from=99, aliases={}):
    specs = [SM] * smem + [VM] * (len(operands) - smem)
    specs = [HB if i >= any_from else spec for i, spec in enumerate(specs)]
    return pl.pallas_call(
        kernel,
        name=name,
        out_shape=[jax.ShapeDtypeStruct(shape, dtype) for shape, dtype in outs],
        in_specs=specs,
        out_specs=[SM if dtype == jnp.int32 else VM for shape, dtype in outs],
        scratch_shapes=[
            pltpu.SemaphoreType.DMA(shape)
            if dtype is None
            else (pltpu.SMEM if dtype == jnp.int32 else pltpu.VMEM)(shape, dtype)
            for shape, dtype in scratch
        ],
        input_output_aliases=aliases,
        compiler_params=pltpu.CompilerParams(vmem_limit_bytes=vmem << 20),
        cost_estimate=pl.CostEstimate(
            flops=int(LENGTH.get(name, 0.02) * RATE), bytes_accessed=1024, transcendentals=0
        ),
    )(*operands)


def on_device(
    inputs,
    bucket,
    norm1_gain,
    norm1_shift,
    conv1_weight,
    conv1_bias,
    norm2_gain,
    norm2_shift,
    conv2_weight,
    conv2_bias,
    norm3_gain,
    norm3_shift,
    query_weight,
    query_bias,
    key_weight,
    value_weight,
    value_bias,
    proj_weight,
    proj_bias,
    cotangent,
):
    C = inputs.shape[-1]
    batches = lax.axis_size("batch")
    bits = batches.bit_length() - 1
    shard_rows = 9 * C // batches
    small_rows = C // batches

    def row(v):
        return v.reshape(1, C)

    def to_core(v):
        return lax.ppermute(v, "height", [(i, i ^ 1) for i in range(4)])

    def to_chip(v):
        return lax.ppermute(v, "height", [(i, i ^ 2) for i in range(4)])

    def to_batch(v, change):
        return lax.ppermute(v, "batch", [(i, i ^ change) for i in range(batches)])

    def after(v, *others):
        return lax.optimization_barrier((v,) + others)[0]

    img16 = ((PIX, C), BF16)
    img32 = ((PIX, C), F32)
    rows8 = ((8, C), F32)
    block = ((PIX, BLK), BF16)
    turned = ((C, PIX), BF16)
    shifts = ((3, PIX + 2 * PAD, C), BF16)

    kinds, away_x, home_x = call(
        pack_kernel, "pack",
        [((2,), jnp.int32), ((128, C), BF16), ((192, C), BF16)],
        [((2,), jnp.int32), (inputs.shape, BF16), ((2,), None)], 54, bucket, inputs,
        smem=0, any_from=0,
    )
    vectors = (
        norm1_gain, norm1_shift, conv1_bias, norm2_gain, norm2_shift, conv2_bias,
        norm3_gain, norm3_shift, query_bias, value_bias, proj_bias,
    )
    recv_x = to_chip(away_x)
    core_x = to_core(home_x)
    vecs, away_c, home_c = call(
        stack_kernel, "stack", [((VECS, C), F32), ((160, C), BF16), ((192, C), BF16)], [], 8,
        kinds, cotangent, *[row(v) for v in vectors],
    )
    recv_c = to_chip(away_c)
    core_c = to_core(home_c)
    core_recv_c = lax.ppermute(away_c, "height", [(i, i ^ 3) for i in range(4)])
    core_recv_x = to_core(after(recv_x, vecs))

    image, conv, act2, stats, act1_t, act2_t, send_t = call(
        first_kernel, "first",
        [img16, img32, img16, rows8, turned, turned, ((2, C // 2, PIX), BF16)],
        [shifts], 14,
        kinds, home_x, core_x, recv_x, core_recv_x, vecs, conv1_weight,
    )
    half_t = to_chip(send_t)
    core_half_t = to_core(half_t)

    attn_out = ((batches // 2, 4 * small_rows, 2 * BLK), BF16)
    middle, mixed, grad2, grad_middle, attn_keep, attn_send, vec_a, block2, block2_send = call(
        second_kernel, "second",
        [img32, img16, img16, img32, attn_out, attn_out, rows8, block, block],
        [shifts, img16, ((PIX, 4 * C), BF16), ((C, 8 * BLK), F32)], 24,
        kinds, image, act2, home_c, core_c, recv_c, core_recv_c, vecs,
        conv2_weight, query_weight, key_weight, value_weight, proj_weight,
    )
    block2_away = to_chip(block2_send)
    attn_got = to_batch(attn_send, 1)

    grad1, block1, block1_send, vec_b = call(
        third_kernel, "third",
        [img16, block, block, rows8],
        [shifts, img32], 14,
        kinds, grad2, conv, stats, vecs, conv2_weight,
    )
    block1_away = to_chip(block1_send)

    def weight_grad(name, act_t, index, own, away):
        return call(
            functools.partial(weight_kernel, layer=index), name,
            [((batches // 2, shard_rows, BLK), BF16)] * 2,
            [((C, 2 * PIX), BF16), ((2 * PIX, 9 * BLK), BF16), ((3, PIX + 2 * PAD, BLK), BF16),
             ((9 * C, BLK), F32)],
            18, kinds, act_t, half_t, core_half_t, own, away,
        )

    keep2, send2 = weight_grad("weight2", act2_t, 1, after(block2, block1), block2_away)
    got2 = to_batch(send2, 1)

    def spread(name, bit, keep, got, tail=None, behind=()):
        ways = 1 << min(2, bits - bit)
        rows = keep.shape[1]
        shape = (keep.shape[0] // ways, rows + (VECS if tail else 0), keep.shape[2])
        parts = call(
            functools.partial(route_kernel, bit=bit, first=0), name + str(bit),
            [(shape, BF16)] * ways, [], 16, keep, got, smem=0,
        )
        if tail:
            parts = call(
                functools.partial(route_kernel, bit=bit, first=rows), name + "tail",
                [(shape, BF16)] * ways, [], 16, *tail, *parts, smem=0,
                aliases={2 + j: j for j in range(ways)},
            )
        return parts, [to_batch(after(parts[j], *behind), j << bit) for j in range(1, ways)]

    def finish(name, parts, got):
        for bit in range(3, bits, 2):
            added = total_of([parts[0]] + got).astype(BF16)
            parts, got = spread(name, bit, added, jnp.zeros_like(added))
        return call(
            sum_kernel, "sum" + name, [(parts[0].shape[1:], BF16)], [], 8, parts[0], *got, smem=0
        )[0]

    def gather(shard, *between):
        far = to_chip(shard)
        near = to_core(shard)
        return shard, far, near, to_core(after(far, *between))

    parts_a, got_a = spread("routea", 1, after(attn_keep, send2), attn_got)
    keep1, send1 = weight_grad("weight1", act1_t, 0, after(block1, *parts_a), block1_away)
    got1 = to_batch(send1, 1)
    shard_a = finish("routea", parts_a, [after(g, send1) for g in got_a])
    out_own, grad_own, image_send, vec_keep, vec_send = call(
        fourth_kernel, "fourth",
        [((192, C), BF16), ((192, C), BF16), ((2, 128, C), BF16),
         ((batches // 2, VECS, BLK), BF16), ((batches // 2, VECS, BLK), BF16)],
        [shifts, img32, img16, ((VECS, C), F32)], 14,
        kinds, after(grad1, send1), image, stats, grad_middle, middle, mixed, vecs,
        conv1_weight, proj_weight, vec_a, vec_b,
    )
    image_away = to_chip(image_send)
    vec_got = to_batch(vec_send, 1)
    parts_b, got_b = spread("routeb", 1, after(keep2, vec_keep, shard_a), got2)
    parts_c, got_c = spread("routec", 1, keep1, got1, (vec_keep, vec_got), behind=got_b)
    shard_b = finish("routeb", parts_b, [after(g, parts_c[0]) for g in got_b])
    gathered_a = gather(shard_a)
    gathered_b = gather(shard_b)
    shard_c = finish(
        "routec", parts_c, [after(g, gathered_b[1], gathered_a[1]) for g in got_c]
    )
    small = call(
        join_attn_kernel, "joina", [((small_rows, C), F32)] * 4, [], 8,
        after(gathered_a[0], shard_c), *gathered_a[1:], smem=0,
    )
    (whole2,) = call(
        join_kernel, "joinb", [((shard_rows, C), F32)], [], 8,
        after(gathered_b[0], shard_c), *gathered_b[1:], smem=0,
    )
    outputs, input_grad = call(
        unpack_kernel, "unpack",
        [(inputs.shape, BF16)] * 2, [], 8,
        kinds, out_own, grad_own, after(image_away, shard_c),
    )
    gathered_c = gather(shard_c, whole2, outputs, *small)
    whole1, *sums = call(
        join_kernel, "joinc", [((shard_rows, C), F32)] + [((1, small_rows), F32)] * 11, [], 8,
        *gathered_c, smem=0,
    )
    v = [row.reshape(small_rows) for row in sums]

    return (
        outputs, input_grad,
        v[9], v[10], whole1, v[8],
        v[6], v[7], whole2, v[5],
        v[0], v[1],
        small[0], v[2], small[1], small[2], v[3], small[3], v[4],
    )


def solution(mesh):
    image = P("batch", "height", None, None)
    vector = P("batch")
    matrix = P("batch", None)
    return jax.shard_map(
        on_device,
        mesh=mesh,
        in_specs=(image, vector) + (P(),) * 17 + (image,),
        out_specs=(
            image, image,
            vector, vector, matrix, vector,
            vector, vector, matrix, vector,
            vector, vector,
            matrix, vector, matrix, matrix, vector, matrix, vector,
        ),
        check_vma=False,
    )
```

```python
import functools

import jax
import jax.numpy as jnp
from jax import lax
from jax.experimental import pallas as pl
from jax.experimental.pallas import tpu as pltpu
from jax.sharding import PartitionSpec as P

GROUPS = 32
UNIT = 8
PIX = 512
PAD = 32
BLK = 128
F32 = jnp.float32
BF16 = jnp.bfloat16
epsilon = 1e-05

VM = pl.BlockSpec(memory_space=pltpu.VMEM)
SM = pl.BlockSpec(memory_space=pltpu.SMEM)
HB = pl.BlockSpec(memory_space=pltpu.HBM)
RATE = 1 << 30
LENGTH = {
    "pack": 10, "stack": 10, "first": 0.02, "second": 30, "third": 20, "fourth": 0.5, "weight2": 1, "weight1": 3, "routeb1": 20,
}


def place(bucket_ref):
    h = lax.axis_index("height")
    upper = lax.div(h, 2)
    tall_first = bucket_ref[0] == 1
    tall_image = jnp.where(tall_first, 0, 1)
    home = jnp.where(upper == 1, tall_image, 1 - tall_image)
    away = 1 - home

    def facts(image):
        kind = bucket_ref[image]
        tall = kind == 1
        stride = jnp.where(tall, 2 * UNIT, 4 * UNIT)
        width = jnp.where(kind == 0, 3 * UNIT, stride)
        return (image, tall, stride, width)

    return h, facts(home), facts(away)


def pixel_col(stride, lanes=1):
    rows = lax.broadcasted_iota(jnp.int32, (PIX, lanes), 0)
    return rows, rows & (stride - 1)


def pixel_mask(facts):
    unused, tall, stride, width = facts
    rows, cols = pixel_col(stride)
    limit = jnp.where(tall, 6 * UNIT * UNIT, 8 * UNIT * UNIT)
    mask = jnp.where((cols < width) & (rows < limit), 1.0, 0.0).astype(F32)
    size = jnp.where(tall | (width == 3 * UNIT), 6 * UNIT * UNIT, 8 * UNIT * UNIT)
    return mask, size.astype(F32)


def group_total(rows):
    members = rows.shape[1] // GROUPS
    lane = lax.broadcasted_iota(jnp.int32, (rows.shape[0], BLK), 1)
    tiles = []
    for tile in range(rows.shape[1] // BLK):
        part = rows[:, tile * BLK : (tile + 1) * BLK]
        step = 1
        while step < members:
            place_in_four = (lane // step) & 3
            added = part
            for d in (1, 2, 3):
                up = pltpu.roll(part, BLK - d * step, 1)
                down = pltpu.roll(part, (4 - d) * step, 1)
                added = added + jnp.where(place_in_four + d < 4, up, down)
            part = added
            step *= 4
        tiles.append(part)
    return jnp.concatenate(tiles, axis=1)


def total(values):
    return jnp.sum(values, axis=0, keepdims=True)


def wide_total(*rows):
    stacked = jnp.concatenate(list(rows) + [rows[0]] * (8 - len(rows)), axis=0)
    sums = group_total(stacked)
    return [sums[i : i + 1] for i in range(len(rows))]


def norm_stats(values, mask, group_size):
    mean = wide_total(total(values))[0] / group_size
    centered = (values - mean) * mask
    variance = wide_total(total(centered * centered))[0] / group_size
    return mean, lax.rsqrt(variance + epsilon)


def silu_norm(values, mean, inverse, gain, shift, mask):
    scale = 0.5 * inverse * gain
    half = values * scale + (0.5 * shift - mean * scale)
    return (half + half * jnp.tanh(half)) * mask


def norm_back(grad, normal, inverse, mask, group_size, gain):
    plain_row = total(grad)
    cross_row = total(grad * normal)
    plain, cross = [v / group_size for v in wide_total(plain_row * gain, cross_row * gain)]
    grad_in = grad * (inverse * gain) - mask * (plain * inverse + normal * (cross * inverse))
    return grad_in, cross_row, plain_row


def silu_slope(u):
    half = 0.5 * u
    t = jnp.tanh(half)
    return (0.5 + 0.5 * t) * (1.0 + half * (1.0 - t))


def mm(a, b):
    return jnp.dot(a, b, preferred_element_type=F32)


def mm_nt(a, b):
    return lax.dot_general(a, b, (((1,), (1,)), ((), ())), preferred_element_type=F32)


def mm_tn(a, b):
    return lax.dot_general(a, b, (((0,), (0,)), ((), ())), preferred_element_type=F32)


def fill_shifts(shift_ref, values, stride):
    unused, cols = pixel_col(stride)
    lanes = values.shape[1]
    zeros = jnp.zeros((PAD, lanes), BF16)
    for q in range(3):
        shift_ref[q, 0:PAD, :] = zeros
        shift_ref[q, PAD + PIX : 2 * PAD + PIX, :] = zeros
    left = jnp.where(cols == 0, 0.0, pltpu.roll(values, 1, 0))
    right = jnp.where(cols == stride - 1, 0.0, pltpu.roll(values, PIX - 1, 0))
    shift_ref[0, PAD : PAD + PIX, :] = left.astype(BF16)
    shift_ref[1, PAD : PAD + PIX, :] = values.astype(BF16)
    shift_ref[2, PAD : PAD + PIX, :] = right.astype(BF16)


def tap(shift_ref, p, q, stride, first=0, count=PIX):
    start = pl.multiple_of(PAD + first + (p - 1) * stride, 16)
    return shift_ref[q, pl.ds(start, count), :]


def conv_forward(shift_ref, weight_ref, stride, out_ref, tile=256):
    for first in range(0, PIX, tile):
        stacked = jnp.concatenate(
            [tap(shift_ref, p, q, stride, first, tile) for p in range(3) for q in range(3)], axis=1
        )
        out_ref[first : first + tile, :] = mm(stacked, weight_ref[...])


def conv_backward(shift_ref, weight_ref, stride, out_ref, tile=256):
    channels = weight_ref.shape[1]
    for first in range(0, PIX, tile):
        acc = None
        for p in range(3):
            for q in range(3):
                row = (8 - (3 * p + q)) * channels
                part = mm_nt(
                    tap(shift_ref, p, q, stride, first, tile), weight_ref[row : row + channels, :]
                )
                acc = part if acc is None else acc + part
        out_ref[first : first + tile, :] = acc


def assemble(out_ref, facts, h, pieces):
    unused, tall, stride, width = facts
    own, partner, received, partner_received = pieces
    other = h ^ 1

    @pl.when(tall)
    def _():
        for ref, index in (
            (own, h),
            (partner, other),
            (received, h ^ 2),
            (partner_received, other ^ 2),
        ):
            out_ref[pl.ds(pl.multiple_of(96 * index, 16), 96), :] = ref[0:96, :]
        out_ref[384:512, :] = jnp.zeros((128, out_ref.shape[1]), out_ref.dtype)

    @pl.when(jnp.logical_not(tall))
    def _():
        low = h & 1
        out_ref[pl.ds(pl.multiple_of(192 * low, 16), 192), :] = own[...]
        out_ref[pl.ds(pl.multiple_of(192 * (1 - low), 16), 192), :] = partner[...]

        @pl.when(low == 0)
        def _():
            out_ref[384:512, :] = received[0:128, :]

        @pl.when(low == 1)
        def _():
            out_ref[384:512, :] = partner_received[0:128, :]


def split_out(full_ref, facts, h, own_ref, send_ref):
    unused, tall, stride, width = facts
    send_h = h ^ 2

    @pl.when(tall)
    def _():
        own_ref[0:96, :] = full_ref[pl.ds(pl.multiple_of(96 * h, 16), 96), :]
        own_ref[96:192, :] = jnp.zeros((96, own_ref.shape[1]), own_ref.dtype)
        send_ref[0:96, :] = full_ref[pl.ds(pl.multiple_of(96 * send_h, 16), 96), :]
        send_ref[96:128, :] = jnp.zeros((32, own_ref.shape[1]), own_ref.dtype)

    @pl.when(jnp.logical_not(tall))
    def _():
        own_ref[...] = full_ref[pl.ds(pl.multiple_of(192 * (h & 1), 16), 192), :]
        send_ref[...] = full_ref[384:512, :]


GAIN1, SHIFT1, BIAS1, GAIN2, SHIFT2, BIAS2, GAIN3, SHIFT3, QB, VB, PB = range(11)
VECS = 16


def vec(vec_ref, index):
    return vec_ref[index : index + 1, :]


def pack(src, facts, dst, wide_rows):
    image, tall, stride, width = facts

    @pl.when(tall)
    def _():
        for row in range(6):
            dst[16 * row : 16 * row + 16, :] = src[image, row, 0:16, :]
        dst[96 : dst.shape[0], :] = jnp.zeros((dst.shape[0] - 96, dst.shape[1]), dst.dtype)

    @pl.when(jnp.logical_not(tall))
    def _():
        for row in range(wide_rows):
            dst[32 * row : 32 * row + 32, :] = src[image, row]


def pack_kernel(bucket_hbm, x_hbm, kinds, away_x, home_x, bucket_ref, x_ref, sems):
    copies = (
        pltpu.make_async_copy(bucket_hbm, bucket_ref, sems.at[0]),
        pltpu.make_async_copy(x_hbm, x_ref, sems.at[1]),
    )
    for copy in copies:
        copy.start()
    for copy in copies:
        copy.wait()
    h, home, away = place(bucket_ref)
    kinds[0] = bucket_ref[0]
    kinds[1] = bucket_ref[1]
    pack(x_ref, away, away_x, 4)
    pack(x_ref, home, home_x, 6)


def stack_kernel(kinds, cot_ref, *refs):
    h, home, away = place(kinds)
    out_ref, away_c, home_c = refs[-3:]
    count = len(refs) - 3
    for index, ref in enumerate(refs[:count]):
        out_ref[index : index + 1, :] = ref[...]
    out_ref[count:, :] = jnp.zeros((VECS - count, out_ref.shape[1]), F32)
    pack(cot_ref, away, away_c, 4)
    pack(cot_ref, home, home_c, 6)


def first_kernel(
    bucket_ref, own, partner, received, partner_received, vecs, weight1,
    image_ref, conv_ref, act2_ref, stats_ref, act1_t, act2_t, send_t,
    shift_ref,
):
    h, home, away = place(bucket_ref)
    stride = home[2]
    mask, pixels = pixel_mask(home)
    channels = vecs.shape[1]
    group_size = pixels * (channels // GROUPS)
    assemble(image_ref, home, h, (own, partner, received, partner_received))
    values = image_ref[...].astype(F32) * mask
    mean1, inverse1 = norm_stats(values, mask, group_size)
    act = silu_norm(values, mean1, inverse1, vec(vecs, GAIN1), vec(vecs, SHIFT1), mask)
    fill_shifts(shift_ref, act, stride)
    act1_t[...] = act.astype(BF16).T
    conv_forward(shift_ref, weight1, stride, conv_ref)
    values = (conv_ref[...] + vec(vecs, BIAS1)) * mask
    conv_ref[...] = values
    mean2, inverse2 = norm_stats(values, mask, group_size)
    act = silu_norm(values, mean2, inverse2, vec(vecs, GAIN2), vec(vecs, SHIFT2), mask)
    act = act.astype(BF16)
    act2_ref[...] = act
    act2_t[...] = act.T
    half = pl.multiple_of((h & 1) * (channels // 2), 16)
    send_t[0] = act1_t[pl.ds(half, channels // 2), :]
    send_t[1] = act2_t[pl.ds(half, channels // 2), :]
    stats_ref[0:1, :] = mean1
    stats_ref[1:2, :] = inverse1
    stats_ref[2:3, :] = mean2
    stats_ref[3:4, :] = inverse2
    stats_ref[4:8, :] = jnp.zeros((4, channels), F32)


def second_kernel(
    bucket_ref, image_ref, act2_ref, own, partner, received, partner_received, vecs,
    weight2, wq, wk, wv, wp,
    middle_ref, mixed_ref, grad2_ref, grad_middle_ref, attn_keep, attn_send, vec_ref,
    block_keep, block_send,
    shift_ref, full_ref, grads_ref, sum_ref,
):
    h, home, away = place(bucket_ref)
    stride = home[2]
    mask, pixels = pixel_mask(home)
    channels = vecs.shape[1]
    group_size = pixels * (channels // GROUPS)
    scaling = channels ** (-0.5)
    assemble(full_ref, home, h, (own, partner, received, partner_received))
    fill_shifts(shift_ref, act2_ref[...].astype(F32), stride)
    conv_forward(shift_ref, weight2, stride, middle_ref)
    middle = mask * (image_ref[...].astype(F32) + (middle_ref[...] + vec(vecs, BIAS2)))
    middle_ref[...] = middle
    mean3, inverse3 = norm_stats(middle, mask, group_size)
    normal = (middle - mean3) * inverse3
    normed = (normal * vec(vecs, GAIN3) + vec(vecs, SHIFT3)).astype(BF16)
    wide = jnp.concatenate([wq[...], wk[...], wv[...]], axis=1)
    joint = mm(normed, wide)
    queries = (joint[:, 0:channels] + vec(vecs, QB)).astype(BF16)
    keys = joint[:, channels : 2 * channels].astype(BF16)
    values = (joint[:, 2 * channels :] + vec(vecs, VB)).astype(BF16)
    lanes = lax.broadcasted_iota(jnp.int32, (1, PIX), 1)
    key_cols = lanes & (stride - 1)
    key_valid = (key_cols < home[3]) & (lanes < jnp.where(home[1], 384, 512))
    scores = jnp.where(key_valid, mm_nt(queries, keys) * scaling, -1000000000.0)
    grad_top = full_ref[...].astype(F32) * mask
    grad_rows = grad_top.astype(BF16)
    grad_mixed = mm_nt(grad_rows, wp[...]).astype(BF16)
    grad_soft = mm_nt(grad_mixed, values)
    raised = jnp.exp(scores - jnp.max(scores, axis=1, keepdims=True))
    soft = raised * (1.0 / jnp.sum(raised, axis=1, keepdims=True))
    soft16 = soft.astype(BF16)
    mixed = mm(soft16, values).astype(BF16)
    mixed_ref[...] = mixed

    grad_values = mm_tn(soft16, grad_mixed).astype(BF16)
    grad_scores = soft * (grad_soft - jnp.sum(soft * grad_soft, axis=1, keepdims=True))
    grad_scores = grad_scores.astype(BF16)
    grad_queries = (mm(grad_scores, keys) * scaling).astype(BF16)
    grad_keys = (mm_tn(grad_scores, queries) * scaling).astype(BF16)
    grads_ref[:, 0:channels] = grad_queries
    grads_ref[:, channels : 2 * channels] = grad_keys
    grads_ref[:, 2 * channels : 3 * channels] = grad_values
    grads_ref[:, 3 * channels : 4 * channels] = grad_rows
    grad_normed = mm_nt(grads_ref[:, 0 : 3 * channels], wide)
    grad_in, gain_grad, shift_grad = norm_back(
        grad_normed, normal, inverse3, mask, group_size, vec(vecs, GAIN3)
    )
    grad_middle = mask * (grad_top + grad_in)
    grad_middle_ref[...] = grad_middle
    grad2 = grad_middle.astype(BF16)
    grad2_ref[...] = grad2
    vec_ref[0:1, :] = gain_grad
    vec_ref[1:2, :] = shift_grad
    vec_ref[2:3, :] = total(grad_queries.astype(F32))
    vec_ref[3:4, :] = total(grad_values.astype(F32))
    vec_ref[4:5, :] = total(grad_top)
    vec_ref[5:6, :] = total(grad2.astype(F32))
    vec_ref[6:8, :] = jnp.zeros((2, channels), F32)

    keep_at = pl.multiple_of(BLK * h, BLK)
    send_at = pl.multiple_of(BLK * (h ^ 2), BLK)
    block_keep[...] = grad2_ref[:, pl.ds(keep_at, BLK)]
    block_send[...] = grad2_ref[:, pl.ds(send_at, BLK)]

    def blocks(index):
        start = index * channels
        return [
            grads_ref[:, pl.ds(pl.multiple_of(start + BLK * h, BLK), BLK)],
            grads_ref[:, pl.ds(pl.multiple_of(start + BLK * (h ^ 2), BLK), BLK)],
        ]

    sum_ref[:, 0 : 6 * BLK] = mm_tn(normed, jnp.concatenate(blocks(0) + blocks(1) + blocks(2), axis=1))
    sum_ref[:, 6 * BLK : 8 * BLK] = mm_tn(mixed, jnp.concatenate(blocks(3), axis=1))
    mine = lax.axis_index("batch") & 1
    pairs = attn_keep.shape[0]
    rows = channels // (2 * pairs)
    for pair in range(pairs):
        for dst, which in ((attn_keep, mine), (attn_send, 1 - mine)):
            part = sum_ref[pl.ds(pl.multiple_of((2 * pair + which) * rows, 8), rows), :].astype(BF16)
            for index in range(4):
                at = index * 2 * BLK
                dst[pair, index * rows : (index + 1) * rows, :] = part[:, at : at + 2 * BLK]


def third_kernel(
    bucket_ref, grad2_ref, conv_ref, stats_ref, vecs, weight2,
    grad1_ref, block_keep, block_send, vec_ref,
    shift_ref, acc_ref,
):
    h, home, away = place(bucket_ref)
    stride = home[2]
    mask, pixels = pixel_mask(home)
    channels = vecs.shape[1]
    group_size = pixels * (channels // GROUPS)
    fill_shifts(shift_ref, grad2_ref[...].astype(F32), stride)
    conv_backward(shift_ref, weight2, stride, acc_ref)
    inverse = stats_ref[3:4, :]
    normal = (conv_ref[...] - stats_ref[2:3, :]) * inverse
    u = normal * vec(vecs, GAIN2) + vec(vecs, SHIFT2)
    grad = mask * acc_ref[...] * silu_slope(u)
    grad_in, gain_grad, shift_grad = norm_back(
        grad, normal, inverse, mask, group_size, vec(vecs, GAIN2)
    )
    grad1 = grad_in.astype(BF16)
    grad1_ref[...] = grad1
    vec_ref[0:1, :] = gain_grad
    vec_ref[1:2, :] = shift_grad
    vec_ref[2:3, :] = total(grad1.astype(F32))
    vec_ref[3:8, :] = jnp.zeros((5, channels), F32)
    block_keep[...] = grad1_ref[:, pl.ds(pl.multiple_of(BLK * h, BLK), BLK)]
    block_send[...] = grad1_ref[:, pl.ds(pl.multiple_of(BLK * (h ^ 2), BLK), BLK)]


def fourth_kernel(
    bucket_ref, grad1_ref, image_ref, stats_ref, grad_middle_ref, vecs, weight1, vec_a, vec_b,
    grad_own, send_ref, vec_keep, vec_send,
    shift_ref, acc_ref, full_ref, vec_ref,
):
    h, home, away = place(bucket_ref)
    stride = home[2]
    mask, pixels = pixel_mask(home)
    channels = vecs.shape[1]
    group_size = pixels * (channels // GROUPS)
    fill_shifts(shift_ref, grad1_ref[...].astype(F32), stride)
    conv_backward(shift_ref, weight1, stride, acc_ref)
    inverse = stats_ref[1:2, :]
    normal = (image_ref[...].astype(F32) * mask - stats_ref[0:1, :]) * inverse
    u = normal * vec(vecs, GAIN1) + vec(vecs, SHIFT1)
    grad = mask * acc_ref[...] * silu_slope(u)
    grad_in, gain_grad, shift_grad = norm_back(
        grad, normal, inverse, mask, group_size, vec(vecs, GAIN1)
    )
    full_ref[...] = (mask * (grad_middle_ref[...] + grad_in)).astype(BF16)
    split_out(full_ref, home, h, grad_own, send_ref)
    vec_ref[0:6, :] = vec_a[0:6, :]
    vec_ref[6:9, :] = vec_b[0:3, :]
    vec_ref[9:10, :] = gain_grad
    vec_ref[10:11, :] = shift_grad
    vec_ref[11:VECS, :] = jnp.zeros((VECS - 11, channels), F32)
    pairs = vec_keep.shape[0]
    rows = channels // (2 * pairs)
    mine = (lax.axis_index("batch") & 1) == 1
    for pair in range(pairs):
        parts = []
        for shard in (2 * pair, 2 * pair + 1):
            start = shard * rows
            tile = start // BLK * BLK
            part = vec_ref[:, tile : tile + BLK]
            parts.append(part if start == tile else pltpu.roll(part, BLK - (start - tile), 1))
        vec_keep[pair] = jnp.where(mine, parts[1], parts[0]).astype(BF16)
        vec_send[pair] = jnp.where(mine, parts[0], parts[1]).astype(BF16)


def output_kernel(
    bucket_ref, middle_ref, mixed_ref, vecs, wp, grad_send, out_own, send_ref, full_ref
):
    h, home, away = place(bucket_ref)
    mask, pixels = pixel_mask(home)
    projected = mm(mixed_ref[...], wp[...]) + vec(vecs, PB)
    full_ref[...] = (mask * (middle_ref[...] + projected)).astype(BF16)
    split_out(full_ref, home, h, out_own, send_ref.at[0])
    send_ref[1] = grad_send[...]


def weight_kernel(
    bucket_ref, act_t, half_t, partner_half_t, block_own, block_away,
    keep_ref, send_ref, left_ref, right_ref, shift_ref, sum_ref, *, layer,
):
    h, home, away = place(bucket_ref)
    channels = act_t.shape[0]
    half = channels // 2
    left_ref[:, 0:PIX] = act_t[...]
    left_ref[pl.ds(pl.multiple_of((h & 1) * half, 16), half), PIX : 2 * PIX] = half_t[layer]
    left_ref[pl.ds(pl.multiple_of((1 - (h & 1)) * half, 16), half), PIX : 2 * PIX] = (
        partner_half_t[layer]
    )
    for index, (facts, block) in enumerate(((home, block_own), (away, block_away))):
        stride = facts[2]
        fill_shifts(shift_ref, block[...].astype(F32), stride)
        for p in range(3):
            for q in range(3):
                column = (3 * p + q) * BLK
                right_ref[index * PIX : (index + 1) * PIX, column : column + BLK] = tap(
                    shift_ref, 2 - p, 2 - q, stride
                )
    joint = mm(left_ref[...], right_ref[...])
    for t in range(9):
        sum_ref[t * channels : (t + 1) * channels, :] = joint[:, t * BLK : (t + 1) * BLK]
    mine = lax.axis_index("batch") & 1
    pairs = keep_ref.shape[0]
    rows = 9 * channels // (2 * pairs)
    for pair in range(pairs):
        for dst, which in ((keep_ref, mine), (send_ref, 1 - mine)):
            shard = 2 * pair + which
            dst[pair] = sum_ref[pl.ds(pl.multiple_of(shard * rows, 8), rows), :].astype(BF16)


def route_kernel(keep_ref, got_ref, *outs, bit, first):
    ways = len(outs) if first == 0 else len(outs) // 2
    group = (lax.axis_index("batch") >> bit) & (ways - 1)
    rows = keep_ref.shape[1]
    for step, dst in enumerate(outs[-ways:]):
        which = group ^ step
        for index in range(dst.shape[0]):
            at = index * ways + which
            dst[index, first : first + rows, :] = (
                keep_ref[at].astype(F32) + got_ref[at].astype(F32)
            ).astype(BF16)


def total_of(refs):
    added = refs[0].astype(F32)
    for ref in refs[1:]:
        added = added + ref.astype(F32)
    return added


def sum_kernel(*refs):
    refs[-1][...] = total_of([ref[0] for ref in refs[:-1]]).astype(BF16)


def join_kernel(own_ref, far_ref, near_ref, diagonal_ref, *out_refs):
    h = lax.axis_index("height")
    first = 0
    for dst in [ref for ref in out_refs if ref.shape[0] > 1]:
        rows = dst.shape[0]
        for ref, index in ((own_ref, h), (far_ref, h ^ 2), (near_ref, h ^ 1), (diagonal_ref, h ^ 3)):
            dst[:, pl.ds(pl.multiple_of(BLK * index, BLK), BLK)] = ref[first : first + rows, :].astype(F32)
        first += rows
    if own_ref.shape[0] > first:
        own, far = own_ref[first:, :].astype(F32), far_ref[first:, :].astype(F32)
        near, diagonal = near_ref[first:, :].astype(F32), diagonal_ref[first:, :].astype(F32)
        sums = 0.5 * ((own + near) + (far + diagonal))
        for index, dst in enumerate([ref for ref in out_refs if ref.shape[0] == 1]):
            dst[...] = sums[index : index + 1, 0 : dst.shape[1]]


def join_attn_kernel(own_ref, far_ref, near_ref, diagonal_ref, *out_refs):
    h = lax.axis_index("height")
    rows = out_refs[0].shape[0]
    for first, second, index in ((own_ref, far_ref, h), (near_ref, diagonal_ref, h ^ 1)):
        for position in range(2):
            lane, other = position * BLK, (1 - position) * BLK
            column = pl.multiple_of(BLK * (index ^ (2 * position)), BLK)
            for number, dst in enumerate(out_refs):
                at = number * rows
                dst[:, pl.ds(column, BLK)] = first[at : at + rows, lane : lane + BLK].astype(
                    F32
                ) + second[at : at + rows, other : other + BLK].astype(F32)


def unpack_kernel(bucket_ref, out_own, grad_own, away_ref, out_ref, grad_ref):
    h, home, away = place(bucket_ref)
    for own, received, dst in (
        (out_own, away_ref.at[0], out_ref),
        (grad_own, away_ref.at[1], grad_ref),
    ):
        channels = dst.shape[3]
        for facts, src, wide_rows in ((away, received, 4), (home, own, 6)):
            image, tall, stride, width = facts

            @pl.when(tall)
            def _():
                for row in range(6):
                    dst[image, row, 0:16, :] = src[16 * row : 16 * row + 16, :]
                    dst[image, row, 16:32, :] = jnp.zeros((16, channels), dst.dtype)

            @pl.when(jnp.logical_not(tall))
            def _():
                for row in range(wide_rows):
                    dst[image, row] = src[32 * row : 32 * row + 32, :]
                for row in range(wide_rows, 6):
                    dst[image, row] = jnp.zeros((32, channels), dst.dtype)

            if wide_rows == 4:

                @pl.when(jnp.logical_not(tall) & (h == 3))
                def _():
                    for row in range(6):
                        dst[image, row] = jnp.zeros((32, channels), dst.dtype)


def call(kernel, name, outs, scratch, vmem, *operands, smem=1, any_from=99, aliases={}):
    specs = [SM] * smem + [VM] * (len(operands) - smem)
    specs = [HB if i >= any_from else spec for i, spec in enumerate(specs)]
    return pl.pallas_call(
        kernel,
        name=name,
        out_shape=[jax.ShapeDtypeStruct(shape, dtype) for shape, dtype in outs],
        in_specs=specs,
        out_specs=[SM if dtype == jnp.int32 else VM for shape, dtype in outs],
        scratch_shapes=[
            pltpu.SemaphoreType.DMA(shape)
            if dtype is None
            else (pltpu.SMEM if dtype == jnp.int32 else pltpu.VMEM)(shape, dtype)
            for shape, dtype in scratch
        ],
        input_output_aliases=aliases,
        compiler_params=pltpu.CompilerParams(vmem_limit_bytes=vmem << 20),
        cost_estimate=pl.CostEstimate(
            flops=int(LENGTH.get(name, 0.02) * RATE), bytes_accessed=1024, transcendentals=0
        ),
    )(*operands)


def on_device(
    inputs,
    bucket,
    norm1_gain,
    norm1_shift,
    conv1_weight,
    conv1_bias,
    norm2_gain,
    norm2_shift,
    conv2_weight,
    conv2_bias,
    norm3_gain,
    norm3_shift,
    query_weight,
    query_bias,
    key_weight,
    value_weight,
    value_bias,
    proj_weight,
    proj_bias,
    cotangent,
):
    C = inputs.shape[-1]
    batches = lax.axis_size("batch")
    bits = batches.bit_length() - 1
    shard_rows = 9 * C // batches
    small_rows = C // batches

    def row(v):
        return v.reshape(1, C)

    def to_core(v):
        return lax.ppermute(v, "height", [(i, i ^ 1) for i in range(4)])

    def to_chip(v):
        return lax.ppermute(v, "height", [(i, i ^ 2) for i in range(4)])

    def to_batch(v, change):
        return lax.ppermute(v, "batch", [(i, i ^ change) for i in range(batches)])

    def after(v, *others):
        return lax.optimization_barrier((v,) + others)[0]

    def together(got, *others):
        return list(lax.optimization_barrier((*got, *others))[: len(got)])

    img16 = ((PIX, C), BF16)
    img32 = ((PIX, C), F32)
    rows8 = ((8, C), F32)
    block = ((PIX, BLK), BF16)
    turned = ((C, PIX), BF16)
    shifts = ((3, PIX + 2 * PAD, C), BF16)

    kinds, away_x, home_x = call(
        pack_kernel, "pack",
        [((2,), jnp.int32), ((128, C), BF16), ((192, C), BF16)],
        [((2,), jnp.int32), (inputs.shape, BF16), ((2,), None)], 54, bucket, inputs,
        smem=0, any_from=0,
    )
    vectors = (
        norm1_gain, norm1_shift, conv1_bias, norm2_gain, norm2_shift, conv2_bias,
        norm3_gain, norm3_shift, query_bias, value_bias, proj_bias,
    )
    recv_x = to_chip(away_x)
    core_x = to_core(home_x)
    vecs, away_c, home_c = call(
        stack_kernel, "stack", [((VECS, C), F32), ((160, C), BF16), ((192, C), BF16)], [], 8,
        kinds, cotangent, *[row(v) for v in vectors],
    )
    recv_c = to_chip(away_c)
    core_c = to_core(home_c)
    core_recv_c = lax.ppermute(away_c, "height", [(i, i ^ 3) for i in range(4)])
    core_recv_x = to_core(after(recv_x, vecs))

    image, conv, act2, stats, act1_t, act2_t, send_t = call(
        first_kernel, "first",
        [img16, img32, img16, rows8, turned, turned, ((2, C // 2, PIX), BF16)],
        [shifts], 14,
        kinds, home_x, core_x, recv_x, core_recv_x, vecs, conv1_weight,
    )
    half_t = to_chip(send_t)
    core_half_t = to_core(half_t)

    attn_out = ((batches // 2, 4 * small_rows, 2 * BLK), BF16)
    middle, mixed, grad2, grad_middle, attn_keep, attn_send, vec_a, block2, block2_send = call(
        second_kernel, "second",
        [img32, img16, img16, img32, attn_out, attn_out, rows8, block, block],
        [shifts, img16, ((PIX, 4 * C), BF16), ((C, 8 * BLK), F32)], 24,
        kinds, image, act2, home_c, core_c, recv_c, core_recv_c, vecs,
        conv2_weight, query_weight, key_weight, value_weight, proj_weight,
    )
    block2_away = to_chip(block2_send)
    attn_got = to_batch(attn_send, 1)

    grad1, block1, block1_send, vec_b = call(
        third_kernel, "third",
        [img16, block, block, rows8],
        [shifts, img32], 14,
        kinds, grad2, conv, stats, vecs, conv2_weight,
    )
    block1_away = to_chip(block1_send)

    def weight_grad(name, act_t, index, own, away):
        return call(
            functools.partial(weight_kernel, layer=index), name,
            [((batches // 2, shard_rows, BLK), BF16)] * 2,
            [((C, 2 * PIX), BF16), ((2 * PIX, 9 * BLK), BF16), ((3, PIX + 2 * PAD, BLK), BF16),
             ((9 * C, BLK), F32)],
            18, kinds, act_t, half_t, core_half_t, own, away,
        )

    keep2, send2 = weight_grad("weight2", act2_t, 1, after(block2, block1), block2_away)
    got2 = to_batch(send2, 1)

    def spread(name, bit, keep, got, tail=None, behind=()):
        ways = 1 << min(2, bits - bit)
        rows = keep.shape[1]
        shape = (keep.shape[0] // ways, rows + (VECS if tail else 0), keep.shape[2])
        parts = call(
            functools.partial(route_kernel, bit=bit, first=0), name + str(bit),
            [(shape, BF16)] * ways, [], 16, keep, got, smem=0,
        )
        if tail:
            parts = call(
                functools.partial(route_kernel, bit=bit, first=rows), name + "tail",
                [(shape, BF16)] * ways, [], 16, *tail, *parts, smem=0,
                aliases={2 + j: j for j in range(ways)},
            )
        return parts, [to_batch(after(parts[j], *behind), j << bit) for j in range(1, ways)]

    def finish(name, parts, got):
        for bit in range(3, bits, 2):
            added = total_of([parts[0]] + got).astype(BF16)
            parts, got = spread(name, bit, added, jnp.zeros_like(added))
        return call(
            sum_kernel, "sum" + name, [(parts[0].shape[1:], BF16)], [], 8, parts[0], *got, smem=0
        )[0]

    def gather(shard, *between):
        far = to_chip(shard)
        near = to_core(shard)
        return shard, far, near, to_core(after(far, *between))

    parts_a, got_a = spread("routea", 1, after(attn_keep, send2), attn_got)
    keep1, send1 = weight_grad("weight1", act1_t, 0, after(block1, *parts_a), block1_away)
    got1 = to_batch(send1, 1)
    shard_a = finish("routea", parts_a, together(got_a, send1))
    grad_own, grad_send, vec_keep, vec_send = call(
        fourth_kernel, "fourth",
        [((192, C), BF16), ((128, C), BF16),
         ((batches // 2, VECS, BLK), BF16), ((batches // 2, VECS, BLK), BF16)],
        [shifts, img32, img16, ((VECS, C), F32)], 14,
        kinds, after(grad1, send1), image, stats, grad_middle, vecs, conv1_weight, vec_a, vec_b,
    )
    vec_got = to_batch(vec_send, 1)
    parts_b, got_b = spread("routeb", 1, after(keep2, vec_keep, shard_a), got2)
    out_own, image_send = call(
        output_kernel, "output", [((192, C), BF16), ((2, 128, C), BF16)], [img16], 10,
        kinds, after(middle, *parts_b), mixed, vecs, proj_weight, grad_send,
    )
    image_away = to_chip(image_send)
    parts_c, got_c = spread("routec", 1, keep1, got1, (vec_keep, vec_got), behind=got_b)
    shard_b = finish("routeb", parts_b, together(got_b, parts_c[0]))
    gathered_a = gather(shard_a)
    gathered_b = gather(shard_b)
    shard_c = finish(
        "routec", parts_c, together(got_c[::-1], gathered_b[1], gathered_a[1])
    )
    small = call(
        join_attn_kernel, "joina", [((small_rows, C), F32)] * 4, [], 8,
        after(gathered_a[0], shard_c), *gathered_a[1:], smem=0,
    )
    (whole2,) = call(
        join_kernel, "joinb", [((shard_rows, C), F32)], [], 8,
        after(gathered_b[0], shard_c), *gathered_b[1:], smem=0,
    )
    outputs, input_grad = call(
        unpack_kernel, "unpack",
        [(inputs.shape, BF16)] * 2, [], 8,
        kinds, out_own, grad_own, after(image_away, shard_c),
    )
    gathered_c = gather(shard_c, whole2, outputs, *small)
    whole1, *sums = call(
        join_kernel, "joinc", [((shard_rows, C), F32)] + [((1, small_rows), F32)] * 11, [], 8,
        *gathered_c, smem=0,
    )
    v = [row.reshape(small_rows) for row in sums]

    return (
        outputs, input_grad,
        v[9], v[10], whole1, v[8],
        v[6], v[7], whole2, v[5],
        v[0], v[1],
        small[0], v[2], small[1], small[2], v[3], small[3], v[4],
    )


def solution(mesh):
    image = P("batch", "height", None, None)
    vector = P("batch")
    matrix = P("batch", None)
    return jax.shard_map(
        on_device,
        mesh=mesh,
        in_specs=(image, vector) + (P(),) * 17 + (image,),
        out_specs=(
            image, image,
            vector, vector, matrix, vector,
            vector, vector, matrix, vector,
            vector, vector,
            matrix, vector, matrix, matrix, vector, matrix, vector,
        ),
        check_vma=False,
    )
```

```python
import functools

import jax
import jax.numpy as jnp
from jax import lax
from jax.experimental import pallas as pl
from jax.experimental.pallas import tpu as pltpu
from jax.sharding import PartitionSpec as P

GROUPS = 32
UNIT = 8
PIX = 512
PAD = 32
BLK = 128
F32 = jnp.float32
BF16 = jnp.bfloat16
epsilon = 1e-05

VM = pl.BlockSpec(memory_space=pltpu.VMEM)
SM = pl.BlockSpec(memory_space=pltpu.SMEM)
HB = pl.BlockSpec(memory_space=pltpu.HBM)
RATE = 1 << 30
LENGTH = {
    "pack": 10, "stack": 10, "first": 0.02, "second": 30, "third": 20, "fourth": 0.5, "weight2": 1, "weight1": 3, "routeb1": 20,
}


def place(bucket_ref):
    h = lax.axis_index("height")
    upper = lax.div(h, 2)
    tall_first = bucket_ref[0] == 1
    tall_image = jnp.where(tall_first, 0, 1)
    home = jnp.where(upper == 1, tall_image, 1 - tall_image)
    away = 1 - home

    def facts(image):
        kind = bucket_ref[image]
        tall = kind == 1
        stride = jnp.where(tall, 2 * UNIT, 4 * UNIT)
        width = jnp.where(kind == 0, 3 * UNIT, stride)
        return (image, tall, stride, width)

    return h, facts(home), facts(away)


def pixel_col(stride, lanes=1):
    rows = lax.broadcasted_iota(jnp.int32, (PIX, lanes), 0)
    return rows, rows & (stride - 1)


def pixel_mask(facts):
    unused, tall, stride, width = facts
    rows, cols = pixel_col(stride)
    limit = jnp.where(tall, 6 * UNIT * UNIT, 8 * UNIT * UNIT)
    mask = jnp.where((cols < width) & (rows < limit), 1.0, 0.0).astype(F32)
    size = jnp.where(tall | (width == 3 * UNIT), 6 * UNIT * UNIT, 8 * UNIT * UNIT)
    return mask, size.astype(F32)


def group_total(rows):
    members = rows.shape[1] // GROUPS
    lane = lax.broadcasted_iota(jnp.int32, (rows.shape[0], BLK), 1)
    tiles = []
    for tile in range(rows.shape[1] // BLK):
        part = rows[:, tile * BLK : (tile + 1) * BLK]
        step = 1
        while step < members:
            place_in_four = (lane // step) & 3
            added = part
            for d in (1, 2, 3):
                up = pltpu.roll(part, BLK - d * step, 1)
                down = pltpu.roll(part, (4 - d) * step, 1)
                added = added + jnp.where(place_in_four + d < 4, up, down)
            part = added
            step *= 4
        tiles.append(part)
    return jnp.concatenate(tiles, axis=1)


def total(values):
    return jnp.sum(values, axis=0, keepdims=True)


def wide_total(*rows):
    stacked = jnp.concatenate(list(rows) + [rows[0]] * (8 - len(rows)), axis=0)
    sums = group_total(stacked)
    return [sums[i : i + 1] for i in range(len(rows))]


def norm_stats(values, mask, group_size):
    mean = wide_total(total(values))[0] / group_size
    centered = (values - mean) * mask
    variance = wide_total(total(centered * centered))[0] / group_size
    return mean, lax.rsqrt(variance + epsilon)


def silu_norm(values, mean, inverse, gain, shift, mask):
    scale = 0.5 * inverse * gain
    half = values * scale + (0.5 * shift - mean * scale)
    return (half + half * jnp.tanh(half)) * mask


def norm_back(grad, normal, inverse, mask, group_size, gain):
    plain_row = total(grad)
    cross_row = total(grad * normal)
    plain, cross = [v / group_size for v in wide_total(plain_row * gain, cross_row * gain)]
    grad_in = grad * (inverse * gain) - mask * (plain * inverse + normal * (cross * inverse))
    return grad_in, cross_row, plain_row


def silu_slope(u):
    half = 0.5 * u
    t = jnp.tanh(half)
    return (0.5 + 0.5 * t) * (1.0 + half * (1.0 - t))


def mm(a, b):
    return jnp.dot(a, b, preferred_element_type=F32)


def mm_nt(a, b):
    return lax.dot_general(a, b, (((1,), (1,)), ((), ())), preferred_element_type=F32)


def mm_tn(a, b):
    return lax.dot_general(a, b, (((0,), (0,)), ((), ())), preferred_element_type=F32)


def fill_shifts(shift_ref, values, stride):
    unused, cols = pixel_col(stride)
    lanes = values.shape[1]
    zeros = jnp.zeros((PAD, lanes), BF16)
    for q in range(3):
        shift_ref[q, 0:PAD, :] = zeros
        shift_ref[q, PAD + PIX : 2 * PAD + PIX, :] = zeros
    left = jnp.where(cols == 0, 0.0, pltpu.roll(values, 1, 0))
    right = jnp.where(cols == stride - 1, 0.0, pltpu.roll(values, PIX - 1, 0))
    shift_ref[0, PAD : PAD + PIX, :] = left.astype(BF16)
    shift_ref[1, PAD : PAD + PIX, :] = values.astype(BF16)
    shift_ref[2, PAD : PAD + PIX, :] = right.astype(BF16)


def tap(shift_ref, p, q, stride, first=0, count=PIX):
    start = pl.multiple_of(PAD + first + (p - 1) * stride, 16)
    return shift_ref[q, pl.ds(start, count), :]


def conv_forward(shift_ref, weight_ref, stride, out_ref, tile=256):
    for first in range(0, PIX, tile):
        stacked = jnp.concatenate(
            [tap(shift_ref, p, q, stride, first, tile) for p in range(3) for q in range(3)], axis=1
        )
        out_ref[first : first + tile, :] = mm(stacked, weight_ref[...])


def conv_backward(shift_ref, weight_ref, stride, out_ref, tile=256):
    channels = weight_ref.shape[1]
    for first in range(0, PIX, tile):
        acc = None
        for p in range(3):
            for q in range(3):
                row = (8 - (3 * p + q)) * channels
                part = mm_nt(
                    tap(shift_ref, p, q, stride, first, tile), weight_ref[row : row + channels, :]
                )
                acc = part if acc is None else acc + part
        out_ref[first : first + tile, :] = acc


def assemble(out_ref, facts, h, pieces):
    unused, tall, stride, width = facts
    own, partner, received, partner_received = pieces
    other = h ^ 1

    @pl.when(tall)
    def _():
        for ref, index in (
            (own, h),
            (partner, other),
            (received, h ^ 2),
            (partner_received, other ^ 2),
        ):
            out_ref[pl.ds(pl.multiple_of(96 * index, 16), 96), :] = ref[0:96, :]
        out_ref[384:512, :] = jnp.zeros((128, out_ref.shape[1]), out_ref.dtype)

    @pl.when(jnp.logical_not(tall))
    def _():
        low = h & 1
        out_ref[pl.ds(pl.multiple_of(192 * low, 16), 192), :] = own[...]
        out_ref[pl.ds(pl.multiple_of(192 * (1 - low), 16), 192), :] = partner[...]

        @pl.when(low == 0)
        def _():
            out_ref[384:512, :] = received[0:128, :]

        @pl.when(low == 1)
        def _():
            out_ref[384:512, :] = partner_received[0:128, :]


def split_out(full_ref, facts, h, own_ref, send_ref):
    unused, tall, stride, width = facts
    send_h = h ^ 2

    @pl.when(tall)
    def _():
        own_ref[0:96, :] = full_ref[pl.ds(pl.multiple_of(96 * h, 16), 96), :]
        own_ref[96:192, :] = jnp.zeros((96, own_ref.shape[1]), own_ref.dtype)
        send_ref[0:96, :] = full_ref[pl.ds(pl.multiple_of(96 * send_h, 16), 96), :]
        send_ref[96:128, :] = jnp.zeros((32, own_ref.shape[1]), own_ref.dtype)

    @pl.when(jnp.logical_not(tall))
    def _():
        own_ref[...] = full_ref[pl.ds(pl.multiple_of(192 * (h & 1), 16), 192), :]
        send_ref[...] = full_ref[384:512, :]


GAIN1, SHIFT1, BIAS1, GAIN2, SHIFT2, BIAS2, GAIN3, SHIFT3, QB, VB, PB = range(11)
VECS = 16


def vec(vec_ref, index):
    return vec_ref[index : index + 1, :]


def pack(src, facts, dst, wide_rows):
    image, tall, stride, width = facts

    @pl.when(tall)
    def _():
        for row in range(6):
            dst[16 * row : 16 * row + 16, :] = src[image, row, 0:16, :]
        dst[96 : dst.shape[0], :] = jnp.zeros((dst.shape[0] - 96, dst.shape[1]), dst.dtype)

    @pl.when(jnp.logical_not(tall))
    def _():
        for row in range(wide_rows):
            dst[32 * row : 32 * row + 32, :] = src[image, row]


def pack_kernel(bucket_hbm, x_hbm, kinds, away_x, home_x, bucket_ref, x_ref, sems):
    copies = (
        pltpu.make_async_copy(bucket_hbm, bucket_ref, sems.at[0]),
        pltpu.make_async_copy(x_hbm, x_ref, sems.at[1]),
    )
    for copy in copies:
        copy.start()
    for copy in copies:
        copy.wait()
    h, home, away = place(bucket_ref)
    kinds[0] = bucket_ref[0]
    kinds[1] = bucket_ref[1]
    pack(x_ref, away, away_x, 4)
    pack(x_ref, home, home_x, 6)


def stack_kernel(kinds, cot_ref, *refs):
    h, home, away = place(kinds)
    out_ref, away_c, home_c = refs[-3:]
    count = len(refs) - 3
    for index, ref in enumerate(refs[:count]):
        out_ref[index : index + 1, :] = ref[...]
    out_ref[count:, :] = jnp.zeros((VECS - count, out_ref.shape[1]), F32)
    pack(cot_ref, away, away_c, 4)
    pack(cot_ref, home, home_c, 6)


def first_kernel(
    bucket_ref, own, partner, received, partner_received, vecs, weight1,
    image_ref, conv_ref, act2_ref, stats_ref, act1_t, act2_t, send_t,
    shift_ref,
):
    h, home, away = place(bucket_ref)
    stride = home[2]
    mask, pixels = pixel_mask(home)
    channels = vecs.shape[1]
    group_size = pixels * (channels // GROUPS)
    assemble(image_ref, home, h, (own, partner, received, partner_received))
    values = image_ref[...].astype(F32) * mask
    mean1, inverse1 = norm_stats(values, mask, group_size)
    act = silu_norm(values, mean1, inverse1, vec(vecs, GAIN1), vec(vecs, SHIFT1), mask)
    fill_shifts(shift_ref, act, stride)
    act1_t[...] = act.astype(BF16).T
    conv_forward(shift_ref, weight1, stride, conv_ref)
    values = (conv_ref[...] + vec(vecs, BIAS1)) * mask
    conv_ref[...] = values
    mean2, inverse2 = norm_stats(values, mask, group_size)
    act = silu_norm(values, mean2, inverse2, vec(vecs, GAIN2), vec(vecs, SHIFT2), mask)
    act = act.astype(BF16)
    act2_ref[...] = act
    act2_t[...] = act.T
    half = pl.multiple_of((h & 1) * (channels // 2), 16)
    send_t[0] = act1_t[pl.ds(half, channels // 2), :]
    send_t[1] = act2_t[pl.ds(half, channels // 2), :]
    stats_ref[0:1, :] = mean1
    stats_ref[1:2, :] = inverse1
    stats_ref[2:3, :] = mean2
    stats_ref[3:4, :] = inverse2
    stats_ref[4:8, :] = jnp.zeros((4, channels), F32)


def second_kernel(
    bucket_ref, image_ref, act2_ref, own, partner, received, partner_received, vecs,
    weight2, wq, wk, wv, wp,
    middle_ref, mixed_ref, grad2_ref, grad_middle_ref, attn_keep, attn_send, vec_ref,
    block_keep, block_send,
    shift_ref, full_ref, grads_ref, sum_ref,
):
    h, home, away = place(bucket_ref)
    stride = home[2]
    mask, pixels = pixel_mask(home)
    channels = vecs.shape[1]
    group_size = pixels * (channels // GROUPS)
    scaling = channels ** (-0.5)
    assemble(full_ref, home, h, (own, partner, received, partner_received))
    fill_shifts(shift_ref, act2_ref[...].astype(F32), stride)
    conv_forward(shift_ref, weight2, stride, middle_ref)
    middle = mask * (image_ref[...].astype(F32) + (middle_ref[...] + vec(vecs, BIAS2)))
    middle_ref[...] = middle
    mean3, inverse3 = norm_stats(middle, mask, group_size)
    normal = (middle - mean3) * inverse3
    normed = (normal * vec(vecs, GAIN3) + vec(vecs, SHIFT3)).astype(BF16)
    wide = jnp.concatenate([wq[...], wk[...], wv[...]], axis=1)
    joint = mm(normed, wide)
    queries = (joint[:, 0:channels] + vec(vecs, QB)).astype(BF16)
    keys = joint[:, channels : 2 * channels].astype(BF16)
    values = (joint[:, 2 * channels :] + vec(vecs, VB)).astype(BF16)
    lanes = lax.broadcasted_iota(jnp.int32, (1, PIX), 1)
    key_cols = lanes & (stride - 1)
    key_valid = (key_cols < home[3]) & (lanes < jnp.where(home[1], 384, 512))
    scores = jnp.where(key_valid, mm_nt(queries, keys) * scaling, -1000000000.0)
    grad_top = full_ref[...].astype(F32) * mask
    grad_rows = grad_top.astype(BF16)
    grad_mixed = mm_nt(grad_rows, wp[...]).astype(BF16)
    grad_soft = mm_nt(grad_mixed, values)
    raised = jnp.exp(scores - jnp.max(scores, axis=1, keepdims=True))
    soft = raised * (1.0 / jnp.sum(raised, axis=1, keepdims=True))
    soft16 = soft.astype(BF16)
    mixed = mm(soft16, values).astype(BF16)
    mixed_ref[...] = mixed

    grad_values = mm_tn(soft16, grad_mixed).astype(BF16)
    grad_scores = soft * (grad_soft - jnp.sum(soft * grad_soft, axis=1, keepdims=True))
    grad_scores = grad_scores.astype(BF16)
    grad_queries = (mm(grad_scores, keys) * scaling).astype(BF16)
    grad_keys = (mm_tn(grad_scores, queries) * scaling).astype(BF16)
    grads_ref[:, 0:channels] = grad_queries
    grads_ref[:, channels : 2 * channels] = grad_keys
    grads_ref[:, 2 * channels : 3 * channels] = grad_values
    grads_ref[:, 3 * channels : 4 * channels] = grad_rows
    grad_normed = mm_nt(grads_ref[:, 0 : 3 * channels], wide)
    grad_in, gain_grad, shift_grad = norm_back(
        grad_normed, normal, inverse3, mask, group_size, vec(vecs, GAIN3)
    )
    grad_middle = mask * (grad_top + grad_in)
    grad_middle_ref[...] = grad_middle
    grad2 = grad_middle.astype(BF16)
    grad2_ref[...] = grad2
    vec_ref[0:1, :] = gain_grad
    vec_ref[1:2, :] = shift_grad
    vec_ref[2:3, :] = total(grad_queries.astype(F32))
    vec_ref[3:4, :] = total(grad_values.astype(F32))
    vec_ref[4:5, :] = total(grad_top)
    vec_ref[5:6, :] = total(grad2.astype(F32))
    vec_ref[6:8, :] = jnp.zeros((2, channels), F32)

    keep_at = pl.multiple_of(BLK * h, BLK)
    send_at = pl.multiple_of(BLK * (h ^ 2), BLK)
    block_keep[...] = grad2_ref[:, pl.ds(keep_at, BLK)]
    block_send[...] = grad2_ref[:, pl.ds(send_at, BLK)]

    def blocks(index):
        start = index * channels
        return [
            grads_ref[:, pl.ds(pl.multiple_of(start + BLK * h, BLK), BLK)],
            grads_ref[:, pl.ds(pl.multiple_of(start + BLK * (h ^ 2), BLK), BLK)],
        ]

    sum_ref[:, 0 : 6 * BLK] = mm_tn(normed, jnp.concatenate(blocks(0) + blocks(1) + blocks(2), axis=1))
    sum_ref[:, 6 * BLK : 8 * BLK] = mm_tn(mixed, jnp.concatenate(blocks(3), axis=1))
    mine = lax.axis_index("batch") & 1
    pairs = attn_keep.shape[0]
    rows = channels // (2 * pairs)
    for pair in range(pairs):
        for dst, which in ((attn_keep, mine), (attn_send, 1 - mine)):
            part = sum_ref[pl.ds(pl.multiple_of((2 * pair + which) * rows, 8), rows), :].astype(BF16)
            for index in range(4):
                at = index * 2 * BLK
                dst[pair, index * rows : (index + 1) * rows, :] = part[:, at : at + 2 * BLK]


def third_kernel(
    bucket_ref, grad2_ref, conv_ref, stats_ref, vecs, weight2,
    grad1_ref, block_keep, block_send, vec_ref,
    shift_ref, acc_ref,
):
    h, home, away = place(bucket_ref)
    stride = home[2]
    mask, pixels = pixel_mask(home)
    channels = vecs.shape[1]
    group_size = pixels * (channels // GROUPS)
    fill_shifts(shift_ref, grad2_ref[...].astype(F32), stride)
    conv_backward(shift_ref, weight2, stride, acc_ref)
    inverse = stats_ref[3:4, :]
    normal = (conv_ref[...] - stats_ref[2:3, :]) * inverse
    u = normal * vec(vecs, GAIN2) + vec(vecs, SHIFT2)
    grad = mask * acc_ref[...] * silu_slope(u)
    grad_in, gain_grad, shift_grad = norm_back(
        grad, normal, inverse, mask, group_size, vec(vecs, GAIN2)
    )
    grad1 = grad_in.astype(BF16)
    grad1_ref[...] = grad1
    vec_ref[0:1, :] = gain_grad
    vec_ref[1:2, :] = shift_grad
    vec_ref[2:3, :] = total(grad1.astype(F32))
    vec_ref[3:8, :] = jnp.zeros((5, channels), F32)
    block_keep[...] = grad1_ref[:, pl.ds(pl.multiple_of(BLK * h, BLK), BLK)]
    block_send[...] = grad1_ref[:, pl.ds(pl.multiple_of(BLK * (h ^ 2), BLK), BLK)]


def fourth_kernel(
    bucket_ref, grad1_ref, image_ref, stats_ref, grad_middle_ref, vecs, weight1, vec_a, vec_b,
    grad_own, send_ref, vec_keep, vec_send,
    shift_ref, acc_ref, full_ref, vec_ref,
):
    h, home, away = place(bucket_ref)
    stride = home[2]
    mask, pixels = pixel_mask(home)
    channels = vecs.shape[1]
    group_size = pixels * (channels // GROUPS)
    fill_shifts(shift_ref, grad1_ref[...].astype(F32), stride)
    conv_backward(shift_ref, weight1, stride, acc_ref)
    inverse = stats_ref[1:2, :]
    normal = (image_ref[...].astype(F32) * mask - stats_ref[0:1, :]) * inverse
    u = normal * vec(vecs, GAIN1) + vec(vecs, SHIFT1)
    grad = mask * acc_ref[...] * silu_slope(u)
    grad_in, gain_grad, shift_grad = norm_back(
        grad, normal, inverse, mask, group_size, vec(vecs, GAIN1)
    )
    full_ref[...] = (mask * (grad_middle_ref[...] + grad_in)).astype(BF16)
    split_out(full_ref, home, h, grad_own, send_ref)
    vec_ref[0:6, :] = vec_a[0:6, :]
    vec_ref[6:9, :] = vec_b[0:3, :]
    vec_ref[9:10, :] = gain_grad
    vec_ref[10:11, :] = shift_grad
    vec_ref[11:VECS, :] = jnp.zeros((VECS - 11, channels), F32)
    pairs = vec_keep.shape[0]
    rows = channels // (2 * pairs)
    mine = (lax.axis_index("batch") & 1) == 1
    for pair in range(pairs):
        parts = []
        for shard in (2 * pair, 2 * pair + 1):
            start = shard * rows
            tile = start // BLK * BLK
            part = vec_ref[:, tile : tile + BLK]
            parts.append(part if start == tile else pltpu.roll(part, BLK - (start - tile), 1))
        vec_keep[pair] = jnp.where(mine, parts[1], parts[0]).astype(BF16)
        vec_send[pair] = jnp.where(mine, parts[0], parts[1]).astype(BF16)


def output_kernel(
    bucket_ref, middle_ref, mixed_ref, vecs, wp, grad_send, out_own, send_ref, full_ref
):
    h, home, away = place(bucket_ref)
    mask, pixels = pixel_mask(home)
    projected = mm(mixed_ref[...], wp[...]) + vec(vecs, PB)
    full_ref[...] = (mask * (middle_ref[...] + projected)).astype(BF16)
    split_out(full_ref, home, h, out_own, send_ref.at[0])
    send_ref[1] = grad_send[...]


def weight_kernel(
    bucket_ref, act_t, half_t, partner_half_t, block_own, block_away,
    keep_ref, send_ref, left_ref, right_ref, shift_ref, sum_ref, *, layer,
):
    h, home, away = place(bucket_ref)
    channels = act_t.shape[0]
    half = channels // 2
    left_ref[:, 0:PIX] = act_t[...]
    left_ref[pl.ds(pl.multiple_of((h & 1) * half, 16), half), PIX : 2 * PIX] = half_t[layer]
    left_ref[pl.ds(pl.multiple_of((1 - (h & 1)) * half, 16), half), PIX : 2 * PIX] = (
        partner_half_t[layer]
    )
    for index, (facts, block) in enumerate(((home, block_own), (away, block_away))):
        stride = facts[2]
        fill_shifts(shift_ref, block[...].astype(F32), stride)
        for p in range(3):
            for q in range(3):
                column = (3 * p + q) * BLK
                right_ref[index * PIX : (index + 1) * PIX, column : column + BLK] = tap(
                    shift_ref, 2 - p, 2 - q, stride
                )
    joint = mm(left_ref[...], right_ref[...])
    for t in range(9):
        sum_ref[t * channels : (t + 1) * channels, :] = joint[:, t * BLK : (t + 1) * BLK]
    mine = lax.axis_index("batch") & 1
    pairs = keep_ref.shape[0]
    rows = 9 * channels // (2 * pairs)
    for pair in range(pairs):
        for dst, which in ((keep_ref, mine), (send_ref, 1 - mine)):
            shard = 2 * pair + which
            dst[pair] = sum_ref[pl.ds(pl.multiple_of(shard * rows, 8), rows), :].astype(BF16)


def route_kernel(keep_ref, got_ref, *outs, bit, first):
    ways = len(outs) if first == 0 else len(outs) // 2
    group = (lax.axis_index("batch") >> bit) & (ways - 1)
    rows = keep_ref.shape[1]
    for step, dst in enumerate(outs[-ways:]):
        which = group ^ step
        for index in range(dst.shape[0]):
            at = index * ways + which
            dst[index, first : first + rows, :] = (
                keep_ref[at].astype(F32) + got_ref[at].astype(F32)
            ).astype(BF16)


def total_of(refs):
    added = refs[0].astype(F32)
    for ref in refs[1:]:
        added = added + ref.astype(F32)
    return added


def sum_kernel(*refs):
    refs[-1][...] = total_of([ref[0] for ref in refs[:-1]]).astype(BF16)


def join_kernel(own_ref, far_ref, near_ref, diagonal_ref, *out_refs):
    h = lax.axis_index("height")
    first = 0
    for dst in [ref for ref in out_refs if ref.shape[0] > 1]:
        rows = dst.shape[0]
        for ref, index in ((own_ref, h), (far_ref, h ^ 2), (near_ref, h ^ 1), (diagonal_ref, h ^ 3)):
            dst[:, pl.ds(pl.multiple_of(BLK * index, BLK), BLK)] = ref[first : first + rows, :].astype(F32)
        first += rows
    if own_ref.shape[0] > first:
        own, far = own_ref[first:, :].astype(F32), far_ref[first:, :].astype(F32)
        near, diagonal = near_ref[first:, :].astype(F32), diagonal_ref[first:, :].astype(F32)
        sums = 0.5 * ((own + near) + (far + diagonal))
        for index, dst in enumerate([ref for ref in out_refs if ref.shape[0] == 1]):
            dst[...] = sums[index : index + 1, 0 : dst.shape[1]]


def join_attn_kernel(own_ref, far_ref, near_ref, diagonal_ref, *out_refs):
    h = lax.axis_index("height")
    rows = out_refs[0].shape[0]
    for first, second, index in ((own_ref, far_ref, h), (near_ref, diagonal_ref, h ^ 1)):
        for position in range(2):
            lane, other = position * BLK, (1 - position) * BLK
            column = pl.multiple_of(BLK * (index ^ (2 * position)), BLK)
            for number, dst in enumerate(out_refs):
                at = number * rows
                dst[:, pl.ds(column, BLK)] = first[at : at + rows, lane : lane + BLK].astype(
                    F32
                ) + second[at : at + rows, other : other + BLK].astype(F32)


def unpack_kernel(bucket_ref, out_own, grad_own, away_ref, out_ref, grad_ref):
    h, home, away = place(bucket_ref)
    for own, received, dst in (
        (out_own, away_ref.at[0], out_ref),
        (grad_own, away_ref.at[1], grad_ref),
    ):
        channels = dst.shape[3]
        for facts, src, wide_rows in ((away, received, 4), (home, own, 6)):
            image, tall, stride, width = facts

            @pl.when(tall)
            def _():
                for row in range(6):
                    dst[image, row, 0:16, :] = src[16 * row : 16 * row + 16, :]
                    dst[image, row, 16:32, :] = jnp.zeros((16, channels), dst.dtype)

            @pl.when(jnp.logical_not(tall))
            def _():
                for row in range(wide_rows):
                    dst[image, row] = src[32 * row : 32 * row + 32, :]
                for row in range(wide_rows, 6):
                    dst[image, row] = jnp.zeros((32, channels), dst.dtype)

            if wide_rows == 4:

                @pl.when(jnp.logical_not(tall) & (h == 3))
                def _():
                    for row in range(6):
                        dst[image, row] = jnp.zeros((32, channels), dst.dtype)


def call(kernel, name, outs, scratch, vmem, *operands, smem=1, any_from=99, aliases={}):
    specs = [SM] * smem + [VM] * (len(operands) - smem)
    specs = [HB if i >= any_from else spec for i, spec in enumerate(specs)]
    return pl.pallas_call(
        kernel,
        name=name,
        out_shape=[jax.ShapeDtypeStruct(shape, dtype) for shape, dtype in outs],
        in_specs=specs,
        out_specs=[SM if dtype == jnp.int32 else VM for shape, dtype in outs],
        scratch_shapes=[
            pltpu.SemaphoreType.DMA(shape)
            if dtype is None
            else (pltpu.SMEM if dtype == jnp.int32 else pltpu.VMEM)(shape, dtype)
            for shape, dtype in scratch
        ],
        input_output_aliases=aliases,
        compiler_params=pltpu.CompilerParams(vmem_limit_bytes=vmem << 20),
        cost_estimate=pl.CostEstimate(
            flops=int(LENGTH.get(name, 0.02) * RATE), bytes_accessed=1024, transcendentals=0
        ),
    )(*operands)


def on_device(
    inputs,
    bucket,
    norm1_gain,
    norm1_shift,
    conv1_weight,
    conv1_bias,
    norm2_gain,
    norm2_shift,
    conv2_weight,
    conv2_bias,
    norm3_gain,
    norm3_shift,
    query_weight,
    query_bias,
    key_weight,
    value_weight,
    value_bias,
    proj_weight,
    proj_bias,
    cotangent,
):
    C = inputs.shape[-1]
    batches = lax.axis_size("batch")
    bits = batches.bit_length() - 1
    shard_rows = 9 * C // batches
    small_rows = C // batches

    def row(v):
        return v.reshape(1, C)

    def to_core(v):
        return lax.ppermute(v, "height", [(i, i ^ 1) for i in range(4)])

    def to_chip(v):
        return lax.ppermute(v, "height", [(i, i ^ 2) for i in range(4)])

    def to_batch(v, change):
        return lax.ppermute(v, "batch", [(i, i ^ change) for i in range(batches)])

    def after(v, *others):
        return lax.optimization_barrier((v,) + others)[0]

    def together(got, *others):
        return list(lax.optimization_barrier((*got, *others))[: len(got)])

    img16 = ((PIX, C), BF16)
    img32 = ((PIX, C), F32)
    rows8 = ((8, C), F32)
    block = ((PIX, BLK), BF16)
    turned = ((C, PIX), BF16)
    shifts = ((3, PIX + 2 * PAD, C), BF16)

    kinds, away_x, home_x = call(
        pack_kernel, "pack",
        [((2,), jnp.int32), ((128, C), BF16), ((192, C), BF16)],
        [((2,), jnp.int32), (inputs.shape, BF16), ((2,), None)], 54, bucket, inputs,
        smem=0, any_from=0,
    )
    vectors = (
        norm1_gain, norm1_shift, conv1_bias, norm2_gain, norm2_shift, conv2_bias,
        norm3_gain, norm3_shift, query_bias, value_bias, proj_bias,
    )
    recv_x = to_chip(away_x)
    core_x = to_core(home_x)
    vecs, away_c, home_c = call(
        stack_kernel, "stack", [((VECS, C), F32), ((160, C), BF16), ((192, C), BF16)], [], 8,
        kinds, cotangent, *[row(v) for v in vectors],
    )
    recv_c = to_chip(away_c)
    core_c = to_core(home_c)
    core_recv_c = lax.ppermute(away_c, "height", [(i, i ^ 3) for i in range(4)])
    core_recv_x = to_core(after(recv_x, vecs))

    image, conv, act2, stats, act1_t, act2_t, send_t = call(
        first_kernel, "first",
        [img16, img32, img16, rows8, turned, turned, ((2, C // 2, PIX), BF16)],
        [shifts], 14,
        kinds, home_x, core_x, recv_x, core_recv_x, vecs, conv1_weight,
    )
    half_t = to_chip(send_t)
    core_half_t = to_core(half_t)

    attn_out = ((batches // 2, 4 * small_rows, 2 * BLK), BF16)
    middle, mixed, grad2, grad_middle, attn_keep, attn_send, vec_a, block2, block2_send = call(
        second_kernel, "second",
        [img32, img16, img16, img32, attn_out, attn_out, rows8, block, block],
        [shifts, img16, ((PIX, 4 * C), BF16), ((C, 8 * BLK), F32)], 24,
        kinds, image, act2, home_c, core_c, recv_c, core_recv_c, vecs,
        conv2_weight, query_weight, key_weight, value_weight, proj_weight,
    )
    block2_away = to_chip(block2_send)
    attn_got = to_batch(attn_send, 1)

    grad1, block1, block1_send, vec_b = call(
        third_kernel, "third",
        [img16, block, block, rows8],
        [shifts, img32], 14,
        kinds, grad2, conv, stats, vecs, conv2_weight,
    )
    block1_away = to_chip(block1_send)

    def weight_grad(name, act_t, index, own, away):
        return call(
            functools.partial(weight_kernel, layer=index), name,
            [((batches // 2, shard_rows, BLK), BF16)] * 2,
            [((C, 2 * PIX), BF16), ((2 * PIX, 9 * BLK), BF16), ((3, PIX + 2 * PAD, BLK), BF16),
             ((9 * C, BLK), F32)],
            18, kinds, act_t, half_t, core_half_t, own, away,
        )

    keep2, send2 = weight_grad("weight2", act2_t, 1, after(block2, block1), block2_away)
    got2 = to_batch(send2, 1)

    def spread(name, bit, keep, got, tail=None, behind=()):
        ways = 1 << min(2, bits - bit)
        rows = keep.shape[1]
        shape = (keep.shape[0] // ways, rows + (VECS if tail else 0), keep.shape[2])
        parts = call(
            functools.partial(route_kernel, bit=bit, first=0), name + str(bit),
            [(shape, BF16)] * ways, [], 16, keep, got, smem=0,
        )
        if tail:
            parts = call(
                functools.partial(route_kernel, bit=bit, first=rows), name + "tail",
                [(shape, BF16)] * ways, [], 16, *tail, *parts, smem=0,
                aliases={2 + j: j for j in range(ways)},
            )
        return parts, [to_batch(after(parts[j], *behind), j << bit) for j in range(1, ways)]

    def finish(name, parts, got):
        for bit in range(3, bits, 2):
            added = total_of([parts[0]] + got).astype(BF16)
            parts, got = spread(name, bit, added, jnp.zeros_like(added))
        return call(
            sum_kernel, "sum" + name, [(parts[0].shape[1:], BF16)], [], 8, parts[0], *got, smem=0
        )[0]

    def gather(shard, *between):
        far = to_chip(shard)
        near = to_core(shard)
        return shard, far, near, to_core(after(far, *between))

    parts_a, got_a = spread("routea", 1, after(attn_keep, send2), attn_got)
    keep1, send1 = weight_grad("weight1", act1_t, 0, after(block1, *parts_a), block1_away)
    got1 = to_batch(send1, 1)
    shard_a = finish("routea", parts_a, together(got_a, send1))
    grad_own, grad_send, vec_keep, vec_send = call(
        fourth_kernel, "fourth",
        [((192, C), BF16), ((128, C), BF16),
         ((batches // 2, VECS, BLK), BF16), ((batches // 2, VECS, BLK), BF16)],
        [shifts, img32, img16, ((VECS, C), F32)], 14,
        kinds, after(grad1, send1), image, stats, grad_middle, vecs, conv1_weight, vec_a, vec_b,
    )
    vec_got = to_batch(vec_send, 1)
    parts_b, got_b = spread("routeb", 1, after(keep2, vec_keep, shard_a), got2)
    parts_c, got_c = spread("routec", 1, keep1, got1, (vec_keep, vec_got))
    out_own, image_send = call(
        output_kernel, "output", [((192, C), BF16), ((2, 128, C), BF16)], [img16], 10,
        kinds, after(middle, *got_b), mixed, vecs, proj_weight, grad_send,
    )
    image_away = to_chip(image_send)
    shard_b = finish("routeb", parts_b, together(got_b, parts_c[0]))
    gathered_a = gather(after(shard_a, *got_b))
    gathered_b = gather(shard_b)
    shard_c = finish(
        "routec", parts_c, together(got_c[::-1], gathered_b[1], gathered_a[1])
    )
    small = call(
        join_attn_kernel, "joina", [((small_rows, C), F32)] * 4, [], 8,
        after(gathered_a[0], shard_c), *gathered_a[1:], smem=0,
    )
    (whole2,) = call(
        join_kernel, "joinb", [((shard_rows, C), F32)], [], 8,
        after(gathered_b[0], shard_c), *gathered_b[1:], smem=0,
    )
    outputs, input_grad = call(
        unpack_kernel, "unpack",
        [(inputs.shape, BF16)] * 2, [], 8,
        kinds, out_own, grad_own, after(image_away, shard_c),
    )
    gathered_c = gather(shard_c, whole2, outputs, *small)
    whole1, *sums = call(
        join_kernel, "joinc", [((shard_rows, C), F32)] + [((1, small_rows), F32)] * 11, [], 8,
        *gathered_c, smem=0,
    )
    v = [row.reshape(small_rows) for row in sums]

    return (
        outputs, input_grad,
        v[9], v[10], whole1, v[8],
        v[6], v[7], whole2, v[5],
        v[0], v[1],
        small[0], v[2], small[1], small[2], v[3], small[3], v[4],
    )


def solution(mesh):
    image = P("batch", "height", None, None)
    vector = P("batch")
    matrix = P("batch", None)
    return jax.shard_map(
        on_device,
        mesh=mesh,
        in_specs=(image, vector) + (P(),) * 17 + (image,),
        out_specs=(
            image, image,
            vector, vector, matrix, vector,
            vector, vector, matrix, vector,
            vector, vector,
            matrix, vector, matrix, matrix, vector, matrix, vector,
        ),
        check_vma=False,
    )
```

```python
import functools

import jax
import jax.numpy as jnp
from jax import lax
from jax.experimental import pallas as pl
from jax.experimental.pallas import tpu as pltpu
from jax.sharding import PartitionSpec as P

GROUPS = 32
UNIT = 8
PIX = 512
PAD = 32
BLK = 128
F32 = jnp.float32
BF16 = jnp.bfloat16
epsilon = 1e-05

VM = pl.BlockSpec(memory_space=pltpu.VMEM)
SM = pl.BlockSpec(memory_space=pltpu.SMEM)
HB = pl.BlockSpec(memory_space=pltpu.HBM)
RATE = 1 << 30
LENGTH = {
    "pack": 10, "stack": 10, "first": 0.02, "second": 30, "third": 20, "fourth": 0.02, "weight2": 1, "weight1": 3, "routeb1": 20,
}


def place(bucket_ref):
    h = lax.axis_index("height")
    upper = lax.div(h, 2)
    tall_first = bucket_ref[0] == 1
    tall_image = jnp.where(tall_first, 0, 1)
    home = jnp.where(upper == 1, tall_image, 1 - tall_image)
    away = 1 - home

    def facts(image):
        kind = bucket_ref[image]
        tall = kind == 1
        stride = jnp.where(tall, 2 * UNIT, 4 * UNIT)
        width = jnp.where(kind == 0, 3 * UNIT, stride)
        return (image, tall, stride, width)

    return h, facts(home), facts(away)


def pixel_col(stride, lanes=1):
    rows = lax.broadcasted_iota(jnp.int32, (PIX, lanes), 0)
    return rows, rows & (stride - 1)


def pixel_mask(facts):
    unused, tall, stride, width = facts
    rows, cols = pixel_col(stride)
    limit = jnp.where(tall, 6 * UNIT * UNIT, 8 * UNIT * UNIT)
    mask = jnp.where((cols < width) & (rows < limit), 1.0, 0.0).astype(F32)
    size = jnp.where(tall | (width == 3 * UNIT), 6 * UNIT * UNIT, 8 * UNIT * UNIT)
    return mask, size.astype(F32)


def group_total(rows):
    members = rows.shape[1] // GROUPS
    lane = lax.broadcasted_iota(jnp.int32, (rows.shape[0], BLK), 1)
    tiles = []
    for tile in range(rows.shape[1] // BLK):
        part = rows[:, tile * BLK : (tile + 1) * BLK]
        step = 1
        while step < members:
            place_in_four = (lane // step) & 3
            added = part
            for d in (1, 2, 3):
                up = pltpu.roll(part, BLK - d * step, 1)
                down = pltpu.roll(part, (4 - d) * step, 1)
                added = added + jnp.where(place_in_four + d < 4, up, down)
            part = added
            step *= 4
        tiles.append(part)
    return jnp.concatenate(tiles, axis=1)


def total(values):
    return jnp.sum(values, axis=0, keepdims=True)


def wide_total(*rows):
    stacked = jnp.concatenate(list(rows) + [rows[0]] * (8 - len(rows)), axis=0)
    sums = group_total(stacked)
    return [sums[i : i + 1] for i in range(len(rows))]


def norm_stats(values, mask, group_size):
    mean = wide_total(total(values))[0] / group_size
    centered = (values - mean) * mask
    variance = wide_total(total(centered * centered))[0] / group_size
    return mean, lax.rsqrt(variance + epsilon)


def silu_norm(values, mean, inverse, gain, shift, mask):
    scale = 0.5 * inverse * gain
    half = values * scale + (0.5 * shift - mean * scale)
    return (half + half * jnp.tanh(half)) * mask


def norm_back(grad, normal, inverse, mask, group_size, gain):
    plain_row = total(grad)
    cross_row = total(grad * normal)
    plain, cross = [v / group_size for v in wide_total(plain_row * gain, cross_row * gain)]
    grad_in = grad * (inverse * gain) - mask * (plain * inverse + normal * (cross * inverse))
    return grad_in, cross_row, plain_row


def silu_slope(u):
    half = 0.5 * u
    t = jnp.tanh(half)
    return (0.5 + 0.5 * t) * (1.0 + half * (1.0 - t))


def mm(a, b):
    return jnp.dot(a, b, preferred_element_type=F32)


def mm_nt(a, b):
    return lax.dot_general(a, b, (((1,), (1,)), ((), ())), preferred_element_type=F32)


def mm_tn(a, b):
    return lax.dot_general(a, b, (((0,), (0,)), ((), ())), preferred_element_type=F32)


def fill_shifts(shift_ref, values, stride):
    unused, cols = pixel_col(stride)
    lanes = values.shape[1]
    zeros = jnp.zeros((PAD, lanes), BF16)
    for q in range(3):
        shift_ref[q, 0:PAD, :] = zeros
        shift_ref[q, PAD + PIX : 2 * PAD + PIX, :] = zeros
    left = jnp.where(cols == 0, 0.0, pltpu.roll(values, 1, 0))
    right = jnp.where(cols == stride - 1, 0.0, pltpu.roll(values, PIX - 1, 0))
    shift_ref[0, PAD : PAD + PIX, :] = left.astype(BF16)
    shift_ref[1, PAD : PAD + PIX, :] = values.astype(BF16)
    shift_ref[2, PAD : PAD + PIX, :] = right.astype(BF16)


def tap(shift_ref, p, q, stride, first=0, count=PIX):
    start = pl.multiple_of(PAD + first + (p - 1) * stride, 16)
    return shift_ref[q, pl.ds(start, count), :]


def conv_forward(shift_ref, weight_ref, stride, out_ref, tile=256):
    for first in range(0, PIX, tile):
        stacked = jnp.concatenate(
            [tap(shift_ref, p, q, stride, first, tile) for p in range(3) for q in range(3)], axis=1
        )
        out_ref[first : first + tile, :] = mm(stacked, weight_ref[...])


def conv_backward(shift_ref, weight_ref, stride, out_ref, tile=256):
    channels = weight_ref.shape[1]
    for first in range(0, PIX, tile):
        acc = None
        for p in range(3):
            for q in range(3):
                row = (8 - (3 * p + q)) * channels
                part = mm_nt(
                    tap(shift_ref, p, q, stride, first, tile), weight_ref[row : row + channels, :]
                )
                acc = part if acc is None else acc + part
        out_ref[first : first + tile, :] = acc


def assemble(out_ref, facts, h, pieces):
    unused, tall, stride, width = facts
    own, partner, received, partner_received = pieces
    other = h ^ 1

    @pl.when(tall)
    def _():
        for ref, index in (
            (own, h),
            (partner, other),
            (received, h ^ 2),
            (partner_received, other ^ 2),
        ):
            out_ref[pl.ds(pl.multiple_of(96 * index, 16), 96), :] = ref[0:96, :]
        out_ref[384:512, :] = jnp.zeros((128, out_ref.shape[1]), out_ref.dtype)

    @pl.when(jnp.logical_not(tall))
    def _():
        low = h & 1
        out_ref[pl.ds(pl.multiple_of(192 * low, 16), 192), :] = own[...]
        out_ref[pl.ds(pl.multiple_of(192 * (1 - low), 16), 192), :] = partner[...]

        @pl.when(low == 0)
        def _():
            out_ref[384:512, :] = received[0:128, :]

        @pl.when(low == 1)
        def _():
            out_ref[384:512, :] = partner_received[0:128, :]


def split_out(full_ref, facts, h, own_ref, send_ref):
    unused, tall, stride, width = facts
    send_h = h ^ 2

    @pl.when(tall)
    def _():
        own_ref[0:96, :] = full_ref[pl.ds(pl.multiple_of(96 * h, 16), 96), :]
        own_ref[96:192, :] = jnp.zeros((96, own_ref.shape[1]), own_ref.dtype)
        send_ref[0:96, :] = full_ref[pl.ds(pl.multiple_of(96 * send_h, 16), 96), :]
        send_ref[96:128, :] = jnp.zeros((32, own_ref.shape[1]), own_ref.dtype)

    @pl.when(jnp.logical_not(tall))
    def _():
        own_ref[...] = full_ref[pl.ds(pl.multiple_of(192 * (h & 1), 16), 192), :]
        send_ref[...] = full_ref[384:512, :]


GAIN1, SHIFT1, BIAS1, GAIN2, SHIFT2, BIAS2, GAIN3, SHIFT3, QB, VB, PB = range(11)
VECS = 16


def vec(vec_ref, index):
    return vec_ref[index : index + 1, :]


def pack(src, facts, dst, wide_rows):
    image, tall, stride, width = facts

    @pl.when(tall)
    def _():
        for row in range(6):
            dst[16 * row : 16 * row + 16, :] = src[image, row, 0:16, :]
        dst[96 : dst.shape[0], :] = jnp.zeros((dst.shape[0] - 96, dst.shape[1]), dst.dtype)

    @pl.when(jnp.logical_not(tall))
    def _():
        for row in range(wide_rows):
            dst[32 * row : 32 * row + 32, :] = src[image, row]


def pack_kernel(bucket_hbm, x_hbm, kinds, away_x, home_x, bucket_ref, x_ref, sems):
    copies = (
        pltpu.make_async_copy(bucket_hbm, bucket_ref, sems.at[0]),
        pltpu.make_async_copy(x_hbm, x_ref, sems.at[1]),
    )
    for copy in copies:
        copy.start()
    for copy in copies:
        copy.wait()
    h, home, away = place(bucket_ref)
    kinds[0] = bucket_ref[0]
    kinds[1] = bucket_ref[1]
    pack(x_ref, away, away_x, 4)
    pack(x_ref, home, home_x, 6)


def stack_kernel(kinds, cot_ref, *refs):
    h, home, away = place(kinds)
    out_ref, away_c, home_c = refs[-3:]
    count = len(refs) - 3
    for index, ref in enumerate(refs[:count]):
        out_ref[index : index + 1, :] = ref[...]
    out_ref[count:, :] = jnp.zeros((VECS - count, out_ref.shape[1]), F32)
    pack(cot_ref, away, away_c, 4)
    pack(cot_ref, home, home_c, 6)


def first_kernel(
    bucket_ref, own, partner, received, partner_received, vecs, weight1,
    image_ref, conv_ref, act2_ref, stats_ref, act1_ref, send_ref,
    shift_ref,
):
    h, home, away = place(bucket_ref)
    stride = home[2]
    mask, pixels = pixel_mask(home)
    channels = vecs.shape[1]
    group_size = pixels * (channels // GROUPS)
    assemble(image_ref, home, h, (own, partner, received, partner_received))
    values = image_ref[...].astype(F32) * mask
    mean1, inverse1 = norm_stats(values, mask, group_size)
    act = silu_norm(values, mean1, inverse1, vec(vecs, GAIN1), vec(vecs, SHIFT1), mask)
    fill_shifts(shift_ref, act, stride)
    act1_ref[...] = act.astype(BF16)
    conv_forward(shift_ref, weight1, stride, conv_ref)
    values = (conv_ref[...] + vec(vecs, BIAS1)) * mask
    conv_ref[...] = values
    mean2, inverse2 = norm_stats(values, mask, group_size)
    act = silu_norm(values, mean2, inverse2, vec(vecs, GAIN2), vec(vecs, SHIFT2), mask)
    act = act.astype(BF16)
    act2_ref[...] = act
    half = pl.multiple_of((h & 1) * (channels // 2), BLK)
    send_ref[0] = act1_ref[:, pl.ds(half, channels // 2)]
    send_ref[1] = act2_ref[:, pl.ds(half, channels // 2)]
    stats_ref[0:1, :] = mean1
    stats_ref[1:2, :] = inverse1
    stats_ref[2:3, :] = mean2
    stats_ref[3:4, :] = inverse2
    stats_ref[4:8, :] = jnp.zeros((4, channels), F32)


def second_kernel(
    bucket_ref, image_ref, act2_ref, own, partner, received, partner_received, vecs,
    weight2, wq, wk, wv, wp,
    middle_ref, mixed_ref, grad2_ref, grad_middle_ref, attn_keep, attn_send, vec_ref,
    block_keep, block_send,
    shift_ref, full_ref, grads_ref, sum_ref,
):
    h, home, away = place(bucket_ref)
    stride = home[2]
    mask, pixels = pixel_mask(home)
    channels = vecs.shape[1]
    group_size = pixels * (channels // GROUPS)
    scaling = channels ** (-0.5)
    assemble(full_ref, home, h, (own, partner, received, partner_received))
    fill_shifts(shift_ref, act2_ref[...].astype(F32), stride)
    conv_forward(shift_ref, weight2, stride, middle_ref)
    middle = mask * (image_ref[...].astype(F32) + (middle_ref[...] + vec(vecs, BIAS2)))
    middle_ref[...] = middle
    mean3, inverse3 = norm_stats(middle, mask, group_size)
    normal = (middle - mean3) * inverse3
    normed = (normal * vec(vecs, GAIN3) + vec(vecs, SHIFT3)).astype(BF16)
    wide = jnp.concatenate([wq[...], wk[...], wv[...]], axis=1)
    joint = mm(normed, wide)
    queries = (joint[:, 0:channels] + vec(vecs, QB)).astype(BF16)
    keys = joint[:, channels : 2 * channels].astype(BF16)
    values = (joint[:, 2 * channels :] + vec(vecs, VB)).astype(BF16)
    lanes = lax.broadcasted_iota(jnp.int32, (1, PIX), 1)
    key_cols = lanes & (stride - 1)
    key_valid = (key_cols < home[3]) & (lanes < jnp.where(home[1], 384, 512))
    scores = jnp.where(key_valid, mm_nt(queries, keys) * scaling, -1000000000.0)
    grad_top = full_ref[...].astype(F32) * mask
    grad_rows = grad_top.astype(BF16)
    grad_mixed = mm_nt(grad_rows, wp[...]).astype(BF16)
    grad_soft = mm_nt(grad_mixed, values)
    raised = jnp.exp(scores - jnp.max(scores, axis=1, keepdims=True))
    soft = raised * (1.0 / jnp.sum(raised, axis=1, keepdims=True))
    soft16 = soft.astype(BF16)
    mixed = mm(soft16, values).astype(BF16)
    mixed_ref[...] = mixed

    grad_values = mm_tn(soft16, grad_mixed).astype(BF16)
    grad_scores = soft * (grad_soft - jnp.sum(soft * grad_soft, axis=1, keepdims=True))
    grad_scores = grad_scores.astype(BF16)
    grad_queries = (mm(grad_scores, keys) * scaling).astype(BF16)
    grad_keys = (mm_tn(grad_scores, queries) * scaling).astype(BF16)
    grads_ref[:, 0:channels] = grad_queries
    grads_ref[:, channels : 2 * channels] = grad_keys
    grads_ref[:, 2 * channels : 3 * channels] = grad_values
    grads_ref[:, 3 * channels : 4 * channels] = grad_rows
    grad_normed = mm_nt(grads_ref[:, 0 : 3 * channels], wide)
    grad_in, gain_grad, shift_grad = norm_back(
        grad_normed, normal, inverse3, mask, group_size, vec(vecs, GAIN3)
    )
    grad_middle = mask * (grad_top + grad_in)
    grad_middle_ref[...] = grad_middle
    grad2 = grad_middle.astype(BF16)
    grad2_ref[...] = grad2
    vec_ref[0:1, :] = gain_grad
    vec_ref[1:2, :] = shift_grad
    vec_ref[2:3, :] = total(grad_queries.astype(F32))
    vec_ref[3:4, :] = total(grad_values.astype(F32))
    vec_ref[4:5, :] = total(grad_top)
    vec_ref[5:6, :] = total(grad2.astype(F32))
    vec_ref[6:8, :] = jnp.zeros((2, channels), F32)

    keep_at = pl.multiple_of(BLK * h, BLK)
    send_at = pl.multiple_of(BLK * (h ^ 2), BLK)
    block_keep[...] = grad2_ref[:, pl.ds(keep_at, BLK)]
    block_send[...] = grad2_ref[:, pl.ds(send_at, BLK)]

    def blocks(index):
        start = index * channels
        return [
            grads_ref[:, pl.ds(pl.multiple_of(start + BLK * h, BLK), BLK)],
            grads_ref[:, pl.ds(pl.multiple_of(start + BLK * (h ^ 2), BLK), BLK)],
        ]

    sum_ref[:, 0 : 6 * BLK] = mm_tn(normed, jnp.concatenate(blocks(0) + blocks(1) + blocks(2), axis=1))
    sum_ref[:, 6 * BLK : 8 * BLK] = mm_tn(mixed, jnp.concatenate(blocks(3), axis=1))
    mine = lax.axis_index("batch") & 1
    pairs = attn_keep.shape[0]
    rows = channels // (2 * pairs)
    for pair in range(pairs):
        for dst, which in ((attn_keep, mine), (attn_send, 1 - mine)):
            part = sum_ref[pl.ds(pl.multiple_of((2 * pair + which) * rows, 8), rows), :].astype(BF16)
            for index in range(4):
                at = index * 2 * BLK
                dst[pair, index * rows : (index + 1) * rows, :] = part[:, at : at + 2 * BLK]


def third_kernel(
    bucket_ref, grad2_ref, conv_ref, stats_ref, vecs, weight2,
    grad1_ref, block_keep, block_send, vec_ref,
    shift_ref, acc_ref,
):
    h, home, away = place(bucket_ref)
    stride = home[2]
    mask, pixels = pixel_mask(home)
    channels = vecs.shape[1]
    group_size = pixels * (channels // GROUPS)
    fill_shifts(shift_ref, grad2_ref[...].astype(F32), stride)
    conv_backward(shift_ref, weight2, stride, acc_ref)
    inverse = stats_ref[3:4, :]
    normal = (conv_ref[...] - stats_ref[2:3, :]) * inverse
    u = normal * vec(vecs, GAIN2) + vec(vecs, SHIFT2)
    grad = mask * acc_ref[...] * silu_slope(u)
    grad_in, gain_grad, shift_grad = norm_back(
        grad, normal, inverse, mask, group_size, vec(vecs, GAIN2)
    )
    grad1 = grad_in.astype(BF16)
    grad1_ref[...] = grad1
    vec_ref[0:1, :] = gain_grad
    vec_ref[1:2, :] = shift_grad
    vec_ref[2:3, :] = total(grad1.astype(F32))
    vec_ref[3:8, :] = jnp.zeros((5, channels), F32)
    block_keep[...] = grad1_ref[:, pl.ds(pl.multiple_of(BLK * h, BLK), BLK)]
    block_send[...] = grad1_ref[:, pl.ds(pl.multiple_of(BLK * (h ^ 2), BLK), BLK)]


def fourth_kernel(
    bucket_ref, grad1_ref, image_ref, stats_ref, grad_middle_ref, vecs, weight1, vec_a, vec_b,
    grad_own, send_ref, vec_keep, vec_send,
    shift_ref, acc_ref, full_ref, vec_ref,
):
    h, home, away = place(bucket_ref)
    stride = home[2]
    mask, pixels = pixel_mask(home)
    channels = vecs.shape[1]
    group_size = pixels * (channels // GROUPS)
    fill_shifts(shift_ref, grad1_ref[...].astype(F32), stride)
    conv_backward(shift_ref, weight1, stride, acc_ref)
    inverse = stats_ref[1:2, :]
    normal = (image_ref[...].astype(F32) * mask - stats_ref[0:1, :]) * inverse
    u = normal * vec(vecs, GAIN1) + vec(vecs, SHIFT1)
    grad = mask * acc_ref[...] * silu_slope(u)
    grad_in, gain_grad, shift_grad = norm_back(
        grad, normal, inverse, mask, group_size, vec(vecs, GAIN1)
    )
    full_ref[...] = (mask * (grad_middle_ref[...] + grad_in)).astype(BF16)
    split_out(full_ref, home, h, grad_own, send_ref)
    vec_ref[0:6, :] = vec_a[0:6, :]
    vec_ref[6:9, :] = vec_b[0:3, :]
    vec_ref[9:10, :] = gain_grad
    vec_ref[10:11, :] = shift_grad
    vec_ref[11:VECS, :] = jnp.zeros((VECS - 11, channels), F32)
    pairs = vec_keep.shape[0]
    rows = channels // (2 * pairs)
    mine = (lax.axis_index("batch") & 1) == 1
    for pair in range(pairs):
        parts = []
        for shard in (2 * pair, 2 * pair + 1):
            start = shard * rows
            tile = start // BLK * BLK
            part = vec_ref[:, tile : tile + BLK]
            parts.append(part if start == tile else pltpu.roll(part, BLK - (start - tile), 1))
        vec_keep[pair] = jnp.where(mine, parts[1], parts[0]).astype(BF16)
        vec_send[pair] = jnp.where(mine, parts[0], parts[1]).astype(BF16)


def output_kernel(
    bucket_ref, middle_ref, mixed_ref, vecs, wp, grad_send, out_own, send_ref, full_ref
):
    h, home, away = place(bucket_ref)
    mask, pixels = pixel_mask(home)
    projected = mm(mixed_ref[...], wp[...]) + vec(vecs, PB)
    full_ref[...] = (mask * (middle_ref[...] + projected)).astype(BF16)
    split_out(full_ref, home, h, out_own, send_ref.at[0])
    send_ref[1] = grad_send[...]


def weight_kernel(
    bucket_ref, act_ref, half_ref, partner_half_ref, block_own, block_away,
    keep_ref, send_ref, left_ref, right_ref, shift_ref, sum_ref, *, layer,
):
    h, home, away = place(bucket_ref)
    channels = act_ref.shape[1]
    half = channels // 2
    left_ref[:, 0:PIX] = act_ref[...].T
    left_ref[pl.ds(pl.multiple_of((h & 1) * half, 16), half), PIX : 2 * PIX] = half_ref[layer].T
    left_ref[pl.ds(pl.multiple_of((1 - (h & 1)) * half, 16), half), PIX : 2 * PIX] = (
        partner_half_ref[layer].T
    )
    for index, (facts, block) in enumerate(((home, block_own), (away, block_away))):
        stride = facts[2]
        fill_shifts(shift_ref, block[...].astype(F32), stride)
        for p in range(3):
            for q in range(3):
                column = (3 * p + q) * BLK
                right_ref[index * PIX : (index + 1) * PIX, column : column + BLK] = tap(
                    shift_ref, 2 - p, 2 - q, stride
                )
    joint = mm(left_ref[...], right_ref[...])
    for t in range(9):
        sum_ref[t * channels : (t + 1) * channels, :] = joint[:, t * BLK : (t + 1) * BLK]
    mine = lax.axis_index("batch") & 1
    pairs = keep_ref.shape[0]
    rows = 9 * channels // (2 * pairs)
    for pair in range(pairs):
        for dst, which in ((keep_ref, mine), (send_ref, 1 - mine)):
            shard = 2 * pair + which
            dst[pair] = sum_ref[pl.ds(pl.multiple_of(shard * rows, 8), rows), :].astype(BF16)


def route_kernel(keep_ref, got_ref, *outs, bit, first):
    ways = len(outs) if first == 0 else len(outs) // 2
    group = (lax.axis_index("batch") >> bit) & (ways - 1)
    rows = keep_ref.shape[1]
    for step, dst in enumerate(outs[-ways:]):
        which = group ^ step
        for index in range(dst.shape[0]):
            at = index * ways + which
            dst[index, first : first + rows, :] = (
                keep_ref[at].astype(F32) + got_ref[at].astype(F32)
            ).astype(BF16)


def total_of(refs):
    added = refs[0].astype(F32)
    for ref in refs[1:]:
        added = added + ref.astype(F32)
    return added


def sum_kernel(*refs):
    refs[-1][...] = total_of([ref[0] for ref in refs[:-1]]).astype(BF16)


def join_kernel(own_ref, far_ref, near_ref, diagonal_ref, *out_refs):
    h = lax.axis_index("height")
    first = 0
    for dst in [ref for ref in out_refs if ref.shape[0] > 1]:
        rows = dst.shape[0]
        for ref, index in ((own_ref, h), (far_ref, h ^ 2), (near_ref, h ^ 1), (diagonal_ref, h ^ 3)):
            dst[:, pl.ds(pl.multiple_of(BLK * index, BLK), BLK)] = ref[first : first + rows, :].astype(F32)
        first += rows
    if own_ref.shape[0] > first:
        own, far = own_ref[first:, :].astype(F32), far_ref[first:, :].astype(F32)
        near, diagonal = near_ref[first:, :].astype(F32), diagonal_ref[first:, :].astype(F32)
        sums = 0.5 * ((own + near) + (far + diagonal))
        for index, dst in enumerate([ref for ref in out_refs if ref.shape[0] == 1]):
            dst[...] = sums[index : index + 1, 0 : dst.shape[1]]


def join_attn_kernel(own_ref, far_ref, near_ref, diagonal_ref, *out_refs):
    h = lax.axis_index("height")
    rows = out_refs[0].shape[0]
    for first, second, index in ((own_ref, far_ref, h), (near_ref, diagonal_ref, h ^ 1)):
        for position in range(2):
            lane, other = position * BLK, (1 - position) * BLK
            column = pl.multiple_of(BLK * (index ^ (2 * position)), BLK)
            for number, dst in enumerate(out_refs):
                at = number * rows
                dst[:, pl.ds(column, BLK)] = first[at : at + rows, lane : lane + BLK].astype(
                    F32
                ) + second[at : at + rows, other : other + BLK].astype(F32)


def unpack_kernel(bucket_ref, out_own, grad_own, away_ref, out_ref, grad_ref):
    h, home, away = place(bucket_ref)
    for own, received, dst in (
        (out_own, away_ref.at[0], out_ref),
        (grad_own, away_ref.at[1], grad_ref),
    ):
        channels = dst.shape[3]
        for facts, src, wide_rows in ((away, received, 4), (home, own, 6)):
            image, tall, stride, width = facts

            @pl.when(tall)
            def _():
                for row in range(6):
                    dst[image, row, 0:16, :] = src[16 * row : 16 * row + 16, :]
                    dst[image, row, 16:32, :] = jnp.zeros((16, channels), dst.dtype)

            @pl.when(jnp.logical_not(tall))
            def _():
                for row in range(wide_rows):
                    dst[image, row] = src[32 * row : 32 * row + 32, :]
                for row in range(wide_rows, 6):
                    dst[image, row] = jnp.zeros((32, channels), dst.dtype)

            if wide_rows == 4:

                @pl.when(jnp.logical_not(tall) & (h == 3))
                def _():
                    for row in range(6):
                        dst[image, row] = jnp.zeros((32, channels), dst.dtype)


def call(kernel, name, outs, scratch, vmem, *operands, smem=1, any_from=99, aliases={}):
    specs = [SM] * smem + [VM] * (len(operands) - smem)
    specs = [HB if i >= any_from else spec for i, spec in enumerate(specs)]
    return pl.pallas_call(
        kernel,
        name=name,
        out_shape=[jax.ShapeDtypeStruct(shape, dtype) for shape, dtype in outs],
        in_specs=specs,
        out_specs=[SM if dtype == jnp.int32 else VM for shape, dtype in outs],
        scratch_shapes=[
            pltpu.SemaphoreType.DMA(shape)
            if dtype is None
            else (pltpu.SMEM if dtype == jnp.int32 else pltpu.VMEM)(shape, dtype)
            for shape, dtype in scratch
        ],
        input_output_aliases=aliases,
        compiler_params=pltpu.CompilerParams(vmem_limit_bytes=vmem << 20),
        cost_estimate=pl.CostEstimate(
            flops=int(LENGTH.get(name, 0.02) * RATE), bytes_accessed=1024, transcendentals=0
        ),
    )(*operands)


def on_device(
    inputs,
    bucket,
    norm1_gain,
    norm1_shift,
    conv1_weight,
    conv1_bias,
    norm2_gain,
    norm2_shift,
    conv2_weight,
    conv2_bias,
    norm3_gain,
    norm3_shift,
    query_weight,
    query_bias,
    key_weight,
    value_weight,
    value_bias,
    proj_weight,
    proj_bias,
    cotangent,
):
    C = inputs.shape[-1]
    batches = lax.axis_size("batch")
    bits = batches.bit_length() - 1
    shard_rows = 9 * C // batches
    small_rows = C // batches

    def row(v):
        return v.reshape(1, C)

    def to_core(v):
        return lax.ppermute(v, "height", [(i, i ^ 1) for i in range(4)])

    def to_chip(v):
        return lax.ppermute(v, "height", [(i, i ^ 2) for i in range(4)])

    def to_batch(v, change):
        return lax.ppermute(v, "batch", [(i, i ^ change) for i in range(batches)])

    def after(v, *others):
        return lax.optimization_barrier((v,) + others)[0]

    def together(got, *others):
        return list(lax.optimization_barrier((*got, *others))[: len(got)])

    img16 = ((PIX, C), BF16)
    img32 = ((PIX, C), F32)
    rows8 = ((8, C), F32)
    block = ((PIX, BLK), BF16)
    shifts = ((3, PIX + 2 * PAD, C), BF16)

    kinds, away_x, home_x = call(
        pack_kernel, "pack",
        [((2,), jnp.int32), ((128, C), BF16), ((192, C), BF16)],
        [((2,), jnp.int32), (inputs.shape, BF16), ((2,), None)], 54, bucket, inputs,
        smem=0, any_from=0,
    )
    vectors = (
        norm1_gain, norm1_shift, conv1_bias, norm2_gain, norm2_shift, conv2_bias,
        norm3_gain, norm3_shift, query_bias, value_bias, proj_bias,
    )
    recv_x = to_chip(away_x)
    core_x = to_core(home_x)
    vecs, away_c, home_c = call(
        stack_kernel, "stack", [((VECS, C), F32), ((160, C), BF16), ((192, C), BF16)], [], 8,
        kinds, cotangent, *[row(v) for v in vectors],
    )
    recv_c = to_chip(away_c)
    core_c = to_core(home_c)
    core_recv_c = lax.ppermute(away_c, "height", [(i, i ^ 3) for i in range(4)])
    core_recv_x = to_core(after(recv_x, vecs))

    image, conv, act2, stats, act1, act_send = call(
        first_kernel, "first",
        [img16, img32, img16, rows8, img16, ((2, PIX, C // 2), BF16)],
        [shifts], 14,
        kinds, home_x, core_x, recv_x, core_recv_x, vecs, conv1_weight,
    )
    half = to_chip(act_send)
    core_half = to_core(half)

    attn_out = ((batches // 2, 4 * small_rows, 2 * BLK), BF16)
    middle, mixed, grad2, grad_middle, attn_keep, attn_send, vec_a, block2, block2_send = call(
        second_kernel, "second",
        [img32, img16, img16, img32, attn_out, attn_out, rows8, block, block],
        [shifts, img16, ((PIX, 4 * C), BF16), ((C, 8 * BLK), F32)], 24,
        kinds, image, act2, home_c, core_c, recv_c, core_recv_c, vecs,
        conv2_weight, query_weight, key_weight, value_weight, proj_weight,
    )
    block2_away = to_chip(block2_send)
    attn_got = to_batch(attn_send, 1)

    grad1, block1, block1_send, vec_b = call(
        third_kernel, "third",
        [img16, block, block, rows8],
        [shifts, img32], 14,
        kinds, grad2, conv, stats, vecs, conv2_weight,
    )
    block1_away = to_chip(block1_send)

    def weight_grad(name, act, index, own, away):
        return call(
            functools.partial(weight_kernel, layer=index), name,
            [((batches // 2, shard_rows, BLK), BF16)] * 2,
            [((C, 2 * PIX), BF16), ((2 * PIX, 9 * BLK), BF16), ((3, PIX + 2 * PAD, BLK), BF16),
             ((9 * C, BLK), F32)],
            18, kinds, act, half, core_half, own, away,
        )

    keep2, send2 = weight_grad("weight2", act2, 1, after(block2, block1), block2_away)
    got2 = to_batch(send2, 1)

    def spread(name, bit, keep, got, tail=None, behind=()):
        ways = 1 << min(2, bits - bit)
        rows = keep.shape[1]
        shape = (keep.shape[0] // ways, rows + (VECS if tail else 0), keep.shape[2])
        parts = call(
            functools.partial(route_kernel, bit=bit, first=0), name + str(bit),
            [(shape, BF16)] * ways, [], 16, keep, got, smem=0,
        )
        if tail:
            parts = call(
                functools.partial(route_kernel, bit=bit, first=rows), name + "tail",
                [(shape, BF16)] * ways, [], 16, *tail, *parts, smem=0,
                aliases={2 + j: j for j in range(ways)},
            )
        return parts, [to_batch(after(parts[j], *behind), j << bit) for j in range(1, ways)]

    def finish(name, parts, got):
        for bit in range(3, bits, 2):
            added = total_of([parts[0]] + got).astype(BF16)
            parts, got = spread(name, bit, added, jnp.zeros_like(added))
        return call(
            sum_kernel, "sum" + name, [(parts[0].shape[1:], BF16)], [], 8, parts[0], *got, smem=0
        )[0]

    def gather(shard, *between):
        far = to_chip(shard)
        near = to_core(shard)
        return shard, far, near, to_core(after(far, *between))

    parts_a, got_a = spread("routea", 1, after(attn_keep, send2), attn_got)
    keep1, send1 = weight_grad("weight1", act1, 0, after(block1, *parts_a), block1_away)
    got1 = to_batch(send1, 1)
    shard_a = finish("routea", parts_a, together(got_a, send1))
    parts_b, got_b = spread("routeb", 1, after(keep2, send1, shard_a), got2)
    grad_own, grad_send, vec_keep, vec_send = call(
        fourth_kernel, "fourth",
        [((192, C), BF16), ((128, C), BF16),
         ((batches // 2, VECS, BLK), BF16), ((batches // 2, VECS, BLK), BF16)],
        [shifts, img32, img16, ((VECS, C), F32)], 14,
        kinds, after(grad1, *parts_b), image, stats, grad_middle, vecs, conv1_weight, vec_a, vec_b,
    )
    vec_got = to_batch(vec_send, 1)
    parts_c, got_c = spread("routec", 1, keep1, got1, (vec_keep, vec_got), behind=got_b)
    out_own, image_send = call(
        output_kernel, "output", [((192, C), BF16), ((2, 128, C), BF16)], [img16], 10,
        kinds, after(middle, parts_c[0]), mixed, vecs, proj_weight, grad_send,
    )
    image_away = to_chip(image_send)
    shard_b = finish("routeb", parts_b, together(got_b, parts_c[0]))
    gathered_a = gather(shard_a)
    gathered_b = gather(shard_b)
    shard_c = finish(
        "routec", parts_c, together(got_c[::-1], gathered_b[1], gathered_a[1])
    )
    small = call(
        join_attn_kernel, "joina", [((small_rows, C), F32)] * 4, [], 8,
        after(gathered_a[0], shard_c), *gathered_a[1:], smem=0,
    )
    (whole2,) = call(
        join_kernel, "joinb", [((shard_rows, C), F32)], [], 8,
        after(gathered_b[0], shard_c), *gathered_b[1:], smem=0,
    )
    outputs, input_grad = call(
        unpack_kernel, "unpack",
        [(inputs.shape, BF16)] * 2, [], 8,
        kinds, out_own, grad_own, after(image_away, shard_c),
    )
    gathered_c = gather(shard_c, whole2, outputs, *small)
    whole1, *sums = call(
        join_kernel, "joinc", [((shard_rows, C), F32)] + [((1, small_rows), F32)] * 11, [], 8,
        *gathered_c, smem=0,
    )
    v = [row.reshape(small_rows) for row in sums]

    return (
        outputs, input_grad,
        v[9], v[10], whole1, v[8],
        v[6], v[7], whole2, v[5],
        v[0], v[1],
        small[0], v[2], small[1], small[2], v[3], small[3], v[4],
    )


def solution(mesh):
    image = P("batch", "height", None, None)
    vector = P("batch")
    matrix = P("batch", None)
    return jax.shard_map(
        on_device,
        mesh=mesh,
        in_specs=(image, vector) + (P(),) * 17 + (image,),
        out_specs=(
            image, image,
            vector, vector, matrix, vector,
            vector, vector, matrix, vector,
            vector, vector,
            matrix, vector, matrix, matrix, vector, matrix, vector,
        ),
        check_vma=False,
    )
```

```python
import functools

import jax
import jax.numpy as jnp
from jax import lax
from jax.experimental import pallas as pl
from jax.experimental.pallas import tpu as pltpu
from jax.sharding import PartitionSpec as P

GROUPS = 32
UNIT = 8
PIX = 512
PAD = 32
BLK = 128
F32 = jnp.float32
BF16 = jnp.bfloat16
epsilon = 1e-05

VM = pl.BlockSpec(memory_space=pltpu.VMEM)
SM = pl.BlockSpec(memory_space=pltpu.SMEM)
HB = pl.BlockSpec(memory_space=pltpu.HBM)
RATE = 1 << 30
LENGTH = {
    "pack": 10, "stack": 10, "first": 0.02, "second": 30, "third": 20, "fourth": 0.5, "weight2": 1, "weight1": 3, "routeb1": 20,
}


def place(bucket_ref):
    h = lax.axis_index("height")
    upper = lax.div(h, 2)
    tall_first = bucket_ref[0] == 1
    tall_image = jnp.where(tall_first, 0, 1)
    home = jnp.where(upper == 1, tall_image, 1 - tall_image)
    away = 1 - home

    def facts(image):
        kind = bucket_ref[image]
        tall = kind == 1
        stride = jnp.where(tall, 2 * UNIT, 4 * UNIT)
        width = jnp.where(kind == 0, 3 * UNIT, stride)
        return (image, tall, stride, width)

    return h, facts(home), facts(away)


def pixel_col(stride, lanes=1):
    rows = lax.broadcasted_iota(jnp.int32, (PIX, lanes), 0)
    return rows, rows & (stride - 1)


def pixel_mask(facts):
    unused, tall, stride, width = facts
    rows, cols = pixel_col(stride)
    limit = jnp.where(tall, 6 * UNIT * UNIT, 8 * UNIT * UNIT)
    mask = jnp.where((cols < width) & (rows < limit), 1.0, 0.0).astype(F32)
    size = jnp.where(tall | (width == 3 * UNIT), 6 * UNIT * UNIT, 8 * UNIT * UNIT)
    return mask, size.astype(F32)


def group_total(rows):
    members = rows.shape[1] // GROUPS
    lane = lax.broadcasted_iota(jnp.int32, (rows.shape[0], BLK), 1)
    tiles = []
    for tile in range(rows.shape[1] // BLK):
        part = rows[:, tile * BLK : (tile + 1) * BLK]
        step = 1
        while step < members:
            place_in_four = (lane // step) & 3
            added = part
            for d in (1, 2, 3):
                up = pltpu.roll(part, BLK - d * step, 1)
                down = pltpu.roll(part, (4 - d) * step, 1)
                added = added + jnp.where(place_in_four + d < 4, up, down)
            part = added
            step *= 4
        tiles.append(part)
    return jnp.concatenate(tiles, axis=1)


def total(values):
    return jnp.sum(values, axis=0, keepdims=True)


def wide_total(*rows):
    stacked = jnp.concatenate(list(rows) + [rows[0]] * (8 - len(rows)), axis=0)
    sums = group_total(stacked)
    return [sums[i : i + 1] for i in range(len(rows))]


def norm_stats(values, mask, group_size):
    mean = wide_total(total(values))[0] / group_size
    centered = (values - mean) * mask
    variance = wide_total(total(centered * centered))[0] / group_size
    return mean, lax.rsqrt(variance + epsilon)


def silu_norm(values, mean, inverse, gain, shift, mask):
    scale = 0.5 * inverse * gain
    half = values * scale + (0.5 * shift - mean * scale)
    return (half + half * jnp.tanh(half)) * mask


def norm_back(grad, normal, inverse, mask, group_size, gain):
    plain_row = total(grad)
    cross_row = total(grad * normal)
    plain, cross = [v / group_size for v in wide_total(plain_row * gain, cross_row * gain)]
    grad_in = grad * (inverse * gain) - mask * (plain * inverse + normal * (cross * inverse))
    return grad_in, cross_row, plain_row


def silu_slope(u):
    half = 0.5 * u
    t = jnp.tanh(half)
    return (0.5 + 0.5 * t) * (1.0 + half * (1.0 - t))


def mm(a, b):
    return jnp.dot(a, b, preferred_element_type=F32)


def mm_nt(a, b):
    return lax.dot_general(a, b, (((1,), (1,)), ((), ())), preferred_element_type=F32)


def mm_tn(a, b):
    return lax.dot_general(a, b, (((0,), (0,)), ((), ())), preferred_element_type=F32)


def fill_shifts(shift_ref, values, stride):
    unused, cols = pixel_col(stride)
    lanes = values.shape[1]
    zeros = jnp.zeros((PAD, lanes), BF16)
    for q in range(3):
        shift_ref[q, 0:PAD, :] = zeros
        shift_ref[q, PAD + PIX : 2 * PAD + PIX, :] = zeros
    left = jnp.where(cols == 0, 0.0, pltpu.roll(values, 1, 0))
    right = jnp.where(cols == stride - 1, 0.0, pltpu.roll(values, PIX - 1, 0))
    shift_ref[0, PAD : PAD + PIX, :] = left.astype(BF16)
    shift_ref[1, PAD : PAD + PIX, :] = values.astype(BF16)
    shift_ref[2, PAD : PAD + PIX, :] = right.astype(BF16)


def tap(shift_ref, p, q, stride, first=0, count=PIX):
    start = pl.multiple_of(PAD + first + (p - 1) * stride, 16)
    return shift_ref[q, pl.ds(start, count), :]


def conv_forward(shift_ref, weight_ref, stride, out_ref, tile=256):
    for first in range(0, PIX, tile):
        stacked = jnp.concatenate(
            [tap(shift_ref, p, q, stride, first, tile) for p in range(3) for q in range(3)], axis=1
        )
        out_ref[first : first + tile, :] = mm(stacked, weight_ref[...])


def conv_backward(shift_ref, weight_ref, stride, out_ref, tile=256):
    channels = weight_ref.shape[1]
    for first in range(0, PIX, tile):
        acc = None
        for p in range(3):
            for q in range(3):
                row = (8 - (3 * p + q)) * channels
                part = mm_nt(
                    tap(shift_ref, p, q, stride, first, tile), weight_ref[row : row + channels, :]
                )
                acc = part if acc is None else acc + part
        out_ref[first : first + tile, :] = acc


def assemble(out_ref, facts, h, pieces):
    unused, tall, stride, width = facts
    own, partner, received, partner_received = pieces
    other = h ^ 1

    @pl.when(tall)
    def _():
        for ref, index in (
            (own, h),
            (partner, other),
            (received, h ^ 2),
            (partner_received, other ^ 2),
        ):
            out_ref[pl.ds(pl.multiple_of(96 * index, 16), 96), :] = ref[0:96, :]
        out_ref[384:512, :] = jnp.zeros((128, out_ref.shape[1]), out_ref.dtype)

    @pl.when(jnp.logical_not(tall))
    def _():
        low = h & 1
        out_ref[pl.ds(pl.multiple_of(192 * low, 16), 192), :] = own[...]
        out_ref[pl.ds(pl.multiple_of(192 * (1 - low), 16), 192), :] = partner[...]

        @pl.when(low == 0)
        def _():
            out_ref[384:512, :] = received[0:128, :]

        @pl.when(low == 1)
        def _():
            out_ref[384:512, :] = partner_received[0:128, :]


def split_out(full_ref, facts, h, own_ref, send_ref):
    unused, tall, stride, width = facts
    send_h = h ^ 2

    @pl.when(tall)
    def _():
        own_ref[0:96, :] = full_ref[pl.ds(pl.multiple_of(96 * h, 16), 96), :]
        own_ref[96:192, :] = jnp.zeros((96, own_ref.shape[1]), own_ref.dtype)
        send_ref[0:96, :] = full_ref[pl.ds(pl.multiple_of(96 * send_h, 16), 96), :]
        send_ref[96:128, :] = jnp.zeros((32, own_ref.shape[1]), own_ref.dtype)

    @pl.when(jnp.logical_not(tall))
    def _():
        own_ref[...] = full_ref[pl.ds(pl.multiple_of(192 * (h & 1), 16), 192), :]
        send_ref[...] = full_ref[384:512, :]


GAIN1, SHIFT1, BIAS1, GAIN2, SHIFT2, BIAS2, GAIN3, SHIFT3, QB, VB, PB = range(11)
VECS = 16


def vec(vec_ref, index):
    return vec_ref[index : index + 1, :]


def pack(src, facts, dst, wide_rows):
    image, tall, stride, width = facts

    @pl.when(tall)
    def _():
        for row in range(6):
            dst[16 * row : 16 * row + 16, :] = src[image, row, 0:16, :]
        dst[96 : dst.shape[0], :] = jnp.zeros((dst.shape[0] - 96, dst.shape[1]), dst.dtype)

    @pl.when(jnp.logical_not(tall))
    def _():
        for row in range(wide_rows):
            dst[32 * row : 32 * row + 32, :] = src[image, row]


def pack_kernel(bucket_hbm, x_hbm, kinds, away_x, home_x, bucket_ref, x_ref, sems):
    copies = (
        pltpu.make_async_copy(bucket_hbm, bucket_ref, sems.at[0]),
        pltpu.make_async_copy(x_hbm, x_ref, sems.at[1]),
    )
    for copy in copies:
        copy.start()
    for copy in copies:
        copy.wait()
    h, home, away = place(bucket_ref)
    kinds[0] = bucket_ref[0]
    kinds[1] = bucket_ref[1]
    pack(x_ref, away, away_x, 4)
    pack(x_ref, home, home_x, 6)


def stack_kernel(kinds, cot_ref, *refs):
    h, home, away = place(kinds)
    out_ref, away_c, home_c = refs[-3:]
    count = len(refs) - 3
    for index, ref in enumerate(refs[:count]):
        out_ref[index : index + 1, :] = ref[...]
    out_ref[count:, :] = jnp.zeros((VECS - count, out_ref.shape[1]), F32)
    pack(cot_ref, away, away_c, 4)
    pack(cot_ref, home, home_c, 6)


def first_kernel(
    bucket_ref, own, partner, received, partner_received, vecs, weight1,
    image_ref, conv_ref, act2_ref, stats_ref, act1_t, act2_t, send_t,
    shift_ref,
):
    h, home, away = place(bucket_ref)
    stride = home[2]
    mask, pixels = pixel_mask(home)
    channels = vecs.shape[1]
    group_size = pixels * (channels // GROUPS)
    assemble(image_ref, home, h, (own, partner, received, partner_received))
    values = image_ref[...].astype(F32) * mask
    mean1, inverse1 = norm_stats(values, mask, group_size)
    act = silu_norm(values, mean1, inverse1, vec(vecs, GAIN1), vec(vecs, SHIFT1), mask)
    fill_shifts(shift_ref, act, stride)
    act1_t[...] = act.astype(BF16).T
    conv_forward(shift_ref, weight1, stride, conv_ref)
    values = (conv_ref[...] + vec(vecs, BIAS1)) * mask
    conv_ref[...] = values
    mean2, inverse2 = norm_stats(values, mask, group_size)
    act = silu_norm(values, mean2, inverse2, vec(vecs, GAIN2), vec(vecs, SHIFT2), mask)
    act = act.astype(BF16)
    act2_ref[...] = act
    act2_t[...] = act.T
    half = pl.multiple_of((h & 1) * (channels // 2), 16)
    send_t[0] = act1_t[pl.ds(half, channels // 2), :]
    send_t[1] = act2_t[pl.ds(half, channels // 2), :]
    stats_ref[0:1, :] = mean1
    stats_ref[1:2, :] = inverse1
    stats_ref[2:3, :] = mean2
    stats_ref[3:4, :] = inverse2
    stats_ref[4:8, :] = jnp.zeros((4, channels), F32)


def second_kernel(
    bucket_ref, image_ref, act2_ref, own, partner, received, partner_received, vecs,
    weight2, wq, wk, wv, wp,
    middle_ref, mixed_ref, grad2_ref, grad_middle_ref, attn_keep, attn_send, vec_ref,
    block_keep, block_send,
    shift_ref, full_ref, grads_ref, sum_ref,
):
    h, home, away = place(bucket_ref)
    stride = home[2]
    mask, pixels = pixel_mask(home)
    channels = vecs.shape[1]
    group_size = pixels * (channels // GROUPS)
    scaling = channels ** (-0.5)
    assemble(full_ref, home, h, (own, partner, received, partner_received))
    fill_shifts(shift_ref, act2_ref[...].astype(F32), stride)
    conv_forward(shift_ref, weight2, stride, middle_ref)
    middle = mask * (image_ref[...].astype(F32) + (middle_ref[...] + vec(vecs, BIAS2)))
    middle_ref[...] = middle
    mean3, inverse3 = norm_stats(middle, mask, group_size)
    normal = (middle - mean3) * inverse3
    normed = (normal * vec(vecs, GAIN3) + vec(vecs, SHIFT3)).astype(BF16)
    wide = jnp.concatenate([wq[...], wk[...], wv[...]], axis=1)
    joint = mm(normed, wide)
    queries = (joint[:, 0:channels] + vec(vecs, QB)).astype(BF16)
    keys = joint[:, channels : 2 * channels].astype(BF16)
    values = (joint[:, 2 * channels :] + vec(vecs, VB)).astype(BF16)
    lanes = lax.broadcasted_iota(jnp.int32, (1, PIX), 1)
    key_cols = lanes & (stride - 1)
    key_valid = (key_cols < home[3]) & (lanes < jnp.where(home[1], 384, 512))
    scores = jnp.where(key_valid, mm_nt(queries, keys) * scaling, -1000000000.0)
    grad_top = full_ref[...].astype(F32) * mask
    grad_rows = grad_top.astype(BF16)
    grad_mixed = mm_nt(grad_rows, wp[...]).astype(BF16)
    grad_soft = mm_nt(grad_mixed, values)
    raised = jnp.exp(scores - jnp.max(scores, axis=1, keepdims=True))
    soft = raised * (1.0 / jnp.sum(raised, axis=1, keepdims=True))
    soft16 = soft.astype(BF16)
    mixed = mm(soft16, values).astype(BF16)
    mixed_ref[...] = mixed

    grad_values = mm_tn(soft16, grad_mixed).astype(BF16)
    grad_scores = soft * (grad_soft - jnp.sum(soft * grad_soft, axis=1, keepdims=True))
    grad_scores = grad_scores.astype(BF16)
    grad_queries = (mm(grad_scores, keys) * scaling).astype(BF16)
    grad_keys = (mm_tn(grad_scores, queries) * scaling).astype(BF16)
    grads_ref[:, 0:channels] = grad_queries
    grads_ref[:, channels : 2 * channels] = grad_keys
    grads_ref[:, 2 * channels : 3 * channels] = grad_values
    grads_ref[:, 3 * channels : 4 * channels] = grad_rows
    grad_normed = mm_nt(grads_ref[:, 0 : 3 * channels], wide)
    grad_in, gain_grad, shift_grad = norm_back(
        grad_normed, normal, inverse3, mask, group_size, vec(vecs, GAIN3)
    )
    grad_middle = mask * (grad_top + grad_in)
    grad_middle_ref[...] = grad_middle
    grad2 = grad_middle.astype(BF16)
    grad2_ref[...] = grad2
    vec_ref[0:1, :] = gain_grad
    vec_ref[1:2, :] = shift_grad
    vec_ref[2:3, :] = total(grad_queries.astype(F32))
    vec_ref[3:4, :] = total(grad_values.astype(F32))
    vec_ref[4:5, :] = total(grad_top)
    vec_ref[5:6, :] = total(grad2.astype(F32))
    vec_ref[6:8, :] = jnp.zeros((2, channels), F32)

    keep_at = pl.multiple_of(BLK * h, BLK)
    send_at = pl.multiple_of(BLK * (h ^ 2), BLK)
    block_keep[...] = grad2_ref[:, pl.ds(keep_at, BLK)]
    block_send[...] = grad2_ref[:, pl.ds(send_at, BLK)]

    def blocks(index):
        start = index * channels
        return [
            grads_ref[:, pl.ds(pl.multiple_of(start + BLK * h, BLK), BLK)],
            grads_ref[:, pl.ds(pl.multiple_of(start + BLK * (h ^ 2), BLK), BLK)],
        ]

    sum_ref[:, 0 : 6 * BLK] = mm_tn(normed, jnp.concatenate(blocks(0) + blocks(1) + blocks(2), axis=1))
    sum_ref[:, 6 * BLK : 8 * BLK] = mm_tn(mixed, jnp.concatenate(blocks(3), axis=1))
    mine = lax.axis_index("batch") & 1
    pairs = attn_keep.shape[0]
    rows = channels // (2 * pairs)
    for pair in range(pairs):
        for dst, which in ((attn_keep, mine), (attn_send, 1 - mine)):
            part = sum_ref[pl.ds(pl.multiple_of((2 * pair + which) * rows, 8), rows), :].astype(BF16)
            for index in range(4):
                at = index * 2 * BLK
                dst[pair, index * rows : (index + 1) * rows, :] = part[:, at : at + 2 * BLK]


def third_kernel(
    bucket_ref, grad2_ref, conv_ref, stats_ref, vecs, weight2,
    grad1_ref, block_keep, block_send, vec_ref,
    shift_ref, acc_ref,
):
    h, home, away = place(bucket_ref)
    stride = home[2]
    mask, pixels = pixel_mask(home)
    channels = vecs.shape[1]
    group_size = pixels * (channels // GROUPS)
    fill_shifts(shift_ref, grad2_ref[...].astype(F32), stride)
    conv_backward(shift_ref, weight2, stride, acc_ref)
    inverse = stats_ref[3:4, :]
    normal = (conv_ref[...] - stats_ref[2:3, :]) * inverse
    u = normal * vec(vecs, GAIN2) + vec(vecs, SHIFT2)
    grad = mask * acc_ref[...] * silu_slope(u)
    grad_in, gain_grad, shift_grad = norm_back(
        grad, normal, inverse, mask, group_size, vec(vecs, GAIN2)
    )
    grad1 = grad_in.astype(BF16)
    grad1_ref[...] = grad1
    vec_ref[0:1, :] = gain_grad
    vec_ref[1:2, :] = shift_grad
    vec_ref[2:3, :] = total(grad1.astype(F32))
    vec_ref[3:8, :] = jnp.zeros((5, channels), F32)
    block_keep[...] = grad1_ref[:, pl.ds(pl.multiple_of(BLK * h, BLK), BLK)]
    block_send[...] = grad1_ref[:, pl.ds(pl.multiple_of(BLK * (h ^ 2), BLK), BLK)]


def fourth_kernel(
    bucket_ref, grad1_ref, image_ref, stats_ref, grad_middle_ref, vecs, weight1, vec_a, vec_b,
    grad_own, send_ref, vec_keep, vec_send,
    shift_ref, acc_ref, full_ref, vec_ref,
):
    h, home, away = place(bucket_ref)
    stride = home[2]
    mask, pixels = pixel_mask(home)
    channels = vecs.shape[1]
    group_size = pixels * (channels // GROUPS)
    fill_shifts(shift_ref, grad1_ref[...].astype(F32), stride)
    conv_backward(shift_ref, weight1, stride, acc_ref)
    inverse = stats_ref[1:2, :]
    normal = (image_ref[...].astype(F32) * mask - stats_ref[0:1, :]) * inverse
    u = normal * vec(vecs, GAIN1) + vec(vecs, SHIFT1)
    grad = mask * acc_ref[...] * silu_slope(u)
    grad_in, gain_grad, shift_grad = norm_back(
        grad, normal, inverse, mask, group_size, vec(vecs, GAIN1)
    )
    full_ref[...] = (mask * (grad_middle_ref[...] + grad_in)).astype(BF16)
    split_out(full_ref, home, h, grad_own, send_ref)
    vec_ref[0:6, :] = vec_a[0:6, :]
    vec_ref[6:9, :] = vec_b[0:3, :]
    vec_ref[9:10, :] = gain_grad
    vec_ref[10:11, :] = shift_grad
    vec_ref[11:VECS, :] = jnp.zeros((VECS - 11, channels), F32)
    pairs = vec_keep.shape[0]
    rows = channels // (2 * pairs)
    mine = (lax.axis_index("batch") & 1) == 1
    for pair in range(pairs):
        parts = []
        for shard in (2 * pair, 2 * pair + 1):
            start = shard * rows
            tile = start // BLK * BLK
            part = vec_ref[:, tile : tile + BLK]
            parts.append(part if start == tile else pltpu.roll(part, BLK - (start - tile), 1))
        vec_keep[pair] = jnp.where(mine, parts[1], parts[0]).astype(BF16)
        vec_send[pair] = jnp.where(mine, parts[0], parts[1]).astype(BF16)


def output_kernel(
    bucket_ref, middle_ref, mixed_ref, vecs, wp, grad_send, out_own, send_ref, full_ref
):
    h, home, away = place(bucket_ref)
    mask, pixels = pixel_mask(home)
    projected = mm(mixed_ref[...], wp[...]) + vec(vecs, PB)
    full_ref[...] = (mask * (middle_ref[...] + projected)).astype(BF16)
    split_out(full_ref, home, h, out_own, send_ref.at[0])
    send_ref[1] = grad_send[...]


def weight_kernel(
    bucket_ref, act_t, half_t, partner_half_t, block_own, block_away,
    keep_ref, send_ref, left_ref, right_ref, shift_ref, sum_ref, *, layer,
):
    h, home, away = place(bucket_ref)
    channels = act_t.shape[0]
    half = channels // 2
    left_ref[:, 0:PIX] = act_t[...]
    left_ref[pl.ds(pl.multiple_of((h & 1) * half, 16), half), PIX : 2 * PIX] = half_t[layer]
    left_ref[pl.ds(pl.multiple_of((1 - (h & 1)) * half, 16), half), PIX : 2 * PIX] = (
        partner_half_t[layer]
    )
    for index, (facts, block) in enumerate(((home, block_own), (away, block_away))):
        stride = facts[2]
        fill_shifts(shift_ref, block[...].astype(F32), stride)
        for p in range(3):
            for q in range(3):
                column = (3 * p + q) * BLK
                right_ref[index * PIX : (index + 1) * PIX, column : column + BLK] = tap(
                    shift_ref, 2 - p, 2 - q, stride
                )
    joint = mm(left_ref[...], right_ref[...])
    for t in range(9):
        sum_ref[t * channels : (t + 1) * channels, :] = joint[:, t * BLK : (t + 1) * BLK]
    mine = lax.axis_index("batch") & 1
    pairs = keep_ref.shape[0]
    rows = 9 * channels // (2 * pairs)
    for pair in range(pairs):
        for dst, which in ((keep_ref, mine), (send_ref, 1 - mine)):
            shard = 2 * pair + which
            dst[pair] = sum_ref[pl.ds(pl.multiple_of(shard * rows, 8), rows), :].astype(BF16)


def route_kernel(keep_ref, got_ref, *outs, bit, first):
    ways = len(outs) if first == 0 else len(outs) // 2
    group = (lax.axis_index("batch") >> bit) & (ways - 1)
    rows = keep_ref.shape[1]
    for step, dst in enumerate(outs[-ways:]):
        which = group ^ step
        for index in range(dst.shape[0]):
            at = index * ways + which
            dst[index, first : first + rows, :] = (
                keep_ref[at].astype(F32) + got_ref[at].astype(F32)
            ).astype(BF16)


def total_of(refs):
    added = refs[0].astype(F32)
    for ref in refs[1:]:
        added = added + ref.astype(F32)
    return added


def sum_kernel(*refs):
    refs[-1][...] = total_of([ref[0] for ref in refs[:-1]]).astype(BF16)


def join_kernel(own_ref, far_ref, near_ref, diagonal_ref, *out_refs):
    h = lax.axis_index("height")
    first = 0
    for dst in [ref for ref in out_refs if ref.shape[0] > 1]:
        rows = dst.shape[0]
        for ref, index in ((own_ref, h), (far_ref, h ^ 2), (near_ref, h ^ 1), (diagonal_ref, h ^ 3)):
            dst[:, pl.ds(pl.multiple_of(BLK * index, BLK), BLK)] = ref[first : first + rows, :].astype(F32)
        first += rows
    if own_ref.shape[0] > first:
        own, far = own_ref[first:, :].astype(F32), far_ref[first:, :].astype(F32)
        near, diagonal = near_ref[first:, :].astype(F32), diagonal_ref[first:, :].astype(F32)
        sums = 0.5 * ((own + near) + (far + diagonal))
        for index, dst in enumerate([ref for ref in out_refs if ref.shape[0] == 1]):
            dst[...] = sums[index : index + 1, 0 : dst.shape[1]]


def join_attn_kernel(own_ref, far_ref, near_ref, diagonal_ref, *out_refs):
    h = lax.axis_index("height")
    rows = out_refs[0].shape[0]
    for first, second, index in ((own_ref, far_ref, h), (near_ref, diagonal_ref, h ^ 1)):
        for position in range(2):
            lane, other = position * BLK, (1 - position) * BLK
            column = pl.multiple_of(BLK * (index ^ (2 * position)), BLK)
            for number, dst in enumerate(out_refs):
                at = number * rows
                dst[:, pl.ds(column, BLK)] = first[at : at + rows, lane : lane + BLK].astype(
                    F32
                ) + second[at : at + rows, other : other + BLK].astype(F32)


def unpack_kernel(bucket_ref, out_own, grad_own, away_ref, out_ref, grad_ref):
    h, home, away = place(bucket_ref)
    for own, received, dst in (
        (out_own, away_ref.at[0], out_ref),
        (grad_own, away_ref.at[1], grad_ref),
    ):
        channels = dst.shape[3]
        for facts, src, wide_rows in ((away, received, 4), (home, own, 6)):
            image, tall, stride, width = facts

            @pl.when(tall)
            def _():
                for row in range(6):
                    dst[image, row, 0:16, :] = src[16 * row : 16 * row + 16, :]
                    dst[image, row, 16:32, :] = jnp.zeros((16, channels), dst.dtype)

            @pl.when(jnp.logical_not(tall))
            def _():
                for row in range(wide_rows):
                    dst[image, row] = src[32 * row : 32 * row + 32, :]
                for row in range(wide_rows, 6):
                    dst[image, row] = jnp.zeros((32, channels), dst.dtype)

            if wide_rows == 4:

                @pl.when(jnp.logical_not(tall) & (h == 3))
                def _():
                    for row in range(6):
                        dst[image, row] = jnp.zeros((32, channels), dst.dtype)


def call(kernel, name, outs, scratch, vmem, *operands, smem=1, any_from=99, aliases={}):
    specs = [SM] * smem + [VM] * (len(operands) - smem)
    specs = [HB if i >= any_from else spec for i, spec in enumerate(specs)]
    return pl.pallas_call(
        kernel,
        name=name,
        out_shape=[jax.ShapeDtypeStruct(shape, dtype) for shape, dtype in outs],
        in_specs=specs,
        out_specs=[SM if dtype == jnp.int32 else VM for shape, dtype in outs],
        scratch_shapes=[
            pltpu.SemaphoreType.DMA(shape)
            if dtype is None
            else (pltpu.SMEM if dtype == jnp.int32 else pltpu.VMEM)(shape, dtype)
            for shape, dtype in scratch
        ],
        input_output_aliases=aliases,
        compiler_params=pltpu.CompilerParams(vmem_limit_bytes=vmem << 20),
        cost_estimate=pl.CostEstimate(
            flops=int(LENGTH.get(name, 0.02) * RATE), bytes_accessed=1024, transcendentals=0
        ),
    )(*operands)


def on_device(
    inputs,
    bucket,
    norm1_gain,
    norm1_shift,
    conv1_weight,
    conv1_bias,
    norm2_gain,
    norm2_shift,
    conv2_weight,
    conv2_bias,
    norm3_gain,
    norm3_shift,
    query_weight,
    query_bias,
    key_weight,
    value_weight,
    value_bias,
    proj_weight,
    proj_bias,
    cotangent,
):
    C = inputs.shape[-1]
    batches = lax.axis_size("batch")
    bits = batches.bit_length() - 1
    shard_rows = 9 * C // batches
    small_rows = C // batches

    def row(v):
        return v.reshape(1, C)

    def to_core(v):
        return lax.ppermute(v, "height", [(i, i ^ 1) for i in range(4)])

    def to_chip(v):
        return lax.ppermute(v, "height", [(i, i ^ 2) for i in range(4)])

    def to_batch(v, change):
        return lax.ppermute(v, "batch", [(i, i ^ change) for i in range(batches)])

    def after(v, *others):
        return lax.optimization_barrier((v,) + others)[0]

    def together(got, *others):
        return list(lax.optimization_barrier((*got, *others))[: len(got)])

    img16 = ((PIX, C), BF16)
    img32 = ((PIX, C), F32)
    rows8 = ((8, C), F32)
    block = ((PIX, BLK), BF16)
    turned = ((C, PIX), BF16)
    shifts = ((3, PIX + 2 * PAD, C), BF16)

    kinds, away_x, home_x = call(
        pack_kernel, "pack",
        [((2,), jnp.int32), ((128, C), BF16), ((192, C), BF16)],
        [((2,), jnp.int32), (inputs.shape, BF16), ((2,), None)], 54, bucket, inputs,
        smem=0, any_from=0,
    )
    vectors = (
        norm1_gain, norm1_shift, conv1_bias, norm2_gain, norm2_shift, conv2_bias,
        norm3_gain, norm3_shift, query_bias, value_bias, proj_bias,
    )
    recv_x = to_chip(away_x)
    core_x = to_core(home_x)
    vecs, away_c, home_c = call(
        stack_kernel, "stack", [((VECS, C), F32), ((160, C), BF16), ((192, C), BF16)], [], 8,
        kinds, cotangent, *[row(v) for v in vectors],
    )
    recv_c = to_chip(away_c)
    core_c = to_core(home_c)
    core_recv_c = lax.ppermute(away_c, "height", [(i, i ^ 3) for i in range(4)])
    core_recv_x = to_core(after(recv_x, vecs))

    image, conv, act2, stats, act1_t, act2_t, send_t = call(
        first_kernel, "first",
        [img16, img32, img16, rows8, turned, turned, ((2, C // 2, PIX), BF16)],
        [shifts], 14,
        kinds, home_x, core_x, recv_x, core_recv_x, vecs, conv1_weight,
    )
    half_t = to_chip(send_t)
    core_half_t = to_core(half_t)

    attn_out = ((batches // 2, 4 * small_rows, 2 * BLK), BF16)
    middle, mixed, grad2, grad_middle, attn_keep, attn_send, vec_a, block2, block2_send = call(
        second_kernel, "second",
        [img32, img16, img16, img32, attn_out, attn_out, rows8, block, block],
        [shifts, img16, ((PIX, 4 * C), BF16), ((C, 8 * BLK), F32)], 24,
        kinds, image, act2, home_c, core_c, recv_c, core_recv_c, vecs,
        conv2_weight, query_weight, key_weight, value_weight, proj_weight,
    )
    block2_away = to_chip(block2_send)
    attn_got = to_batch(attn_send, 1)

    grad1, block1, block1_send, vec_b = call(
        third_kernel, "third",
        [img16, block, block, rows8],
        [shifts, img32], 14,
        kinds, grad2, conv, stats, vecs, conv2_weight,
    )
    block1_away = to_chip(block1_send)

    def weight_grad(name, act_t, index, own, away):
        return call(
            functools.partial(weight_kernel, layer=index), name,
            [((batches // 2, shard_rows, BLK), BF16)] * 2,
            [((C, 2 * PIX), BF16), ((2 * PIX, 9 * BLK), BF16), ((3, PIX + 2 * PAD, BLK), BF16),
             ((9 * C, BLK), F32)],
            18, kinds, act_t, half_t, core_half_t, own, away,
        )

    keep2, send2 = weight_grad("weight2", act2_t, 1, after(block2, block1), block2_away)
    got2 = to_batch(send2, 1)

    def spread(name, bit, keep, got, tail=None, behind=()):
        ways = 1 << min(2, bits - bit)
        rows = keep.shape[1]
        shape = (keep.shape[0] // ways, rows + (VECS if tail else 0), keep.shape[2])
        parts = call(
            functools.partial(route_kernel, bit=bit, first=0), name + str(bit),
            [(shape, BF16)] * ways, [], 16, keep, got, smem=0,
        )
        if tail:
            parts = call(
                functools.partial(route_kernel, bit=bit, first=rows), name + "tail",
                [(shape, BF16)] * ways, [], 16, *tail, *parts, smem=0,
                aliases={2 + j: j for j in range(ways)},
            )
        return parts, [to_batch(after(parts[j], *behind), j << bit) for j in range(1, ways)]

    def finish(name, parts, got):
        for bit in range(3, bits, 2):
            added = total_of([parts[0]] + got).astype(BF16)
            parts, got = spread(name, bit, added, jnp.zeros_like(added))
        return call(
            sum_kernel, "sum" + name, [(parts[0].shape[1:], BF16)], [], 8, parts[0], *got, smem=0
        )[0]

    def gather(shard, *between):
        far = to_chip(shard)
        near = to_core(shard)
        return shard, far, near, to_core(after(far, *between))

    parts_a, got_a = spread("routea", 1, after(attn_keep, send2), attn_got)
    keep1, send1 = weight_grad("weight1", act1_t, 0, after(block1, *parts_a), block1_away)
    got1 = to_batch(send1, 1)
    shard_a = finish("routea", parts_a, together(got_a, send1))
    grad_own, grad_send, vec_keep, vec_send = call(
        fourth_kernel, "fourth",
        [((192, C), BF16), ((128, C), BF16),
         ((batches // 2, VECS, BLK), BF16), ((batches // 2, VECS, BLK), BF16)],
        [shifts, img32, img16, ((VECS, C), F32)], 14,
        kinds, after(grad1, send1), image, stats, grad_middle, vecs, conv1_weight, vec_a, vec_b,
    )
    vec_got = to_batch(vec_send, 1)
    parts_b, got_b = spread("routeb", 1, after(keep2, vec_keep, shard_a), got2)
    parts_c, got_c = spread("routec", 1, keep1, got1, (vec_keep, vec_got), behind=got_b)
    shard_b = finish("routeb", parts_b, together(got_b, parts_c[0]))
    out_own, image_send = call(
        output_kernel, "output", [((192, C), BF16), ((2, 128, C), BF16)], [img16], 10,
        kinds, after(middle, shard_b), mixed, vecs, proj_weight, grad_send,
    )
    image_away = to_chip(image_send)
    gathered_a = gather(shard_a)
    gathered_b = gather(shard_b)
    shard_c = finish(
        "routec", parts_c, together(got_c[::-1], gathered_b[1], gathered_a[1])
    )
    small = call(
        join_attn_kernel, "joina", [((small_rows, C), F32)] * 4, [], 8,
        after(gathered_a[0], shard_c), *gathered_a[1:], smem=0,
    )
    (whole2,) = call(
        join_kernel, "joinb", [((shard_rows, C), F32)], [], 8,
        after(gathered_b[0], shard_c), *gathered_b[1:], smem=0,
    )
    outputs, input_grad = call(
        unpack_kernel, "unpack",
        [(inputs.shape, BF16)] * 2, [], 8,
        kinds, out_own, grad_own, after(image_away, shard_c),
    )
    gathered_c = gather(shard_c, whole2, outputs, *small)
    whole1, *sums = call(
        join_kernel, "joinc", [((shard_rows, C), F32)] + [((1, small_rows), F32)] * 11, [], 8,
        *gathered_c, smem=0,
    )
    v = [row.reshape(small_rows) for row in sums]

    return (
        outputs, input_grad,
        v[9], v[10], whole1, v[8],
        v[6], v[7], whole2, v[5],
        v[0], v[1],
        small[0], v[2], small[1], small[2], v[3], small[3], v[4],
    )


def solution(mesh):
    image = P("batch", "height", None, None)
    vector = P("batch")
    matrix = P("batch", None)
    return jax.shard_map(
        on_device,
        mesh=mesh,
        in_specs=(image, vector) + (P(),) * 17 + (image,),
        out_specs=(
            image, image,
            vector, vector, matrix, vector,
            vector, vector, matrix, vector,
            vector, vector,
            matrix, vector, matrix, matrix, vector, matrix, vector,
        ),
        check_vma=False,
    )
```

```python
import functools

import jax
import jax.numpy as jnp
from jax import lax
from jax.experimental import pallas as pl
from jax.experimental.pallas import tpu as pltpu
from jax.sharding import PartitionSpec as P

GROUPS = 32
UNIT = 8
PIX = 512
PAD = 32
BLK = 128
F32 = jnp.float32
BF16 = jnp.bfloat16
epsilon = 1e-05

VM = pl.BlockSpec(memory_space=pltpu.VMEM)
SM = pl.BlockSpec(memory_space=pltpu.SMEM)
HB = pl.BlockSpec(memory_space=pltpu.HBM)
RATE = 1 << 30
LENGTH = {
    "pack": 10, "stack": 10, "first": 0.02, "second": 30, "third": 20, "fourth": 0.5, "weight2": 1, "weight1": 3, "routeb1": 20,
}


def place(bucket_ref):
    h = lax.axis_index("height")
    upper = lax.div(h, 2)
    tall_first = bucket_ref[0] == 1
    tall_image = jnp.where(tall_first, 0, 1)
    home = jnp.where(upper == 1, tall_image, 1 - tall_image)
    away = 1 - home

    def facts(image):
        kind = bucket_ref[image]
        tall = kind == 1
        stride = jnp.where(tall, 2 * UNIT, 4 * UNIT)
        width = jnp.where(kind == 0, 3 * UNIT, stride)
        return (image, tall, stride, width)

    return h, facts(home), facts(away)


def pixel_col(stride, lanes=1):
    rows = lax.broadcasted_iota(jnp.int32, (PIX, lanes), 0)
    return rows, rows & (stride - 1)


def pixel_mask(facts):
    unused, tall, stride, width = facts
    rows, cols = pixel_col(stride)
    limit = jnp.where(tall, 6 * UNIT * UNIT, 8 * UNIT * UNIT)
    mask = jnp.where((cols < width) & (rows < limit), 1.0, 0.0).astype(F32)
    size = jnp.where(tall | (width == 3 * UNIT), 6 * UNIT * UNIT, 8 * UNIT * UNIT)
    return mask, size.astype(F32)


def group_total(rows):
    members = rows.shape[1] // GROUPS
    lane = lax.broadcasted_iota(jnp.int32, (rows.shape[0], BLK), 1)
    tiles = []
    for tile in range(rows.shape[1] // BLK):
        part = rows[:, tile * BLK : (tile + 1) * BLK]
        step = 1
        while step < members:
            place_in_four = (lane // step) & 3
            added = part
            for d in (1, 2, 3):
                up = pltpu.roll(part, BLK - d * step, 1)
                down = pltpu.roll(part, (4 - d) * step, 1)
                added = added + jnp.where(place_in_four + d < 4, up, down)
            part = added
            step *= 4
        tiles.append(part)
    return jnp.concatenate(tiles, axis=1)


def total(values):
    return jnp.sum(values, axis=0, keepdims=True)


def wide_total(*rows):
    stacked = jnp.concatenate(list(rows) + [rows[0]] * (8 - len(rows)), axis=0)
    sums = group_total(stacked)
    return [sums[i : i + 1] for i in range(len(rows))]


def norm_stats(values, mask, group_size):
    mean = wide_total(total(values))[0] / group_size
    centered = (values - mean) * mask
    variance = wide_total(total(centered * centered))[0] / group_size
    return mean, lax.rsqrt(variance + epsilon)


def silu_norm(values, mean, inverse, gain, shift, mask):
    scale = 0.5 * inverse * gain
    half = values * scale + (0.5 * shift - mean * scale)
    return (half + half * jnp.tanh(half)) * mask


def norm_back(grad, normal, inverse, mask, group_size, gain):
    plain_row = total(grad)
    cross_row = total(grad * normal)
    plain, cross = [v / group_size for v in wide_total(plain_row * gain, cross_row * gain)]
    grad_in = grad * (inverse * gain) - mask * (plain * inverse + normal * (cross * inverse))
    return grad_in, cross_row, plain_row


def silu_slope(u):
    half = 0.5 * u
    t = jnp.tanh(half)
    return (0.5 + 0.5 * t) * (1.0 + half * (1.0 - t))


def mm(a, b):
    return jnp.dot(a, b, preferred_element_type=F32)


def mm_nt(a, b):
    return lax.dot_general(a, b, (((1,), (1,)), ((), ())), preferred_element_type=F32)


def mm_tn(a, b):
    return lax.dot_general(a, b, (((0,), (0,)), ((), ())), preferred_element_type=F32)


def fill_shifts(shift_ref, values, stride):
    unused, cols = pixel_col(stride)
    lanes = values.shape[1]
    zeros = jnp.zeros((PAD, lanes), BF16)
    for q in range(3):
        shift_ref[q, 0:PAD, :] = zeros
        shift_ref[q, PAD + PIX : 2 * PAD + PIX, :] = zeros
    left = jnp.where(cols == 0, 0.0, pltpu.roll(values, 1, 0))
    right = jnp.where(cols == stride - 1, 0.0, pltpu.roll(values, PIX - 1, 0))
    shift_ref[0, PAD : PAD + PIX, :] = left.astype(BF16)
    shift_ref[1, PAD : PAD + PIX, :] = values.astype(BF16)
    shift_ref[2, PAD : PAD + PIX, :] = right.astype(BF16)


def tap(shift_ref, p, q, stride, first=0, count=PIX):
    start = pl.multiple_of(PAD + first + (p - 1) * stride, 16)
    return shift_ref[q, pl.ds(start, count), :]


def conv_forward(shift_ref, weight_ref, stride, out_ref, tile=256):
    for first in range(0, PIX, tile):
        stacked = jnp.concatenate(
            [tap(shift_ref, p, q, stride, first, tile) for p in range(3) for q in range(3)], axis=1
        )
        out_ref[first : first + tile, :] = mm(stacked, weight_ref[...])


def conv_backward(shift_ref, weight_ref, stride, out_ref, tile=256):
    channels = weight_ref.shape[1]
    for first in range(0, PIX, tile):
        acc = None
        for p in range(3):
            for q in range(3):
                row = (8 - (3 * p + q)) * channels
                part = mm_nt(
                    tap(shift_ref, p, q, stride, first, tile), weight_ref[row : row + channels, :]
                )
                acc = part if acc is None else acc + part
        out_ref[first : first + tile, :] = acc


def assemble(out_ref, facts, h, pieces):
    unused, tall, stride, width = facts
    own, partner, received, partner_received = pieces
    other = h ^ 1

    @pl.when(tall)
    def _():
        for ref, index in (
            (own, h),
            (partner, other),
            (received, h ^ 2),
            (partner_received, other ^ 2),
        ):
            out_ref[pl.ds(pl.multiple_of(96 * index, 16), 96), :] = ref[0:96, :]
        out_ref[384:512, :] = jnp.zeros((128, out_ref.shape[1]), out_ref.dtype)

    @pl.when(jnp.logical_not(tall))
    def _():
        low = h & 1
        out_ref[pl.ds(pl.multiple_of(192 * low, 16), 192), :] = own[...]
        out_ref[pl.ds(pl.multiple_of(192 * (1 - low), 16), 192), :] = partner[...]

        @pl.when(low == 0)
        def _():
            out_ref[384:512, :] = received[0:128, :]

        @pl.when(low == 1)
        def _():
            out_ref[384:512, :] = partner_received[0:128, :]


def split_out(full_ref, facts, h, own_ref, send_ref):
    unused, tall, stride, width = facts
    send_h = h ^ 2

    @pl.when(tall)
    def _():
        own_ref[0:96, :] = full_ref[pl.ds(pl.multiple_of(96 * h, 16), 96), :]
        own_ref[96:192, :] = jnp.zeros((96, own_ref.shape[1]), own_ref.dtype)
        send_ref[0:96, :] = full_ref[pl.ds(pl.multiple_of(96 * send_h, 16), 96), :]
        send_ref[96:128, :] = jnp.zeros((32, own_ref.shape[1]), own_ref.dtype)

    @pl.when(jnp.logical_not(tall))
    def _():
        own_ref[...] = full_ref[pl.ds(pl.multiple_of(192 * (h & 1), 16), 192), :]
        send_ref[...] = full_ref[384:512, :]


GAIN1, SHIFT1, BIAS1, GAIN2, SHIFT2, BIAS2, GAIN3, SHIFT3, QB, VB, PB = range(11)
VECS = 16


def vec(vec_ref, index):
    return vec_ref[index : index + 1, :]


def pack(src, facts, dst, wide_rows):
    image, tall, stride, width = facts

    @pl.when(tall)
    def _():
        for row in range(6):
            dst[16 * row : 16 * row + 16, :] = src[image, row, 0:16, :]
        dst[96 : dst.shape[0], :] = jnp.zeros((dst.shape[0] - 96, dst.shape[1]), dst.dtype)

    @pl.when(jnp.logical_not(tall))
    def _():
        for row in range(wide_rows):
            dst[32 * row : 32 * row + 32, :] = src[image, row]


def pack_kernel(bucket_hbm, x_hbm, kinds, away_x, home_x, bucket_ref, x_ref, sems):
    copies = (
        pltpu.make_async_copy(bucket_hbm, bucket_ref, sems.at[0]),
        pltpu.make_async_copy(x_hbm, x_ref, sems.at[1]),
    )
    for copy in copies:
        copy.start()
    for copy in copies:
        copy.wait()
    h, home, away = place(bucket_ref)
    kinds[0] = bucket_ref[0]
    kinds[1] = bucket_ref[1]
    pack(x_ref, away, away_x, 4)
    pack(x_ref, home, home_x, 6)


def stack_kernel(kinds, cot_ref, *refs):
    h, home, away = place(kinds)
    out_ref, away_c, home_c = refs[-3:]
    count = len(refs) - 3
    for index, ref in enumerate(refs[:count]):
        out_ref[index : index + 1, :] = ref[...]
    out_ref[count:, :] = jnp.zeros((VECS - count, out_ref.shape[1]), F32)
    pack(cot_ref, away, away_c, 4)
    pack(cot_ref, home, home_c, 6)


def first_kernel(
    bucket_ref, own, partner, received, partner_received, vecs, weight1,
    image_ref, conv_ref, act2_ref, stats_ref, act1_t, act2_t, send_t,
    shift_ref,
):
    h, home, away = place(bucket_ref)
    stride = home[2]
    mask, pixels = pixel_mask(home)
    channels = vecs.shape[1]
    group_size = pixels * (channels // GROUPS)
    assemble(image_ref, home, h, (own, partner, received, partner_received))
    values = image_ref[...].astype(F32) * mask
    mean1, inverse1 = norm_stats(values, mask, group_size)
    act = silu_norm(values, mean1, inverse1, vec(vecs, GAIN1), vec(vecs, SHIFT1), mask)
    fill_shifts(shift_ref, act, stride)
    act1_t[...] = act.astype(BF16).T
    conv_forward(shift_ref, weight1, stride, conv_ref)
    values = (conv_ref[...] + vec(vecs, BIAS1)) * mask
    conv_ref[...] = values
    mean2, inverse2 = norm_stats(values, mask, group_size)
    act = silu_norm(values, mean2, inverse2, vec(vecs, GAIN2), vec(vecs, SHIFT2), mask)
    act = act.astype(BF16)
    act2_ref[...] = act
    act2_t[...] = act.T
    half = pl.multiple_of((h & 1) * (channels // 2), 16)
    send_t[0] = act1_t[pl.ds(half, channels // 2), :]
    send_t[1] = act2_t[pl.ds(half, channels // 2), :]
    stats_ref[0:1, :] = mean1
    stats_ref[1:2, :] = inverse1
    stats_ref[2:3, :] = mean2
    stats_ref[3:4, :] = inverse2
    stats_ref[4:8, :] = jnp.zeros((4, channels), F32)


def second_kernel(
    bucket_ref, image_ref, act2_ref, own, partner, received, partner_received, vecs,
    weight2, wq, wk, wv, wp,
    middle_ref, mixed_ref, grad2_ref, grad_middle_ref, attn_keep, attn_send, vec_ref,
    block_keep, block_send,
    shift_ref, full_ref, grads_ref, sum_ref,
):
    h, home, away = place(bucket_ref)
    stride = home[2]
    mask, pixels = pixel_mask(home)
    channels = vecs.shape[1]
    group_size = pixels * (channels // GROUPS)
    scaling = channels ** (-0.5)
    assemble(full_ref, home, h, (own, partner, received, partner_received))
    fill_shifts(shift_ref, act2_ref[...].astype(F32), stride)
    conv_forward(shift_ref, weight2, stride, middle_ref)
    middle = mask * (image_ref[...].astype(F32) + (middle_ref[...] + vec(vecs, BIAS2)))
    middle_ref[...] = middle
    mean3, inverse3 = norm_stats(middle, mask, group_size)
    normal = (middle - mean3) * inverse3
    normed = (normal * vec(vecs, GAIN3) + vec(vecs, SHIFT3)).astype(BF16)
    wide = jnp.concatenate([wq[...], wk[...], wv[...]], axis=1)
    joint = mm(normed, wide)
    queries = (joint[:, 0:channels] + vec(vecs, QB)).astype(BF16)
    keys = joint[:, channels : 2 * channels].astype(BF16)
    values = (joint[:, 2 * channels :] + vec(vecs, VB)).astype(BF16)
    lanes = lax.broadcasted_iota(jnp.int32, (1, PIX), 1)
    key_cols = lanes & (stride - 1)
    key_valid = (key_cols < home[3]) & (lanes < jnp.where(home[1], 384, 512))
    scores = jnp.where(key_valid, mm_nt(queries, keys) * scaling, -1000000000.0)
    grad_top = full_ref[...].astype(F32) * mask
    grad_rows = grad_top.astype(BF16)
    grad_mixed = mm_nt(grad_rows, wp[...]).astype(BF16)
    grad_soft = mm_nt(grad_mixed, values)
    raised = jnp.exp(scores - jnp.max(scores, axis=1, keepdims=True))
    soft = raised * (1.0 / jnp.sum(raised, axis=1, keepdims=True))
    soft16 = soft.astype(BF16)
    mixed = mm(soft16, values).astype(BF16)
    mixed_ref[...] = mixed

    grad_values = mm_tn(soft16, grad_mixed).astype(BF16)
    grad_scores = soft * (grad_soft - jnp.sum(soft * grad_soft, axis=1, keepdims=True))
    grad_scores = grad_scores.astype(BF16)
    grad_queries = (mm(grad_scores, keys) * scaling).astype(BF16)
    grad_keys = (mm_tn(grad_scores, queries) * scaling).astype(BF16)
    grads_ref[:, 0:channels] = grad_queries
    grads_ref[:, channels : 2 * channels] = grad_keys
    grads_ref[:, 2 * channels : 3 * channels] = grad_values
    grads_ref[:, 3 * channels : 4 * channels] = grad_rows
    grad_normed = mm_nt(grads_ref[:, 0 : 3 * channels], wide)
    grad_in, gain_grad, shift_grad = norm_back(
        grad_normed, normal, inverse3, mask, group_size, vec(vecs, GAIN3)
    )
    grad_middle = mask * (grad_top + grad_in)
    grad_middle_ref[...] = grad_middle
    grad2 = grad_middle.astype(BF16)
    grad2_ref[...] = grad2
    vec_ref[0:1, :] = gain_grad
    vec_ref[1:2, :] = shift_grad
    vec_ref[2:3, :] = total(grad_queries.astype(F32))
    vec_ref[3:4, :] = total(grad_values.astype(F32))
    vec_ref[4:5, :] = total(grad_top)
    vec_ref[5:6, :] = total(grad2.astype(F32))
    vec_ref[6:8, :] = jnp.zeros((2, channels), F32)

    keep_at = pl.multiple_of(BLK * h, BLK)
    send_at = pl.multiple_of(BLK * (h ^ 2), BLK)
    block_keep[...] = grad2_ref[:, pl.ds(keep_at, BLK)]
    block_send[...] = grad2_ref[:, pl.ds(send_at, BLK)]

    def blocks(index):
        start = index * channels
        return [
            grads_ref[:, pl.ds(pl.multiple_of(start + BLK * h, BLK), BLK)],
            grads_ref[:, pl.ds(pl.multiple_of(start + BLK * (h ^ 2), BLK), BLK)],
        ]

    sum_ref[:, 0 : 6 * BLK] = mm_tn(normed, jnp.concatenate(blocks(0) + blocks(1) + blocks(2), axis=1))
    sum_ref[:, 6 * BLK : 8 * BLK] = mm_tn(mixed, jnp.concatenate(blocks(3), axis=1))
    mine = lax.axis_index("batch") & 1
    pairs = attn_keep.shape[0]
    rows = channels // (2 * pairs)
    for pair in range(pairs):
        for dst, which in ((attn_keep, mine), (attn_send, 1 - mine)):
            part = sum_ref[pl.ds(pl.multiple_of((2 * pair + which) * rows, 8), rows), :].astype(BF16)
            for index in range(4):
                at = index * 2 * BLK
                dst[pair, index * rows : (index + 1) * rows, :] = part[:, at : at + 2 * BLK]


def third_kernel(
    bucket_ref, grad2_ref, conv_ref, stats_ref, vecs, weight2,
    grad1_ref, block_keep, block_send, vec_ref,
    shift_ref, acc_ref,
):
    h, home, away = place(bucket_ref)
    stride = home[2]
    mask, pixels = pixel_mask(home)
    channels = vecs.shape[1]
    group_size = pixels * (channels // GROUPS)
    fill_shifts(shift_ref, grad2_ref[...].astype(F32), stride)
    conv_backward(shift_ref, weight2, stride, acc_ref)
    inverse = stats_ref[3:4, :]
    normal = (conv_ref[...] - stats_ref[2:3, :]) * inverse
    u = normal * vec(vecs, GAIN2) + vec(vecs, SHIFT2)
    grad = mask * acc_ref[...] * silu_slope(u)
    grad_in, gain_grad, shift_grad = norm_back(
        grad, normal, inverse, mask, group_size, vec(vecs, GAIN2)
    )
    grad1 = grad_in.astype(BF16)
    grad1_ref[...] = grad1
    vec_ref[0:1, :] = gain_grad
    vec_ref[1:2, :] = shift_grad
    vec_ref[2:3, :] = total(grad1.astype(F32))
    vec_ref[3:8, :] = jnp.zeros((5, channels), F32)
    block_keep[...] = grad1_ref[:, pl.ds(pl.multiple_of(BLK * h, BLK), BLK)]
    block_send[...] = grad1_ref[:, pl.ds(pl.multiple_of(BLK * (h ^ 2), BLK), BLK)]


def fourth_kernel(
    bucket_ref, grad1_ref, image_ref, stats_ref, grad_middle_ref, middle_ref, mixed_ref, vecs,
    weight1, wp, vec_a, vec_b,
    out_own, grad_own, send_ref, vec_keep, vec_send,
    shift_ref, acc_ref, full_ref, vec_ref,
):
    h, home, away = place(bucket_ref)
    stride = home[2]
    mask, pixels = pixel_mask(home)
    channels = vecs.shape[1]
    group_size = pixels * (channels // GROUPS)
    projected = mm(mixed_ref[...], wp[...]) + vec(vecs, PB)
    full_ref[...] = (mask * (middle_ref[...] + projected)).astype(BF16)
    split_out(full_ref, home, h, out_own, send_ref.at[0])
    fill_shifts(shift_ref, grad1_ref[...].astype(F32), stride)
    conv_backward(shift_ref, weight1, stride, acc_ref)
    inverse = stats_ref[1:2, :]
    normal = (image_ref[...].astype(F32) * mask - stats_ref[0:1, :]) * inverse
    u = normal * vec(vecs, GAIN1) + vec(vecs, SHIFT1)
    grad = mask * acc_ref[...] * silu_slope(u)
    grad_in, gain_grad, shift_grad = norm_back(
        grad, normal, inverse, mask, group_size, vec(vecs, GAIN1)
    )
    full_ref[...] = (mask * (grad_middle_ref[...] + grad_in)).astype(BF16)
    split_out(full_ref, home, h, grad_own, send_ref.at[1])
    vec_ref[0:6, :] = vec_a[0:6, :]
    vec_ref[6:9, :] = vec_b[0:3, :]
    vec_ref[9:10, :] = gain_grad
    vec_ref[10:11, :] = shift_grad
    vec_ref[11:VECS, :] = jnp.zeros((VECS - 11, channels), F32)
    pairs = vec_keep.shape[0]
    rows = channels // (2 * pairs)
    mine = (lax.axis_index("batch") & 1) == 1
    for pair in range(pairs):
        parts = []
        for shard in (2 * pair, 2 * pair + 1):
            start = shard * rows
            tile = start // BLK * BLK
            part = vec_ref[:, tile : tile + BLK]
            parts.append(part if start == tile else pltpu.roll(part, BLK - (start - tile), 1))
        vec_keep[pair] = jnp.where(mine, parts[1], parts[0]).astype(BF16)
        vec_send[pair] = jnp.where(mine, parts[0], parts[1]).astype(BF16)


def weight_kernel(
    bucket_ref, act_t, half_t, partner_half_t, block_own, block_away,
    keep_ref, send_ref, left_ref, right_ref, shift_ref, sum_ref, *, layer,
):
    h, home, away = place(bucket_ref)
    channels = act_t.shape[0]
    half = channels // 2
    left_ref[:, 0:PIX] = act_t[...]
    left_ref[pl.ds(pl.multiple_of((h & 1) * half, 16), half), PIX : 2 * PIX] = half_t[layer]
    left_ref[pl.ds(pl.multiple_of((1 - (h & 1)) * half, 16), half), PIX : 2 * PIX] = (
        partner_half_t[layer]
    )
    for index, (facts, block) in enumerate(((home, block_own), (away, block_away))):
        stride = facts[2]
        fill_shifts(shift_ref, block[...].astype(F32), stride)
        for p in range(3):
            for q in range(3):
                column = (3 * p + q) * BLK
                right_ref[index * PIX : (index + 1) * PIX, column : column + BLK] = tap(
                    shift_ref, 2 - p, 2 - q, stride
                )
    joint = mm(left_ref[...], right_ref[...])
    for t in range(9):
        sum_ref[t * channels : (t + 1) * channels, :] = joint[:, t * BLK : (t + 1) * BLK]
    mine = lax.axis_index("batch") & 1
    pairs = keep_ref.shape[0]
    rows = 9 * channels // (2 * pairs)
    for pair in range(pairs):
        for dst, which in ((keep_ref, mine), (send_ref, 1 - mine)):
            shard = 2 * pair + which
            dst[pair] = sum_ref[pl.ds(pl.multiple_of(shard * rows, 8), rows), :].astype(BF16)


def route_kernel(keep_ref, got_ref, *outs, bit, first):
    ways = len(outs) if first == 0 else len(outs) // 2
    group = (lax.axis_index("batch") >> bit) & (ways - 1)
    rows = keep_ref.shape[1]
    for step, dst in enumerate(outs[-ways:]):
        which = group ^ step
        for index in range(dst.shape[0]):
            at = index * ways + which
            dst[index, first : first + rows, :] = (
                keep_ref[at].astype(F32) + got_ref[at].astype(F32)
            ).astype(BF16)


def total_of(refs):
    added = refs[0].astype(F32)
    for ref in refs[1:]:
        added = added + ref.astype(F32)
    return added


def sum_kernel(*refs):
    refs[-1][...] = total_of([ref[0] for ref in refs[:-1]]).astype(BF16)


def join_kernel(own_ref, far_ref, near_ref, diagonal_ref, *out_refs):
    h = lax.axis_index("height")
    first = 0
    for dst in [ref for ref in out_refs if ref.shape[0] > 1]:
        rows = dst.shape[0]
        for ref, index in ((own_ref, h), (far_ref, h ^ 2), (near_ref, h ^ 1), (diagonal_ref, h ^ 3)):
            dst[:, pl.ds(pl.multiple_of(BLK * index, BLK), BLK)] = ref[first : first + rows, :].astype(F32)
        first += rows
    if own_ref.shape[0] > first:
        own, far = own_ref[first:, :].astype(F32), far_ref[first:, :].astype(F32)
        near, diagonal = near_ref[first:, :].astype(F32), diagonal_ref[first:, :].astype(F32)
        sums = 0.5 * ((own + near) + (far + diagonal))
        for index, dst in enumerate([ref for ref in out_refs if ref.shape[0] == 1]):
            dst[...] = sums[index : index + 1, 0 : dst.shape[1]]


def join_attn_kernel(own_ref, far_ref, near_ref, diagonal_ref, *out_refs):
    h = lax.axis_index("height")
    rows = out_refs[0].shape[0]
    for first, second, index in ((own_ref, far_ref, h), (near_ref, diagonal_ref, h ^ 1)):
        for position in range(2):
            lane, other = position * BLK, (1 - position) * BLK
            column = pl.multiple_of(BLK * (index ^ (2 * position)), BLK)
            for number, dst in enumerate(out_refs):
                at = number * rows
                dst[:, pl.ds(column, BLK)] = first[at : at + rows, lane : lane + BLK].astype(
                    F32
                ) + second[at : at + rows, other : other + BLK].astype(F32)


def unpack_kernel(bucket_ref, out_own, grad_own, away_ref, out_ref, grad_ref):
    h, home, away = place(bucket_ref)
    for own, received, dst in (
        (out_own, away_ref.at[0], out_ref),
        (grad_own, away_ref.at[1], grad_ref),
    ):
        channels = dst.shape[3]
        for facts, src, wide_rows in ((away, received, 4), (home, own, 6)):
            image, tall, stride, width = facts

            @pl.when(tall)
            def _():
                for row in range(6):
                    dst[image, row, 0:16, :] = src[16 * row : 16 * row + 16, :]
                    dst[image, row, 16:32, :] = jnp.zeros((16, channels), dst.dtype)

            @pl.when(jnp.logical_not(tall))
            def _():
                for row in range(wide_rows):
                    dst[image, row] = src[32 * row : 32 * row + 32, :]
                for row in range(wide_rows, 6):
                    dst[image, row] = jnp.zeros((32, channels), dst.dtype)

            if wide_rows == 4:

                @pl.when(jnp.logical_not(tall) & (h == 3))
                def _():
                    for row in range(6):
                        dst[image, row] = jnp.zeros((32, channels), dst.dtype)


def call(kernel, name, outs, scratch, vmem, *operands, smem=1, any_from=99, aliases={}):
    specs = [SM] * smem + [VM] * (len(operands) - smem)
    specs = [HB if i >= any_from else spec for i, spec in enumerate(specs)]
    return pl.pallas_call(
        kernel,
        name=name,
        out_shape=[jax.ShapeDtypeStruct(shape, dtype) for shape, dtype in outs],
        in_specs=specs,
        out_specs=[SM if dtype == jnp.int32 else VM for shape, dtype in outs],
        scratch_shapes=[
            pltpu.SemaphoreType.DMA(shape)
            if dtype is None
            else (pltpu.SMEM if dtype == jnp.int32 else pltpu.VMEM)(shape, dtype)
            for shape, dtype in scratch
        ],
        input_output_aliases=aliases,
        compiler_params=pltpu.CompilerParams(vmem_limit_bytes=vmem << 20),
        cost_estimate=pl.CostEstimate(
            flops=int(LENGTH.get(name, 0.02) * RATE), bytes_accessed=1024, transcendentals=0
        ),
    )(*operands)


def on_device(
    inputs,
    bucket,
    norm1_gain,
    norm1_shift,
    conv1_weight,
    conv1_bias,
    norm2_gain,
    norm2_shift,
    conv2_weight,
    conv2_bias,
    norm3_gain,
    norm3_shift,
    query_weight,
    query_bias,
    key_weight,
    value_weight,
    value_bias,
    proj_weight,
    proj_bias,
    cotangent,
):
    C = inputs.shape[-1]
    batches = lax.axis_size("batch")
    bits = batches.bit_length() - 1
    shard_rows = 9 * C // batches
    small_rows = C // batches

    def row(v):
        return v.reshape(1, C)

    def to_core(v):
        return lax.ppermute(v, "height", [(i, i ^ 1) for i in range(4)])

    def to_chip(v):
        return lax.ppermute(v, "height", [(i, i ^ 2) for i in range(4)])

    def to_batch(v, change):
        return lax.ppermute(v, "batch", [(i, i ^ change) for i in range(batches)])

    def after(v, *others):
        return lax.optimization_barrier((v,) + others)[0]

    def together(got, *others):
        return list(lax.optimization_barrier((*others, *got))[len(others) :])

    img16 = ((PIX, C), BF16)
    img32 = ((PIX, C), F32)
    rows8 = ((8, C), F32)
    block = ((PIX, BLK), BF16)
    turned = ((C, PIX), BF16)
    shifts = ((3, PIX + 2 * PAD, C), BF16)

    kinds, away_x, home_x = call(
        pack_kernel, "pack",
        [((2,), jnp.int32), ((128, C), BF16), ((192, C), BF16)],
        [((2,), jnp.int32), (inputs.shape, BF16), ((2,), None)], 54, bucket, inputs,
        smem=0, any_from=0,
    )
    vectors = (
        norm1_gain, norm1_shift, conv1_bias, norm2_gain, norm2_shift, conv2_bias,
        norm3_gain, norm3_shift, query_bias, value_bias, proj_bias,
    )
    recv_x = to_chip(away_x)
    core_x = to_core(home_x)
    vecs, away_c, home_c = call(
        stack_kernel, "stack", [((VECS, C), F32), ((160, C), BF16), ((192, C), BF16)], [], 8,
        kinds, cotangent, *[row(v) for v in vectors],
    )
    recv_c = to_chip(away_c)
    core_c = to_core(home_c)
    core_recv_c = lax.ppermute(away_c, "height", [(i, i ^ 3) for i in range(4)])
    core_recv_x = to_core(after(recv_x, vecs))

    image, conv, act2, stats, act1_t, act2_t, send_t = call(
        first_kernel, "first",
        [img16, img32, img16, rows8, turned, turned, ((2, C // 2, PIX), BF16)],
        [shifts], 14,
        kinds, home_x, core_x, recv_x, core_recv_x, vecs, conv1_weight,
    )
    half_t = to_chip(send_t)
    core_half_t = to_core(half_t)

    attn_out = ((batches // 2, 4 * small_rows, 2 * BLK), BF16)
    middle, mixed, grad2, grad_middle, attn_keep, attn_send, vec_a, block2, block2_send = call(
        second_kernel, "second",
        [img32, img16, img16, img32, attn_out, attn_out, rows8, block, block],
        [shifts, img16, ((PIX, 4 * C), BF16), ((C, 8 * BLK), F32)], 24,
        kinds, image, act2, home_c, core_c, recv_c, core_recv_c, vecs,
        conv2_weight, query_weight, key_weight, value_weight, proj_weight,
    )
    block2_away = to_chip(block2_send)
    attn_got = to_batch(attn_send, 1)

    grad1, block1, block1_send, vec_b = call(
        third_kernel, "third",
        [img16, block, block, rows8],
        [shifts, img32], 14,
        kinds, grad2, conv, stats, vecs, conv2_weight,
    )
    block1_away = to_chip(block1_send)

    def weight_grad(name, act_t, index, own, away):
        return call(
            functools.partial(weight_kernel, layer=index), name,
            [((batches // 2, shard_rows, BLK), BF16)] * 2,
            [((C, 2 * PIX), BF16), ((2 * PIX, 9 * BLK), BF16), ((3, PIX + 2 * PAD, BLK), BF16),
             ((9 * C, BLK), F32)],
            18, kinds, act_t, half_t, core_half_t, own, away,
        )

    keep2, send2 = weight_grad("weight2", act2_t, 1, after(block2, block1), block2_away)
    got2 = to_batch(send2, 1)

    def spread(name, bit, keep, got, tail=None, behind=()):
        ways = 1 << min(2, bits - bit)
        rows = keep.shape[1]
        shape = (keep.shape[0] // ways, rows + (VECS if tail else 0), keep.shape[2])
        parts = call(
            functools.partial(route_kernel, bit=bit, first=0), name + str(bit),
            [(shape, BF16)] * ways, [], 16, keep, got, smem=0,
        )
        if tail:
            parts = call(
                functools.partial(route_kernel, bit=bit, first=rows), name + "tail",
                [(shape, BF16)] * ways, [], 16, *tail, *parts, smem=0,
                aliases={2 + j: j for j in range(ways)},
            )
        return parts, [to_batch(after(parts[j], *behind), j << bit) for j in range(1, ways)]

    def finish(name, parts, got):
        for bit in range(3, bits, 2):
            added = total_of([parts[0]] + got).astype(BF16)
            parts, got = spread(name, bit, added, jnp.zeros_like(added))
        return call(
            sum_kernel, "sum" + name, [(parts[0].shape[1:], BF16)], [], 8, parts[0], *got, smem=0
        )[0]

    def gather(shard, *between):
        far = to_chip(shard)
        near = to_core(shard)
        return shard, far, near, to_core(after(far, *between))

    parts_a, got_a = spread("routea", 1, after(attn_keep, send2), attn_got)
    keep1, send1 = weight_grad("weight1", act1_t, 0, after(block1, *parts_a), block1_away)
    got1 = to_batch(send1, 1)
    shard_a = finish("routea", parts_a, together(got_a, send1))
    out_own, grad_own, image_send, vec_keep, vec_send = call(
        fourth_kernel, "fourth",
        [((192, C), BF16), ((192, C), BF16), ((2, 128, C), BF16),
         ((batches // 2, VECS, BLK), BF16), ((batches // 2, VECS, BLK), BF16)],
        [shifts, img32, img16, ((VECS, C), F32)], 14,
        kinds, after(grad1, send1), image, stats, grad_middle, middle, mixed, vecs,
        conv1_weight, proj_weight, vec_a, vec_b,
    )
    image_away = to_chip(image_send)
    vec_got = to_batch(vec_send, 1)
    parts_b, got_b = spread("routeb", 1, after(keep2, vec_keep, shard_a), got2)
    parts_c, got_c = spread("routec", 1, keep1, got1, (vec_keep, vec_got), behind=got_b)
    shard_b = finish("routeb", parts_b, together(got_b, parts_c[0]))
    gathered_a = gather(shard_a)
    gathered_b = gather(shard_b)
    shard_c = finish(
        "routec", parts_c, together(got_c, gathered_b[1], gathered_a[1])
    )
    small = call(
        join_attn_kernel, "joina", [((small_rows, C), F32)] * 4, [], 8,
        after(gathered_a[0], shard_c), *gathered_a[1:], smem=0,
    )
    (whole2,) = call(
        join_kernel, "joinb", [((shard_rows, C), F32)], [], 8,
        after(gathered_b[0], shard_c), *gathered_b[1:], smem=0,
    )
    outputs, input_grad = call(
        unpack_kernel, "unpack",
        [(inputs.shape, BF16)] * 2, [], 8,
        kinds, out_own, grad_own, after(image_away, shard_c),
    )
    gathered_c = gather(shard_c, whole2, outputs, *small)
    whole1, *sums = call(
        join_kernel, "joinc", [((shard_rows, C), F32)] + [((1, small_rows), F32)] * 11, [], 8,
        *gathered_c, smem=0,
    )
    v = [row.reshape(small_rows) for row in sums]

    return (
        outputs, input_grad,
        v[9], v[10], whole1, v[8],
        v[6], v[7], whole2, v[5],
        v[0], v[1],
        small[0], v[2], small[1], small[2], v[3], small[3], v[4],
    )


def solution(mesh):
    image = P("batch", "height", None, None)
    vector = P("batch")
    matrix = P("batch", None)
    return jax.shard_map(
        on_device,
        mesh=mesh,
        in_specs=(image, vector) + (P(),) * 17 + (image,),
        out_specs=(
            image, image,
            vector, vector, matrix, vector,
            vector, vector, matrix, vector,
            vector, vector,
            matrix, vector, matrix, matrix, vector, matrix, vector,
        ),
        check_vma=False,
    )
```

```python
import functools

import jax
import jax.numpy as jnp
from jax import lax
from jax.experimental import pallas as pl
from jax.experimental.pallas import tpu as pltpu
from jax.sharding import PartitionSpec as P

GROUPS = 32
UNIT = 8
PIX = 512
PAD = 32
BLK = 128
F32 = jnp.float32
BF16 = jnp.bfloat16
epsilon = 1e-05

VM = pl.BlockSpec(memory_space=pltpu.VMEM)
SM = pl.BlockSpec(memory_space=pltpu.SMEM)
HB = pl.BlockSpec(memory_space=pltpu.HBM)
RATE = 1 << 30
LENGTH = {
    "pack": 10, "stack": 10, "first": 0.02, "second": 30, "third": 20, "fourth": 0.5, "weight2": 1, "weight1": 3, "routeb1": 20,
}


def place(bucket_ref):
    h = lax.axis_index("height")
    upper = lax.div(h, 2)
    tall_first = bucket_ref[0] == 1
    tall_image = jnp.where(tall_first, 0, 1)
    home = jnp.where(upper == 1, tall_image, 1 - tall_image)
    away = 1 - home

    def facts(image):
        kind = bucket_ref[image]
        tall = kind == 1
        stride = jnp.where(tall, 2 * UNIT, 4 * UNIT)
        width = jnp.where(kind == 0, 3 * UNIT, stride)
        return (image, tall, stride, width)

    return h, facts(home), facts(away)


def pixel_col(stride, lanes=1):
    rows = lax.broadcasted_iota(jnp.int32, (PIX, lanes), 0)
    return rows, rows & (stride - 1)


def pixel_mask(facts):
    unused, tall, stride, width = facts
    rows, cols = pixel_col(stride)
    limit = jnp.where(tall, 6 * UNIT * UNIT, 8 * UNIT * UNIT)
    mask = jnp.where((cols < width) & (rows < limit), 1.0, 0.0).astype(F32)
    size = jnp.where(tall | (width == 3 * UNIT), 6 * UNIT * UNIT, 8 * UNIT * UNIT)
    return mask, size.astype(F32)


def group_total(rows):
    members = rows.shape[1] // GROUPS
    lane = lax.broadcasted_iota(jnp.int32, (rows.shape[0], BLK), 1)
    tiles = []
    for tile in range(rows.shape[1] // BLK):
        part = rows[:, tile * BLK : (tile + 1) * BLK]
        step = 1
        while step < members:
            place_in_four = (lane // step) & 3
            added = part
            for d in (1, 2, 3):
                up = pltpu.roll(part, BLK - d * step, 1)
                down = pltpu.roll(part, (4 - d) * step, 1)
                added = added + jnp.where(place_in_four + d < 4, up, down)
            part = added
            step *= 4
        tiles.append(part)
    return jnp.concatenate(tiles, axis=1)


def total(values):
    return jnp.sum(values, axis=0, keepdims=True)


def wide_total(*rows):
    stacked = jnp.concatenate(list(rows) + [rows[0]] * (8 - len(rows)), axis=0)
    sums = group_total(stacked)
    return [sums[i : i + 1] for i in range(len(rows))]


def norm_stats(values, mask, group_size):
    mean = wide_total(total(values))[0] / group_size
    centered = (values - mean) * mask
    variance = wide_total(total(centered * centered))[0] / group_size
    return mean, lax.rsqrt(variance + epsilon)


def silu_norm(values, mean, inverse, gain, shift, mask):
    scale = 0.5 * inverse * gain
    half = values * scale + (0.5 * shift - mean * scale)
    return (half + half * jnp.tanh(half)) * mask


def norm_back(grad, normal, inverse, mask, group_size, gain):
    plain_row = total(grad)
    cross_row = total(grad * normal)
    plain, cross = [v / group_size for v in wide_total(plain_row * gain, cross_row * gain)]
    grad_in = grad * (inverse * gain) - mask * (plain * inverse + normal * (cross * inverse))
    return grad_in, cross_row, plain_row


def silu_slope(u):
    half = 0.5 * u
    t = jnp.tanh(half)
    return (0.5 + 0.5 * t) * (1.0 + half * (1.0 - t))


def mm(a, b):
    return jnp.dot(a, b, preferred_element_type=F32)


def mm_nt(a, b):
    return lax.dot_general(a, b, (((1,), (1,)), ((), ())), preferred_element_type=F32)


def mm_tn(a, b):
    return lax.dot_general(a, b, (((0,), (0,)), ((), ())), preferred_element_type=F32)


def fill_shifts(shift_ref, values, stride):
    unused, cols = pixel_col(stride)
    lanes = values.shape[1]
    zeros = jnp.zeros((PAD, lanes), BF16)
    for q in range(3):
        shift_ref[q, 0:PAD, :] = zeros
        shift_ref[q, PAD + PIX : 2 * PAD + PIX, :] = zeros
    left = jnp.where(cols == 0, 0.0, pltpu.roll(values, 1, 0))
    right = jnp.where(cols == stride - 1, 0.0, pltpu.roll(values, PIX - 1, 0))
    shift_ref[0, PAD : PAD + PIX, :] = left.astype(BF16)
    shift_ref[1, PAD : PAD + PIX, :] = values.astype(BF16)
    shift_ref[2, PAD : PAD + PIX, :] = right.astype(BF16)


def tap(shift_ref, p, q, stride, first=0, count=PIX):
    start = pl.multiple_of(PAD + first + (p - 1) * stride, 16)
    return shift_ref[q, pl.ds(start, count), :]


def conv_forward(shift_ref, weight_ref, stride, out_ref, tile=256):
    for first in range(0, PIX, tile):
        stacked = jnp.concatenate(
            [tap(shift_ref, p, q, stride, first, tile) for p in range(3) for q in range(3)], axis=1
        )
        out_ref[first : first + tile, :] = mm(stacked, weight_ref[...])


def conv_backward(shift_ref, weight_ref, stride, out_ref, tile=256):
    channels = weight_ref.shape[1]
    for first in range(0, PIX, tile):
        acc = None
        for p in range(3):
            for q in range(3):
                row = (8 - (3 * p + q)) * channels
                part = mm_nt(
                    tap(shift_ref, p, q, stride, first, tile), weight_ref[row : row + channels, :]
                )
                acc = part if acc is None else acc + part
        out_ref[first : first + tile, :] = acc


def assemble(out_ref, facts, h, pieces):
    unused, tall, stride, width = facts
    own, partner, received, partner_received = pieces
    other = h ^ 1

    @pl.when(tall)
    def _():
        for ref, index in (
            (own, h),
            (partner, other),
            (received, h ^ 2),
            (partner_received, other ^ 2),
        ):
            out_ref[pl.ds(pl.multiple_of(96 * index, 16), 96), :] = ref[0:96, :]
        out_ref[384:512, :] = jnp.zeros((128, out_ref.shape[1]), out_ref.dtype)

    @pl.when(jnp.logical_not(tall))
    def _():
        low = h & 1
        out_ref[pl.ds(pl.multiple_of(192 * low, 16), 192), :] = own[...]
        out_ref[pl.ds(pl.multiple_of(192 * (1 - low), 16), 192), :] = partner[...]

        @pl.when(low == 0)
        def _():
            out_ref[384:512, :] = received[0:128, :]

        @pl.when(low == 1)
        def _():
            out_ref[384:512, :] = partner_received[0:128, :]


def split_out(full_ref, facts, h, own_ref, send_ref):
    unused, tall, stride, width = facts
    send_h = h ^ 2

    @pl.when(tall)
    def _():
        own_ref[0:96, :] = full_ref[pl.ds(pl.multiple_of(96 * h, 16), 96), :]
        own_ref[96:192, :] = jnp.zeros((96, own_ref.shape[1]), own_ref.dtype)
        send_ref[0:96, :] = full_ref[pl.ds(pl.multiple_of(96 * send_h, 16), 96), :]
        send_ref[96:128, :] = jnp.zeros((32, own_ref.shape[1]), own_ref.dtype)

    @pl.when(jnp.logical_not(tall))
    def _():
        own_ref[...] = full_ref[pl.ds(pl.multiple_of(192 * (h & 1), 16), 192), :]
        send_ref[...] = full_ref[384:512, :]


GAIN1, SHIFT1, BIAS1, GAIN2, SHIFT2, BIAS2, GAIN3, SHIFT3, QB, VB, PB = range(11)
VECS = 16


def vec(vec_ref, index):
    return vec_ref[index : index + 1, :]


def pack(src, facts, dst, wide_rows):
    image, tall, stride, width = facts

    @pl.when(tall)
    def _():
        for row in range(6):
            dst[16 * row : 16 * row + 16, :] = src[image, row, 0:16, :]
        dst[96 : dst.shape[0], :] = jnp.zeros((dst.shape[0] - 96, dst.shape[1]), dst.dtype)

    @pl.when(jnp.logical_not(tall))
    def _():
        for row in range(wide_rows):
            dst[32 * row : 32 * row + 32, :] = src[image, row]


def pack_kernel(bucket_hbm, x_hbm, kinds, away_x, home_x, bucket_ref, x_ref, sems):
    copies = (
        pltpu.make_async_copy(bucket_hbm, bucket_ref, sems.at[0]),
        pltpu.make_async_copy(x_hbm, x_ref, sems.at[1]),
    )
    for copy in copies:
        copy.start()
    for copy in copies:
        copy.wait()
    h, home, away = place(bucket_ref)
    kinds[0] = bucket_ref[0]
    kinds[1] = bucket_ref[1]
    pack(x_ref, away, away_x, 4)
    pack(x_ref, home, home_x, 6)


def stack_kernel(kinds, cot_ref, *refs):
    h, home, away = place(kinds)
    out_ref, away_c, home_c = refs[-3:]
    count = len(refs) - 3
    for index, ref in enumerate(refs[:count]):
        out_ref[index : index + 1, :] = ref[...]
    out_ref[count:, :] = jnp.zeros((VECS - count, out_ref.shape[1]), F32)
    pack(cot_ref, away, away_c, 4)
    pack(cot_ref, home, home_c, 6)


def first_kernel(
    bucket_ref, own, partner, received, partner_received, vecs, weight1,
    image_ref, conv_ref, act2_ref, stats_ref, act1_t, act2_t, send_t,
    shift_ref,
):
    h, home, away = place(bucket_ref)
    stride = home[2]
    mask, pixels = pixel_mask(home)
    channels = vecs.shape[1]
    group_size = pixels * (channels // GROUPS)
    assemble(image_ref, home, h, (own, partner, received, partner_received))
    values = image_ref[...].astype(F32) * mask
    mean1, inverse1 = norm_stats(values, mask, group_size)
    act = silu_norm(values, mean1, inverse1, vec(vecs, GAIN1), vec(vecs, SHIFT1), mask)
    fill_shifts(shift_ref, act, stride)
    act1_t[...] = act.astype(BF16).T
    conv_forward(shift_ref, weight1, stride, conv_ref)
    values = (conv_ref[...] + vec(vecs, BIAS1)) * mask
    conv_ref[...] = values
    mean2, inverse2 = norm_stats(values, mask, group_size)
    act = silu_norm(values, mean2, inverse2, vec(vecs, GAIN2), vec(vecs, SHIFT2), mask)
    act = act.astype(BF16)
    act2_ref[...] = act
    act2_t[...] = act.T
    half = pl.multiple_of((h & 1) * (channels // 2), 16)
    send_t[0] = act1_t[pl.ds(half, channels // 2), :]
    send_t[1] = act2_t[pl.ds(half, channels // 2), :]
    stats_ref[0:1, :] = mean1
    stats_ref[1:2, :] = inverse1
    stats_ref[2:3, :] = mean2
    stats_ref[3:4, :] = inverse2
    stats_ref[4:8, :] = jnp.zeros((4, channels), F32)


def second_kernel(
    bucket_ref, image_ref, act2_ref, own, partner, received, partner_received, vecs,
    weight2, wq, wk, wv, wp,
    middle_ref, mixed_ref, grad2_ref, grad_middle_ref, attn_keep, attn_send, vec_ref,
    block_keep, block_send,
    shift_ref, full_ref, grads_ref, sum_ref,
):
    h, home, away = place(bucket_ref)
    stride = home[2]
    mask, pixels = pixel_mask(home)
    channels = vecs.shape[1]
    group_size = pixels * (channels // GROUPS)
    scaling = channels ** (-0.5)
    assemble(full_ref, home, h, (own, partner, received, partner_received))
    fill_shifts(shift_ref, act2_ref[...].astype(F32), stride)
    conv_forward(shift_ref, weight2, stride, middle_ref)
    middle = mask * (image_ref[...].astype(F32) + (middle_ref[...] + vec(vecs, BIAS2)))
    middle_ref[...] = middle
    mean3, inverse3 = norm_stats(middle, mask, group_size)
    normal = (middle - mean3) * inverse3
    normed = (normal * vec(vecs, GAIN3) + vec(vecs, SHIFT3)).astype(BF16)
    wide = jnp.concatenate([wq[...], wk[...], wv[...]], axis=1)
    joint = mm(normed, wide)
    queries = (joint[:, 0:channels] + vec(vecs, QB)).astype(BF16)
    keys = joint[:, channels : 2 * channels].astype(BF16)
    values = (joint[:, 2 * channels :] + vec(vecs, VB)).astype(BF16)
    lanes = lax.broadcasted_iota(jnp.int32, (1, PIX), 1)
    key_cols = lanes & (stride - 1)
    key_valid = (key_cols < home[3]) & (lanes < jnp.where(home[1], 384, 512))
    scores = jnp.where(key_valid, mm_nt(queries, keys) * scaling, -1000000000.0)
    grad_top = full_ref[...].astype(F32) * mask
    grad_rows = grad_top.astype(BF16)
    grad_mixed = mm_nt(grad_rows, wp[...]).astype(BF16)
    grad_soft = mm_nt(grad_mixed, values)
    raised = jnp.exp(scores - jnp.max(scores, axis=1, keepdims=True))
    soft = raised * (1.0 / jnp.sum(raised, axis=1, keepdims=True))
    soft16 = soft.astype(BF16)
    mixed = mm(soft16, values).astype(BF16)
    mixed_ref[...] = mixed

    grad_values = mm_tn(soft16, grad_mixed).astype(BF16)
    grad_scores = soft * (grad_soft - jnp.sum(soft * grad_soft, axis=1, keepdims=True))
    grad_scores = grad_scores.astype(BF16)
    grad_queries = (mm(grad_scores, keys) * scaling).astype(BF16)
    grad_keys = (mm_tn(grad_scores, queries) * scaling).astype(BF16)
    grads_ref[:, 0:channels] = grad_queries
    grads_ref[:, channels : 2 * channels] = grad_keys
    grads_ref[:, 2 * channels : 3 * channels] = grad_values
    grads_ref[:, 3 * channels : 4 * channels] = grad_rows
    grad_normed = mm_nt(grads_ref[:, 0 : 3 * channels], wide)
    grad_in, gain_grad, shift_grad = norm_back(
        grad_normed, normal, inverse3, mask, group_size, vec(vecs, GAIN3)
    )
    grad_middle = mask * (grad_top + grad_in)
    grad_middle_ref[...] = grad_middle
    grad2 = grad_middle.astype(BF16)
    grad2_ref[...] = grad2
    vec_ref[0:1, :] = gain_grad
    vec_ref[1:2, :] = shift_grad
    vec_ref[2:3, :] = total(grad_queries.astype(F32))
    vec_ref[3:4, :] = total(grad_values.astype(F32))
    vec_ref[4:5, :] = total(grad_top)
    vec_ref[5:6, :] = total(grad2.astype(F32))
    vec_ref[6:8, :] = jnp.zeros((2, channels), F32)

    keep_at = pl.multiple_of(BLK * h, BLK)
    send_at = pl.multiple_of(BLK * (h ^ 2), BLK)
    block_keep[...] = grad2_ref[:, pl.ds(keep_at, BLK)]
    block_send[...] = grad2_ref[:, pl.ds(send_at, BLK)]

    def blocks(index):
        start = index * channels
        return [
            grads_ref[:, pl.ds(pl.multiple_of(start + BLK * h, BLK), BLK)],
            grads_ref[:, pl.ds(pl.multiple_of(start + BLK * (h ^ 2), BLK), BLK)],
        ]

    sum_ref[:, 0 : 6 * BLK] = mm_tn(normed, jnp.concatenate(blocks(0) + blocks(1) + blocks(2), axis=1))
    sum_ref[:, 6 * BLK : 8 * BLK] = mm_tn(mixed, jnp.concatenate(blocks(3), axis=1))
    mine = lax.axis_index("batch") & 1
    pairs = attn_keep.shape[0]
    rows = channels // (2 * pairs)
    for pair in range(pairs):
        for dst, which in ((attn_keep, mine), (attn_send, 1 - mine)):
            part = sum_ref[pl.ds(pl.multiple_of((2 * pair + which) * rows, 8), rows), :].astype(BF16)
            for index in range(4):
                at = index * 2 * BLK
                dst[pair, index * rows : (index + 1) * rows, :] = part[:, at : at + 2 * BLK]


def third_kernel(
    bucket_ref, grad2_ref, conv_ref, stats_ref, vecs, weight2,
    grad1_ref, block_keep, block_send, vec_ref,
    shift_ref, acc_ref,
):
    h, home, away = place(bucket_ref)
    stride = home[2]
    mask, pixels = pixel_mask(home)
    channels = vecs.shape[1]
    group_size = pixels * (channels // GROUPS)
    fill_shifts(shift_ref, grad2_ref[...].astype(F32), stride)
    conv_backward(shift_ref, weight2, stride, acc_ref)
    inverse = stats_ref[3:4, :]
    normal = (conv_ref[...] - stats_ref[2:3, :]) * inverse
    u = normal * vec(vecs, GAIN2) + vec(vecs, SHIFT2)
    grad = mask * acc_ref[...] * silu_slope(u)
    grad_in, gain_grad, shift_grad = norm_back(
        grad, normal, inverse, mask, group_size, vec(vecs, GAIN2)
    )
    grad1 = grad_in.astype(BF16)
    grad1_ref[...] = grad1
    vec_ref[0:1, :] = gain_grad
    vec_ref[1:2, :] = shift_grad
    vec_ref[2:3, :] = total(grad1.astype(F32))
    vec_ref[3:8, :] = jnp.zeros((5, channels), F32)
    block_keep[...] = grad1_ref[:, pl.ds(pl.multiple_of(BLK * h, BLK), BLK)]
    block_send[...] = grad1_ref[:, pl.ds(pl.multiple_of(BLK * (h ^ 2), BLK), BLK)]


def fourth_kernel(
    bucket_ref, grad1_ref, image_ref, stats_ref, grad_middle_ref, middle_ref, mixed_ref, vecs,
    weight1, wp, vec_a, vec_b,
    out_own, grad_own, send_ref, vec_keep, vec_send,
    shift_ref, acc_ref, full_ref, vec_ref,
):
    h, home, away = place(bucket_ref)
    stride = home[2]
    mask, pixels = pixel_mask(home)
    channels = vecs.shape[1]
    group_size = pixels * (channels // GROUPS)
    projected = mm(mixed_ref[...], wp[...]) + vec(vecs, PB)
    full_ref[...] = (mask * (middle_ref[...] + projected)).astype(BF16)
    split_out(full_ref, home, h, out_own, send_ref.at[0])
    fill_shifts(shift_ref, grad1_ref[...].astype(F32), stride)
    conv_backward(shift_ref, weight1, stride, acc_ref)
    inverse = stats_ref[1:2, :]
    normal = (image_ref[...].astype(F32) * mask - stats_ref[0:1, :]) * inverse
    u = normal * vec(vecs, GAIN1) + vec(vecs, SHIFT1)
    grad = mask * acc_ref[...] * silu_slope(u)
    grad_in, gain_grad, shift_grad = norm_back(
        grad, normal, inverse, mask, group_size, vec(vecs, GAIN1)
    )
    full_ref[...] = (mask * (grad_middle_ref[...] + grad_in)).astype(BF16)
    split_out(full_ref, home, h, grad_own, send_ref.at[1])
    vec_ref[0:6, :] = vec_a[0:6, :]
    vec_ref[6:9, :] = vec_b[0:3, :]
    vec_ref[9:10, :] = gain_grad
    vec_ref[10:11, :] = shift_grad
    vec_ref[11:VECS, :] = jnp.zeros((VECS - 11, channels), F32)
    pairs = vec_keep.shape[0]
    rows = channels // (2 * pairs)
    mine = (lax.axis_index("batch") & 1) == 1
    for pair in range(pairs):
        parts = []
        for shard in (2 * pair, 2 * pair + 1):
            start = shard * rows
            tile = start // BLK * BLK
            part = vec_ref[:, tile : tile + BLK]
            parts.append(part if start == tile else pltpu.roll(part, BLK - (start - tile), 1))
        vec_keep[pair] = jnp.where(mine, parts[1], parts[0]).astype(BF16)
        vec_send[pair] = jnp.where(mine, parts[0], parts[1]).astype(BF16)


def weight_kernel(
    bucket_ref, act_t, half_t, partner_half_t, block_own, block_away,
    keep_ref, send_ref, left_ref, right_ref, shift_ref, sum_ref, *, layer,
):
    h, home, away = place(bucket_ref)
    channels = act_t.shape[0]
    half = channels // 2
    left_ref[:, 0:PIX] = act_t[...]
    left_ref[pl.ds(pl.multiple_of((h & 1) * half, 16), half), PIX : 2 * PIX] = half_t[layer]
    left_ref[pl.ds(pl.multiple_of((1 - (h & 1)) * half, 16), half), PIX : 2 * PIX] = (
        partner_half_t[layer]
    )
    for index, (facts, block) in enumerate(((home, block_own), (away, block_away))):
        stride = facts[2]
        fill_shifts(shift_ref, block[...].astype(F32), stride)
        for p in range(3):
            for q in range(3):
                column = (3 * p + q) * BLK
                right_ref[index * PIX : (index + 1) * PIX, column : column + BLK] = tap(
                    shift_ref, 2 - p, 2 - q, stride
                )
    joint = mm(left_ref[...], right_ref[...])
    for t in range(9):
        sum_ref[t * channels : (t + 1) * channels, :] = joint[:, t * BLK : (t + 1) * BLK]
    mine = lax.axis_index("batch") & 1
    pairs = keep_ref.shape[0]
    rows = 9 * channels // (2 * pairs)
    for pair in range(pairs):
        for dst, which in ((keep_ref, mine), (send_ref, 1 - mine)):
            shard = 2 * pair + which
            dst[pair] = sum_ref[pl.ds(pl.multiple_of(shard * rows, 8), rows), :].astype(BF16)


def route_kernel(keep_ref, got_ref, *outs, bit, first):
    ways = len(outs) if first == 0 else len(outs) // 2
    group = (lax.axis_index("batch") >> bit) & (ways - 1)
    rows = keep_ref.shape[1]
    for step, dst in enumerate(outs[-ways:]):
        which = group ^ step
        for index in range(dst.shape[0]):
            at = index * ways + which
            dst[index, first : first + rows, :] = (
                keep_ref[at].astype(F32) + got_ref[at].astype(F32)
            ).astype(BF16)


def total_of(refs):
    added = refs[0].astype(F32)
    for ref in refs[1:]:
        added = added + ref.astype(F32)
    return added


def sum_kernel(*refs):
    refs[-1][...] = total_of([ref[0] for ref in refs[:-1]]).astype(BF16)


def join_kernel(own_ref, far_ref, near_ref, diagonal_ref, out_ref, *refs):
    h = lax.axis_index("height")
    rows = out_ref.shape[0]
    tail_refs, wide_ref, sems = refs[:-2], refs[-2], refs[-1]
    copies = []
    for slot, (ref, index) in enumerate(
        ((own_ref, h), (near_ref, h ^ 1), (far_ref, h ^ 2), (diagonal_ref, h ^ 3))
    ):
        wide_ref[slot] = ref[0:rows, :].astype(F32)
        column = pl.ds(pl.multiple_of(BLK * index, BLK), BLK)
        copies.append(pltpu.make_async_copy(wide_ref.at[slot], out_ref.at[:, column], sems.at[slot]))
        copies[-1].start()
    if tail_refs:
        own, far = own_ref[rows:, :].astype(F32), far_ref[rows:, :].astype(F32)
        near, diagonal = near_ref[rows:, :].astype(F32), diagonal_ref[rows:, :].astype(F32)
        sums = 0.5 * ((own + near) + (far + diagonal))
        for index, dst in enumerate(tail_refs):
            dst[...] = sums[index : index + 1, 0 : dst.shape[1]]
    for copy in copies:
        copy.wait()


def join_attn_kernel(own_ref, far_ref, near_ref, diagonal_ref, *out_refs):
    h = lax.axis_index("height")
    rows = out_refs[0].shape[0]
    for first, second, index in ((own_ref, far_ref, h), (near_ref, diagonal_ref, h ^ 1)):
        for position in range(2):
            lane, other = position * BLK, (1 - position) * BLK
            column = pl.multiple_of(BLK * (index ^ (2 * position)), BLK)
            for number, dst in enumerate(out_refs):
                at = number * rows
                dst[:, pl.ds(column, BLK)] = first[at : at + rows, lane : lane + BLK].astype(
                    F32
                ) + second[at : at + rows, other : other + BLK].astype(F32)


def unpack_kernel(bucket_ref, out_own, grad_own, away_ref, out_ref, grad_ref):
    h, home, away = place(bucket_ref)
    for own, received, dst in (
        (out_own, away_ref.at[0], out_ref),
        (grad_own, away_ref.at[1], grad_ref),
    ):
        channels = dst.shape[3]
        for facts, src, wide_rows in ((away, received, 4), (home, own, 6)):
            image, tall, stride, width = facts

            @pl.when(tall)
            def _():
                for row in range(6):
                    dst[image, row, 0:16, :] = src[16 * row : 16 * row + 16, :]
                    dst[image, row, 16:32, :] = jnp.zeros((16, channels), dst.dtype)

            @pl.when(jnp.logical_not(tall))
            def _():
                for row in range(wide_rows):
                    dst[image, row] = src[32 * row : 32 * row + 32, :]
                for row in range(wide_rows, 6):
                    dst[image, row] = jnp.zeros((32, channels), dst.dtype)

            if wide_rows == 4:

                @pl.when(jnp.logical_not(tall) & (h == 3))
                def _():
                    for row in range(6):
                        dst[image, row] = jnp.zeros((32, channels), dst.dtype)


def call(kernel, name, outs, scratch, vmem, *operands, smem=1, any_from=99, aliases={}, far_outs=0):
    specs = [SM] * smem + [VM] * (len(operands) - smem)
    specs = [HB if i >= any_from else spec for i, spec in enumerate(specs)]
    return pl.pallas_call(
        kernel,
        name=name,
        out_shape=[jax.ShapeDtypeStruct(shape, dtype) for shape, dtype in outs],
        in_specs=specs,
        out_specs=[HB] * far_outs
        + [SM if dtype == jnp.int32 else VM for shape, dtype in outs[far_outs:]],
        scratch_shapes=[
            pltpu.SemaphoreType.DMA(shape)
            if dtype is None
            else (pltpu.SMEM if dtype == jnp.int32 else pltpu.VMEM)(shape, dtype)
            for shape, dtype in scratch
        ],
        input_output_aliases=aliases,
        compiler_params=pltpu.CompilerParams(vmem_limit_bytes=vmem << 20),
        cost_estimate=pl.CostEstimate(
            flops=int(LENGTH.get(name, 0.02) * RATE), bytes_accessed=1024, transcendentals=0
        ),
    )(*operands)


def on_device(
    inputs,
    bucket,
    norm1_gain,
    norm1_shift,
    conv1_weight,
    conv1_bias,
    norm2_gain,
    norm2_shift,
    conv2_weight,
    conv2_bias,
    norm3_gain,
    norm3_shift,
    query_weight,
    query_bias,
    key_weight,
    value_weight,
    value_bias,
    proj_weight,
    proj_bias,
    cotangent,
):
    C = inputs.shape[-1]
    batches = lax.axis_size("batch")
    bits = batches.bit_length() - 1
    shard_rows = 9 * C // batches
    small_rows = C // batches

    def row(v):
        return v.reshape(1, C)

    def to_core(v):
        return lax.ppermute(v, "height", [(i, i ^ 1) for i in range(4)])

    def to_chip(v):
        return lax.ppermute(v, "height", [(i, i ^ 2) for i in range(4)])

    def to_batch(v, change):
        return lax.ppermute(v, "batch", [(i, i ^ change) for i in range(batches)])

    def after(v, *others):
        return lax.optimization_barrier((v,) + others)[0]

    img16 = ((PIX, C), BF16)
    img32 = ((PIX, C), F32)
    rows8 = ((8, C), F32)
    block = ((PIX, BLK), BF16)
    turned = ((C, PIX), BF16)
    shifts = ((3, PIX + 2 * PAD, C), BF16)

    kinds, away_x, home_x = call(
        pack_kernel, "pack",
        [((2,), jnp.int32), ((128, C), BF16), ((192, C), BF16)],
        [((2,), jnp.int32), (inputs.shape, BF16), ((2,), None)], 54, bucket, inputs,
        smem=0, any_from=0,
    )
    vectors = (
        norm1_gain, norm1_shift, conv1_bias, norm2_gain, norm2_shift, conv2_bias,
        norm3_gain, norm3_shift, query_bias, value_bias, proj_bias,
    )
    recv_x = to_chip(away_x)
    core_x = to_core(home_x)
    vecs, away_c, home_c = call(
        stack_kernel, "stack", [((VECS, C), F32), ((160, C), BF16), ((192, C), BF16)], [], 8,
        kinds, cotangent, *[row(v) for v in vectors],
    )
    recv_c = to_chip(away_c)
    core_c = to_core(home_c)
    core_recv_c = lax.ppermute(away_c, "height", [(i, i ^ 3) for i in range(4)])
    core_recv_x = to_core(after(recv_x, vecs))

    image, conv, act2, stats, act1_t, act2_t, send_t = call(
        first_kernel, "first",
        [img16, img32, img16, rows8, turned, turned, ((2, C // 2, PIX), BF16)],
        [shifts], 14,
        kinds, home_x, core_x, recv_x, core_recv_x, vecs, conv1_weight,
    )
    half_t = to_chip(send_t)
    core_half_t = to_core(half_t)

    attn_out = ((batches // 2, 4 * small_rows, 2 * BLK), BF16)
    middle, mixed, grad2, grad_middle, attn_keep, attn_send, vec_a, block2, block2_send = call(
        second_kernel, "second",
        [img32, img16, img16, img32, attn_out, attn_out, rows8, block, block],
        [shifts, img16, ((PIX, 4 * C), BF16), ((C, 8 * BLK), F32)], 24,
        kinds, image, act2, home_c, core_c, recv_c, core_recv_c, vecs,
        conv2_weight, query_weight, key_weight, value_weight, proj_weight,
    )
    block2_away = to_chip(block2_send)
    attn_got = to_batch(attn_send, 1)

    grad1, block1, block1_send, vec_b = call(
        third_kernel, "third",
        [img16, block, block, rows8],
        [shifts, img32], 14,
        kinds, grad2, conv, stats, vecs, conv2_weight,
    )
    block1_away = to_chip(block1_send)

    def weight_grad(name, act_t, index, own, away):
        return call(
            functools.partial(weight_kernel, layer=index), name,
            [((batches // 2, shard_rows, BLK), BF16)] * 2,
            [((C, 2 * PIX), BF16), ((2 * PIX, 9 * BLK), BF16), ((3, PIX + 2 * PAD, BLK), BF16),
             ((9 * C, BLK), F32)],
            18, kinds, act_t, half_t, core_half_t, own, away,
        )

    keep2, send2 = weight_grad("weight2", act2_t, 1, after(block2, block1), block2_away)
    got2 = to_batch(send2, 1)

    def spread(name, bit, keep, got, tail=None, behind=()):
        ways = 1 << min(2, bits - bit)
        rows = keep.shape[1]
        shape = (keep.shape[0] // ways, rows + (VECS if tail else 0), keep.shape[2])
        parts = call(
            functools.partial(route_kernel, bit=bit, first=0), name + str(bit),
            [(shape, BF16)] * ways, [], 16, keep, got, smem=0,
        )
        if tail:
            parts = call(
                functools.partial(route_kernel, bit=bit, first=rows), name + "tail",
                [(shape, BF16)] * ways, [], 16, *tail, *parts, smem=0,
                aliases={2 + j: j for j in range(ways)},
            )
        return parts, [to_batch(after(parts[j], *behind), j << bit) for j in range(1, ways)]

    def finish(name, parts, got):
        for bit in range(3, bits, 2):
            added = total_of([parts[0]] + got).astype(BF16)
            parts, got = spread(name, bit, added, jnp.zeros_like(added))
        return call(
            sum_kernel, "sum" + name, [(parts[0].shape[1:], BF16)], [], 8, parts[0], *got, smem=0
        )[0]

    def gather(shard, *between):
        far = to_chip(shard)
        near = to_core(shard)
        return shard, far, near, to_core(after(far, *between))

    parts_a, got_a = spread("routea", 1, after(attn_keep, send2), attn_got)
    keep1, send1 = weight_grad("weight1", act1_t, 0, after(block1, *parts_a), block1_away)
    got1 = to_batch(send1, 1)
    shard_a = finish("routea", parts_a, [after(g, send1) for g in got_a])
    out_own, grad_own, image_send, vec_keep, vec_send = call(
        fourth_kernel, "fourth",
        [((192, C), BF16), ((192, C), BF16), ((2, 128, C), BF16),
         ((batches // 2, VECS, BLK), BF16), ((batches // 2, VECS, BLK), BF16)],
        [shifts, img32, img16, ((VECS, C), F32)], 14,
        kinds, after(grad1, send1), image, stats, grad_middle, middle, mixed, vecs,
        conv1_weight, proj_weight, vec_a, vec_b,
    )
    image_away = to_chip(image_send)
    vec_got = to_batch(vec_send, 1)
    parts_b, got_b = spread("routeb", 1, after(keep2, vec_keep, shard_a), got2)
    parts_c, got_c = spread("routec", 1, keep1, got1, (vec_keep, vec_got), behind=got_b)
    shard_b = finish("routeb", parts_b, [after(g, parts_c[0]) for g in got_b])
    gathered_a = gather(shard_a)
    gathered_b = gather(shard_b)
    shard_c = finish(
        "routec", parts_c, [after(g, gathered_b[1], gathered_a[1]) for g in got_c]
    )
    small = call(
        join_attn_kernel, "joina", [((small_rows, C), F32)] * 4, [], 8,
        after(gathered_a[0], shard_c), *gathered_a[1:], smem=0,
    )
    joined = [((4, shard_rows, BLK), F32), ((4,), None)]
    (whole2,) = call(
        join_kernel, "joinb", [((shard_rows, C), F32)], joined, 8,
        after(gathered_b[0], shard_c), *gathered_b[1:], smem=0, far_outs=1,
    )
    outputs, input_grad = call(
        unpack_kernel, "unpack",
        [(inputs.shape, BF16)] * 2, [], 8,
        kinds, out_own, grad_own, after(image_away, shard_c),
    )
    gathered_c = gather(shard_c, whole2, outputs, *small)
    whole1, *sums = call(
        join_kernel, "joinc", [((shard_rows, C), F32)] + [((1, small_rows), F32)] * 11, joined, 8,
        *gathered_c, smem=0, far_outs=1,
    )
    v = [row.reshape(small_rows) for row in sums]

    return (
        outputs, input_grad,
        v[9], v[10], whole1, v[8],
        v[6], v[7], whole2, v[5],
        v[0], v[1],
        small[0], v[2], small[1], small[2], v[3], small[3], v[4],
    )


def solution(mesh):
    image = P("batch", "height", None, None)
    vector = P("batch")
    matrix = P("batch", None)
    return jax.shard_map(
        on_device,
        mesh=mesh,
        in_specs=(image, vector) + (P(),) * 17 + (image,),
        out_specs=(
            image, image,
            vector, vector, matrix, vector,
            vector, vector, matrix, vector,
            vector, vector,
            matrix, vector, matrix, matrix, vector, matrix, vector,
        ),
        check_vma=False,
    )
```

```python
import functools

import jax
import jax.numpy as jnp
from jax import lax
from jax.experimental import pallas as pl
from jax.experimental.pallas import tpu as pltpu
from jax.sharding import PartitionSpec as P

GROUPS = 32
UNIT = 8
PIX = 512
PAD = 32
BLK = 128
F32 = jnp.float32
BF16 = jnp.bfloat16
epsilon = 1e-05

VM = pl.BlockSpec(memory_space=pltpu.VMEM)
SM = pl.BlockSpec(memory_space=pltpu.SMEM)
HB = pl.BlockSpec(memory_space=pltpu.HBM)
RATE = 1 << 30
LENGTH = {
    "pack": 10, "stack": 10, "first": 0.02, "second": 30, "third": 20, "fourth": 0.02, "weight2": 1, "weight1": 3, "routeb1": 20,
}


def place(bucket_ref):
    h = lax.axis_index("height")
    upper = lax.div(h, 2)
    tall_first = bucket_ref[0] == 1
    tall_image = jnp.where(tall_first, 0, 1)
    home = jnp.where(upper == 1, tall_image, 1 - tall_image)
    away = 1 - home

    def facts(image):
        kind = bucket_ref[image]
        tall = kind == 1
        stride = jnp.where(tall, 2 * UNIT, 4 * UNIT)
        width = jnp.where(kind == 0, 3 * UNIT, stride)
        return (image, tall, stride, width)

    return h, facts(home), facts(away)


def pixel_col(stride, lanes=1):
    rows = lax.broadcasted_iota(jnp.int32, (PIX, lanes), 0)
    return rows, rows & (stride - 1)


def pixel_mask(facts):
    unused, tall, stride, width = facts
    rows, cols = pixel_col(stride)
    limit = jnp.where(tall, 6 * UNIT * UNIT, 8 * UNIT * UNIT)
    mask = jnp.where((cols < width) & (rows < limit), 1.0, 0.0).astype(F32)
    size = jnp.where(tall | (width == 3 * UNIT), 6 * UNIT * UNIT, 8 * UNIT * UNIT)
    return mask, size.astype(F32)


def group_total(rows):
    members = rows.shape[1] // GROUPS
    lane = lax.broadcasted_iota(jnp.int32, (rows.shape[0], BLK), 1)
    tiles = []
    for tile in range(rows.shape[1] // BLK):
        part = rows[:, tile * BLK : (tile + 1) * BLK]
        step = 1
        while step < members:
            place_in_four = (lane // step) & 3
            added = part
            for d in (1, 2, 3):
                up = pltpu.roll(part, BLK - d * step, 1)
                down = pltpu.roll(part, (4 - d) * step, 1)
                added = added + jnp.where(place_in_four + d < 4, up, down)
            part = added
            step *= 4
        tiles.append(part)
    return jnp.concatenate(tiles, axis=1)


def total(values):
    return jnp.sum(values, axis=0, keepdims=True)


def wide_total(*rows):
    stacked = jnp.concatenate(list(rows) + [rows[0]] * (8 - len(rows)), axis=0)
    sums = group_total(stacked)
    return [sums[i : i + 1] for i in range(len(rows))]


def norm_stats(values, mask, group_size):
    mean = wide_total(total(values))[0] / group_size
    centered = (values - mean) * mask
    variance = wide_total(total(centered * centered))[0] / group_size
    return mean, lax.rsqrt(variance + epsilon)


def silu_norm(values, mean, inverse, gain, shift, mask):
    scale = 0.5 * inverse * gain
    half = values * scale + (0.5 * shift - mean * scale)
    return (half + half * jnp.tanh(half)) * mask


def norm_back(grad, normal, inverse, mask, group_size, gain):
    plain_row = total(grad)
    cross_row = total(grad * normal)
    plain, cross = [v / group_size for v in wide_total(plain_row * gain, cross_row * gain)]
    grad_in = grad * (inverse * gain) - mask * (plain * inverse + normal * (cross * inverse))
    return grad_in, cross_row, plain_row


def silu_slope(u):
    half = 0.5 * u
    t = jnp.tanh(half)
    return (0.5 + 0.5 * t) * (1.0 + half * (1.0 - t))


def mm(a, b):
    return jnp.dot(a, b, preferred_element_type=F32)


def mm_nt(a, b):
    return lax.dot_general(a, b, (((1,), (1,)), ((), ())), preferred_element_type=F32)


def mm_tn(a, b):
    return lax.dot_general(a, b, (((0,), (0,)), ((), ())), preferred_element_type=F32)


def fill_shifts(shift_ref, values, stride):
    unused, cols = pixel_col(stride)
    lanes = values.shape[1]
    zeros = jnp.zeros((PAD, lanes), BF16)
    for q in range(3):
        shift_ref[q, 0:PAD, :] = zeros
        shift_ref[q, PAD + PIX : 2 * PAD + PIX, :] = zeros
    left = jnp.where(cols == 0, 0.0, pltpu.roll(values, 1, 0))
    right = jnp.where(cols == stride - 1, 0.0, pltpu.roll(values, PIX - 1, 0))
    shift_ref[0, PAD : PAD + PIX, :] = left.astype(BF16)
    shift_ref[1, PAD : PAD + PIX, :] = values.astype(BF16)
    shift_ref[2, PAD : PAD + PIX, :] = right.astype(BF16)


def tap(shift_ref, p, q, stride, first=0, count=PIX):
    start = pl.multiple_of(PAD + first + (p - 1) * stride, 16)
    return shift_ref[q, pl.ds(start, count), :]


def conv_forward(shift_ref, weight_ref, stride, out_ref, tile=256):
    for first in range(0, PIX, tile):
        stacked = jnp.concatenate(
            [tap(shift_ref, p, q, stride, first, tile) for p in range(3) for q in range(3)], axis=1
        )
        out_ref[first : first + tile, :] = mm(stacked, weight_ref[...])


def conv_backward(shift_ref, weight_ref, stride, out_ref, tile=256):
    channels = weight_ref.shape[1]
    for first in range(0, PIX, tile):
        acc = None
        for p in range(3):
            for q in range(3):
                row = (8 - (3 * p + q)) * channels
                part = mm_nt(
                    tap(shift_ref, p, q, stride, first, tile), weight_ref[row : row + channels, :]
                )
                acc = part if acc is None else acc + part
        out_ref[first : first + tile, :] = acc


def assemble(out_ref, facts, h, pieces):
    unused, tall, stride, width = facts
    own, partner, received, partner_received = pieces
    other = h ^ 1

    @pl.when(tall)
    def _():
        for ref, index in (
            (own, h),
            (partner, other),
            (received, h ^ 2),
            (partner_received, other ^ 2),
        ):
            out_ref[pl.ds(pl.multiple_of(96 * index, 16), 96), :] = ref[0:96, :]
        out_ref[384:512, :] = jnp.zeros((128, out_ref.shape[1]), out_ref.dtype)

    @pl.when(jnp.logical_not(tall))
    def _():
        low = h & 1
        out_ref[pl.ds(pl.multiple_of(192 * low, 16), 192), :] = own[...]
        out_ref[pl.ds(pl.multiple_of(192 * (1 - low), 16), 192), :] = partner[...]

        @pl.when(low == 0)
        def _():
            out_ref[384:512, :] = received[0:128, :]

        @pl.when(low == 1)
        def _():
            out_ref[384:512, :] = partner_received[0:128, :]


def split_out(full_ref, facts, h, own_ref, send_ref):
    unused, tall, stride, width = facts
    send_h = h ^ 2

    @pl.when(tall)
    def _():
        own_ref[0:96, :] = full_ref[pl.ds(pl.multiple_of(96 * h, 16), 96), :]
        own_ref[96:192, :] = jnp.zeros((96, own_ref.shape[1]), own_ref.dtype)
        send_ref[0:96, :] = full_ref[pl.ds(pl.multiple_of(96 * send_h, 16), 96), :]
        send_ref[96:128, :] = jnp.zeros((32, own_ref.shape[1]), own_ref.dtype)

    @pl.when(jnp.logical_not(tall))
    def _():
        own_ref[...] = full_ref[pl.ds(pl.multiple_of(192 * (h & 1), 16), 192), :]
        send_ref[...] = full_ref[384:512, :]


GAIN1, SHIFT1, BIAS1, GAIN2, SHIFT2, BIAS2, GAIN3, SHIFT3, QB, VB, PB = range(11)
VECS = 16


def vec(vec_ref, index):
    return vec_ref[index : index + 1, :]


def pack(src, facts, dst, wide_rows):
    image, tall, stride, width = facts

    @pl.when(tall)
    def _():
        for row in range(6):
            dst[16 * row : 16 * row + 16, :] = src[image, row, 0:16, :]
        dst[96 : dst.shape[0], :] = jnp.zeros((dst.shape[0] - 96, dst.shape[1]), dst.dtype)

    @pl.when(jnp.logical_not(tall))
    def _():
        for row in range(wide_rows):
            dst[32 * row : 32 * row + 32, :] = src[image, row]


def pack_kernel(bucket_hbm, x_hbm, kinds, away_x, home_x, bucket_ref, x_ref, sems):
    copies = (
        pltpu.make_async_copy(bucket_hbm, bucket_ref, sems.at[0]),
        pltpu.make_async_copy(x_hbm, x_ref, sems.at[1]),
    )
    for copy in copies:
        copy.start()
    for copy in copies:
        copy.wait()
    h, home, away = place(bucket_ref)
    kinds[0] = bucket_ref[0]
    kinds[1] = bucket_ref[1]
    pack(x_ref, away, away_x, 4)
    pack(x_ref, home, home_x, 6)


def stack_kernel(kinds, cot_ref, *refs):
    h, home, away = place(kinds)
    out_ref, away_c, home_c = refs[-3:]
    count = len(refs) - 3
    for index, ref in enumerate(refs[:count]):
        out_ref[index : index + 1, :] = ref[...]
    out_ref[count:, :] = jnp.zeros((VECS - count, out_ref.shape[1]), F32)
    pack(cot_ref, away, away_c, 4)
    pack(cot_ref, home, home_c, 6)


def first_kernel(
    bucket_ref, own, partner, received, partner_received, vecs, weight1,
    image_ref, conv_ref, act2_ref, stats_ref, act1_t, act2_t, send_t,
    shift_ref,
):
    h, home, away = place(bucket_ref)
    stride = home[2]
    mask, pixels = pixel_mask(home)
    channels = vecs.shape[1]
    group_size = pixels * (channels // GROUPS)
    assemble(image_ref, home, h, (own, partner, received, partner_received))
    values = image_ref[...].astype(F32) * mask
    mean1, inverse1 = norm_stats(values, mask, group_size)
    act = silu_norm(values, mean1, inverse1, vec(vecs, GAIN1), vec(vecs, SHIFT1), mask)
    fill_shifts(shift_ref, act, stride)
    act1_t[...] = act.astype(BF16).T
    conv_forward(shift_ref, weight1, stride, conv_ref)
    values = (conv_ref[...] + vec(vecs, BIAS1)) * mask
    conv_ref[...] = values
    mean2, inverse2 = norm_stats(values, mask, group_size)
    act = silu_norm(values, mean2, inverse2, vec(vecs, GAIN2), vec(vecs, SHIFT2), mask)
    act = act.astype(BF16)
    act2_ref[...] = act
    act2_t[...] = act.T
    half = pl.multiple_of((h & 1) * (channels // 2), 16)
    send_t[0] = act1_t[pl.ds(half, channels // 2), :]
    send_t[1] = act2_t[pl.ds(half, channels // 2), :]
    stats_ref[0:1, :] = mean1
    stats_ref[1:2, :] = inverse1
    stats_ref[2:3, :] = mean2
    stats_ref[3:4, :] = inverse2
    stats_ref[4:8, :] = jnp.zeros((4, channels), F32)


def second_kernel(
    bucket_ref, image_ref, act2_ref, own, partner, received, partner_received, vecs,
    weight2, wq, wk, wv, wp,
    middle_ref, mixed_ref, grad2_ref, grad_middle_ref, attn_keep, attn_send, vec_ref,
    block_keep, block_send,
    shift_ref, full_ref, grads_ref, sum_ref,
):
    h, home, away = place(bucket_ref)
    stride = home[2]
    mask, pixels = pixel_mask(home)
    channels = vecs.shape[1]
    group_size = pixels * (channels // GROUPS)
    scaling = channels ** (-0.5)
    assemble(full_ref, home, h, (own, partner, received, partner_received))
    fill_shifts(shift_ref, act2_ref[...].astype(F32), stride)
    conv_forward(shift_ref, weight2, stride, middle_ref)
    middle = mask * (image_ref[...].astype(F32) + (middle_ref[...] + vec(vecs, BIAS2)))
    middle_ref[...] = middle
    mean3, inverse3 = norm_stats(middle, mask, group_size)
    normal = (middle - mean3) * inverse3
    normed = (normal * vec(vecs, GAIN3) + vec(vecs, SHIFT3)).astype(BF16)
    wide = jnp.concatenate([wq[...], wk[...], wv[...]], axis=1)
    joint = mm(normed, wide)
    queries = (joint[:, 0:channels] + vec(vecs, QB)).astype(BF16)
    keys = joint[:, channels : 2 * channels].astype(BF16)
    values = (joint[:, 2 * channels :] + vec(vecs, VB)).astype(BF16)
    lanes = lax.broadcasted_iota(jnp.int32, (1, PIX), 1)
    key_cols = lanes & (stride - 1)
    key_valid = (key_cols < home[3]) & (lanes < jnp.where(home[1], 384, 512))
    scores = jnp.where(key_valid, mm_nt(queries, keys) * scaling, -1000000000.0)
    grad_top = full_ref[...].astype(F32) * mask
    grad_rows = grad_top.astype(BF16)
    grad_mixed = mm_nt(grad_rows, wp[...]).astype(BF16)
    grad_soft = mm_nt(grad_mixed, values)
    raised = jnp.exp(scores - jnp.max(scores, axis=1, keepdims=True))
    soft = raised * (1.0 / jnp.sum(raised, axis=1, keepdims=True))
    soft16 = soft.astype(BF16)
    mixed = mm(soft16, values).astype(BF16)
    mixed_ref[...] = mixed

    grad_values = mm_tn(soft16, grad_mixed).astype(BF16)
    grad_scores = soft * (grad_soft - jnp.sum(soft * grad_soft, axis=1, keepdims=True))
    grad_scores = grad_scores.astype(BF16)
    grad_queries = (mm(grad_scores, keys) * scaling).astype(BF16)
    grad_keys = (mm_tn(grad_scores, queries) * scaling).astype(BF16)
    grads_ref[:, 0:channels] = grad_queries
    grads_ref[:, channels : 2 * channels] = grad_keys
    grads_ref[:, 2 * channels : 3 * channels] = grad_values
    grads_ref[:, 3 * channels : 4 * channels] = grad_rows
    grad_normed = mm_nt(grads_ref[:, 0 : 3 * channels], wide)
    grad_in, gain_grad, shift_grad = norm_back(
        grad_normed, normal, inverse3, mask, group_size, vec(vecs, GAIN3)
    )
    grad_middle = mask * (grad_top + grad_in)
    grad_middle_ref[...] = grad_middle
    grad2 = grad_middle.astype(BF16)
    grad2_ref[...] = grad2
    vec_ref[0:1, :] = gain_grad
    vec_ref[1:2, :] = shift_grad
    vec_ref[2:3, :] = total(grad_queries.astype(F32))
    vec_ref[3:4, :] = total(grad_values.astype(F32))
    vec_ref[4:5, :] = total(grad_top)
    vec_ref[5:6, :] = total(grad2.astype(F32))
    vec_ref[6:8, :] = jnp.zeros((2, channels), F32)

    keep_at = pl.multiple_of(BLK * h, BLK)
    send_at = pl.multiple_of(BLK * (h ^ 2), BLK)
    block_keep[...] = grad2_ref[:, pl.ds(keep_at, BLK)]
    block_send[...] = grad2_ref[:, pl.ds(send_at, BLK)]

    def blocks(index):
        start = index * channels
        return [
            grads_ref[:, pl.ds(pl.multiple_of(start + BLK * h, BLK), BLK)],
            grads_ref[:, pl.ds(pl.multiple_of(start + BLK * (h ^ 2), BLK), BLK)],
        ]

    sum_ref[:, 0 : 6 * BLK] = mm_tn(normed, jnp.concatenate(blocks(0) + blocks(1) + blocks(2), axis=1))
    sum_ref[:, 6 * BLK : 8 * BLK] = mm_tn(mixed, jnp.concatenate(blocks(3), axis=1))
    mine = lax.axis_index("batch") & 1
    pairs = attn_keep.shape[0]
    rows = channels // (2 * pairs)
    for pair in range(pairs):
        for dst, which in ((attn_keep, mine), (attn_send, 1 - mine)):
            part = sum_ref[pl.ds(pl.multiple_of((2 * pair + which) * rows, 8), rows), :].astype(BF16)
            for index in range(4):
                at = index * 2 * BLK
                dst[pair, index * rows : (index + 1) * rows, :] = part[:, at : at + 2 * BLK]


def third_kernel(
    bucket_ref, grad2_ref, conv_ref, stats_ref, vecs, weight2,
    grad1_ref, block_keep, block_send, vec_ref,
    shift_ref, acc_ref,
):
    h, home, away = place(bucket_ref)
    stride = home[2]
    mask, pixels = pixel_mask(home)
    channels = vecs.shape[1]
    group_size = pixels * (channels // GROUPS)
    fill_shifts(shift_ref, grad2_ref[...].astype(F32), stride)
    conv_backward(shift_ref, weight2, stride, acc_ref)
    inverse = stats_ref[3:4, :]
    normal = (conv_ref[...] - stats_ref[2:3, :]) * inverse
    u = normal * vec(vecs, GAIN2) + vec(vecs, SHIFT2)
    grad = mask * acc_ref[...] * silu_slope(u)
    grad_in, gain_grad, shift_grad = norm_back(
        grad, normal, inverse, mask, group_size, vec(vecs, GAIN2)
    )
    grad1 = grad_in.astype(BF16)
    grad1_ref[...] = grad1
    vec_ref[0:1, :] = gain_grad
    vec_ref[1:2, :] = shift_grad
    vec_ref[2:3, :] = total(grad1.astype(F32))
    vec_ref[3:8, :] = jnp.zeros((5, channels), F32)
    block_keep[...] = grad1_ref[:, pl.ds(pl.multiple_of(BLK * h, BLK), BLK)]
    block_send[...] = grad1_ref[:, pl.ds(pl.multiple_of(BLK * (h ^ 2), BLK), BLK)]


def fourth_kernel(
    bucket_ref, grad1_ref, image_ref, stats_ref, grad_middle_ref, middle_ref, mixed_ref, vecs,
    weight1, wp, vec_a, vec_b,
    out_own, grad_own, send_ref, vec_keep, vec_send,
    shift_ref, acc_ref, full_ref, vec_ref,
):
    h, home, away = place(bucket_ref)
    stride = home[2]
    mask, pixels = pixel_mask(home)
    channels = vecs.shape[1]
    group_size = pixels * (channels // GROUPS)
    projected = mm(mixed_ref[...], wp[...]) + vec(vecs, PB)
    full_ref[...] = (mask * (middle_ref[...] + projected)).astype(BF16)
    split_out(full_ref, home, h, out_own, send_ref.at[0])
    fill_shifts(shift_ref, grad1_ref[...].astype(F32), stride)
    conv_backward(shift_ref, weight1, stride, acc_ref)
    inverse = stats_ref[1:2, :]
    normal = (image_ref[...].astype(F32) * mask - stats_ref[0:1, :]) * inverse
    u = normal * vec(vecs, GAIN1) + vec(vecs, SHIFT1)
    grad = mask * acc_ref[...] * silu_slope(u)
    grad_in, gain_grad, shift_grad = norm_back(
        grad, normal, inverse, mask, group_size, vec(vecs, GAIN1)
    )
    full_ref[...] = (mask * (grad_middle_ref[...] + grad_in)).astype(BF16)
    split_out(full_ref, home, h, grad_own, send_ref.at[1])
    vec_ref[0:6, :] = vec_a[0:6, :]
    vec_ref[6:9, :] = vec_b[0:3, :]
    vec_ref[9:10, :] = gain_grad
    vec_ref[10:11, :] = shift_grad
    vec_ref[11:VECS, :] = jnp.zeros((VECS - 11, channels), F32)
    pairs = vec_keep.shape[0]
    rows = channels // (2 * pairs)
    mine = (lax.axis_index("batch") & 1) == 1
    for pair in range(pairs):
        parts = []
        for shard in (2 * pair, 2 * pair + 1):
            start = shard * rows
            tile = start // BLK * BLK
            part = vec_ref[:, tile : tile + BLK]
            parts.append(part if start == tile else pltpu.roll(part, BLK - (start - tile), 1))
        vec_keep[pair] = jnp.where(mine, parts[1], parts[0]).astype(BF16)
        vec_send[pair] = jnp.where(mine, parts[0], parts[1]).astype(BF16)


def weight_kernel(
    bucket_ref, act_t, half_t, partner_half_t, block_own, block_away,
    keep_ref, send_ref, left_ref, right_ref, shift_ref, sum_ref, *, layer,
):
    h, home, away = place(bucket_ref)
    channels = act_t.shape[0]
    half = channels // 2
    left_ref[:, 0:PIX] = act_t[...]
    left_ref[pl.ds(pl.multiple_of((h & 1) * half, 16), half), PIX : 2 * PIX] = half_t[layer]
    left_ref[pl.ds(pl.multiple_of((1 - (h & 1)) * half, 16), half), PIX : 2 * PIX] = (
        partner_half_t[layer]
    )
    for index, (facts, block) in enumerate(((home, block_own), (away, block_away))):
        stride = facts[2]
        fill_shifts(shift_ref, block[...].astype(F32), stride)
        for p in range(3):
            for q in range(3):
                column = (3 * p + q) * BLK
                right_ref[index * PIX : (index + 1) * PIX, column : column + BLK] = tap(
                    shift_ref, 2 - p, 2 - q, stride
                )
    joint = mm(left_ref[...], right_ref[...])
    for t in range(9):
        sum_ref[t * channels : (t + 1) * channels, :] = joint[:, t * BLK : (t + 1) * BLK]
    mine = lax.axis_index("batch") & 1
    pairs = keep_ref.shape[0]
    rows = 9 * channels // (2 * pairs)
    for pair in range(pairs):
        for dst, which in ((keep_ref, mine), (send_ref, 1 - mine)):
            shard = 2 * pair + which
            dst[pair] = sum_ref[pl.ds(pl.multiple_of(shard * rows, 8), rows), :].astype(BF16)


def route_kernel(keep_ref, got_ref, *outs, bit, first):
    ways = len(outs) if first == 0 else len(outs) // 2
    group = (lax.axis_index("batch") >> bit) & (ways - 1)
    rows = keep_ref.shape[1]
    for step, dst in enumerate(outs[-ways:]):
        which = group ^ step
        for index in range(dst.shape[0]):
            at = index * ways + which
            dst[index, first : first + rows, :] = (
                keep_ref[at].astype(F32) + got_ref[at].astype(F32)
            ).astype(BF16)


def total_of(refs):
    added = refs[0].astype(F32)
    for ref in refs[1:]:
        added = added + ref.astype(F32)
    return added


def sum_kernel(*refs):
    refs[-1][...] = total_of([ref[0] for ref in refs[:-1]]).astype(BF16)


def join_kernel(own_ref, far_ref, near_ref, diagonal_ref, *out_refs):
    h = lax.axis_index("height")
    first = 0
    for dst in [ref for ref in out_refs if ref.shape[0] > 1]:
        rows = dst.shape[0]
        for ref, index in ((own_ref, h), (far_ref, h ^ 2), (near_ref, h ^ 1), (diagonal_ref, h ^ 3)):
            dst[:, pl.ds(pl.multiple_of(BLK * index, BLK), BLK)] = ref[first : first + rows, :].astype(F32)
        first += rows
    if own_ref.shape[0] > first:
        own, far = own_ref[first:, :].astype(F32), far_ref[first:, :].astype(F32)
        near, diagonal = near_ref[first:, :].astype(F32), diagonal_ref[first:, :].astype(F32)
        sums = 0.5 * ((own + near) + (far + diagonal))
        for index, dst in enumerate([ref for ref in out_refs if ref.shape[0] == 1]):
            dst[...] = sums[index : index + 1, 0 : dst.shape[1]]


def join_attn_kernel(own_ref, far_ref, near_ref, diagonal_ref, *out_refs):
    h = lax.axis_index("height")
    rows = out_refs[0].shape[0]
    for first, second, index in ((own_ref, far_ref, h), (near_ref, diagonal_ref, h ^ 1)):
        for position in range(2):
            lane, other = position * BLK, (1 - position) * BLK
            column = pl.multiple_of(BLK * (index ^ (2 * position)), BLK)
            for number, dst in enumerate(out_refs):
                at = number * rows
                dst[:, pl.ds(column, BLK)] = first[at : at + rows, lane : lane + BLK].astype(
                    F32
                ) + second[at : at + rows, other : other + BLK].astype(F32)


def unpack_kernel(bucket_ref, out_own, grad_own, away_ref, out_ref, grad_ref):
    h, home, away = place(bucket_ref)
    for own, received, dst in (
        (out_own, away_ref.at[0], out_ref),
        (grad_own, away_ref.at[1], grad_ref),
    ):
        channels = dst.shape[3]
        for facts, src, wide_rows in ((away, received, 4), (home, own, 6)):
            image, tall, stride, width = facts

            @pl.when(tall)
            def _():
                for row in range(6):
                    dst[image, row, 0:16, :] = src[16 * row : 16 * row + 16, :]
                    dst[image, row, 16:32, :] = jnp.zeros((16, channels), dst.dtype)

            @pl.when(jnp.logical_not(tall))
            def _():
                for row in range(wide_rows):
                    dst[image, row] = src[32 * row : 32 * row + 32, :]
                for row in range(wide_rows, 6):
                    dst[image, row] = jnp.zeros((32, channels), dst.dtype)

            if wide_rows == 4:

                @pl.when(jnp.logical_not(tall) & (h == 3))
                def _():
                    for row in range(6):
                        dst[image, row] = jnp.zeros((32, channels), dst.dtype)


def call(kernel, name, outs, scratch, vmem, *operands, smem=1, any_from=99, aliases={}):
    specs = [SM] * smem + [VM] * (len(operands) - smem)
    specs = [HB if i >= any_from else spec for i, spec in enumerate(specs)]
    return pl.pallas_call(
        kernel,
        name=name,
        out_shape=[jax.ShapeDtypeStruct(shape, dtype) for shape, dtype in outs],
        in_specs=specs,
        out_specs=[SM if dtype == jnp.int32 else VM for shape, dtype in outs],
        scratch_shapes=[
            pltpu.SemaphoreType.DMA(shape)
            if dtype is None
            else (pltpu.SMEM if dtype == jnp.int32 else pltpu.VMEM)(shape, dtype)
            for shape, dtype in scratch
        ],
        input_output_aliases=aliases,
        compiler_params=pltpu.CompilerParams(vmem_limit_bytes=vmem << 20),
        cost_estimate=pl.CostEstimate(
            flops=int(LENGTH.get(name, 0.02) * RATE), bytes_accessed=1024, transcendentals=0
        ),
    )(*operands)


def on_device(
    inputs,
    bucket,
    norm1_gain,
    norm1_shift,
    conv1_weight,
    conv1_bias,
    norm2_gain,
    norm2_shift,
    conv2_weight,
    conv2_bias,
    norm3_gain,
    norm3_shift,
    query_weight,
    query_bias,
    key_weight,
    value_weight,
    value_bias,
    proj_weight,
    proj_bias,
    cotangent,
):
    C = inputs.shape[-1]
    batches = lax.axis_size("batch")
    bits = batches.bit_length() - 1
    shard_rows = 9 * C // batches
    small_rows = C // batches

    def row(v):
        return v.reshape(1, C)

    def to_core(v):
        return lax.ppermute(v, "height", [(i, i ^ 1) for i in range(4)])

    def to_chip(v):
        return lax.ppermute(v, "height", [(i, i ^ 2) for i in range(4)])

    def to_batch(v, change):
        return lax.ppermute(v, "batch", [(i, i ^ change) for i in range(batches)])

    def after(v, *others):
        return lax.optimization_barrier((v,) + others)[0]

    img16 = ((PIX, C), BF16)
    img32 = ((PIX, C), F32)
    rows8 = ((8, C), F32)
    block = ((PIX, BLK), BF16)
    turned = ((C, PIX), BF16)
    shifts = ((3, PIX + 2 * PAD, C), BF16)

    kinds, away_x, home_x = call(
        pack_kernel, "pack",
        [((2,), jnp.int32), ((128, C), BF16), ((192, C), BF16)],
        [((2,), jnp.int32), (inputs.shape, BF16), ((2,), None)], 54, bucket, inputs,
        smem=0, any_from=0,
    )
    vectors = (
        norm1_gain, norm1_shift, conv1_bias, norm2_gain, norm2_shift, conv2_bias,
        norm3_gain, norm3_shift, query_bias, value_bias, proj_bias,
    )
    recv_x = to_chip(away_x)
    core_x = to_core(home_x)
    vecs, away_c, home_c = call(
        stack_kernel, "stack", [((VECS, C), F32), ((160, C), BF16), ((192, C), BF16)], [], 8,
        kinds, cotangent, *[row(v) for v in vectors],
    )
    recv_c = to_chip(away_c)
    core_c = to_core(home_c)
    core_recv_c = lax.ppermute(away_c, "height", [(i, i ^ 3) for i in range(4)])
    core_recv_x = to_core(after(recv_x, vecs))

    image, conv, act2, stats, act1_t, act2_t, send_t = call(
        first_kernel, "first",
        [img16, img32, img16, rows8, turned, turned, ((2, C // 2, PIX), BF16)],
        [shifts], 14,
        kinds, home_x, core_x, recv_x, core_recv_x, vecs, conv1_weight,
    )
    half_t = to_chip(send_t)
    core_half_t = to_core(half_t)

    attn_out = ((batches // 2, 4 * small_rows, 2 * BLK), BF16)
    middle, mixed, grad2, grad_middle, attn_keep, attn_send, vec_a, block2, block2_send = call(
        second_kernel, "second",
        [img32, img16, img16, img32, attn_out, attn_out, rows8, block, block],
        [shifts, img16, ((PIX, 4 * C), BF16), ((C, 8 * BLK), F32)], 24,
        kinds, image, act2, home_c, core_c, recv_c, core_recv_c, vecs,
        conv2_weight, query_weight, key_weight, value_weight, proj_weight,
    )
    block2_away = to_chip(block2_send)
    attn_got = to_batch(attn_send, 1)

    grad1, block1, block1_send, vec_b = call(
        third_kernel, "third",
        [img16, block, block, rows8],
        [shifts, img32], 14,
        kinds, grad2, conv, stats, vecs, conv2_weight,
    )

    def weight_grad(name, act_t, index, own, away):
        return call(
            functools.partial(weight_kernel, layer=index), name,
            [((batches // 2, shard_rows, BLK), BF16)] * 2,
            [((C, 2 * PIX), BF16), ((2 * PIX, 9 * BLK), BF16), ((3, PIX + 2 * PAD, BLK), BF16),
             ((9 * C, BLK), F32)],
            18, kinds, act_t, half_t, core_half_t, own, away,
        )

    keep2, send2 = weight_grad("weight2", act2_t, 1, after(block2, block1), block2_away)
    got2 = to_batch(send2, 1)

    def spread(name, bit, keep, got, tail=None, behind=()):
        ways = 1 << min(2, bits - bit)
        rows = keep.shape[1]
        shape = (keep.shape[0] // ways, rows + (VECS if tail else 0), keep.shape[2])
        parts = call(
            functools.partial(route_kernel, bit=bit, first=0), name + str(bit),
            [(shape, BF16)] * ways, [], 16, keep, got, smem=0,
        )
        if tail:
            parts = call(
                functools.partial(route_kernel, bit=bit, first=rows), name + "tail",
                [(shape, BF16)] * ways, [], 16, *tail, *parts, smem=0,
                aliases={2 + j: j for j in range(ways)},
            )
        return parts, [to_batch(after(parts[j], *behind), j << bit) for j in range(1, ways)]

    def finish(name, parts, got):
        for bit in range(3, bits, 2):
            added = total_of([parts[0]] + got).astype(BF16)
            parts, got = spread(name, bit, added, jnp.zeros_like(added))
        return call(
            sum_kernel, "sum" + name, [(parts[0].shape[1:], BF16)], [], 8, parts[0], *got, smem=0
        )[0]

    def gather(shard, *between):
        far = to_chip(shard)
        near = to_core(shard)
        return shard, far, near, to_core(after(far, *between))

    parts_a, got_a = spread("routea", 1, after(attn_keep, send2), attn_got)
    block1_away = to_chip(after(block1_send, *parts_a))
    keep1, send1 = weight_grad("weight1", act1_t, 0, after(block1, *parts_a), block1_away)
    got1 = to_batch(send1, 1)
    shard_a = finish("routea", parts_a, [after(g, send1) for g in got_a])
    parts_b, got_b = spread("routeb", 1, after(keep2, send1, shard_a), got2)
    out_own, grad_own, image_send, vec_keep, vec_send = call(
        fourth_kernel, "fourth",
        [((192, C), BF16), ((192, C), BF16), ((2, 128, C), BF16),
         ((batches // 2, VECS, BLK), BF16), ((batches // 2, VECS, BLK), BF16)],
        [shifts, img32, img16, ((VECS, C), F32)], 14,
        kinds, after(grad1, *parts_b), image, stats, grad_middle, middle, mixed, vecs,
        conv1_weight, proj_weight, vec_a, vec_b,
    )
    image_away = to_chip(image_send)
    vec_got = to_batch(vec_send, 1)
    parts_c, got_c = spread("routec", 1, keep1, got1, (vec_keep, vec_got), behind=got_b)
    shard_b = finish("routeb", parts_b, [after(g, parts_c[0]) for g in got_b])
    gathered_a = gather(shard_a)
    gathered_b = gather(shard_b)
    shard_c = finish(
        "routec", parts_c, [after(g, gathered_b[1], gathered_a[1]) for g in got_c]
    )
    small = call(
        join_attn_kernel, "joina", [((small_rows, C), F32)] * 4, [], 8,
        after(gathered_a[0], shard_c), *gathered_a[1:], smem=0,
    )
    (whole2,) = call(
        join_kernel, "joinb", [((shard_rows, C), F32)], [], 8,
        after(gathered_b[0], shard_c), *gathered_b[1:], smem=0,
    )
    outputs, input_grad = call(
        unpack_kernel, "unpack",
        [(inputs.shape, BF16)] * 2, [], 8,
        kinds, out_own, grad_own, after(image_away, shard_c),
    )
    gathered_c = gather(shard_c, whole2, outputs, *small)
    whole1, *sums = call(
        join_kernel, "joinc", [((shard_rows, C), F32)] + [((1, small_rows), F32)] * 11, [], 8,
        *gathered_c, smem=0,
    )
    v = [row.reshape(small_rows) for row in sums]

    return (
        outputs, input_grad,
        v[9], v[10], whole1, v[8],
        v[6], v[7], whole2, v[5],
        v[0], v[1],
        small[0], v[2], small[1], small[2], v[3], small[3], v[4],
    )


def solution(mesh):
    image = P("batch", "height", None, None)
    vector = P("batch")
    matrix = P("batch", None)
    return jax.shard_map(
        on_device,
        mesh=mesh,
        in_specs=(image, vector) + (P(),) * 17 + (image,),
        out_specs=(
            image, image,
            vector, vector, matrix, vector,
            vector, vector, matrix, vector,
            vector, vector,
            matrix, vector, matrix, matrix, vector, matrix, vector,
        ),
        check_vma=False,
    )
```

```python
import functools

import jax
import jax.numpy as jnp
from jax import lax
from jax.experimental import pallas as pl
from jax.experimental.pallas import tpu as pltpu
from jax.sharding import PartitionSpec as P

GROUPS = 32
UNIT = 8
PIX = 512
PAD = 32
BLK = 128
F32 = jnp.float32
BF16 = jnp.bfloat16
epsilon = 1e-05

VM = pl.BlockSpec(memory_space=pltpu.VMEM)
SM = pl.BlockSpec(memory_space=pltpu.SMEM)
HB = pl.BlockSpec(memory_space=pltpu.HBM)
RATE = 1 << 30
LENGTH = {
    "pack": 10, "stack": 10, "first": 0.02, "second": 30, "third": 20, "fourth": 10, "weight2": 1, "weight1": 3, "routeb1": 20,
}


def place(bucket_ref):
    h = lax.axis_index("height")
    upper = lax.div(h, 2)
    tall_first = bucket_ref[0] == 1
    tall_image = jnp.where(tall_first, 0, 1)
    home = jnp.where(upper == 1, tall_image, 1 - tall_image)
    away = 1 - home

    def facts(image):
        kind = bucket_ref[image]
        tall = kind == 1
        stride = jnp.where(tall, 2 * UNIT, 4 * UNIT)
        width = jnp.where(kind == 0, 3 * UNIT, stride)
        return (image, tall, stride, width)

    return h, facts(home), facts(away)


def pixel_col(stride, lanes=1):
    rows = lax.broadcasted_iota(jnp.int32, (PIX, lanes), 0)
    return rows, rows & (stride - 1)


def pixel_mask(facts):
    unused, tall, stride, width = facts
    rows, cols = pixel_col(stride)
    limit = jnp.where(tall, 6 * UNIT * UNIT, 8 * UNIT * UNIT)
    mask = jnp.where((cols < width) & (rows < limit), 1.0, 0.0).astype(F32)
    size = jnp.where(tall | (width == 3 * UNIT), 6 * UNIT * UNIT, 8 * UNIT * UNIT)
    return mask, size.astype(F32)


def group_total(rows):
    members = rows.shape[1] // GROUPS
    lane = lax.broadcasted_iota(jnp.int32, (rows.shape[0], BLK), 1)
    tiles = []
    for tile in range(rows.shape[1] // BLK):
        part = rows[:, tile * BLK : (tile + 1) * BLK]
        step = 1
        while step < members:
            place_in_four = (lane // step) & 3
            added = part
            for d in (1, 2, 3):
                up = pltpu.roll(part, BLK - d * step, 1)
                down = pltpu.roll(part, (4 - d) * step, 1)
                added = added + jnp.where(place_in_four + d < 4, up, down)
            part = added
            step *= 4
        tiles.append(part)
    return jnp.concatenate(tiles, axis=1)


def total(values):
    return jnp.sum(values, axis=0, keepdims=True)


def wide_total(*rows):
    stacked = jnp.concatenate(list(rows) + [rows[0]] * (8 - len(rows)), axis=0)
    sums = group_total(stacked)
    return [sums[i : i + 1] for i in range(len(rows))]


def norm_stats(values, mask, group_size):
    mean = wide_total(total(values))[0] / group_size
    centered = (values - mean) * mask
    variance = wide_total(total(centered * centered))[0] / group_size
    return mean, lax.rsqrt(variance + epsilon)


def silu_norm(values, mean, inverse, gain, shift, mask):
    scale = 0.5 * inverse * gain
    half = values * scale + (0.5 * shift - mean * scale)
    return (half + half * jnp.tanh(half)) * mask


def norm_back(grad, normal, inverse, mask, group_size, gain):
    plain_row = total(grad)
    cross_row = total(grad * normal)
    plain, cross = [v / group_size for v in wide_total(plain_row * gain, cross_row * gain)]
    grad_in = grad * (inverse * gain) - mask * (plain * inverse + normal * (cross * inverse))
    return grad_in, cross_row, plain_row


def silu_slope(u):
    half = 0.5 * u
    t = jnp.tanh(half)
    return (0.5 + 0.5 * t) * (1.0 + half * (1.0 - t))


def mm(a, b):
    return jnp.dot(a, b, preferred_element_type=F32)


def mm_nt(a, b):
    return lax.dot_general(a, b, (((1,), (1,)), ((), ())), preferred_element_type=F32)


def mm_tn(a, b):
    return lax.dot_general(a, b, (((0,), (0,)), ((), ())), preferred_element_type=F32)


def fill_shifts(shift_ref, values, stride):
    unused, cols = pixel_col(stride)
    lanes = values.shape[1]
    zeros = jnp.zeros((PAD, lanes), BF16)
    for q in range(3):
        shift_ref[q, 0:PAD, :] = zeros
        shift_ref[q, PAD + PIX : 2 * PAD + PIX, :] = zeros
    left = jnp.where(cols == 0, 0.0, pltpu.roll(values, 1, 0))
    right = jnp.where(cols == stride - 1, 0.0, pltpu.roll(values, PIX - 1, 0))
    shift_ref[0, PAD : PAD + PIX, :] = left.astype(BF16)
    shift_ref[1, PAD : PAD + PIX, :] = values.astype(BF16)
    shift_ref[2, PAD : PAD + PIX, :] = right.astype(BF16)


def tap(shift_ref, p, q, stride, first=0, count=PIX):
    start = pl.multiple_of(PAD + first + (p - 1) * stride, 16)
    return shift_ref[q, pl.ds(start, count), :]


def conv_forward(shift_ref, weight_ref, stride, out_ref, tile=256):
    for first in range(0, PIX, tile):
        stacked = jnp.concatenate(
            [tap(shift_ref, p, q, stride, first, tile) for p in range(3) for q in range(3)], axis=1
        )
        out_ref[first : first + tile, :] = mm(stacked, weight_ref[...])


def conv_backward(shift_ref, weight_ref, stride, out_ref, tile=256):
    channels = weight_ref.shape[1]
    for first in range(0, PIX, tile):
        acc = None
        for p in range(3):
            for q in range(3):
                row = (8 - (3 * p + q)) * channels
                part = mm_nt(
                    tap(shift_ref, p, q, stride, first, tile), weight_ref[row : row + channels, :]
                )
                acc = part if acc is None else acc + part
        out_ref[first : first + tile, :] = acc


def assemble(out_ref, facts, h, pieces):
    unused, tall, stride, width = facts
    own, partner, received, partner_received = pieces
    other = h ^ 1

    @pl.when(tall)
    def _():
        for ref, index in (
            (own, h),
            (partner, other),
            (received, h ^ 2),
            (partner_received, other ^ 2),
        ):
            out_ref[pl.ds(pl.multiple_of(96 * index, 16), 96), :] = ref[0:96, :]
        out_ref[384:512, :] = jnp.zeros((128, out_ref.shape[1]), out_ref.dtype)

    @pl.when(jnp.logical_not(tall))
    def _():
        low = h & 1
        out_ref[pl.ds(pl.multiple_of(192 * low, 16), 192), :] = own[...]
        out_ref[pl.ds(pl.multiple_of(192 * (1 - low), 16), 192), :] = partner[...]

        @pl.when(low == 0)
        def _():
            out_ref[384:512, :] = received[0:128, :]

        @pl.when(low == 1)
        def _():
            out_ref[384:512, :] = partner_received[0:128, :]


def split_out(full_ref, facts, h, own_ref, send_ref):
    unused, tall, stride, width = facts
    send_h = h ^ 2

    @pl.when(tall)
    def _():
        own_ref[0:96, :] = full_ref[pl.ds(pl.multiple_of(96 * h, 16), 96), :]
        own_ref[96:192, :] = jnp.zeros((96, own_ref.shape[1]), own_ref.dtype)
        send_ref[0:96, :] = full_ref[pl.ds(pl.multiple_of(96 * send_h, 16), 96), :]
        send_ref[96:128, :] = jnp.zeros((32, own_ref.shape[1]), own_ref.dtype)

    @pl.when(jnp.logical_not(tall))
    def _():
        own_ref[...] = full_ref[pl.ds(pl.multiple_of(192 * (h & 1), 16), 192), :]
        send_ref[...] = full_ref[384:512, :]


GAIN1, SHIFT1, BIAS1, GAIN2, SHIFT2, BIAS2, GAIN3, SHIFT3, QB, VB, PB = range(11)
VECS = 16


def vec(vec_ref, index):
    return vec_ref[index : index + 1, :]


def pack(src, facts, dst, wide_rows):
    image, tall, stride, width = facts

    @pl.when(tall)
    def _():
        for row in range(6):
            dst[16 * row : 16 * row + 16, :] = src[image, row, 0:16, :]
        dst[96 : dst.shape[0], :] = jnp.zeros((dst.shape[0] - 96, dst.shape[1]), dst.dtype)

    @pl.when(jnp.logical_not(tall))
    def _():
        for row in range(wide_rows):
            dst[32 * row : 32 * row + 32, :] = src[image, row]


def pack_kernel(bucket_hbm, x_hbm, kinds, away_x, home_x, bucket_ref, x_ref, sems):
    copies = (
        pltpu.make_async_copy(bucket_hbm, bucket_ref, sems.at[0]),
        pltpu.make_async_copy(x_hbm, x_ref, sems.at[1]),
    )
    for copy in copies:
        copy.start()
    for copy in copies:
        copy.wait()
    h, home, away = place(bucket_ref)
    kinds[0] = bucket_ref[0]
    kinds[1] = bucket_ref[1]
    pack(x_ref, away, away_x, 4)
    pack(x_ref, home, home_x, 6)


def stack_kernel(kinds, cot_ref, wq, wk, wv, *refs):
    h, home, away = place(kinds)
    out_ref, away_c, home_c, wide_ref = refs[-4:]
    count = len(refs) - 4
    for index, ref in enumerate(refs[:count]):
        out_ref[index : index + 1, :] = ref[...]
    out_ref[count:, :] = jnp.zeros((VECS - count, out_ref.shape[1]), F32)
    pack(cot_ref, away, away_c, 4)
    pack(cot_ref, home, home_c, 6)
    channels = wq.shape[1]
    for index, ref in enumerate((wq, wk, wv)):
        wide_ref[:, index * channels : (index + 1) * channels] = ref[...]


def first_kernel(
    bucket_ref, own, partner, received, partner_received, vecs, weight1,
    image_ref, conv_ref, act2_ref, stats_ref, act1_t, act2_t, send_t,
    shift_ref,
):
    h, home, away = place(bucket_ref)
    stride = home[2]
    mask, pixels = pixel_mask(home)
    channels = vecs.shape[1]
    group_size = pixels * (channels // GROUPS)
    assemble(image_ref, home, h, (own, partner, received, partner_received))
    values = image_ref[...].astype(F32) * mask
    mean1, inverse1 = norm_stats(values, mask, group_size)
    act = silu_norm(values, mean1, inverse1, vec(vecs, GAIN1), vec(vecs, SHIFT1), mask)
    fill_shifts(shift_ref, act, stride)
    act1_t[...] = act.astype(BF16).T
    conv_forward(shift_ref, weight1, stride, conv_ref)
    values = (conv_ref[...] + vec(vecs, BIAS1)) * mask
    conv_ref[...] = values
    mean2, inverse2 = norm_stats(values, mask, group_size)
    act = silu_norm(values, mean2, inverse2, vec(vecs, GAIN2), vec(vecs, SHIFT2), mask)
    act = act.astype(BF16)
    act2_ref[...] = act
    act2_t[...] = act.T
    half = pl.multiple_of((h & 1) * (channels // 2), 16)
    send_t[0] = act1_t[pl.ds(half, channels // 2), :]
    send_t[1] = act2_t[pl.ds(half, channels // 2), :]
    stats_ref[0:1, :] = mean1
    stats_ref[1:2, :] = inverse1
    stats_ref[2:3, :] = mean2
    stats_ref[3:4, :] = inverse2
    stats_ref[4:8, :] = jnp.zeros((4, channels), F32)


def second_kernel(
    bucket_ref, image_ref, act2_ref, own, partner, received, partner_received, vecs,
    weight2, wide_ref, wp,
    middle_ref, mixed_ref, grad2_ref, grad_middle_ref, attn_keep, attn_send, vec_ref,
    block_keep, block_send,
    shift_ref, full_ref, grads_ref, sum_ref,
):
    h, home, away = place(bucket_ref)
    stride = home[2]
    mask, pixels = pixel_mask(home)
    channels = vecs.shape[1]
    group_size = pixels * (channels // GROUPS)
    scaling = channels ** (-0.5)
    assemble(full_ref, home, h, (own, partner, received, partner_received))
    fill_shifts(shift_ref, act2_ref[...].astype(F32), stride)
    conv_forward(shift_ref, weight2, stride, middle_ref)
    middle = mask * (image_ref[...].astype(F32) + (middle_ref[...] + vec(vecs, BIAS2)))
    middle_ref[...] = middle
    mean3, inverse3 = norm_stats(middle, mask, group_size)
    normal = (middle - mean3) * inverse3
    normed = (normal * vec(vecs, GAIN3) + vec(vecs, SHIFT3)).astype(BF16)
    joint = mm(normed, wide_ref[...])
    queries = (joint[:, 0:channels] + vec(vecs, QB)).astype(BF16)
    keys = joint[:, channels : 2 * channels].astype(BF16)
    values = (joint[:, 2 * channels :] + vec(vecs, VB)).astype(BF16)
    lanes = lax.broadcasted_iota(jnp.int32, (1, PIX), 1)
    key_cols = lanes & (stride - 1)
    key_valid = (key_cols < home[3]) & (lanes < jnp.where(home[1], 384, 512))
    scores = jnp.where(key_valid, mm_nt(queries, keys) * scaling, -1000000000.0)
    grad_top = full_ref[...].astype(F32) * mask
    grad_rows = grad_top.astype(BF16)
    grad_mixed = mm_nt(grad_rows, wp[...]).astype(BF16)
    grad_soft = mm_nt(grad_mixed, values)
    raised = jnp.exp(scores - jnp.max(scores, axis=1, keepdims=True))
    soft = raised * (1.0 / jnp.sum(raised, axis=1, keepdims=True))
    soft16 = soft.astype(BF16)
    mixed = mm(soft16, values).astype(BF16)
    mixed_ref[...] = mixed

    grad_values = mm_tn(soft16, grad_mixed).astype(BF16)
    grad_scores = soft * (grad_soft - jnp.sum(soft * grad_soft, axis=1, keepdims=True))
    grad_scores = grad_scores.astype(BF16)
    grad_queries = (mm(grad_scores, keys) * scaling).astype(BF16)
    grad_keys = (mm_tn(grad_scores, queries) * scaling).astype(BF16)
    grads_ref[:, 0:channels] = grad_queries
    grads_ref[:, channels : 2 * channels] = grad_keys
    grads_ref[:, 2 * channels : 3 * channels] = grad_values
    grads_ref[:, 3 * channels : 4 * channels] = grad_rows
    grad_normed = mm_nt(grads_ref[:, 0 : 3 * channels], wide_ref[...])
    grad_in, gain_grad, shift_grad = norm_back(
        grad_normed, normal, inverse3, mask, group_size, vec(vecs, GAIN3)
    )
    grad_middle = mask * (grad_top + grad_in)
    grad_middle_ref[...] = grad_middle
    grad2 = grad_middle.astype(BF16)
    grad2_ref[...] = grad2
    vec_ref[0:1, :] = gain_grad
    vec_ref[1:2, :] = shift_grad
    vec_ref[2:3, :] = total(grad_queries.astype(F32))
    vec_ref[3:4, :] = total(grad_values.astype(F32))
    vec_ref[4:5, :] = total(grad_top)
    vec_ref[5:6, :] = total(grad2.astype(F32))
    vec_ref[6:8, :] = jnp.zeros((2, channels), F32)

    keep_at = pl.multiple_of(BLK * h, BLK)
    send_at = pl.multiple_of(BLK * (h ^ 2), BLK)
    block_keep[...] = grad2_ref[:, pl.ds(keep_at, BLK)]
    block_send[...] = grad2_ref[:, pl.ds(send_at, BLK)]

    def blocks(index):
        start = index * channels
        return [
            grads_ref[:, pl.ds(pl.multiple_of(start + BLK * h, BLK), BLK)],
            grads_ref[:, pl.ds(pl.multiple_of(start + BLK * (h ^ 2), BLK), BLK)],
        ]

    sum_ref[:, 0 : 6 * BLK] = mm_tn(normed, jnp.concatenate(blocks(0) + blocks(1) + blocks(2), axis=1))
    sum_ref[:, 6 * BLK : 8 * BLK] = mm_tn(mixed, jnp.concatenate(blocks(3), axis=1))
    mine = lax.axis_index("batch") & 1
    pairs = attn_keep.shape[0]
    rows = channels // (2 * pairs)
    for pair in range(pairs):
        for dst, which in ((attn_keep, mine), (attn_send, 1 - mine)):
            part = sum_ref[pl.ds(pl.multiple_of((2 * pair + which) * rows, 8), rows), :].astype(BF16)
            for index in range(4):
                at = index * 2 * BLK
                dst[pair, index * rows : (index + 1) * rows, :] = part[:, at : at + 2 * BLK]


def third_kernel(
    bucket_ref, grad2_ref, conv_ref, stats_ref, vecs, weight2,
    grad1_ref, block_keep, block_send, vec_ref,
    shift_ref, acc_ref,
):
    h, home, away = place(bucket_ref)
    stride = home[2]
    mask, pixels = pixel_mask(home)
    channels = vecs.shape[1]
    group_size = pixels * (channels // GROUPS)
    fill_shifts(shift_ref, grad2_ref[...].astype(F32), stride)
    conv_backward(shift_ref, weight2, stride, acc_ref)
    inverse = stats_ref[3:4, :]
    normal = (conv_ref[...] - stats_ref[2:3, :]) * inverse
    u = normal * vec(vecs, GAIN2) + vec(vecs, SHIFT2)
    grad = mask * acc_ref[...] * silu_slope(u)
    grad_in, gain_grad, shift_grad = norm_back(
        grad, normal, inverse, mask, group_size, vec(vecs, GAIN2)
    )
    grad1 = grad_in.astype(BF16)
    grad1_ref[...] = grad1
    vec_ref[0:1, :] = gain_grad
    vec_ref[1:2, :] = shift_grad
    vec_ref[2:3, :] = total(grad1.astype(F32))
    vec_ref[3:8, :] = jnp.zeros((5, channels), F32)
    block_keep[...] = grad1_ref[:, pl.ds(pl.multiple_of(BLK * h, BLK), BLK)]
    block_send[...] = grad1_ref[:, pl.ds(pl.multiple_of(BLK * (h ^ 2), BLK), BLK)]


def fourth_kernel(
    bucket_ref, grad1_ref, image_ref, stats_ref, grad_middle_ref, middle_ref, mixed_ref, vecs,
    weight1, wp, vec_a, vec_b,
    out_own, grad_own, send_ref, vec_keep, vec_send,
    shift_ref, acc_ref, full_ref, vec_ref,
):
    h, home, away = place(bucket_ref)
    stride = home[2]
    mask, pixels = pixel_mask(home)
    channels = vecs.shape[1]
    group_size = pixels * (channels // GROUPS)
    projected = mm(mixed_ref[...], wp[...]) + vec(vecs, PB)
    full_ref[...] = (mask * (middle_ref[...] + projected)).astype(BF16)
    split_out(full_ref, home, h, out_own, send_ref.at[0])
    fill_shifts(shift_ref, grad1_ref[...].astype(F32), stride)
    conv_backward(shift_ref, weight1, stride, acc_ref)
    inverse = stats_ref[1:2, :]
    normal = (image_ref[...].astype(F32) * mask - stats_ref[0:1, :]) * inverse
    u = normal * vec(vecs, GAIN1) + vec(vecs, SHIFT1)
    grad = mask * acc_ref[...] * silu_slope(u)
    grad_in, gain_grad, shift_grad = norm_back(
        grad, normal, inverse, mask, group_size, vec(vecs, GAIN1)
    )
    full_ref[...] = (mask * (grad_middle_ref[...] + grad_in)).astype(BF16)
    split_out(full_ref, home, h, grad_own, send_ref.at[1])
    vec_ref[0:6, :] = vec_a[0:6, :]
    vec_ref[6:9, :] = vec_b[0:3, :]
    vec_ref[9:10, :] = gain_grad
    vec_ref[10:11, :] = shift_grad
    vec_ref[11:VECS, :] = jnp.zeros((VECS - 11, channels), F32)
    pairs = vec_keep.shape[0]
    rows = channels // (2 * pairs)
    mine = (lax.axis_index("batch") & 1) == 1
    for pair in range(pairs):
        parts = []
        for shard in (2 * pair, 2 * pair + 1):
            start = shard * rows
            tile = start // BLK * BLK
            part = vec_ref[:, tile : tile + BLK]
            parts.append(part if start == tile else pltpu.roll(part, BLK - (start - tile), 1))
        vec_keep[pair] = jnp.where(mine, parts[1], parts[0]).astype(BF16)
        vec_send[pair] = jnp.where(mine, parts[0], parts[1]).astype(BF16)


def weight_kernel(
    bucket_ref, act_t, half_t, partner_half_t, block_own, block_away,
    keep_ref, send_ref, left_ref, right_ref, shift_ref, sum_ref, *, layer,
):
    h, home, away = place(bucket_ref)
    channels = act_t.shape[0]
    half = channels // 2
    left_ref[:, 0:PIX] = act_t[...]
    left_ref[pl.ds(pl.multiple_of((h & 1) * half, 16), half), PIX : 2 * PIX] = half_t[layer]
    left_ref[pl.ds(pl.multiple_of((1 - (h & 1)) * half, 16), half), PIX : 2 * PIX] = (
        partner_half_t[layer]
    )
    for index, (facts, block) in enumerate(((home, block_own), (away, block_away))):
        stride = facts[2]
        fill_shifts(shift_ref, block[...].astype(F32), stride)
        for p in range(3):
            for q in range(3):
                column = (3 * p + q) * BLK
                right_ref[index * PIX : (index + 1) * PIX, column : column + BLK] = tap(
                    shift_ref, 2 - p, 2 - q, stride
                )
    joint = mm(left_ref[...], right_ref[...])
    for t in range(9):
        sum_ref[t * channels : (t + 1) * channels, :] = joint[:, t * BLK : (t + 1) * BLK]
    mine = lax.axis_index("batch") & 1
    pairs = keep_ref.shape[0]
    rows = 9 * channels // (2 * pairs)
    for pair in range(pairs):
        for dst, which in ((keep_ref, mine), (send_ref, 1 - mine)):
            shard = 2 * pair + which
            dst[pair] = sum_ref[pl.ds(pl.multiple_of(shard * rows, 8), rows), :].astype(BF16)


def route_kernel(keep_ref, got_ref, *outs, bit, first):
    ways = len(outs) if first == 0 else len(outs) // 2
    group = (lax.axis_index("batch") >> bit) & (ways - 1)
    rows = keep_ref.shape[1]
    for step, dst in enumerate(outs[-ways:]):
        which = group ^ step
        for index in range(dst.shape[0]):
            at = index * ways + which
            dst[index, first : first + rows, :] = (
                keep_ref[at].astype(F32) + got_ref[at].astype(F32)
            ).astype(BF16)


def total_of(refs):
    added = refs[0].astype(F32)
    for ref in refs[1:]:
        added = added + ref.astype(F32)
    return added


def sum_kernel(*refs):
    refs[-1][...] = total_of([ref[0] for ref in refs[:-1]]).astype(BF16)


def join_kernel(own_ref, far_ref, near_ref, diagonal_ref, *out_refs):
    h = lax.axis_index("height")
    first = 0
    for dst in [ref for ref in out_refs if ref.shape[0] > 1]:
        rows = dst.shape[0]
        for ref, index in ((own_ref, h), (far_ref, h ^ 2), (near_ref, h ^ 1), (diagonal_ref, h ^ 3)):
            dst[:, pl.ds(pl.multiple_of(BLK * index, BLK), BLK)] = ref[first : first + rows, :].astype(F32)
        first += rows
    if own_ref.shape[0] > first:
        own, far = own_ref[first:, :].astype(F32), far_ref[first:, :].astype(F32)
        near, diagonal = near_ref[first:, :].astype(F32), diagonal_ref[first:, :].astype(F32)
        sums = 0.5 * ((own + near) + (far + diagonal))
        for index, dst in enumerate([ref for ref in out_refs if ref.shape[0] == 1]):
            dst[...] = sums[index : index + 1, 0 : dst.shape[1]]


def join_attn_kernel(own_ref, far_ref, near_ref, diagonal_ref, *out_refs):
    h = lax.axis_index("height")
    rows = out_refs[0].shape[0]
    for first, second, index in ((own_ref, far_ref, h), (near_ref, diagonal_ref, h ^ 1)):
        for position in range(2):
            lane, other = position * BLK, (1 - position) * BLK
            column = pl.multiple_of(BLK * (index ^ (2 * position)), BLK)
            for number, dst in enumerate(out_refs):
                at = number * rows
                dst[:, pl.ds(column, BLK)] = first[at : at + rows, lane : lane + BLK].astype(
                    F32
                ) + second[at : at + rows, other : other + BLK].astype(F32)


def unpack_kernel(bucket_ref, out_own, grad_own, away_ref, out_ref, grad_ref):
    h, home, away = place(bucket_ref)
    for own, received, dst in (
        (out_own, away_ref.at[0], out_ref),
        (grad_own, away_ref.at[1], grad_ref),
    ):
        channels = dst.shape[3]
        for facts, src, wide_rows in ((away, received, 4), (home, own, 6)):
            image, tall, stride, width = facts

            @pl.when(tall)
            def _():
                for row in range(6):
                    dst[image, row, 0:16, :] = src[16 * row : 16 * row + 16, :]
                    dst[image, row, 16:32, :] = jnp.zeros((16, channels), dst.dtype)

            @pl.when(jnp.logical_not(tall))
            def _():
                for row in range(wide_rows):
                    dst[image, row] = src[32 * row : 32 * row + 32, :]
                for row in range(wide_rows, 6):
                    dst[image, row] = jnp.zeros((32, channels), dst.dtype)

            if wide_rows == 4:

                @pl.when(jnp.logical_not(tall) & (h == 3))
                def _():
                    for row in range(6):
                        dst[image, row] = jnp.zeros((32, channels), dst.dtype)


def call(kernel, name, outs, scratch, vmem, *operands, smem=1, any_from=99, aliases={}):
    specs = [SM] * smem + [VM] * (len(operands) - smem)
    specs = [HB if i >= any_from else spec for i, spec in enumerate(specs)]
    return pl.pallas_call(
        kernel,
        name=name,
        out_shape=[jax.ShapeDtypeStruct(shape, dtype) for shape, dtype in outs],
        in_specs=specs,
        out_specs=[SM if dtype == jnp.int32 else VM for shape, dtype in outs],
        scratch_shapes=[
            pltpu.SemaphoreType.DMA(shape)
            if dtype is None
            else (pltpu.SMEM if dtype == jnp.int32 else pltpu.VMEM)(shape, dtype)
            for shape, dtype in scratch
        ],
        input_output_aliases=aliases,
        compiler_params=pltpu.CompilerParams(vmem_limit_bytes=vmem << 20),
        cost_estimate=pl.CostEstimate(
            flops=int(LENGTH.get(name, 0.02) * RATE), bytes_accessed=1024, transcendentals=0
        ),
    )(*operands)


def on_device(
    inputs,
    bucket,
    norm1_gain,
    norm1_shift,
    conv1_weight,
    conv1_bias,
    norm2_gain,
    norm2_shift,
    conv2_weight,
    conv2_bias,
    norm3_gain,
    norm3_shift,
    query_weight,
    query_bias,
    key_weight,
    value_weight,
    value_bias,
    proj_weight,
    proj_bias,
    cotangent,
):
    C = inputs.shape[-1]
    batches = lax.axis_size("batch")
    bits = batches.bit_length() - 1
    shard_rows = 9 * C // batches
    small_rows = C // batches

    def row(v):
        return v.reshape(1, C)

    def to_core(v):
        return lax.ppermute(v, "height", [(i, i ^ 1) for i in range(4)])

    def to_chip(v):
        return lax.ppermute(v, "height", [(i, i ^ 2) for i in range(4)])

    def to_batch(v, change):
        return lax.ppermute(v, "batch", [(i, i ^ change) for i in range(batches)])

    def after(v, *others):
        return lax.optimization_barrier((v,) + others)[0]

    img16 = ((PIX, C), BF16)
    img32 = ((PIX, C), F32)
    rows8 = ((8, C), F32)
    block = ((PIX, BLK), BF16)
    turned = ((C, PIX), BF16)
    shifts = ((3, PIX + 2 * PAD, C), BF16)

    kinds, away_x, home_x = call(
        pack_kernel, "pack",
        [((2,), jnp.int32), ((128, C), BF16), ((192, C), BF16)],
        [((2,), jnp.int32), (inputs.shape, BF16), ((2,), None)], 54, bucket, inputs,
        smem=0, any_from=0,
    )
    vectors = (
        norm1_gain, norm1_shift, conv1_bias, norm2_gain, norm2_shift, conv2_bias,
        norm3_gain, norm3_shift, query_bias, value_bias, proj_bias,
    )
    recv_x = to_chip(away_x)
    core_x = to_core(home_x)
    vecs, away_c, home_c, wide = call(
        stack_kernel, "stack",
        [((VECS, C), F32), ((160, C), BF16), ((192, C), BF16), ((C, 3 * C), BF16)], [], 8,
        kinds, cotangent, query_weight, key_weight, value_weight, *[row(v) for v in vectors],
    )
    recv_c = to_chip(away_c)
    core_c = to_core(home_c)
    core_recv_c = lax.ppermute(away_c, "height", [(i, i ^ 3) for i in range(4)])
    core_recv_x = to_core(after(recv_x, vecs))

    image, conv, act2, stats, act1_t, act2_t, send_t = call(
        first_kernel, "first",
        [img16, img32, img16, rows8, turned, turned, ((2, C // 2, PIX), BF16)],
        [shifts], 14,
        kinds, home_x, core_x, recv_x, core_recv_x, vecs, conv1_weight,
    )
    half_t = to_chip(send_t)
    core_half_t = to_core(half_t)

    attn_out = ((batches // 2, 4 * small_rows, 2 * BLK), BF16)
    middle, mixed, grad2, grad_middle, attn_keep, attn_send, vec_a, block2, block2_send = call(
        second_kernel, "second",
        [img32, img16, img16, img32, attn_out, attn_out, rows8, block, block],
        [shifts, img16, ((PIX, 4 * C), BF16), ((C, 8 * BLK), F32)], 24,
        kinds, image, act2, home_c, core_c, recv_c, core_recv_c, vecs,
        conv2_weight, wide, proj_weight,
    )
    block2_away = to_chip(block2_send)
    attn_got = to_batch(attn_send, 1)

    grad1, block1, block1_send, vec_b = call(
        third_kernel, "third",
        [img16, block, block, rows8],
        [shifts, img32], 14,
        kinds, grad2, conv, stats, vecs, conv2_weight,
    )
    block1_away = to_chip(block1_send)

    def weight_grad(name, act_t, index, own, away):
        return call(
            functools.partial(weight_kernel, layer=index), name,
            [((batches // 2, shard_rows, BLK), BF16)] * 2,
            [((C, 2 * PIX), BF16), ((2 * PIX, 9 * BLK), BF16), ((3, PIX + 2 * PAD, BLK), BF16),
             ((9 * C, BLK), F32)],
            18, kinds, act_t, half_t, core_half_t, own, away,
        )

    keep2, send2 = weight_grad("weight2", act2_t, 1, after(block2, block1), block2_away)
    got2 = to_batch(send2, 1)

    def spread(name, bit, keep, got, tail=None, behind=()):
        ways = 1 << min(2, bits - bit)
        rows = keep.shape[1]
        shape = (keep.shape[0] // ways, rows + (VECS if tail else 0), keep.shape[2])
        parts = call(
            functools.partial(route_kernel, bit=bit, first=0), name + str(bit),
            [(shape, BF16)] * ways, [], 16, keep, got, smem=0,
        )
        if tail:
            parts = call(
                functools.partial(route_kernel, bit=bit, first=rows), name + "tail",
                [(shape, BF16)] * ways, [], 16, *tail, *parts, smem=0,
                aliases={2 + j: j for j in range(ways)},
            )
        return parts, [to_batch(after(parts[j], *behind), j << bit) for j in range(1, ways)]

    def finish(name, parts, got):
        for bit in range(3, bits, 2):
            added = total_of([parts[0]] + got).astype(BF16)
            parts, got = spread(name, bit, added, jnp.zeros_like(added))
        return call(
            sum_kernel, "sum" + name, [(parts[0].shape[1:], BF16)], [], 8, parts[0], *got, smem=0
        )[0]

    def gather(shard, *between):
        far = to_chip(shard)
        near = to_core(shard)
        return shard, far, near, to_core(after(far, *between))

    parts_a, got_a = spread("routea", 1, after(attn_keep, send2), attn_got)
    keep1, send1 = weight_grad("weight1", act1_t, 0, after(block1, *parts_a), block1_away)
    got1 = to_batch(send1, 1)
    shard_a = finish("routea", parts_a, [after(g, send1) for g in got_a])
    out_own, grad_own, image_send, vec_keep, vec_send = call(
        fourth_kernel, "fourth",
        [((192, C), BF16), ((192, C), BF16), ((2, 128, C), BF16),
         ((batches // 2, VECS, BLK), BF16), ((batches // 2, VECS, BLK), BF16)],
        [shifts, img32, img16, ((VECS, C), F32)], 14,
        kinds, after(grad1, send1), image, stats, grad_middle, middle, mixed, vecs,
        conv1_weight, proj_weight, vec_a, vec_b,
    )
    image_away = to_chip(image_send)
    vec_got = to_batch(vec_send, 1)
    parts_b, got_b = spread("routeb", 1, after(keep2, vec_keep, shard_a), got2)
    parts_c, got_c = spread("routec", 1, keep1, got1, (vec_keep, vec_got), behind=got_b)
    shard_b = finish("routeb", parts_b, [after(g, parts_c[0]) for g in got_b])
    gathered_a = gather(shard_a)
    gathered_b = gather(shard_b)
    shard_c = finish(
        "routec", parts_c, [after(g, gathered_b[1], gathered_a[1]) for g in got_c]
    )
    small = call(
        join_attn_kernel, "joina", [((small_rows, C), F32)] * 4, [], 8,
        after(gathered_a[0], shard_c), *gathered_a[1:], smem=0,
    )
    (whole2,) = call(
        join_kernel, "joinb", [((shard_rows, C), F32)], [], 8,
        after(gathered_b[0], shard_c), *gathered_b[1:], smem=0,
    )
    outputs, input_grad = call(
        unpack_kernel, "unpack",
        [(inputs.shape, BF16)] * 2, [], 8,
        kinds, out_own, grad_own, after(image_away, shard_c),
    )
    gathered_c = gather(shard_c, whole2, outputs, *small)
    whole1, *sums = call(
        join_kernel, "joinc", [((shard_rows, C), F32)] + [((1, small_rows), F32)] * 11, [], 8,
        *gathered_c, smem=0,
    )
    v = [row.reshape(small_rows) for row in sums]

    return (
        outputs, input_grad,
        v[9], v[10], whole1, v[8],
        v[6], v[7], whole2, v[5],
        v[0], v[1],
        small[0], v[2], small[1], small[2], v[3], small[3], v[4],
    )


def solution(mesh):
    image = P("batch", "height", None, None)
    vector = P("batch")
    matrix = P("batch", None)
    return jax.shard_map(
        on_device,
        mesh=mesh,
        in_specs=(image, vector) + (P(),) * 17 + (image,),
        out_specs=(
            image, image,
            vector, vector, matrix, vector,
            vector, vector, matrix, vector,
            vector, vector,
            matrix, vector, matrix, matrix, vector, matrix, vector,
        ),
        check_vma=False,
    )
```

```python
import functools

import jax
import jax.numpy as jnp
from jax import lax
from jax.experimental import pallas as pl
from jax.experimental.pallas import tpu as pltpu
from jax.sharding import PartitionSpec as P

GROUPS = 32
UNIT = 8
PIX = 512
PAD = 32
BLK = 128
F32 = jnp.float32
BF16 = jnp.bfloat16
epsilon = 1e-05

VM = pl.BlockSpec(memory_space=pltpu.VMEM)
SM = pl.BlockSpec(memory_space=pltpu.SMEM)
HB = pl.BlockSpec(memory_space=pltpu.HBM)
RATE = 1 << 30
LENGTH = {
    "pack": 10, "stack": 10, "first": 0.02, "second": 30, "third": 20, "fourth": 0.02, "weight2": 1, "weight1": 3, "routeb1": 20,
}


def place(bucket_ref):
    h = lax.axis_index("height")
    upper = lax.div(h, 2)
    tall_first = bucket_ref[0] == 1
    tall_image = jnp.where(tall_first, 0, 1)
    home = jnp.where(upper == 1, tall_image, 1 - tall_image)
    away = 1 - home

    def facts(image):
        kind = bucket_ref[image]
        tall = kind == 1
        stride = jnp.where(tall, 2 * UNIT, 4 * UNIT)
        width = jnp.where(kind == 0, 3 * UNIT, stride)
        return (image, tall, stride, width)

    return h, facts(home), facts(away)


def pixel_col(stride, lanes=1):
    rows = lax.broadcasted_iota(jnp.int32, (PIX, lanes), 0)
    return rows, rows & (stride - 1)


def pixel_mask(facts):
    unused, tall, stride, width = facts
    rows, cols = pixel_col(stride)
    limit = jnp.where(tall, 6 * UNIT * UNIT, 8 * UNIT * UNIT)
    mask = jnp.where((cols < width) & (rows < limit), 1.0, 0.0).astype(F32)
    size = jnp.where(tall | (width == 3 * UNIT), 6 * UNIT * UNIT, 8 * UNIT * UNIT)
    return mask, size.astype(F32)


def group_total(rows):
    members = rows.shape[1] // GROUPS
    lane = lax.broadcasted_iota(jnp.int32, (rows.shape[0], BLK), 1)
    tiles = []
    for tile in range(rows.shape[1] // BLK):
        part = rows[:, tile * BLK : (tile + 1) * BLK]
        step = 1
        while step < members:
            place_in_four = (lane // step) & 3
            added = part
            for d in (1, 2, 3):
                up = pltpu.roll(part, BLK - d * step, 1)
                down = pltpu.roll(part, (4 - d) * step, 1)
                added = added + jnp.where(place_in_four + d < 4, up, down)
            part = added
            step *= 4
        tiles.append(part)
    return jnp.concatenate(tiles, axis=1)


def total(values):
    return jnp.sum(values, axis=0, keepdims=True)


def wide_total(*rows):
    stacked = jnp.concatenate(list(rows) + [rows[0]] * (8 - len(rows)), axis=0)
    sums = group_total(stacked)
    return [sums[i : i + 1] for i in range(len(rows))]


def norm_stats(values, mask, group_size):
    mean = wide_total(total(values))[0] / group_size
    centered = (values - mean) * mask
    variance = wide_total(total(centered * centered))[0] / group_size
    return mean, lax.rsqrt(variance + epsilon)


def silu_norm(values, mean, inverse, gain, shift, mask):
    scale = 0.5 * inverse * gain
    half = values * scale + (0.5 * shift - mean * scale)
    return (half + half * jnp.tanh(half)) * mask


def norm_back(grad, normal, inverse, mask, group_size, gain):
    plain_row = total(grad)
    cross_row = total(grad * normal)
    plain, cross = [v / group_size for v in wide_total(plain_row * gain, cross_row * gain)]
    grad_in = grad * (inverse * gain) - mask * (plain * inverse + normal * (cross * inverse))
    return grad_in, cross_row, plain_row


def silu_slope(u):
    half = 0.5 * u
    t = jnp.tanh(half)
    return (0.5 + 0.5 * t) * (1.0 + half * (1.0 - t))


def mm(a, b):
    return jnp.dot(a, b, preferred_element_type=F32)


def mm_nt(a, b):
    return lax.dot_general(a, b, (((1,), (1,)), ((), ())), preferred_element_type=F32)


def mm_tn(a, b):
    return lax.dot_general(a, b, (((0,), (0,)), ((), ())), preferred_element_type=F32)


def fill_shifts(shift_ref, values, stride):
    unused, cols = pixel_col(stride)
    lanes = values.shape[1]
    zeros = jnp.zeros((PAD, lanes), BF16)
    for q in range(3):
        shift_ref[q, 0:PAD, :] = zeros
        shift_ref[q, PAD + PIX : 2 * PAD + PIX, :] = zeros
    left = jnp.where(cols == 0, 0.0, pltpu.roll(values, 1, 0))
    right = jnp.where(cols == stride - 1, 0.0, pltpu.roll(values, PIX - 1, 0))
    shift_ref[0, PAD : PAD + PIX, :] = left.astype(BF16)
    shift_ref[1, PAD : PAD + PIX, :] = values.astype(BF16)
    shift_ref[2, PAD : PAD + PIX, :] = right.astype(BF16)


def tap(shift_ref, p, q, stride, first=0, count=PIX):
    start = pl.multiple_of(PAD + first + (p - 1) * stride, 16)
    return shift_ref[q, pl.ds(start, count), :]


def conv_forward(shift_ref, weight_ref, stride, out_ref, tile=256):
    for first in range(0, PIX, tile):
        stacked = jnp.concatenate(
            [tap(shift_ref, p, q, stride, first, tile) for p in range(3) for q in range(3)], axis=1
        )
        out_ref[first : first + tile, :] = mm(stacked, weight_ref[...])


def conv_backward(shift_ref, weight_ref, stride, out_ref, tile=256):
    channels = weight_ref.shape[1]
    for first in range(0, PIX, tile):
        acc = None
        for p in range(3):
            for q in range(3):
                row = (8 - (3 * p + q)) * channels
                part = mm_nt(
                    tap(shift_ref, p, q, stride, first, tile), weight_ref[row : row + channels, :]
                )
                acc = part if acc is None else acc + part
        out_ref[first : first + tile, :] = acc


def assemble(out_ref, facts, h, pieces):
    unused, tall, stride, width = facts
    own, partner, received, partner_received = pieces
    other = h ^ 1

    @pl.when(tall)
    def _():
        for ref, index in (
            (own, h),
            (partner, other),
            (received, h ^ 2),
            (partner_received, other ^ 2),
        ):
            out_ref[pl.ds(pl.multiple_of(96 * index, 16), 96), :] = ref[0:96, :]
        out_ref[384:512, :] = jnp.zeros((128, out_ref.shape[1]), out_ref.dtype)

    @pl.when(jnp.logical_not(tall))
    def _():
        low = h & 1
        out_ref[pl.ds(pl.multiple_of(192 * low, 16), 192), :] = own[...]
        out_ref[pl.ds(pl.multiple_of(192 * (1 - low), 16), 192), :] = partner[...]

        @pl.when(low == 0)
        def _():
            out_ref[384:512, :] = received[0:128, :]

        @pl.when(low == 1)
        def _():
            out_ref[384:512, :] = partner_received[0:128, :]


def split_out(full_ref, facts, h, own_ref, send_ref):
    unused, tall, stride, width = facts
    send_h = h ^ 2

    @pl.when(tall)
    def _():
        own_ref[0:96, :] = full_ref[pl.ds(pl.multiple_of(96 * h, 16), 96), :]
        own_ref[96:192, :] = jnp.zeros((96, own_ref.shape[1]), own_ref.dtype)
        send_ref[0:96, :] = full_ref[pl.ds(pl.multiple_of(96 * send_h, 16), 96), :]
        send_ref[96:128, :] = jnp.zeros((32, own_ref.shape[1]), own_ref.dtype)

    @pl.when(jnp.logical_not(tall))
    def _():
        own_ref[...] = full_ref[pl.ds(pl.multiple_of(192 * (h & 1), 16), 192), :]
        send_ref[...] = full_ref[384:512, :]


GAIN1, SHIFT1, BIAS1, GAIN2, SHIFT2, BIAS2, GAIN3, SHIFT3, QB, VB, PB = range(11)
VECS = 16


def vec(vec_ref, index):
    return vec_ref[index : index + 1, :]


def pack(src, facts, dst, wide_rows):
    image, tall, stride, width = facts

    @pl.when(tall)
    def _():
        for row in range(6):
            dst[16 * row : 16 * row + 16, :] = src[image, row, 0:16, :]
        dst[96 : dst.shape[0], :] = jnp.zeros((dst.shape[0] - 96, dst.shape[1]), dst.dtype)

    @pl.when(jnp.logical_not(tall))
    def _():
        for row in range(wide_rows):
            dst[32 * row : 32 * row + 32, :] = src[image, row]


def pack_kernel(bucket_hbm, x_hbm, kinds, away_x, home_x, bucket_ref, x_ref, sems):
    copies = (
        pltpu.make_async_copy(bucket_hbm, bucket_ref, sems.at[0]),
        pltpu.make_async_copy(x_hbm, x_ref, sems.at[1]),
    )
    for copy in copies:
        copy.start()
    for copy in copies:
        copy.wait()
    h, home, away = place(bucket_ref)
    kinds[0] = bucket_ref[0]
    kinds[1] = bucket_ref[1]
    pack(x_ref, away, away_x, 4)
    pack(x_ref, home, home_x, 6)


def stack_kernel(kinds, cot_ref, *refs):
    h, home, away = place(kinds)
    out_ref, away_c, home_c = refs[-3:]
    count = len(refs) - 3
    for index, ref in enumerate(refs[:count]):
        out_ref[index : index + 1, :] = ref[...]
    out_ref[count:, :] = jnp.zeros((VECS - count, out_ref.shape[1]), F32)
    pack(cot_ref, away, away_c, 4)
    pack(cot_ref, home, home_c, 6)


def first_kernel(
    bucket_ref, own, partner, received, partner_received, vecs, weight1,
    image_ref, conv_ref, act2_ref, stats_ref, act1_t, act2_t, send_t,
    shift_ref,
):
    h, home, away = place(bucket_ref)
    stride = home[2]
    mask, pixels = pixel_mask(home)
    channels = vecs.shape[1]
    group_size = pixels * (channels // GROUPS)
    assemble(image_ref, home, h, (own, partner, received, partner_received))
    values = image_ref[...].astype(F32) * mask
    mean1, inverse1 = norm_stats(values, mask, group_size)
    act = silu_norm(values, mean1, inverse1, vec(vecs, GAIN1), vec(vecs, SHIFT1), mask)
    fill_shifts(shift_ref, act, stride)
    act1_t[...] = act.astype(BF16).T
    conv_forward(shift_ref, weight1, stride, conv_ref)
    values = (conv_ref[...] + vec(vecs, BIAS1)) * mask
    conv_ref[...] = values
    mean2, inverse2 = norm_stats(values, mask, group_size)
    act = silu_norm(values, mean2, inverse2, vec(vecs, GAIN2), vec(vecs, SHIFT2), mask)
    act = act.astype(BF16)
    act2_ref[...] = act
    act2_t[...] = act.T
    half = pl.multiple_of((h & 1) * (channels // 2), 16)
    send_t[0] = act1_t[pl.ds(half, channels // 2), :]
    send_t[1] = act2_t[pl.ds(half, channels // 2), :]
    stats_ref[0:1, :] = mean1
    stats_ref[1:2, :] = inverse1
    stats_ref[2:3, :] = mean2
    stats_ref[3:4, :] = inverse2
    stats_ref[4:8, :] = jnp.zeros((4, channels), F32)


def second_kernel(
    bucket_ref, image_ref, act2_ref, own, partner, received, partner_received, vecs,
    weight2, wq, wk, wv, wp,
    middle_ref, mixed_ref, grad2_ref, grad_middle_ref, attn_keep, attn_send, vec_ref,
    block_keep, block_send,
    shift_ref, full_ref, grads_ref, sum_ref,
):
    h, home, away = place(bucket_ref)
    stride = home[2]
    mask, pixels = pixel_mask(home)
    channels = vecs.shape[1]
    group_size = pixels * (channels // GROUPS)
    scaling = channels ** (-0.5)
    assemble(full_ref, home, h, (own, partner, received, partner_received))
    fill_shifts(shift_ref, act2_ref[...].astype(F32), stride)
    conv_forward(shift_ref, weight2, stride, middle_ref)
    middle = mask * (image_ref[...].astype(F32) + (middle_ref[...] + vec(vecs, BIAS2)))
    middle_ref[...] = middle
    mean3, inverse3 = norm_stats(middle, mask, group_size)
    normal = (middle - mean3) * inverse3
    normed = (normal * vec(vecs, GAIN3) + vec(vecs, SHIFT3)).astype(BF16)
    wide = jnp.concatenate([wq[...], wk[...], wv[...]], axis=1)
    joint = mm(normed, wide)
    queries = (joint[:, 0:channels] + vec(vecs, QB)).astype(BF16)
    keys = joint[:, channels : 2 * channels].astype(BF16)
    values = (joint[:, 2 * channels :] + vec(vecs, VB)).astype(BF16)
    lanes = lax.broadcasted_iota(jnp.int32, (1, PIX), 1)
    key_cols = lanes & (stride - 1)
    key_valid = (key_cols < home[3]) & (lanes < jnp.where(home[1], 384, 512))
    scores = jnp.where(key_valid, mm_nt(queries, keys) * scaling, -1000000000.0)
    grad_top = full_ref[...].astype(F32) * mask
    grad_rows = grad_top.astype(BF16)
    grad_mixed = mm_nt(grad_rows, wp[...]).astype(BF16)
    grad_soft = mm_nt(grad_mixed, values)
    raised = jnp.exp(scores - jnp.max(scores, axis=1, keepdims=True))
    soft = raised * (1.0 / jnp.sum(raised, axis=1, keepdims=True))
    soft16 = soft.astype(BF16)
    mixed = mm(soft16, values).astype(BF16)
    mixed_ref[...] = mixed

    grad_values = mm_tn(soft16, grad_mixed).astype(BF16)
    grad_scores = soft * (grad_soft - jnp.sum(soft * grad_soft, axis=1, keepdims=True))
    grad_scores = grad_scores.astype(BF16)
    grad_queries = (mm(grad_scores, keys) * scaling).astype(BF16)
    grad_keys = (mm_tn(grad_scores, queries) * scaling).astype(BF16)
    grads_ref[:, 0:channels] = grad_queries
    grads_ref[:, channels : 2 * channels] = grad_keys
    grads_ref[:, 2 * channels : 3 * channels] = grad_values
    grads_ref[:, 3 * channels : 4 * channels] = grad_rows
    grad_normed = mm_nt(grads_ref[:, 0 : 3 * channels], wide)
    grad_in, gain_grad, shift_grad = norm_back(
        grad_normed, normal, inverse3, mask, group_size, vec(vecs, GAIN3)
    )
    grad_middle = mask * (grad_top + grad_in)
    grad_middle_ref[...] = grad_middle
    grad2 = grad_middle.astype(BF16)
    grad2_ref[...] = grad2
    vec_ref[0:1, :] = gain_grad
    vec_ref[1:2, :] = shift_grad
    vec_ref[2:3, :] = total(grad_queries.astype(F32))
    vec_ref[3:4, :] = total(grad_values.astype(F32))
    vec_ref[4:5, :] = total(grad_top)
    vec_ref[5:6, :] = total(grad2.astype(F32))
    vec_ref[6:8, :] = jnp.zeros((2, channels), F32)

    keep_at = pl.multiple_of(BLK * h, BLK)
    send_at = pl.multiple_of(BLK * (h ^ 2), BLK)
    block_keep[...] = grad2_ref[:, pl.ds(keep_at, BLK)]
    block_send[...] = grad2_ref[:, pl.ds(send_at, BLK)]

    def blocks(index):
        start = index * channels
        return [
            grads_ref[:, pl.ds(pl.multiple_of(start + BLK * h, BLK), BLK)],
            grads_ref[:, pl.ds(pl.multiple_of(start + BLK * (h ^ 2), BLK), BLK)],
        ]

    sum_ref[:, 0 : 6 * BLK] = mm_tn(normed, jnp.concatenate(blocks(0) + blocks(1) + blocks(2), axis=1))
    sum_ref[:, 6 * BLK : 8 * BLK] = mm_tn(mixed, jnp.concatenate(blocks(3), axis=1))
    mine = lax.axis_index("batch") & 1
    pairs = attn_keep.shape[0]
    rows = channels // (2 * pairs)
    for pair in range(pairs):
        for dst, which in ((attn_keep, mine), (attn_send, 1 - mine)):
            part = sum_ref[pl.ds(pl.multiple_of((2 * pair + which) * rows, 8), rows), :].astype(BF16)
            for index in range(4):
                at = index * 2 * BLK
                dst[pair, index * rows : (index + 1) * rows, :] = part[:, at : at + 2 * BLK]


def third_kernel(
    bucket_ref, grad2_ref, conv_ref, stats_ref, vecs, weight2,
    grad1_ref, block_keep, block_send, vec_ref,
    shift_ref, acc_ref,
):
    h, home, away = place(bucket_ref)
    stride = home[2]
    mask, pixels = pixel_mask(home)
    channels = vecs.shape[1]
    group_size = pixels * (channels // GROUPS)
    fill_shifts(shift_ref, grad2_ref[...].astype(F32), stride)
    conv_backward(shift_ref, weight2, stride, acc_ref)
    inverse = stats_ref[3:4, :]
    normal = (conv_ref[...] - stats_ref[2:3, :]) * inverse
    u = normal * vec(vecs, GAIN2) + vec(vecs, SHIFT2)
    grad = mask * acc_ref[...] * silu_slope(u)
    grad_in, gain_grad, shift_grad = norm_back(
        grad, normal, inverse, mask, group_size, vec(vecs, GAIN2)
    )
    grad1 = grad_in.astype(BF16)
    grad1_ref[...] = grad1
    vec_ref[0:1, :] = gain_grad
    vec_ref[1:2, :] = shift_grad
    vec_ref[2:3, :] = total(grad1.astype(F32))
    vec_ref[3:8, :] = jnp.zeros((5, channels), F32)
    block_keep[...] = grad1_ref[:, pl.ds(pl.multiple_of(BLK * h, BLK), BLK)]
    block_send[...] = grad1_ref[:, pl.ds(pl.multiple_of(BLK * (h ^ 2), BLK), BLK)]


def fourth_kernel(
    bucket_ref, grad1_ref, image_ref, stats_ref, grad_middle_ref, middle_ref, mixed_ref, vecs,
    weight1, wp, vec_a, vec_b,
    out_own, grad_own, send_ref, vec_keep, vec_send,
    shift_ref, acc_ref, full_ref, vec_ref,
):
    h, home, away = place(bucket_ref)
    stride = home[2]
    mask, pixels = pixel_mask(home)
    channels = vecs.shape[1]
    group_size = pixels * (channels // GROUPS)
    projected = mm(mixed_ref[...], wp[...]) + vec(vecs, PB)
    full_ref[...] = (mask * (middle_ref[...] + projected)).astype(BF16)
    split_out(full_ref, home, h, out_own, send_ref.at[0])
    fill_shifts(shift_ref, grad1_ref[...].astype(F32), stride)
    conv_backward(shift_ref, weight1, stride, acc_ref)
    inverse = stats_ref[1:2, :]
    normal = (image_ref[...].astype(F32) * mask - stats_ref[0:1, :]) * inverse
    u = normal * vec(vecs, GAIN1) + vec(vecs, SHIFT1)
    grad = mask * acc_ref[...] * silu_slope(u)
    grad_in, gain_grad, shift_grad = norm_back(
        grad, normal, inverse, mask, group_size, vec(vecs, GAIN1)
    )
    full_ref[...] = (mask * (grad_middle_ref[...] + grad_in)).astype(BF16)
    split_out(full_ref, home, h, grad_own, send_ref.at[1])
    vec_ref[0:6, :] = vec_a[0:6, :]
    vec_ref[6:9, :] = vec_b[0:3, :]
    vec_ref[9:10, :] = gain_grad
    vec_ref[10:11, :] = shift_grad
    vec_ref[11:VECS, :] = jnp.zeros((VECS - 11, channels), F32)
    pairs = vec_keep.shape[0]
    rows = channels // (2 * pairs)
    mine = (lax.axis_index("batch") & 1) == 1
    for pair in range(pairs):
        parts = []
        for shard in (2 * pair, 2 * pair + 1):
            start = shard * rows
            tile = start // BLK * BLK
            part = vec_ref[:, tile : tile + BLK]
            parts.append(part if start == tile else pltpu.roll(part, BLK - (start - tile), 1))
        vec_keep[pair] = jnp.where(mine, parts[1], parts[0]).astype(BF16)
        vec_send[pair] = jnp.where(mine, parts[0], parts[1]).astype(BF16)


def weight_kernel(
    bucket_ref, act_t, half_t, partner_half_t, block_own, block_away,
    keep_ref, send_ref, left_ref, right_ref, shift_ref, sum_ref, *, layer,
):
    h, home, away = place(bucket_ref)
    channels = act_t.shape[0]
    half = channels // 2
    left_ref[:, 0:PIX] = act_t[...]
    left_ref[pl.ds(pl.multiple_of((h & 1) * half, 16), half), PIX : 2 * PIX] = half_t[layer]
    left_ref[pl.ds(pl.multiple_of((1 - (h & 1)) * half, 16), half), PIX : 2 * PIX] = (
        partner_half_t[layer]
    )
    for index, (facts, block) in enumerate(((home, block_own), (away, block_away))):
        stride = facts[2]
        fill_shifts(shift_ref, block[...].astype(F32), stride)
        for p in range(3):
            for q in range(3):
                column = (3 * p + q) * BLK
                right_ref[index * PIX : (index + 1) * PIX, column : column + BLK] = tap(
                    shift_ref, 2 - p, 2 - q, stride
                )
    joint = mm(left_ref[...], right_ref[...])
    for t in range(9):
        sum_ref[t * channels : (t + 1) * channels, :] = joint[:, t * BLK : (t + 1) * BLK]
    mine = lax.axis_index("batch") & 1
    pairs = keep_ref.shape[0]
    rows = 9 * channels // (2 * pairs)
    for pair in range(pairs):
        for dst, which in ((keep_ref, mine), (send_ref, 1 - mine)):
            shard = 2 * pair + which
            dst[pair] = sum_ref[pl.ds(pl.multiple_of(shard * rows, 8), rows), :].astype(BF16)


def route_kernel(keep_ref, got_ref, *outs, bit, first):
    ways = len(outs) if first == 0 else len(outs) // 2
    group = (lax.axis_index("batch") >> bit) & (ways - 1)
    rows = keep_ref.shape[1]
    for step, dst in enumerate(outs[-ways:]):
        which = group ^ step
        for index in range(dst.shape[0]):
            at = index * ways + which
            dst[index, first : first + rows, :] = (
                keep_ref[at].astype(F32) + got_ref[at].astype(F32)
            ).astype(BF16)


def total_of(refs):
    added = refs[0].astype(F32)
    for ref in refs[1:]:
        added = added + ref.astype(F32)
    return added


def sum_kernel(*refs):
    refs[-1][...] = total_of([ref[0] for ref in refs[:-1]]).astype(BF16)


def join_kernel(own_ref, far_ref, near_ref, diagonal_ref, *out_refs):
    h = lax.axis_index("height")
    first = 0
    for dst in [ref for ref in out_refs if ref.shape[0] > 1]:
        rows = dst.shape[0]
        for ref, index in ((own_ref, h), (far_ref, h ^ 2), (near_ref, h ^ 1), (diagonal_ref, h ^ 3)):
            dst[:, pl.ds(pl.multiple_of(BLK * index, BLK), BLK)] = ref[first : first + rows, :].astype(F32)
        first += rows
    if own_ref.shape[0] > first:
        own, far = own_ref[first:, :].astype(F32), far_ref[first:, :].astype(F32)
        near, diagonal = near_ref[first:, :].astype(F32), diagonal_ref[first:, :].astype(F32)
        sums = 0.5 * ((own + near) + (far + diagonal))
        for index, dst in enumerate([ref for ref in out_refs if ref.shape[0] == 1]):
            dst[...] = sums[index : index + 1, 0 : dst.shape[1]]


def join_attn_kernel(own_ref, far_ref, near_ref, diagonal_ref, *out_refs):
    h = lax.axis_index("height")
    rows = out_refs[0].shape[0]
    for first, second, index in ((own_ref, far_ref, h), (near_ref, diagonal_ref, h ^ 1)):
        for position in range(2):
            lane, other = position * BLK, (1 - position) * BLK
            column = pl.multiple_of(BLK * (index ^ (2 * position)), BLK)
            for number, dst in enumerate(out_refs):
                at = number * rows
                dst[:, pl.ds(column, BLK)] = first[at : at + rows, lane : lane + BLK].astype(
                    F32
                ) + second[at : at + rows, other : other + BLK].astype(F32)


def unpack_kernel(bucket_ref, out_own, grad_own, away_ref, out_ref, grad_ref):
    h, home, away = place(bucket_ref)
    for own, received, dst in (
        (out_own, away_ref.at[0], out_ref),
        (grad_own, away_ref.at[1], grad_ref),
    ):
        channels = dst.shape[3]
        for facts, src, wide_rows in ((away, received, 4), (home, own, 6)):
            image, tall, stride, width = facts

            @pl.when(tall)
            def _():
                for row in range(6):
                    dst[image, row, 0:16, :] = src[16 * row : 16 * row + 16, :]
                    dst[image, row, 16:32, :] = jnp.zeros((16, channels), dst.dtype)

            @pl.when(jnp.logical_not(tall))
            def _():
                for row in range(wide_rows):
                    dst[image, row] = src[32 * row : 32 * row + 32, :]
                for row in range(wide_rows, 6):
                    dst[image, row] = jnp.zeros((32, channels), dst.dtype)

            if wide_rows == 4:

                @pl.when(jnp.logical_not(tall) & (h == 3))
                def _():
                    for row in range(6):
                        dst[image, row] = jnp.zeros((32, channels), dst.dtype)


def call(kernel, name, outs, scratch, vmem, *operands, smem=1, any_from=99, aliases={}):
    specs = [SM] * smem + [VM] * (len(operands) - smem)
    specs = [HB if i >= any_from else spec for i, spec in enumerate(specs)]
    return pl.pallas_call(
        kernel,
        name=name,
        out_shape=[jax.ShapeDtypeStruct(shape, dtype) for shape, dtype in outs],
        in_specs=specs,
        out_specs=[SM if dtype == jnp.int32 else VM for shape, dtype in outs],
        scratch_shapes=[
            pltpu.SemaphoreType.DMA(shape)
            if dtype is None
            else (pltpu.SMEM if dtype == jnp.int32 else pltpu.VMEM)(shape, dtype)
            for shape, dtype in scratch
        ],
        input_output_aliases=aliases,
        compiler_params=pltpu.CompilerParams(vmem_limit_bytes=vmem << 20),
        cost_estimate=pl.CostEstimate(
            flops=int(LENGTH.get(name, 0.02) * RATE), bytes_accessed=1024, transcendentals=0
        ),
    )(*operands)


def on_device(
    inputs,
    bucket,
    norm1_gain,
    norm1_shift,
    conv1_weight,
    conv1_bias,
    norm2_gain,
    norm2_shift,
    conv2_weight,
    conv2_bias,
    norm3_gain,
    norm3_shift,
    query_weight,
    query_bias,
    key_weight,
    value_weight,
    value_bias,
    proj_weight,
    proj_bias,
    cotangent,
):
    C = inputs.shape[-1]
    batches = lax.axis_size("batch")
    bits = batches.bit_length() - 1
    shard_rows = 9 * C // batches
    small_rows = C // batches

    def row(v):
        return v.reshape(1, C)

    def to_core(v):
        return lax.ppermute(v, "height", [(i, i ^ 1) for i in range(4)])

    def to_chip(v):
        return lax.ppermute(v, "height", [(i, i ^ 2) for i in range(4)])

    def to_batch(v, change):
        return lax.ppermute(v, "batch", [(i, i ^ change) for i in range(batches)])

    def after(v, *others):
        return lax.optimization_barrier((v,) + others)[0]

    img16 = ((PIX, C), BF16)
    img32 = ((PIX, C), F32)
    rows8 = ((8, C), F32)
    block = ((PIX, BLK), BF16)
    turned = ((C, PIX), BF16)
    shifts = ((3, PIX + 2 * PAD, C), BF16)

    kinds, away_x, home_x = call(
        pack_kernel, "pack",
        [((2,), jnp.int32), ((128, C), BF16), ((192, C), BF16)],
        [((2,), jnp.int32), (inputs.shape, BF16), ((2,), None)], 54, bucket, inputs,
        smem=0, any_from=0,
    )
    vectors = (
        norm1_gain, norm1_shift, conv1_bias, norm2_gain, norm2_shift, conv2_bias,
        norm3_gain, norm3_shift, query_bias, value_bias, proj_bias,
    )
    recv_x = to_chip(away_x)
    core_x = to_core(home_x)
    vecs, away_c, home_c = call(
        stack_kernel, "stack", [((VECS, C), F32), ((160, C), BF16), ((192, C), BF16)], [], 8,
        kinds, cotangent, *[row(v) for v in vectors],
    )
    recv_c = to_chip(away_c)
    core_c = to_core(home_c)
    core_recv_c = lax.ppermute(away_c, "height", [(i, i ^ 3) for i in range(4)])
    core_recv_x = to_core(after(recv_x, vecs))

    image, conv, act2, stats, act1_t, act2_t, send_t = call(
        first_kernel, "first",
        [img16, img32, img16, rows8, turned, turned, ((2, C // 2, PIX), BF16)],
        [shifts], 14,
        kinds, home_x, core_x, recv_x, core_recv_x, vecs, conv1_weight,
    )
    half_t = to_chip(send_t)
    core_half_t = to_core(half_t)

    attn_out = ((batches // 2, 4 * small_rows, 2 * BLK), BF16)
    middle, mixed, grad2, grad_middle, attn_keep, attn_send, vec_a, block2, block2_send = call(
        second_kernel, "second",
        [img32, img16, img16, img32, attn_out, attn_out, rows8, block, block],
        [shifts, img16, ((PIX, 4 * C), BF16), ((C, 8 * BLK), F32)], 24,
        kinds, image, act2, home_c, core_c, recv_c, core_recv_c, vecs,
        conv2_weight, query_weight, key_weight, value_weight, proj_weight,
    )
    block2_away = to_chip(block2_send)
    attn_got = to_batch(attn_send, 1)

    grad1, block1, block1_send, vec_b = call(
        third_kernel, "third",
        [img16, block, block, rows8],
        [shifts, img32], 14,
        kinds, grad2, conv, stats, vecs, conv2_weight,
    )
    block1_away = to_chip(block1_send)

    def weight_grad(name, act_t, index, own, away):
        return call(
            functools.partial(weight_kernel, layer=index), name,
            [((batches // 2, shard_rows, BLK), BF16)] * 2,
            [((C, 2 * PIX), BF16), ((2 * PIX, 9 * BLK), BF16), ((3, PIX + 2 * PAD, BLK), BF16),
             ((9 * C, BLK), F32)],
            18, kinds, act_t, half_t, core_half_t, own, away,
        )

    keep2, send2 = weight_grad("weight2", act2_t, 1, after(block2, block1), block2_away)
    got2 = to_batch(send2, 1)

    def spread(name, bit, keep, got, tail=None, behind=()):
        ways = 1 << min(2, bits - bit)
        rows = keep.shape[1]
        shape = (keep.shape[0] // ways, rows + (VECS if tail else 0), keep.shape[2])
        parts = call(
            functools.partial(route_kernel, bit=bit, first=0), name + str(bit),
            [(shape, BF16)] * ways, [], 16, keep, got, smem=0,
        )
        if tail:
            parts = call(
                functools.partial(route_kernel, bit=bit, first=rows), name + "tail",
                [(shape, BF16)] * ways, [], 16, *tail, *parts, smem=0,
                aliases={2 + j: j for j in range(ways)},
            )
        return parts, [to_batch(after(parts[j], *behind), j << bit) for j in range(1, ways)]

    def finish(name, parts, got):
        for bit in range(3, bits, 2):
            added = total_of([parts[0]] + got).astype(BF16)
            parts, got = spread(name, bit, added, jnp.zeros_like(added))
        return call(
            sum_kernel, "sum" + name, [(parts[0].shape[1:], BF16)], [], 8, parts[0], *got, smem=0
        )[0]

    def gather(shard, *between):
        far = to_chip(shard)
        near = to_core(shard)
        return shard, far, near, to_core(after(far, *between))

    parts_a, got_a = spread("routea", 1, after(attn_keep, send2), attn_got)
    keep1, send1 = weight_grad("weight1", act1_t, 0, after(block1, *parts_a), block1_away)
    got1 = to_batch(send1, 1)
    shard_a = finish("routea", parts_a, [after(g, send1) for g in got_a])
    parts_b, got_b = spread("routeb", 1, after(keep2, send1, shard_a), got2)
    out_own, grad_own, image_send, vec_keep, vec_send = call(
        fourth_kernel, "fourth",
        [((192, C), BF16), ((192, C), BF16), ((2, 128, C), BF16),
         ((batches // 2, VECS, BLK), BF16), ((batches // 2, VECS, BLK), BF16)],
        [shifts, img32, img16, ((VECS, C), F32)], 14,
        kinds, after(grad1, *parts_b), image, stats, grad_middle, middle, mixed, vecs,
        conv1_weight, proj_weight, vec_a, vec_b,
    )
    image_away = to_chip(image_send)
    vec_got = to_batch(vec_send, 1)
    parts_c, got_c = spread("routec", 1, keep1, got1, (vec_keep, vec_got), behind=got_b)
    shard_b = finish("routeb", parts_b, [after(g, parts_c[0]) for g in got_b])
    gathered_a = gather(shard_a)
    gathered_b = gather(shard_b)
    shard_c = finish(
        "routec", parts_c, [after(g, gathered_b[1], gathered_a[1]) for g in got_c]
    )
    small = call(
        join_attn_kernel, "joina", [((small_rows, C), F32)] * 4, [], 8,
        after(gathered_a[0], shard_c), *gathered_a[1:], smem=0,
    )
    (whole2,) = call(
        join_kernel, "joinb", [((shard_rows, C), F32)], [], 8,
        after(gathered_b[0], shard_c), *gathered_b[1:], smem=0,
    )
    outputs, input_grad = call(
        unpack_kernel, "unpack",
        [(inputs.shape, BF16)] * 2, [], 8,
        kinds, out_own, grad_own, after(image_away, shard_c),
    )
    gathered_c = gather(shard_c, whole2, outputs, *small)
    whole1, *sums = call(
        join_kernel, "joinc", [((shard_rows, C), F32)] + [((1, small_rows), F32)] * 11, [], 8,
        *gathered_c, smem=0,
    )
    v = [row.reshape(small_rows) for row in sums]

    return (
        outputs, input_grad,
        v[9], v[10], whole1, v[8],
        v[6], v[7], whole2, v[5],
        v[0], v[1],
        small[0], v[2], small[1], small[2], v[3], small[3], v[4],
    )


def solution(mesh):
    image = P("batch", "height", None, None)
    vector = P("batch")
    matrix = P("batch", None)
    return jax.shard_map(
        on_device,
        mesh=mesh,
        in_specs=(image, vector) + (P(),) * 17 + (image,),
        out_specs=(
            image, image,
            vector, vector, matrix, vector,
            vector, vector, matrix, vector,
            vector, vector,
            matrix, vector, matrix, matrix, vector, matrix, vector,
        ),
        check_vma=False,
    )
```
